32 devices in a mesh: parts: 2 (over x), row: 16 (over z, y, core).
Axes of the slice: x: 2, y: 2, z: 4, core: 2. Of those that a mesh axis runs over, the one named last changes fastest.
Arguments:
- features: bfloat16 [768, 32, 512], P(('parts', 'row')), parts along dimension 0, may hold values from -40 to 40
- row_bands: int32 [32], P('parts'), parts along dimension 0, may hold values from 1 to 3, as said below
- w_expand: bfloat16 [512, 2048], replicated, may hold values from -0.25 to 0.25
- kernel: bfloat16 [9, 2048], replicated, may hold values from -2 to 2
- w_project: bfloat16 [2048, 512], replicated, may hold values from -0.125 to 0.125
- w_qkv: bfloat16 [512, 1536], replicated, may hold values from -0.25 to 0.25
- w_out: bfloat16 [512, 512], replicated, may hold values from -0.25 to 0.25
- cotangent: bfloat16 [768, 32, 512], P(('parts', 'row')), parts along dimension 0, may hold values from -6 to 6
Outputs:
- block_out: bfloat16 [768, 32, 512], P(('parts', 'row')), parts along dimension 0
- input_grad: bfloat16 [768, 32, 512], P(('parts', 'row')), parts along dimension 0
The draws below stay inside these ranges and needn't reach their ends.
There are 2 independent parts, one for each index of `parts`. The reference program is written for one: setup_inputs(seed, part) draws one part's arguments, and reference() takes and returns one part's arrays. A program takes and returns all parts, laid end to end along the dimension named above; an argument that names none is the same for every part. Nothing has to cross between parts.
Inputs may be any that keep to these rules, and one draw needn't show every extreme that they name: `row_bands`: devices 2k and 2k + 1 together hold 32 rows of the slab.
All inputs are finite; a program needn't handle non-finite values.
Results may differ from the reference program's by a relative error of at most 0.007.
Values may be sent and summed in bfloat16 or wider, within the bound.
No kernel may reach another device: no remote copies, remote signals or barrier semaphores. Data moves between devices by JAX's collectives and lax.ppermute only.
A program may use at most 256 MiB of HBM per device.

```python
import math
import jax
import jax.numpy as jnp
from jax import lax

C = 512
HID = 2048
HEADS = 16
ROWS_MEAN = 16
COLS = 32
CAP = 24
ROWS = 256
N_ROW = 16


def draw_features(key, part):
    key = jax.random.fold_in(key, 5)
    subkeys = jax.random.split(key, 3)
    shape = (N_ROW * CAP, COLS, C)
    base = jax.random.truncated_normal(subkeys[0], -4.0, 4.0, shape, jnp.float32)
    spread = math.log(10.0)
    token_scale = jnp.exp(jax.random.uniform(subkeys[1], (N_ROW * CAP, COLS, 1), jnp.float32, -0.5, 0.5) * spread)
    channel_scale = jnp.exp(jax.random.uniform(subkeys[2], (1, 1, C), jnp.float32, -0.5, 0.5) * spread)
    return (base * token_scale * channel_scale).astype(jnp.bfloat16)


def draw_row_bands(key, part):
    key = jax.random.fold_in(key, 11)
    middle = ROWS_MEAN // 8
    shifts = jax.random.randint(key, (N_ROW // 2,), -1, 2)
    shifts = shifts.at[0].set(1)
    paired = jnp.stack([middle + shifts, middle - shifts], axis=1)
    return paired.reshape(N_ROW).astype(jnp.int32)


def block_scale(own_key, dims, cuts, smallest, high):
    loudness, own = 1.0, jax.random.fold_in(own_key, 6)
    for position, parts in cuts:
        draws = jnp.exp(jax.random.uniform(jax.random.fold_in(own, position), (parts,), jnp.float32, smallest / len(cuts), high / len(cuts)))
        loudness = loudness * jnp.repeat(draws, dims[position] // parts).reshape([-1 if axis == position else 1 for axis in range(len(dims))])
    return loudness


def gaussian(rng, dims, scale, most, cuts=(), kind=jnp.bfloat16):
    loudness = block_scale(rng, dims, cuts, -0.22, 0.18) if cuts else 1.0
    array = jax.random.normal(rng, dims, jnp.float32) * scale * loudness
    return jnp.minimum(jnp.maximum(array, -most), most).astype(kind)


def setup_inputs(seed: int = 0, part: int = 0) -> dict:
    keys = jax.random.split(jax.random.key(seed), 9)
    part_keys = jax.random.split(jax.random.fold_in(keys[8], part), 9)
    return {
        "features": draw_features(jax.random.fold_in(jax.random.fold_in(keys[8], part), 71), part),
        "row_bands": draw_row_bands(jax.random.fold_in(jax.random.fold_in(keys[8], part), 71), part),
        "w_expand": gaussian(keys[2], (C, HID), C ** -0.5, 0.25),
        "kernel": gaussian(keys[3], (9, HID), 9 ** -0.5, 2.0),
        "w_project": gaussian(keys[4], (HID, C), HID ** -0.5, 0.125),
        "w_qkv": gaussian(keys[5], (C, 3 * C), C ** -0.5, 0.25),
        "w_out": gaussian(keys[6], (C, C), C ** -0.5, 0.25),
        "cotangent": gaussian(part_keys[7], (N_ROW * CAP, COLS, C), 1.0, 6.0, ((0, 16),)),
    }


EPSILON = 1e-06

def matmul(left, weight):
    flat = left.reshape(-1, left.shape[-1])
    result = jnp.dot(flat, weight, preferred_element_type=jnp.float32)
    return result.reshape(left.shape[:-1] + (weight.shape[1],))

def gelu_slope(values):
    return jax.vjp(jax.nn.gelu, values)[1](jnp.ones_like(values))[0]

def depthwise(fields, kernel):
    height, width_cols = (fields.shape[0], fields.shape[1])
    padded = jnp.pad(fields.astype(jnp.float32), ((1, 1), (1, 1), (0, 0)))
    total = jnp.zeros(fields.shape, jnp.float32)
    for offset_row in range(3):
        for offset_col in range(3):
            tap = kernel[3 * offset_row + offset_col].astype(jnp.float32)
            total = total + tap * padded[offset_row:offset_row + height, offset_col:offset_col + width_cols]
    return total

def depthwise_adjoint(fields, kernel):
    height, width_cols = (fields.shape[0], fields.shape[1])
    padded = jnp.pad(fields.astype(jnp.float32), ((1, 1), (1, 1), (0, 0)))
    total = jnp.zeros(fields.shape, jnp.float32)
    for offset_row in range(3):
        for offset_col in range(3):
            tap = kernel[3 * offset_row + offset_col].astype(jnp.float32)
            total = total + tap * padded[2 - offset_row:2 - offset_row + height, 2 - offset_col:2 - offset_col + width_cols]
    return total

def into_windows(fields):
    height, width_cols = (fields.shape[0], fields.shape[1])
    trailing = fields.shape[2:]
    shaped = fields.reshape((8, height // 8, 8, width_cols // 8) + trailing)
    order = (1, 3, 0, 2) + tuple(range(4, 4 + len(trailing)))
    return jnp.transpose(shaped, order).reshape((height // 8 * (width_cols // 8), 64) + trailing)

def out_of_windows(windows, height, width_cols):
    trailing = windows.shape[2:]
    shaped = windows.reshape((height // 8, width_cols // 8, 8, 8) + trailing)
    order = (2, 0, 3, 1) + tuple(range(4, 4 + len(trailing)))
    return jnp.transpose(shaped, order).reshape((height, width_cols) + trailing)

def rms_scale(values):
    return lax.rsqrt(lax.optimization_barrier(jnp.mean(values * values, -1, keepdims=True)) + EPSILON)

def reference(features, row_bands, w_expand, kernel, w_project, w_qkv, w_out, cotangent):
    capacity = features.shape[0] // N_ROW
    head_dim = C // HEADS
    scale = 1.0 / math.sqrt(head_dim)
    live = jnp.arange(capacity)[None, :] < (8 * row_bands)[:, None]
    order = jnp.nonzero(live.reshape(-1), size=ROWS)[0].astype(jnp.int32)
    slab = jnp.take(features, order, axis=0)
    grad_slab = jnp.take(cotangent, order, axis=0)
    inputs32 = slab.astype(jnp.float32)
    rms_one = rms_scale(inputs32)
    normed_one = inputs32 * rms_one
    expanded = matmul(normed_one.astype(jnp.bfloat16), w_expand)
    hidden_one = jax.nn.gelu(expanded).astype(jnp.bfloat16)
    mixed = depthwise(hidden_one, kernel)
    hidden_two = jax.nn.gelu(mixed).astype(jnp.bfloat16)
    first_out = inputs32 + matmul(hidden_two, w_project)
    rms_two = rms_scale(first_out)
    normed_two = first_out * rms_two
    projected = matmul(normed_two.astype(jnp.bfloat16), w_qkv).astype(jnp.bfloat16)
    grouped = into_windows(projected.reshape(ROWS, COLS, 3, HEADS, head_dim)).astype(jnp.float32)
    query_rows = grouped[:, :, 0]
    key_rows = grouped[:, :, 1]
    value_rows = grouped[:, :, 2]
    scores = jnp.einsum('nthd,nshd->nhts', query_rows, key_rows) * scale
    weights = jnp.exp(scores)
    weights = weights / lax.optimization_barrier(jnp.sum(weights, -1, keepdims=True))
    weights_half = lax.optimization_barrier(weights.astype(jnp.bfloat16))
    attended = jnp.einsum('nhts,nshd->nthd', weights_half.astype(jnp.float32), value_rows).astype(jnp.bfloat16)
    attended_slab = out_of_windows(attended, ROWS, COLS).reshape(ROWS, COLS, C)
    final = first_out + matmul(attended_slab, w_out)
    grad_attended = matmul(grad_slab, w_out.T).astype(jnp.bfloat16)
    grad_windows = into_windows(grad_attended.reshape(ROWS, COLS, HEADS, head_dim)).astype(jnp.float32)
    grad_weights = jnp.einsum('nthd,nshd->nhts', grad_windows, value_rows)
    grad_values = jnp.einsum('nhts,nthd->nshd', weights_half.astype(jnp.float32), grad_windows)
    row_dot = lax.optimization_barrier(jnp.sum(weights * grad_weights, -1, keepdims=True))
    grad_scores = lax.optimization_barrier((weights * (grad_weights - row_dot)).astype(jnp.bfloat16))
    grad_scores = grad_scores.astype(jnp.float32)
    grad_queries = jnp.einsum('nhts,nshd->nthd', grad_scores, key_rows) * scale
    grad_keys = jnp.einsum('nhts,nthd->nshd', grad_scores, query_rows) * scale
    stacked = jnp.stack([grad_queries, grad_keys, grad_values], 2).astype(jnp.bfloat16)
    grad_projected = out_of_windows(stacked, ROWS, COLS).reshape(ROWS, COLS, 3 * C)
    grad_normed_two = matmul(grad_projected, w_qkv.T)
    grad_first = grad_slab.astype(jnp.float32) + rms_two * (grad_normed_two - normed_two * lax.optimization_barrier(jnp.mean(grad_normed_two * normed_two, -1, keepdims=True)))
    grad_hidden_two = matmul(grad_first.astype(jnp.bfloat16), w_project.T)
    grad_mixed = (grad_hidden_two * gelu_slope(mixed)).astype(jnp.bfloat16)
    grad_hidden_one = depthwise_adjoint(grad_mixed, kernel)
    grad_expanded = (grad_hidden_one * gelu_slope(expanded)).astype(jnp.bfloat16)
    grad_normed_one = matmul(grad_expanded, w_expand.T)
    grad_input = grad_first + rms_one * (grad_normed_one - normed_one * lax.optimization_barrier(jnp.mean(grad_normed_one * normed_one, -1, keepdims=True)))
    output_rows = jnp.zeros(features.shape, jnp.bfloat16).at[order].set(final.astype(jnp.bfloat16))
    gradient_rows = jnp.zeros(features.shape, jnp.bfloat16).at[order].set(grad_input.astype(jnp.bfloat16))
    return (output_rows, gradient_rows)
```

```python
import math

import jax
import jax.numpy as jnp
from jax import lax
from jax.experimental import pallas as pl
from jax.experimental.pallas import tpu as pltpu
from jax.sharding import PartitionSpec as P

HEADS = 16
GRID_ROWS = 16
BAND = 8
RIM = 2
EPSILON = 1e-06
CHUNK = 256
ROOT = math.sqrt(2.0 / math.pi)
CUBIC = 0.044715
F32 = jnp.float32
BF16 = jnp.bfloat16
VMEM_LIMIT = 56 * 1024 * 1024


def nt_dot(left, right):
    return lax.dot_general(left, right, (((1,), (1,)), ((), ())), preferred_element_type=F32)


def tn_dot(left, right):
    return lax.dot_general(left, right, (((0,), (0,)), ((), ())), preferred_element_type=F32)


def nn_dot(left, right):
    return jnp.dot(left, right, preferred_element_type=F32)


def rms_scale(values):
    return lax.rsqrt(jnp.mean(values * values, -1, keepdims=True) + EPSILON)


def gelu_and_slope(v):
    square = v * v
    cdf = 0.5 + 0.5 * jnp.tanh(v * (ROOT + (ROOT * CUBIC) * square))
    value = v * cdf
    slope = cdf + (value - value * cdf) * (2.0 * ROOT + (6.0 * ROOT * CUBIC) * square)
    return value, slope


def whole(shape, space=None):
    zeros = (0,) * len(shape)
    return pl.BlockSpec(shape, lambda *_: zeros)


def params():
    return pltpu.CompilerParams(vmem_limit_bytes=VMEM_LIMIT)


def assemble_body(index_ref, features_ref, cotangent_ref, pair_ref, edge_ref, slab_ref, grad_ref, both):
    capacity = features_ref.shape[0]
    sent = GRID_ROWS - BAND + RIM
    both[0:capacity] = features_ref[...]
    both[capacity : capacity + sent] = pair_ref[0:sent]
    both[capacity + sent : capacity + sent + RIM] = edge_ref[...]
    for row in range(GRID_ROWS + 2 * RIM):
        slab_ref[row] = both[index_ref[row]]
    both[0:capacity] = cotangent_ref[...]
    both[capacity : capacity + BAND] = pair_ref[sent : sent + BAND]
    for row in range(GRID_ROWS):
        grad_ref[row] = both[index_ref[GRID_ROWS + 2 * RIM + row]]


def assemble(index, features, cotangent, pair_rows, edge_rows):
    capacity, cols, width = features.shape
    sent = GRID_ROWS - BAND + RIM
    return pl.pallas_call(
        assemble_body,
        in_specs=[
            pl.BlockSpec(memory_space=pltpu.SMEM),
            whole(features.shape),
            whole(cotangent.shape),
            whole(pair_rows.shape),
            whole(edge_rows.shape),
        ],
        out_specs=[whole((GRID_ROWS + 2 * RIM, cols, width)), whole((GRID_ROWS, cols, width))],
        out_shape=[
            jax.ShapeDtypeStruct((GRID_ROWS + 2 * RIM, cols, width), BF16),
            jax.ShapeDtypeStruct((GRID_ROWS, cols, width), BF16),
        ],
        grid=(1,),
        scratch_shapes=[pltpu.VMEM((capacity + sent + RIM, cols, width), BF16)],
        compiler_params=params(),
        name="assemble",
    )(index, features, cotangent, pair_rows, edge_rows)


def column_sums(total_left, total_mid, total_right, column, last):
    from_left = pltpu.roll(total_left, 1, 0)
    from_right = pltpu.roll(total_right, last, 0)
    return (
        total_mid
        + jnp.where(column == 0, 0.0, from_left)
        + jnp.where(column == last, 0.0, from_right)
    )


def forward_body(slab_ref, expand_ref, taps_ref, project_ref, first_ref, normed_ref, slope_one_ref,
                 slope_two_ref, normed_one, hidden, hidden_two, total):
    step = pl.program_id(0)
    rows, cols, width = slab_ref.shape
    own = rows - 2 * RIM
    chunk = expand_ref.shape[1]

    @pl.when(step == 0)
    def _():
        values = slab_ref[...].astype(F32).reshape(rows * cols, width)
        normed_one[...] = (values * rms_scale(values)).astype(BF16)
        total[...] = values[RIM * cols : (RIM + own) * cols]

    def expand(row, carry):
        start = pl.multiple_of(row * (2 * cols), 2 * cols)
        expanded = nn_dot(normed_one[pl.ds(start, 2 * cols), :], expand_ref[...])
        value, slope = gelu_and_slope(expanded)
        hidden[pl.ds(2 * row, 2)] = value.astype(BF16).astype(F32).reshape(2, cols, chunk)
        slope_one_ref[pl.ds(2 * row, 2)] = slope.astype(BF16).reshape(2, cols, chunk)
        return carry

    lax.fori_loop(0, rows // 2, expand, 0, unroll=2)

    taps = taps_ref[...].astype(F32)
    column = lax.broadcasted_iota(jnp.int32, (cols, chunk), 0)

    def mix(row, carry):
        above, here, below = hidden[row], hidden[row + 1], hidden[row + 2]
        sums = [
            taps[b : b + 1] * above + taps[3 + b : 4 + b] * here + taps[6 + b : 7 + b] * below
            for b in range(3)
        ]
        mixed = column_sums(sums[0], sums[1], sums[2], column, cols - 1)
        value, slope = gelu_and_slope(mixed)
        hidden_two[pl.ds(pl.multiple_of(row * cols, cols), cols), :] = value.astype(BF16)
        slope_two_ref[row] = slope.astype(BF16)
        return carry

    lax.fori_loop(0, rows - 2, mix, 0, unroll=2)
    total[...] += nn_dot(hidden_two[cols : cols + own * cols, :], project_ref[...])

    @pl.when(step == pl.num_programs(0) - 1)
    def _():
        first = total[...]
        first_ref[...] = first.reshape(own, cols, width)
        normed_ref[...] = (first * rms_scale(first)).astype(BF16).reshape(own, cols, width)


def forward(slab, w_expand, kernel, w_project):
    rows, cols, width = slab.shape
    own = rows - 2 * RIM
    hidden_width = w_expand.shape[1]
    steps = hidden_width // CHUNK
    return pl.pallas_call(
        forward_body,
        grid=(steps,),
        in_specs=[
            whole(slab.shape),
            pl.BlockSpec((width, CHUNK), lambda j: (0, j)),
            pl.BlockSpec((9, CHUNK), lambda j: (0, j)),
            pl.BlockSpec((CHUNK, width), lambda j: (j, 0)),
        ],
        out_specs=[
            whole((own, cols, width)),
            whole((own, cols, width)),
            pl.BlockSpec((rows, cols, CHUNK), lambda j: (0, 0, j)),
            pl.BlockSpec((rows - 2, cols, CHUNK), lambda j: (0, 0, j)),
        ],
        out_shape=[
            jax.ShapeDtypeStruct((own, cols, width), F32),
            jax.ShapeDtypeStruct((own, cols, width), BF16),
            jax.ShapeDtypeStruct((rows, cols, hidden_width), BF16),
            jax.ShapeDtypeStruct((rows - 2, cols, hidden_width), BF16),
        ],
        scratch_shapes=[
            pltpu.VMEM((rows * cols, width), BF16),
            pltpu.VMEM((rows, cols, CHUNK), F32),
            pltpu.VMEM(((rows - 2) * cols, CHUNK), BF16),
            pltpu.VMEM((own * cols, width), F32),
        ],
        compiler_params=params(),
        cost_estimate=pl.CostEstimate(
            flops=4 * rows * cols * width * hidden_width,
            bytes_accessed=12 * 1024 * 1024,
            transcendentals=2 * rows * cols * hidden_width,
        ),
        name="bottleneck_forward",
    )(slab, w_expand, kernel, w_project)


def attention_body(normed_ref, cotangent_ref, qkv_ref, out_ref, attended_ref, grad_ref,
                   projected, grad_attended, grad_projected, attended):
    groups, _, cols, width = normed_ref.shape
    tokens = groups * cols
    windows = cols // 8
    span = groups * 8
    head_dim = width // HEADS
    lanes = 128
    heads = lanes // head_dim
    scale = 1.0 / math.sqrt(head_dim)

    inner = lax.broadcasted_iota(jnp.int32, (tokens, tokens), 0)
    outer = lax.broadcasted_iota(jnp.int32, (tokens, tokens), 1)

    def window_place(order):
        return (order // 8) % groups * cols + order % 8 * windows + order // span

    to_windows = (window_place(inner) == outer).astype(BF16)
    to_rows = (window_place(outer) == inner).astype(BF16)

    normed = nn_dot(to_windows, normed_ref[...].reshape(tokens, width)).astype(BF16)
    projected[...] = nn_dot(normed, qkv_ref[...]).astype(BF16)
    grad_rows = nn_dot(to_windows, cotangent_ref[...].reshape(tokens, width)).astype(BF16)
    grad_attended[...] = nt_dot(grad_rows, out_ref[...]).astype(BF16)

    lane_head = lax.broadcasted_iota(jnp.int32, (heads, span, lanes), 2) // head_dim
    own_head = lane_head == lax.broadcasted_iota(jnp.int32, (heads, span, lanes), 0)

    def spread(values):
        zeros = jnp.zeros((heads, span, lanes), F32)
        wide = jnp.where(own_head, values.astype(F32)[None], zeros)
        return wide.astype(BF16).reshape(heads * span, lanes)

    def collect(values):
        return jnp.sum(jnp.where(own_head, values.reshape(heads, span, lanes), 0.0), axis=0)

    def window(index, carry):
        rows = pl.ds(pl.multiple_of(index * span, span), span)
        for part in range(width // lanes):
            at = part * lanes
            q = projected[rows, at : at + lanes]
            k = projected[rows, width + at : width + at + lanes]
            v = projected[rows, 2 * width + at : 2 * width + at + lanes]
            g = grad_attended[rows, at : at + lanes]
            q_wide = spread(q)
            g_wide = spread(g)
            scores = nt_dot(k, q_wide) * scale
            powers = jnp.exp(scores - jnp.max(scores, axis=0, keepdims=True))
            weights = powers / jnp.sum(powers, axis=0, keepdims=True)
            half = weights.astype(BF16)
            grad_weights = nt_dot(v, g_wide)
            row_dot = jnp.sum(weights * grad_weights, axis=0, keepdims=True)
            grad_scores = (weights * (grad_weights - row_dot)).astype(BF16)
            attended[rows, at : at + lanes] = collect(tn_dot(half, v)).astype(BF16)
            grad_projected[rows, at : at + lanes] = (
                collect(tn_dot(grad_scores, k)) * scale
            ).astype(BF16)
            grad_projected[rows, width + at : width + at + lanes] = (
                nn_dot(grad_scores, q_wide) * scale
            ).astype(BF16)
            grad_projected[rows, 2 * width + at : 2 * width + at + lanes] = nn_dot(
                half, g_wide
            ).astype(BF16)
        return carry

    lax.fori_loop(0, windows, window, 0)

    grad_normed = nt_dot(grad_projected[...], qkv_ref[...]).astype(BF16)
    shape = (groups, 1, cols, width)
    grad_ref[...] = nn_dot(to_rows, grad_normed).astype(BF16).reshape(shape)
    attended_ref[...] = nn_dot(to_rows, attended[...]).astype(BF16).reshape(shape)


def attention(normed, cotangent, w_qkv, w_out):
    groups, own, cols, width = normed.shape
    tokens = groups * cols
    block = pl.BlockSpec((groups, 1, cols, width), lambda r: (0, r, 0, 0))
    out = jax.ShapeDtypeStruct(normed.shape, BF16)
    return pl.pallas_call(
        attention_body,
        grid=(own,),
        in_specs=[block, block, whole(w_qkv.shape), whole(w_out.shape)],
        out_specs=[block, block],
        out_shape=[out, out],
        scratch_shapes=[
            pltpu.VMEM((tokens, 3 * width), BF16),
            pltpu.VMEM((tokens, width), BF16),
            pltpu.VMEM((tokens, 3 * width), BF16),
            pltpu.VMEM((tokens, width), BF16),
        ],
        compiler_params=params(),
        cost_estimate=pl.CostEstimate(
            flops=20 * own * tokens * width * width,
            bytes_accessed=4 * 1024 * 1024,
            transcendentals=own * tokens * 64 * HEADS,
        ),
        name="window_attention",
    )(normed, cotangent, w_qkv, w_out)


def norm_grad_body(first_ref, grad_ref, cotangent_ref, grad_first_ref, grad_half_ref):
    rows, cols, width = first_ref.shape
    first = first_ref[...]
    rms = rms_scale(first)
    normed = first * rms
    grad = grad_ref[...].astype(F32)
    inner = jnp.mean(grad * normed, -1, keepdims=True)
    result = cotangent_ref[...].astype(F32) + rms * (grad - normed * inner)
    grad_first_ref[...] = result
    grad_half_ref[...] = result.astype(BF16)


def norm_grad(first, grad, cotangent):
    rows, cols, width = first.shape
    block = pl.BlockSpec((4, cols, width), lambda r: (r, 0, 0))
    return pl.pallas_call(
        norm_grad_body,
        grid=(rows // 4,),
        in_specs=[block, block, block],
        out_specs=[block, block],
        out_shape=[
            jax.ShapeDtypeStruct(first.shape, F32),
            jax.ShapeDtypeStruct(first.shape, BF16),
        ],
        compiler_params=params(),
        name="norm_grad",
    )(first, grad, cotangent)


def backward_body(slab_ref, grad_first_ref, half_ref, above_ref, below_ref, slope_one_ref, slope_two_ref,
                  expand_ref, taps_ref, project_ref, out_ref, grad_rows, mixed, expanded, total):
    step = pl.program_id(0)
    own, cols, width = half_ref.shape
    chunk = expand_ref.shape[1]

    @pl.when(step == 0)
    def _():
        grad_rows[0:cols] = above_ref[...].reshape(cols, width)
        grad_rows[cols : cols + own * cols] = half_ref[...].reshape(own * cols, width)
        grad_rows[cols + own * cols :] = below_ref[...].reshape(cols, width)
        total[...] = jnp.zeros_like(total)

    def spread(row, carry):
        start = pl.multiple_of(row * (2 * cols), 2 * cols)
        grad = nt_dot(grad_rows[pl.ds(start, 2 * cols), :], project_ref[...])
        slope = slope_two_ref[pl.ds(2 * row, 2)].astype(F32).reshape(2 * cols, chunk)
        mixed[pl.ds(2 * row, 2)] = (grad * slope).astype(BF16).astype(F32).reshape(2, cols, chunk)
        return carry

    lax.fori_loop(0, (own + 2) // 2, spread, 0, unroll=2)

    taps = taps_ref[...].astype(F32)
    column = lax.broadcasted_iota(jnp.int32, (cols, chunk), 0)

    def unmix(row, carry):
        above, here, below = mixed[row], mixed[row + 1], mixed[row + 2]
        sums = [
            taps[8 - b : 9 - b] * above + taps[5 - b : 6 - b] * here + taps[2 - b : 3 - b] * below
            for b in range(3)
        ]
        grad = column_sums(sums[0], sums[1], sums[2], column, cols - 1)
        slope = slope_one_ref[row + RIM].astype(F32)
        expanded[pl.ds(pl.multiple_of(row * cols, cols), cols), :] = (grad * slope).astype(BF16)
        return carry

    lax.fori_loop(0, own, unmix, 0, unroll=2)
    total[...] += nt_dot(expanded[...], expand_ref[...])

    @pl.when(step == pl.num_programs(0) - 1)
    def _():
        values = slab_ref[RIM : RIM + own].astype(F32).reshape(own * cols, width)
        rms = rms_scale(values)
        normed = values * rms
        grad = total[...]
        inner = jnp.mean(grad * normed, -1, keepdims=True)
        result = grad_first_ref[...].reshape(own * cols, width) + rms * (grad - normed * inner)
        out_ref[...] = result.astype(BF16).reshape(own, cols, width)


def backward(slab, grad_first, grad_half, above, below, slope_one, slope_two, w_expand, kernel, w_project):
    own, cols, width = grad_half.shape
    hidden_width = w_expand.shape[1]
    rows = slab.shape[0]
    return pl.pallas_call(
        backward_body,
        grid=(hidden_width // CHUNK,),
        in_specs=[
            whole(slab.shape),
            whole(grad_first.shape),
            whole(grad_half.shape),
            whole(above.shape),
            whole(below.shape),
            pl.BlockSpec((rows, cols, CHUNK), lambda j: (0, 0, j)),
            pl.BlockSpec((rows - 2, cols, CHUNK), lambda j: (0, 0, j)),
            pl.BlockSpec((width, CHUNK), lambda j: (0, j)),
            pl.BlockSpec((9, CHUNK), lambda j: (0, j)),
            pl.BlockSpec((CHUNK, width), lambda j: (j, 0)),
        ],
        out_specs=whole((own, cols, width)),
        out_shape=jax.ShapeDtypeStruct((own, cols, width), BF16),
        scratch_shapes=[
            pltpu.VMEM(((own + 2) * cols, width), BF16),
            pltpu.VMEM((own + 2, cols, CHUNK), F32),
            pltpu.VMEM((own * cols, CHUNK), BF16),
            pltpu.VMEM((own * cols, width), F32),
        ],
        compiler_params=params(),
        cost_estimate=pl.CostEstimate(
            flops=4 * rows * cols * width * hidden_width,
            bytes_accessed=12 * 1024 * 1024,
            transcendentals=0,
        ),
        name="bottleneck_backward",
    )(slab, grad_first, grad_half, above, below, slope_one, slope_two, w_expand, kernel, w_project)


def project_body(first_ref, attended_ref, out_ref, final_ref):
    rows, cols, width = first_ref.shape
    added = nn_dot(attended_ref[...].reshape(rows * cols, width), out_ref[...])
    final_ref[...] = (first_ref[...] + added.reshape(rows, cols, width)).astype(BF16)


def project(first, attended, w_out):
    rows, cols, width = first.shape
    block = pl.BlockSpec((4, cols, width), lambda r: (r, 0, 0))
    return pl.pallas_call(
        project_body,
        grid=(rows // 4,),
        in_specs=[block, block, whole(w_out.shape)],
        out_specs=block,
        out_shape=jax.ShapeDtypeStruct(first.shape, BF16),
        compiler_params=params(),
        name="output_projection",
    )(first, attended, w_out)


def window_groups(size):
    stride = size // 8
    return [[first + stride * k for k in range(8)] for first in range(stride)]


def exchange_windows(rows):
    return lax.all_to_all(
        rows, "row", split_axis=0, concat_axis=0, tiled=True, axis_index_groups=window_groups(lax.axis_size("row"))
    )


def swap_pair(rows):
    size = lax.axis_size("row")
    return lax.ppermute(rows, "row", [(i, i ^ 1) for i in range(size)])


def place_rows(even, parity, leader_share):
    size = GRID_ROWS
    first, second = even[:BAND], even[BAND:]
    other = swap_pair(jnp.where(parity == 0, second, first))
    share = jnp.where(parity == 0, leader_share, 2 * size - leader_share)
    zeros = jnp.zeros_like(first)
    leads = parity == 0
    low = jnp.where(leads | (share == size), first, jnp.where(share < size, second, other))
    mid = jnp.where(share < size, zeros, jnp.where(leads | (share == size), second, first))
    high = jnp.where(share > size, jnp.where(leads, other, second), zeros)
    return jnp.concatenate([low, mid, high], 0)


def on_device(features, row_bands, w_expand, kernel, w_project, w_qkv, w_out, cotangent):
    capacity, cols, width = features.shape
    size = lax.axis_size("row")
    device = lax.axis_index("row")
    parity = device % 2
    leads = parity == 0
    leader_share = BAND * row_bands[device - parity]
    own_share = BAND * row_bands[device]
    sent = GRID_ROWS - BAND + RIM

    payload = jnp.concatenate(
        [
            lax.dynamic_slice_in_dim(features, jnp.where(leads, capacity - sent, 0), sent, 0),
            lax.dynamic_slice_in_dim(cotangent, jnp.where(leads, capacity - BAND, 0), BAND, 0),
        ],
        0,
    )
    pair_rows = swap_pair(payload)
    rim = lax.dynamic_slice_in_dim(features, jnp.where(leads, 0, own_share - RIM), RIM, 0)
    pairs = [(i, i + 1) for i in range(1, size - 1, 2)]
    edge_rows = lax.ppermute(rim, "row", pairs + [(j, i) for i, j in pairs])

    place = jnp.arange(GRID_ROWS + 2 * RIM) - RIM + GRID_ROWS * parity
    in_own = jnp.where(leads, place < leader_share, place >= leader_share)
    own_index = jnp.where(leads, place, place - leader_share)
    pair_index = jnp.where(leads, place - leader_share, place - (GRID_ROWS - RIM))
    slab_index = jnp.where(in_own, own_index, capacity + pair_index)
    slab_index = jnp.where(leads & (place < 0), capacity + sent + RIM + place, slab_index)
    beyond = place - 2 * GRID_ROWS
    slab_index = jnp.where(~leads & (beyond >= 0), capacity + sent + beyond, slab_index)
    pair_index = jnp.where(leads, place - leader_share, place - GRID_ROWS)
    grad_index = jnp.where(in_own, own_index, capacity + pair_index)[RIM : RIM + GRID_ROWS]
    index = jnp.concatenate([slab_index, grad_index]).astype(jnp.int32)

    slab, grad_slab = assemble(index, features, cotangent, pair_rows, edge_rows)
    grad_windows = exchange_windows(grad_slab)
    first, normed, slope_one, slope_two = forward(slab, w_expand, kernel, w_project)
    normed_windows = exchange_windows(normed)
    shape = (8, GRID_ROWS // 8, cols, width)
    attended, grad_normed = attention(
        normed_windows.reshape(shape), grad_windows.reshape(shape), w_qkv, w_out
    )
    grad_normed_rows = exchange_windows(grad_normed.reshape(GRID_ROWS, cols, width))
    attended_rows = exchange_windows(attended.reshape(GRID_ROWS, cols, width))
    grad_first, grad_half = norm_grad(first, grad_normed_rows, grad_slab)
    up = [(i, i + 1) for i in range(size - 1)]
    above = lax.ppermute(grad_half[GRID_ROWS - 1 :], "row", up)
    below = lax.ppermute(grad_half[:1], "row", [(j, i) for i, j in up])
    grad_input = backward(
        slab, grad_first, grad_half, above, below, slope_one, slope_two, w_expand, kernel, w_project
    )
    final = project(first, attended_rows, w_out)
    return (
        place_rows(final, parity, leader_share),
        place_rows(grad_input, parity, leader_share),
    )


def solution(mesh):
    return jax.shard_map(
        on_device,
        mesh=mesh,
        in_specs=(
            P(("parts", "row"), None, None),
            P("parts"),
            P(),
            P(),
            P(),
            P(),
            P(),
            P(("parts", "row"), None, None),
        ),
        out_specs=(P(("parts", "row"), None, None), P(("parts", "row"), None, None)),
        check_vma=False,
    )
```

```python
import math

import jax
import jax.numpy as jnp
import numpy as np
from jax import lax
from jax.experimental import pallas as pl
from jax.experimental.pallas import tpu as pltpu
from jax.sharding import PartitionSpec as P

HEADS = 16
GRID_ROWS = 16
BAND = 8
RIM = 2
EPSILON = 1e-06
CHUNK = 256
LANES = 128
ROOT = math.sqrt(2.0 / math.pi)
CUBIC = 0.044715
F32 = jnp.float32
BF16 = jnp.bfloat16
VMEM_LIMIT = 56 * 1024 * 1024


def nt_dot(left, right):
    return lax.dot_general(left, right, (((1,), (1,)), ((), ())), preferred_element_type=F32)


def tn_dot(left, right):
    return lax.dot_general(left, right, (((0,), (0,)), ((), ())), preferred_element_type=F32)


def nn_dot(left, right):
    return jnp.dot(left, right, preferred_element_type=F32)


def rms_scale(values):
    return lax.rsqrt(jnp.mean(values * values, -1, keepdims=True) + EPSILON)


def gelu_and_slope(v):
    square = v * v
    cdf = 0.5 + 0.5 * jnp.tanh(v * (ROOT + (ROOT * CUBIC) * square))
    value = v * cdf
    slope = cdf + (value - value * cdf) * (2.0 * ROOT + (6.0 * ROOT * CUBIC) * square)
    return value, slope


def whole(shape, space=None):
    zeros = (0,) * len(shape)
    return pl.BlockSpec(shape, lambda *_: zeros)


def params():
    return pltpu.CompilerParams(vmem_limit_bytes=VMEM_LIMIT)


def start_pull(place_ref, index, sources, rows, target, sem):
    first = place_ref[2 * index + 1]
    for number, source in enumerate(sources):

        @pl.when(place_ref[2 * index] == number)
        def _():
            pltpu.make_async_copy(source.at[pl.ds(first, rows)], target, sem).start()


def wait_pull(sources, rows, target, sem):
    pltpu.make_async_copy(sources[0].at[pl.ds(0, rows)], target, sem).wait()


def even_body(place_ref, own_ref, other_ref, out_ref, sems):
    sources = (own_ref, other_ref)
    targets = [out_ref.at[pl.ds(BAND * half, BAND)] for half in range(2)]
    for half in range(2):
        start_pull(place_ref, half, sources, BAND, targets[half], sems.at[half])
    for half in range(2):
        wait_pull(sources, BAND, targets[half], sems.at[half])


def even_rows(places, own, other):
    capacity, cols, width = own.shape
    anywhere = pl.BlockSpec(memory_space=pl.ANY)
    return pl.pallas_call(
        even_body,
        in_specs=[pl.BlockSpec(memory_space=pltpu.SMEM), anywhere, anywhere],
        out_specs=anywhere,
        out_shape=jax.ShapeDtypeStruct((GRID_ROWS, cols, width), own.dtype),
        scratch_shapes=[pltpu.SemaphoreType.DMA((2,))],
        name="even_rows",
    )(places, own, other)


def column_sums(left, mid, right, column, last):
    from_left = jnp.where(column == 0, 0.0, pltpu.roll(left, 1, 0))
    from_right = jnp.where(column == last, 0.0, pltpu.roll(right, last, 0))
    return mid + from_left + from_right


def spread_taps(taps_ref, lanes, cols):
    taps = taps_ref[...].astype(F32)
    return [jnp.broadcast_to(taps[i : i + 1, lanes], (cols, LANES)) for i in range(9)]


def forward_body(place_ref, features_ref, other_ref, rim_ref, expand_ref, taps_ref, project_ref, first_ref,
                 normed_ref, slab_ref, slope_one_ref, slope_two_ref, slab, normed_one, hidden, hidden_two,
                 total, sems):
    step = pl.program_id(0)
    rows, cols, width = slab.shape
    own = rows - 2 * RIM
    chunk = expand_ref.shape[1]

    @pl.when(step == 0)
    def _():
        sources = (features_ref, other_ref, rim_ref)
        pieces = [(0, RIM), (RIM, BAND), (RIM + BAND, BAND), (RIM + 2 * BAND, RIM)]
        for index, (first, count) in enumerate(pieces):
            start_pull(place_ref, index, sources, count, slab.at[pl.ds(first, count)], sems.at[index])
        for index, (first, count) in enumerate(pieces):
            wait_pull(sources, count, slab.at[pl.ds(first, count)], sems.at[index])
        slab_ref[...] = slab[RIM : RIM + own]
        for row in range(0, rows, 2):
            at = slice(row * cols, (row + 2) * cols)
            values = slab[row : row + 2].astype(F32).reshape(2 * cols, width)
            normed_one[at] = (values * rms_scale(values)).astype(BF16)
        total[...] = slab[1 : rows - 1].astype(F32).reshape((rows - 2) * cols, width)

    for row in range(0, rows, 4):
        expanded = nn_dot(normed_one[row * cols : (row + 4) * cols, :], expand_ref[...])
        for inner in range(4):
            for lane in range(0, chunk, LANES):
                lanes = slice(lane, lane + LANES)
                value, slope = gelu_and_slope(expanded[inner * cols : (inner + 1) * cols, lanes])
                hidden[row + inner, :, lanes] = value.astype(BF16).astype(F32)
                if RIM <= row + inner < RIM + own:
                    slope_one_ref[row + inner - RIM, :, lanes] = slope.astype(BF16)

    column = lax.broadcasted_iota(jnp.int32, (cols, LANES), 0)
    for lane in range(0, chunk, LANES):
        lanes = slice(lane, lane + LANES)
        taps = spread_taps(taps_ref, lanes, cols)
        for row in range(rows - 2):
            near = [hidden[row + a, :, lanes] for a in range(3)]
            sums = [
                taps[b] * near[0] + taps[3 + b] * near[1] + taps[6 + b] * near[2] for b in range(3)
            ]
            mixed = column_sums(sums[0], sums[1], sums[2], column, cols - 1)
            value, slope = gelu_and_slope(mixed)
            hidden_two[row * cols : (row + 1) * cols, lanes] = value.astype(BF16)
            slope_two_ref[row, :, lanes] = slope.astype(BF16)
    total[...] += nn_dot(hidden_two[...], project_ref[...])

    @pl.when(step == pl.num_programs(0) - 1)
    def _():
        for row in range(rows - 2):
            first = total[row * cols : (row + 1) * cols]
            first_ref[row] = first
            if 1 <= row <= own:
                normed_ref[row - 1] = (first * rms_scale(first)).astype(BF16)


def forward(places, features, other, rim, w_expand, kernel, w_project):
    capacity, cols, width = features.shape
    own, rows = GRID_ROWS, GRID_ROWS + 2 * RIM
    hidden_width = w_expand.shape[1]
    anywhere = pl.BlockSpec(memory_space=pl.ANY)
    return pl.pallas_call(
        forward_body,
        grid=(hidden_width // CHUNK,),
        in_specs=[
            pl.BlockSpec(memory_space=pltpu.SMEM),
            anywhere,
            anywhere,
            anywhere,
            pl.BlockSpec((width, CHUNK), lambda j: (0, j)),
            pl.BlockSpec((9, CHUNK), lambda j: (0, j)),
            pl.BlockSpec((CHUNK, width), lambda j: (j, 0)),
        ],
        out_specs=[
            whole((rows - 2, cols, width)),
            whole((own, cols, width)),
            whole((own, cols, width)),
            pl.BlockSpec((own, cols, CHUNK), lambda j: (0, 0, j)),
            pl.BlockSpec((rows - 2, cols, CHUNK), lambda j: (0, 0, j)),
        ],
        out_shape=[
            jax.ShapeDtypeStruct((rows - 2, cols, width), F32),
            jax.ShapeDtypeStruct((own, cols, width), BF16),
            jax.ShapeDtypeStruct((own, cols, width), BF16),
            jax.ShapeDtypeStruct((own, cols, hidden_width), BF16),
            jax.ShapeDtypeStruct((rows - 2, cols, hidden_width), BF16),
        ],
        scratch_shapes=[
            pltpu.VMEM((rows, cols, width), BF16),
            pltpu.VMEM((rows * cols, width), BF16),
            pltpu.VMEM((rows, cols, CHUNK), F32),
            pltpu.VMEM(((rows - 2) * cols, CHUNK), BF16),
            pltpu.VMEM(((rows - 2) * cols, width), F32),
            pltpu.SemaphoreType.DMA((4,)),
        ],
        compiler_params=params(),
        cost_estimate=pl.CostEstimate(
            flops=4 * rows * cols * width * hidden_width,
            bytes_accessed=12 * 1024 * 1024,
            transcendentals=2 * rows * cols * hidden_width,
        ),
        name="bottleneck_forward",
    )(places, features, other, rim, w_expand, kernel, w_project)


def window_order(groups, cols):
    order = np.arange(groups * cols)
    span = groups * 8
    place = (order // 8) % groups * cols + order % 8 * (cols // 8) + order // span
    return (place[:, None] == order[None, :]).astype(np.float32)


def head_mask(span, head_dim):
    heads = LANES // head_dim
    row_head = np.arange(heads * span)[:, None] // span
    return (row_head == np.arange(LANES)[None, :] // head_dim).astype(np.float32)


def attention_body(normed_ref, cotangent_ref, order_ref, back_ref, mask_ref, qkv_ref, out_ref, added_ref,
                   grad_ref, projected, grad_attended, grad_projected, attended):
    groups, _, cols, width = normed_ref.shape
    tokens = groups * cols
    span = groups * 8
    head_dim = width // HEADS
    heads = LANES // head_dim
    scale = 1.0 / math.sqrt(head_dim)
    steepness = scale * math.log2(math.e)

    normed = nn_dot(order_ref[...], normed_ref[...].reshape(tokens, width)).astype(BF16)
    projected[...] = nn_dot(normed, qkv_ref[...]).astype(BF16)
    grad_rows = nn_dot(order_ref[...], cotangent_ref[...].reshape(tokens, width)).astype(BF16)
    grad_attended[...] = nt_dot(grad_rows, out_ref[...]).astype(BF16)

    lane_head = lax.broadcasted_iota(jnp.int32, (span, LANES), 1) // head_dim

    def spread(values):
        return jnp.concatenate([values] * heads, axis=0) * mask_ref[...]

    def collect(values):
        result = values[0:span]
        for head in range(1, heads):
            result = jnp.where(lane_head == head, values[head * span : (head + 1) * span], result)
        return result

    for index in range(cols // 8):
        rows = slice(index * span, (index + 1) * span)
        for part in range(width // LANES):
            q_at, k_at, v_at = (
                slice(t * width + part * LANES, t * width + (part + 1) * LANES) for t in range(3)
            )
            q, k, v = projected[rows, q_at], projected[rows, k_at], projected[rows, v_at]
            q_wide = spread(q)
            g_wide = spread(grad_attended[rows, q_at])
            scores = nt_dot(k, q_wide)
            powers = jnp.exp2((scores - jnp.max(scores, axis=0, keepdims=True)) * steepness)
            weights = powers * (1.0 / jnp.sum(powers, axis=0, keepdims=True))
            half = weights.astype(BF16)
            grad_weights = nt_dot(v, g_wide)
            row_dot = jnp.sum(weights * grad_weights, axis=0, keepdims=True)
            grad_scores = (weights * (grad_weights - row_dot)).astype(BF16)
            attended[rows, q_at] = collect(tn_dot(half, v)).astype(BF16)
            grad_projected[rows, q_at] = (collect(tn_dot(grad_scores, k)) * scale).astype(BF16)
            grad_projected[rows, k_at] = (nn_dot(grad_scores, q_wide) * scale).astype(BF16)
            grad_projected[rows, v_at] = nn_dot(half, g_wide).astype(BF16)

    shape = (groups, 1, cols, width)
    grad_normed = nt_dot(grad_projected[...], qkv_ref[...]).astype(BF16)
    grad_ref[...] = nn_dot(back_ref[...], grad_normed).astype(BF16).reshape(shape)
    in_rows = nn_dot(back_ref[...], attended[...]).astype(BF16)
    added_ref[...] = nn_dot(in_rows, out_ref[...]).astype(BF16).reshape(shape)


def attention(normed, cotangent, w_qkv, w_out):
    groups, own, cols, width = normed.shape
    tokens = groups * cols
    order = window_order(groups, cols)
    mask = head_mask(groups * 8, width // HEADS)
    block = pl.BlockSpec((groups, 1, cols, width), lambda r: (0, r, 0, 0))
    out = jax.ShapeDtypeStruct(normed.shape, BF16)
    return pl.pallas_call(
        attention_body,
        grid=(own,),
        in_specs=[
            block,
            block,
            whole(order.shape),
            whole(order.shape),
            whole(mask.shape),
            whole(w_qkv.shape),
            whole(w_out.shape),
        ],
        out_specs=[block, block],
        out_shape=[out, out],
        scratch_shapes=[
            pltpu.VMEM((tokens, 3 * width), BF16),
            pltpu.VMEM((tokens, width), BF16),
            pltpu.VMEM((tokens, 3 * width), BF16),
            pltpu.VMEM((tokens, width), BF16),
        ],
        compiler_params=params(),
        cost_estimate=pl.CostEstimate(
            flops=20 * own * tokens * width * width,
            bytes_accessed=4 * 1024 * 1024,
            transcendentals=own * tokens * 64 * HEADS,
        ),
        name="window_attention",
    )(
        normed,
        cotangent,
        jnp.asarray(order, BF16),
        jnp.asarray(order.T, BF16),
        jnp.asarray(mask, BF16),
        w_qkv,
        w_out,
    )


def backward_body(place_ref, cotangent_ref, other_ref, rim_ref, slab_ref, first_ref, grad_slab_ref, grad_ref,
                  pair_ref, next_ref, slope_one_ref, slope_two_ref, expand_ref, taps_ref, project_ref,
                  out_ref, rim_rows, grad_first, grad_rows, mixed, expanded, total, sems):
    step = pl.program_id(0)
    own, cols, width = slab_ref.shape
    chunk = expand_ref.shape[1]

    @pl.when(step == 0)
    def _():
        sources = (cotangent_ref, other_ref, rim_ref)
        for side in range(2):
            start_pull(place_ref, side, sources, 1, rim_rows.at[pl.ds(side, 1)], sems.at[side])
        total[...] = jnp.zeros_like(total)

        def through_norm(cotangent, grad, first):
            rms = rms_scale(first)
            normed = first * rms
            grad = grad.astype(F32)
            inner = jnp.mean(grad * normed, -1, keepdims=True)
            return cotangent.astype(F32) + rms * (grad - normed * inner)

        for row in range(own):
            result = through_norm(grad_slab_ref[row], grad_ref[row], first_ref[row + 1])
            grad_first[row * cols : (row + 1) * cols] = result
            grad_rows[(row + 1) * cols : (row + 2) * cols] = result.astype(BF16)
        for side in range(2):
            wait_pull(sources, 1, rim_rows.at[pl.ds(side, 1)], sems.at[side])
        leads = place_ref[4] == 0
        above = jnp.where(leads, next_ref[0].astype(F32), pair_ref[0].astype(F32))
        below = jnp.where(leads, pair_ref[0].astype(F32), next_ref[0].astype(F32))
        grad_rows[0:cols] = through_norm(rim_rows[0], above, first_ref[0]).astype(BF16)
        grad_rows[(own + 1) * cols :] = through_norm(rim_rows[1], below, first_ref[own + 1]).astype(BF16)

    for row in range(0, own + 2, 6):
        grad = nt_dot(grad_rows[row * cols : (row + 6) * cols, :], project_ref[...])
        for inner in range(6):
            for lane in range(0, chunk, LANES):
                lanes = slice(lane, lane + LANES)
                slope = slope_two_ref[row + inner, :, lanes].astype(F32)
                value = grad[inner * cols : (inner + 1) * cols, lanes] * slope
                mixed[row + inner, :, lanes] = value.astype(BF16).astype(F32)

    column = lax.broadcasted_iota(jnp.int32, (cols, LANES), 0)
    for lane in range(0, chunk, LANES):
        lanes = slice(lane, lane + LANES)
        taps = spread_taps(taps_ref, lanes, cols)
        for row in range(own):
            near = [mixed[row + a, :, lanes] for a in range(3)]
            sums = [
                taps[8 - b] * near[0] + taps[5 - b] * near[1] + taps[2 - b] * near[2] for b in range(3)
            ]
            grad = column_sums(sums[0], sums[1], sums[2], column, cols - 1)
            slope = slope_one_ref[row, :, lanes].astype(F32)
            expanded[row * cols : (row + 1) * cols, lanes] = (grad * slope).astype(BF16)
    total[...] += nt_dot(expanded[...], expand_ref[...])

    @pl.when(step == pl.num_programs(0) - 1)
    def _():
        for row in range(own):
            at = slice(row * cols, (row + 1) * cols)
            values = slab_ref[row].astype(F32)
            rms = rms_scale(values)
            normed = values * rms
            grad = total[at]
            inner = jnp.mean(grad * normed, -1, keepdims=True)
            out_ref[row] = (grad_first[at] + rms * (grad - normed * inner)).astype(BF16)


def backward(places, cotangent, other, rim, slab, first, grad_slab, grad, pair_row, next_row, slope_one,
             slope_two, w_expand, kernel, w_project):
    own, cols, width = slab.shape
    hidden_width = w_expand.shape[1]
    anywhere = pl.BlockSpec(memory_space=pl.ANY)
    return pl.pallas_call(
        backward_body,
        grid=(hidden_width // CHUNK,),
        in_specs=[
            pl.BlockSpec(memory_space=pltpu.SMEM),
            anywhere,
            anywhere,
            anywhere,
            whole(slab.shape),
            whole(first.shape),
            whole(grad_slab.shape),
            whole(grad.shape),
            whole(pair_row.shape),
            whole(next_row.shape),
            pl.BlockSpec((own, cols, CHUNK), lambda j: (0, 0, j)),
            pl.BlockSpec((own + 2, cols, CHUNK), lambda j: (0, 0, j)),
            pl.BlockSpec((width, CHUNK), lambda j: (0, j)),
            pl.BlockSpec((9, CHUNK), lambda j: (0, j)),
            pl.BlockSpec((CHUNK, width), lambda j: (j, 0)),
        ],
        out_specs=whole((own, cols, width)),
        out_shape=jax.ShapeDtypeStruct((own, cols, width), BF16),
        scratch_shapes=[
            pltpu.VMEM((2, cols, width), BF16),
            pltpu.VMEM((own * cols, width), F32),
            pltpu.VMEM(((own + 2) * cols, width), BF16),
            pltpu.VMEM((own + 2, cols, CHUNK), F32),
            pltpu.VMEM((own * cols, CHUNK), BF16),
            pltpu.VMEM((own * cols, width), F32),
            pltpu.SemaphoreType.DMA((2,)),
        ],
        compiler_params=params(),
        cost_estimate=pl.CostEstimate(
            flops=4 * (own + 2) * cols * width * hidden_width,
            bytes_accessed=12 * 1024 * 1024,
            transcendentals=0,
        ),
        name="bottleneck_backward",
    )(places, cotangent, other, rim, slab, first, grad_slab, grad, pair_row, next_row, slope_one,
      slope_two, w_expand, kernel, w_project)


def window_groups(size):
    stride = size // 8
    return [[first + stride * k for k in range(8)] for first in range(stride)]


def exchange_windows(rows):
    groups = window_groups(lax.axis_size("row"))
    return lax.all_to_all(
        rows, "row", split_axis=0, concat_axis=0, tiled=True, axis_index_groups=groups
    )


def swap_pair(rows):
    size = lax.axis_size("row")
    return lax.ppermute(rows, "row", [(i, i ^ 1) for i in range(size)])


def swap_next(rows):
    size = lax.axis_size("row")
    pairs = [(i, i + 1) for i in range(1, size - 1, 2)]
    return lax.ppermute(rows, "row", pairs + [(j, i) for i, j in pairs])


def place_rows(even, other, leads, leader_share):
    size = GRID_ROWS
    first, second = even[:BAND], even[BAND:]
    share = jnp.where(leads, leader_share, 2 * size - leader_share)
    zeros = jnp.zeros_like(first)
    low = jnp.where(leads | (share == size), first, jnp.where(share < size, second, other))
    mid = jnp.where(share < size, zeros, jnp.where(leads | (share == size), second, first))
    high = jnp.where(share > size, jnp.where(leads, other, second), zeros)
    return jnp.concatenate([low, mid, high], 0)


def on_device(features, row_bands, w_expand, kernel, w_project, w_qkv, w_out, cotangent):
    capacity, cols, width = features.shape
    device = lax.axis_index("row")
    parity = device % 2
    leads = parity == 0
    leader_share = BAND * row_bands[device - parity]
    own_share = BAND * row_bands[device]

    def place(first, count):
        row = first + GRID_ROWS * parity
        beyond = (row < 0) | (row >= 2 * GRID_ROWS)
        in_own = jnp.where(leads, row < leader_share, row >= leader_share)
        local = jnp.where(row < leader_share, row, row - leader_share)
        source = jnp.where(beyond, 2, jnp.where(in_own, 0, 1))
        return [source, jnp.where(beyond, 0, local)]

    rim_first = jnp.where(leads, 0, own_share - RIM)
    rim_cotangent = jnp.where(leads, 0, own_share - 1)
    rim = swap_next(
        jnp.concatenate(
            [
                lax.dynamic_slice_in_dim(features, rim_first, RIM, 0),
                lax.dynamic_slice_in_dim(cotangent, rim_cotangent, 1, 0),
            ],
            0,
        )
    )
    other_cotangent = swap_pair(cotangent)
    other_features = swap_pair(features)

    halves = place(0, BAND) + place(BAND, BAND)
    slab_places = jnp.stack(place(-RIM, RIM) + halves + place(GRID_ROWS, RIM))
    above, below = place(-1, 1), place(GRID_ROWS, 1)
    grad_places = jnp.stack(
        [above[0], jnp.where(above[0] == 2, RIM, above[1]), below[0], jnp.where(below[0] == 2, RIM, below[1]), parity]
    )

    grad_slab = even_rows(jnp.stack(halves), cotangent, other_cotangent)
    grad_windows = exchange_windows(grad_slab)
    first, normed, slab, slope_one, slope_two = forward(
        slab_places, features, other_features, rim, w_expand, kernel, w_project
    )
    normed, grad_windows = lax.optimization_barrier((normed, grad_windows))
    normed_windows = exchange_windows(normed)
    shape = (8, GRID_ROWS // 8, cols, width)
    added, grad_normed = attention(
        normed_windows.reshape(shape), grad_windows.reshape(shape), w_qkv, w_out
    )
    grad_rows = exchange_windows(grad_normed.reshape(GRID_ROWS, cols, width))
    added, grad_rows = lax.optimization_barrier((added, grad_rows))
    added_rows = exchange_windows(added.reshape(GRID_ROWS, cols, width))
    top, bottom = grad_rows[:1], grad_rows[GRID_ROWS - 1 :]
    pair_row = swap_pair(jnp.where(leads, bottom, top))
    next_row = swap_next(jnp.where(leads, top, bottom))
    grad_input = backward(
        grad_places, cotangent, other_cotangent, rim, slab, first, grad_slab, grad_rows, pair_row, next_row,
        slope_one, slope_two, w_expand, kernel, w_project,
    )
    grad_input, added_rows = lax.optimization_barrier((grad_input, added_rows))
    final = (first[1 : GRID_ROWS + 1] + added_rows.astype(F32)).astype(BF16)
    sent = [jnp.where(leads, rows[BAND:], rows[:BAND]) for rows in (final, grad_input)]
    swapped = swap_pair(jnp.stack(sent))
    return (
        place_rows(final, swapped[0], leads, leader_share),
        place_rows(grad_input, swapped[1], leads, leader_share),
    )


def solution(mesh):
    return jax.shard_map(
        on_device,
        mesh=mesh,
        in_specs=(
            P(("parts", "row"), None, None),
            P("parts"),
            P(),
            P(),
            P(),
            P(),
            P(),
            P(("parts", "row"), None, None),
        ),
        out_specs=(P(("parts", "row"), None, None), P(("parts", "row"), None, None)),
        check_vma=False,
    )
```

```python
import math

import jax
import jax.numpy as jnp
import numpy as np
from jax import lax
from jax.experimental import pallas as pl
from jax.experimental.pallas import tpu as pltpu
from jax.sharding import PartitionSpec as P

HEADS = 16
GRID_ROWS = 16
BAND = 8
RIM = 2
EPSILON = 1e-06
CHUNK = 512
LANES = 128
ROOT = math.sqrt(2.0 / math.pi)
CUBIC = 0.044715
F32 = jnp.float32
BF16 = jnp.bfloat16
VMEM_LIMIT = 56 * 1024 * 1024


def nt_dot(left, right):
    return lax.dot_general(left, right, (((1,), (1,)), ((), ())), preferred_element_type=F32)


def tn_dot(left, right):
    return lax.dot_general(left, right, (((0,), (0,)), ((), ())), preferred_element_type=F32)


def nn_dot(left, right):
    return jnp.dot(left, right, preferred_element_type=F32)


def rms_scale(values):
    return lax.rsqrt(jnp.mean(values * values, -1, keepdims=True) + EPSILON)


def gelu_and_slope(v):
    square = v * v
    cdf = 0.5 + 0.5 * jnp.tanh(v * (ROOT + (ROOT * CUBIC) * square))
    value = v * cdf
    slope = cdf + (value - value * cdf) * (2.0 * ROOT + (6.0 * ROOT * CUBIC) * square)
    return value, slope


def whole(shape, space=None):
    zeros = (0,) * len(shape)
    return pl.BlockSpec(shape, lambda *_: zeros)


def params():
    return pltpu.CompilerParams(vmem_limit_bytes=VMEM_LIMIT)


def anywhere():
    return pl.BlockSpec(memory_space=pl.ANY)


def in_scalars():
    return pl.BlockSpec(memory_space=pltpu.SMEM)


def shares(bands_ref):
    device = lax.axis_index("row")
    parity = lax.rem(device, 2)
    return parity, BAND * bands_ref[device - parity], BAND * bands_ref[device]


def place(bands_ref, first):
    parity, leader_share, _ = shares(bands_ref)
    row = first + GRID_ROWS * parity
    beyond = (row < 0) | (row >= 2 * GRID_ROWS)
    in_leader = row < leader_share
    in_own = in_leader == (parity == 0)
    source = jnp.where(beyond, 2, jnp.where(in_own, 0, 1))
    return source, jnp.where(beyond, 0, jnp.where(in_leader, row, row - leader_share))


def start_pull(bands_ref, first, sources, rows, target, sem, rim_row=0):
    where, row = place(bands_ref, first)
    row = jnp.where(where == 2, rim_row, row)
    for number, source in enumerate(sources):

        @pl.when(where == number)
        def _():
            pltpu.make_async_copy(source.at[pl.ds(row, rows)], target, sem).start()


def wait_pull(sources, rows, target, sem):
    pltpu.make_async_copy(sources[0].at[pl.ds(0, rows)], target, sem).wait()


def even_body(bands_ref, own_ref, other_ref, out_ref, sems):
    sources = (own_ref, other_ref)
    targets = [out_ref.at[pl.ds(BAND * half, BAND)] for half in range(2)]
    for half in range(2):
        start_pull(bands_ref, BAND * half, sources, BAND, targets[half], sems.at[half])
    for half in range(2):
        wait_pull(sources, BAND, targets[half], sems.at[half])


def even_rows(bands, own, other):
    capacity, cols, width = own.shape
    shape = (GRID_ROWS, cols, width)
    return pl.pallas_call(
        even_body,
        grid=(1,),
        in_specs=[in_scalars(), anywhere(), anywhere()],
        out_specs=whole(shape),
        out_shape=jax.ShapeDtypeStruct(shape, own.dtype),
        scratch_shapes=[pltpu.SemaphoreType.DMA((2,))],
        compiler_params=params(),
        name="even_rows",
    )(bands, own, other)


def rim_body(bands_ref, features_ref, cotangent_ref, out_ref, sems):
    parity, _, share = shares(bands_ref)
    leads = parity == 0
    copies = [
        pltpu.make_async_copy(
            features_ref.at[pl.ds(jnp.where(leads, 0, share - RIM), RIM)], out_ref.at[pl.ds(0, RIM)], sems.at[0]
        ),
        pltpu.make_async_copy(
            cotangent_ref.at[pl.ds(jnp.where(leads, 0, share - 1), 1)], out_ref.at[pl.ds(RIM, 1)], sems.at[1]
        ),
    ]
    for copy in copies:
        copy.start()
    for copy in copies:
        copy.wait()


def rim_rows(bands, features, cotangent):
    capacity, cols, width = features.shape
    shape = (RIM + 1, cols, width)
    return pl.pallas_call(
        rim_body,
        grid=(1,),
        in_specs=[in_scalars(), anywhere(), anywhere()],
        out_specs=whole(shape),
        out_shape=jax.ShapeDtypeStruct(shape, features.dtype),
        scratch_shapes=[pltpu.SemaphoreType.DMA((2,))],
        compiler_params=params(),
        name="rim_rows",
    )(bands, features, cotangent)


def column_sums(left, mid, right, column, last):
    from_left = jnp.where(column == 0, 0.0, pltpu.roll(left, 1, 0))
    from_right = jnp.where(column == last, 0.0, pltpu.roll(right, last, 0))
    return mid + from_left + from_right


def spread_taps(taps_ref, lanes, cols):
    taps = taps_ref[...].astype(F32)
    return [jnp.broadcast_to(taps[i : i + 1, lanes], (cols, LANES)) for i in range(9)]


def forward_body(bands_ref, features_ref, other_ref, rim_ref, expand_ref, taps_ref, project_ref, first_ref,
                 normed_ref, slab_ref, slope_one_ref, slope_two_ref, slab, normed_one, hidden, hidden_two,
                 total, sems):
    step = pl.program_id(0)
    rows, cols, width = slab.shape
    own = rows - 2 * RIM
    chunk = expand_ref.shape[1]

    @pl.when(step == 0)
    def _():
        sources = (features_ref, other_ref, rim_ref)
        pieces = [(0, RIM), (RIM, BAND), (RIM + BAND, BAND), (RIM + 2 * BAND, RIM)]
        for index, (first, count) in enumerate(pieces):
            start_pull(bands_ref, first - RIM, sources, count, slab.at[pl.ds(first, count)], sems.at[index])
        for index, (first, count) in enumerate(pieces):
            wait_pull(sources, count, slab.at[pl.ds(first, count)], sems.at[index])
        slab_ref[...] = slab[RIM : RIM + own]
        for row in range(0, rows, 2):
            at = slice(row * cols, (row + 2) * cols)
            values = slab[row : row + 2].astype(F32).reshape(2 * cols, width)
            normed_one[at] = (values * rms_scale(values)).astype(BF16)
        total[...] = slab[1 : rows - 1].astype(F32).reshape((rows - 2) * cols, width)

    for row in range(0, rows, 4):
        expanded = nn_dot(normed_one[row * cols : (row + 4) * cols, :], expand_ref[...])
        for inner in range(4):
            for lane in range(0, chunk, LANES):
                lanes = slice(lane, lane + LANES)
                value, slope = gelu_and_slope(expanded[inner * cols : (inner + 1) * cols, lanes])
                hidden[row + inner, :, lanes] = value.astype(BF16).astype(F32)
                if RIM <= row + inner < RIM + own:
                    slope_one_ref[row + inner - RIM, :, lanes] = slope.astype(BF16)

    column = lax.broadcasted_iota(jnp.int32, (cols, LANES), 0)
    for lane in range(0, chunk, LANES):
        lanes = slice(lane, lane + LANES)
        taps = spread_taps(taps_ref, lanes, cols)
        for row in range(rows - 2):
            near = [hidden[row + a, :, lanes] for a in range(3)]
            sums = [
                taps[b] * near[0] + taps[3 + b] * near[1] + taps[6 + b] * near[2] for b in range(3)
            ]
            mixed = column_sums(sums[0], sums[1], sums[2], column, cols - 1)
            value, slope = gelu_and_slope(mixed)
            hidden_two[row * cols : (row + 1) * cols, lanes] = value.astype(BF16)
            slope_two_ref[row, :, lanes] = slope.astype(BF16)
    total[...] += nn_dot(hidden_two[...], project_ref[...])

    @pl.when(step == pl.num_programs(0) - 1)
    def _():
        for row in range(rows - 2):
            first = total[row * cols : (row + 1) * cols]
            first_ref[row] = first
            if 1 <= row <= own:
                normed_ref[row - 1] = (first * rms_scale(first)).astype(BF16)


def forward(bands, features, other, rim, w_expand, kernel, w_project):
    capacity, cols, width = features.shape
    own, rows = GRID_ROWS, GRID_ROWS + 2 * RIM
    hidden_width = w_expand.shape[1]
    return pl.pallas_call(
        forward_body,
        grid=(hidden_width // CHUNK,),
        in_specs=[
            in_scalars(),
            anywhere(),
            anywhere(),
            anywhere(),
            pl.BlockSpec((width, CHUNK), lambda j: (0, j)),
            pl.BlockSpec((9, CHUNK), lambda j: (0, j)),
            pl.BlockSpec((CHUNK, width), lambda j: (j, 0)),
        ],
        out_specs=[
            whole((rows - 2, cols, width)),
            whole((own, cols, width)),
            whole((own, cols, width)),
            pl.BlockSpec((own, cols, CHUNK), lambda j: (0, 0, j)),
            pl.BlockSpec((rows - 2, cols, CHUNK), lambda j: (0, 0, j)),
        ],
        out_shape=[
            jax.ShapeDtypeStruct((rows - 2, cols, width), F32),
            jax.ShapeDtypeStruct((own, cols, width), BF16),
            jax.ShapeDtypeStruct((own, cols, width), BF16),
            jax.ShapeDtypeStruct((own, cols, hidden_width), BF16),
            jax.ShapeDtypeStruct((rows - 2, cols, hidden_width), BF16),
        ],
        scratch_shapes=[
            pltpu.VMEM((rows, cols, width), BF16),
            pltpu.VMEM((rows * cols, width), BF16),
            pltpu.VMEM((rows, cols, CHUNK), F32),
            pltpu.VMEM(((rows - 2) * cols, CHUNK), BF16),
            pltpu.VMEM(((rows - 2) * cols, width), F32),
            pltpu.SemaphoreType.DMA((4,)),
        ],
        compiler_params=params(),
        cost_estimate=pl.CostEstimate(
            flops=4 * rows * cols * width * hidden_width,
            bytes_accessed=12 * 1024 * 1024,
            transcendentals=2 * rows * cols * hidden_width,
        ),
        name="bottleneck_forward",
    )(bands, features, other, rim, w_expand, kernel, w_project)


def window_order(groups, cols):
    order = np.arange(groups * cols)
    span = groups * 8
    place = (order // 8) % groups * cols + order % 8 * (cols // 8) + order // span
    return (place[:, None] == order[None, :]).astype(np.float32)


def head_mask(span, head_dim):
    heads = LANES // head_dim
    row_head = np.arange(heads * span)[:, None] // span
    return (row_head == np.arange(LANES)[None, :] // head_dim).astype(np.float32)


def attention_body(normed_ref, cotangent_ref, order_ref, back_ref, mask_ref, qkv_ref, out_ref, added_ref,
                   grad_ref, projected, grad_attended, grad_projected, attended):
    groups, _, cols, width = normed_ref.shape
    tokens = groups * cols
    span = groups * 8
    head_dim = width // HEADS
    heads = LANES // head_dim
    scale = 1.0 / math.sqrt(head_dim)
    steepness = scale * math.log2(math.e)

    normed = nn_dot(order_ref[...], normed_ref[...].reshape(tokens, width)).astype(BF16)
    projected[...] = nn_dot(normed, qkv_ref[...]).astype(BF16)
    grad_rows = nn_dot(order_ref[...], cotangent_ref[...].reshape(tokens, width)).astype(BF16)
    grad_attended[...] = nt_dot(grad_rows, out_ref[...]).astype(BF16)

    lane_head = lax.broadcasted_iota(jnp.int32, (span, LANES), 1) // head_dim

    def spread(values):
        return jnp.concatenate([values] * heads, axis=0) * mask_ref[...]

    def per_query(values, weights):
        wide = nn_dot(values.T, weights)
        half = LANES // 2
        own = jnp.concatenate([wide[:half, :LANES], wide[half:, LANES:]], axis=0).T
        return jnp.where(lane_head % 2 == 0, own[:span], own[span:])

    for index in range(cols // 8):
        rows = slice(index * span, (index + 1) * span)
        for part in range(width // LANES):
            q_at, k_at, v_at = (
                slice(t * width + part * LANES, t * width + (part + 1) * LANES) for t in range(3)
            )
            q, k, v = projected[rows, q_at], projected[rows, k_at], projected[rows, v_at]
            q_wide = spread(q)
            g_wide = spread(grad_attended[rows, q_at])
            scores = nt_dot(k, q_wide)
            powers = jnp.exp2((scores - jnp.max(scores, axis=0, keepdims=True)) * steepness)
            weights = powers * (1.0 / jnp.sum(powers, axis=0, keepdims=True))
            half = weights.astype(BF16)
            grad_weights = nt_dot(v, g_wide)
            row_dot = jnp.sum(weights * grad_weights, axis=0, keepdims=True)
            grad_scores = (weights * (grad_weights - row_dot)).astype(BF16)
            attended[rows, q_at] = per_query(v, half).astype(BF16)
            grad_projected[rows, q_at] = (per_query(k, grad_scores) * scale).astype(BF16)
            grad_projected[rows, k_at] = (nn_dot(grad_scores, q_wide) * scale).astype(BF16)
            grad_projected[rows, v_at] = nn_dot(half, g_wide).astype(BF16)

    shape = (groups, 1, cols, width)
    grad_normed = nt_dot(grad_projected[...], qkv_ref[...]).astype(BF16)
    grad_ref[...] = nn_dot(back_ref[...], grad_normed).astype(BF16).reshape(shape)
    in_rows = nn_dot(back_ref[...], attended[...]).astype(BF16)
    added_ref[...] = nn_dot(in_rows, out_ref[...]).astype(BF16).reshape(shape)


def attention(normed, cotangent, w_qkv, w_out):
    groups, own, cols, width = normed.shape
    tokens = groups * cols
    order = window_order(groups, cols)
    mask = head_mask(groups * 8, width // HEADS)
    block = pl.BlockSpec((groups, 1, cols, width), lambda r: (0, r, 0, 0))
    out = jax.ShapeDtypeStruct(normed.shape, BF16)
    return pl.pallas_call(
        attention_body,
        grid=(own,),
        in_specs=[
            block,
            block,
            whole(order.shape),
            whole(order.shape),
            whole(mask.shape),
            whole(w_qkv.shape),
            whole(w_out.shape),
        ],
        out_specs=[block, block],
        out_shape=[out, out],
        scratch_shapes=[
            pltpu.VMEM((tokens, 3 * width), BF16),
            pltpu.VMEM((tokens, width), BF16),
            pltpu.VMEM((tokens, 3 * width), BF16),
            pltpu.VMEM((tokens, width), BF16),
        ],
        compiler_params=params(),
        cost_estimate=pl.CostEstimate(
            flops=20 * own * tokens * width * width,
            bytes_accessed=4 * 1024 * 1024,
            transcendentals=own * tokens * 64 * HEADS,
        ),
        name="window_attention",
    )(
        normed,
        cotangent,
        jnp.asarray(order, BF16),
        jnp.asarray(order.T, BF16),
        jnp.asarray(mask, BF16),
        w_qkv,
        w_out,
    )


def backward_body(bands_ref, cotangent_ref, other_ref, rim_ref, slab_ref, first_ref, grad_slab_ref, grad_ref,
                  pair_ref, next_ref, slope_one_ref, slope_two_ref, expand_ref, taps_ref, project_ref,
                  out_ref, rims, grad_first, grad_rows, mixed, expanded, total, sems):
    step = pl.program_id(0)
    own, cols, width = slab_ref.shape
    chunk = expand_ref.shape[1]

    @pl.when(step == 0)
    def _():
        sources = (cotangent_ref, other_ref, rim_ref)
        for side, first in enumerate((-1, own)):
            start_pull(bands_ref, first, sources, 1, rims.at[pl.ds(side, 1)], sems.at[side], RIM)
        total[...] = jnp.zeros_like(total)

        def through_norm(cotangent, grad, first):
            rms = rms_scale(first)
            normed = first * rms
            grad = grad.astype(F32)
            inner = jnp.mean(grad * normed, -1, keepdims=True)
            return cotangent.astype(F32) + rms * (grad - normed * inner)

        for row in range(own):
            result = through_norm(grad_slab_ref[row], grad_ref[row], first_ref[row + 1])
            grad_first[row * cols : (row + 1) * cols] = result
            grad_rows[(row + 1) * cols : (row + 2) * cols] = result.astype(BF16)
        for side in range(2):
            wait_pull(sources, 1, rims.at[pl.ds(side, 1)], sems.at[side])
        leads = lax.rem(lax.axis_index("row"), 2) == 0
        above = jnp.where(leads, next_ref[0].astype(F32), pair_ref[0].astype(F32))
        below = jnp.where(leads, pair_ref[0].astype(F32), next_ref[0].astype(F32))
        grad_rows[0:cols] = through_norm(rims[0], above, first_ref[0]).astype(BF16)
        grad_rows[(own + 1) * cols :] = through_norm(rims[1], below, first_ref[own + 1]).astype(BF16)

    for row in range(0, own + 2, 6):
        grad = nt_dot(grad_rows[row * cols : (row + 6) * cols, :], project_ref[...])
        for inner in range(6):
            for lane in range(0, chunk, LANES):
                lanes = slice(lane, lane + LANES)
                slope = slope_two_ref[row + inner, :, lanes].astype(F32)
                value = grad[inner * cols : (inner + 1) * cols, lanes] * slope
                mixed[row + inner, :, lanes] = value.astype(BF16).astype(F32)

    column = lax.broadcasted_iota(jnp.int32, (cols, LANES), 0)
    for lane in range(0, chunk, LANES):
        lanes = slice(lane, lane + LANES)
        taps = spread_taps(taps_ref, lanes, cols)
        for row in range(own):
            near = [mixed[row + a, :, lanes] for a in range(3)]
            sums = [
                taps[8 - b] * near[0] + taps[5 - b] * near[1] + taps[2 - b] * near[2] for b in range(3)
            ]
            grad = column_sums(sums[0], sums[1], sums[2], column, cols - 1)
            slope = slope_one_ref[row, :, lanes].astype(F32)
            expanded[row * cols : (row + 1) * cols, lanes] = (grad * slope).astype(BF16)
    total[...] += nt_dot(expanded[...], expand_ref[...])

    @pl.when(step == pl.num_programs(0) - 1)
    def _():
        for row in range(own):
            at = slice(row * cols, (row + 1) * cols)
            values = slab_ref[row].astype(F32)
            rms = rms_scale(values)
            normed = values * rms
            grad = total[at]
            inner = jnp.mean(grad * normed, -1, keepdims=True)
            out_ref[row] = (grad_first[at] + rms * (grad - normed * inner)).astype(BF16)


def backward(bands, cotangent, other, rim, slab, first, grad_slab, grad, pair_row, next_row, slope_one,
             slope_two, w_expand, kernel, w_project):
    own, cols, width = slab.shape
    hidden_width = w_expand.shape[1]
    return pl.pallas_call(
        backward_body,
        grid=(hidden_width // CHUNK,),
        in_specs=[
            in_scalars(),
            anywhere(),
            anywhere(),
            anywhere(),
            whole(slab.shape),
            whole(first.shape),
            whole(grad_slab.shape),
            whole(grad.shape),
            whole(pair_row.shape),
            whole(next_row.shape),
            pl.BlockSpec((own, cols, CHUNK), lambda j: (0, 0, j)),
            pl.BlockSpec((own + 2, cols, CHUNK), lambda j: (0, 0, j)),
            pl.BlockSpec((width, CHUNK), lambda j: (0, j)),
            pl.BlockSpec((9, CHUNK), lambda j: (0, j)),
            pl.BlockSpec((CHUNK, width), lambda j: (j, 0)),
        ],
        out_specs=whole((own, cols, width)),
        out_shape=jax.ShapeDtypeStruct((own, cols, width), BF16),
        scratch_shapes=[
            pltpu.VMEM((2, cols, width), BF16),
            pltpu.VMEM((own * cols, width), F32),
            pltpu.VMEM(((own + 2) * cols, width), BF16),
            pltpu.VMEM((own + 2, cols, CHUNK), F32),
            pltpu.VMEM((own * cols, CHUNK), BF16),
            pltpu.VMEM((own * cols, width), F32),
            pltpu.SemaphoreType.DMA((2,)),
        ],
        compiler_params=params(),
        cost_estimate=pl.CostEstimate(
            flops=4 * (own + 2) * cols * width * hidden_width,
            bytes_accessed=12 * 1024 * 1024,
            transcendentals=0,
        ),
        name="bottleneck_backward",
    )(bands, cotangent, other, rim, slab, first, grad_slab, grad, pair_row, next_row, slope_one,
      slope_two, w_expand, kernel, w_project)


def window_groups(size):
    stride = size // 8
    return [[first + stride * k for k in range(8)] for first in range(stride)]


def exchange_windows(rows):
    groups = window_groups(lax.axis_size("row"))
    return lax.all_to_all(
        rows, "row", split_axis=0, concat_axis=0, tiled=True, axis_index_groups=groups
    )


def swap_pair(rows):
    size = lax.axis_size("row")
    return lax.ppermute(rows, "row", [(i, i ^ 1) for i in range(size)])


def swap_next(rows):
    size = lax.axis_size("row")
    pairs = [(i, i + 1) for i in range(1, size - 1, 2)]
    return lax.ppermute(rows, "row", pairs + [(j, i) for i, j in pairs])


def place_rows(even, other, leads, leader_share):
    size = GRID_ROWS
    first, second = even[:BAND], even[BAND:]
    share = jnp.where(leads, leader_share, 2 * size - leader_share)
    zeros = jnp.zeros_like(first)
    low = jnp.where(leads | (share == size), first, jnp.where(share < size, second, other))
    mid = jnp.where(share < size, zeros, jnp.where(leads | (share == size), second, first))
    high = jnp.where(share > size, jnp.where(leads, other, second), zeros)
    return jnp.concatenate([low, mid, high], 0)


def on_device(features, row_bands, w_expand, kernel, w_project, w_qkv, w_out, cotangent):
    capacity, cols, width = features.shape
    device = lax.axis_index("row")
    parity = device % 2
    leads = parity == 0

    rim = swap_next(rim_rows(row_bands, features, cotangent))
    other_cotangent = swap_pair(cotangent)
    other_features = swap_pair(features)
    grad_slab = even_rows(row_bands, cotangent, other_cotangent)
    rim, grad_slab = lax.optimization_barrier((rim, grad_slab))

    grad_windows = exchange_windows(grad_slab)
    first, normed, slab, slope_one, slope_two = forward(
        row_bands, features, other_features, rim, w_expand, kernel, w_project
    )
    normed, grad_windows = lax.optimization_barrier((normed, grad_windows))
    normed_windows = exchange_windows(normed)
    shape = (8, GRID_ROWS // 8, cols, width)
    added, grad_normed = attention(
        normed_windows.reshape(shape), grad_windows.reshape(shape), w_qkv, w_out
    )
    grad_rows = exchange_windows(grad_normed.reshape(GRID_ROWS, cols, width))
    top, bottom = grad_rows[:1], grad_rows[GRID_ROWS - 1 :]
    pair_row = swap_pair(jnp.where(leads, bottom, top))
    next_row = swap_next(jnp.where(leads, top, bottom))
    added, pair_row, next_row = lax.optimization_barrier((added, pair_row, next_row))
    added_rows = exchange_windows(added.reshape(GRID_ROWS, cols, width))
    grad_input = backward(
        row_bands, cotangent, other_cotangent, rim, slab, first, grad_slab, grad_rows, pair_row, next_row,
        slope_one, slope_two, w_expand, kernel, w_project,
    )
    grad_input, added_rows = lax.optimization_barrier((grad_input, added_rows))
    final = (first[1 : GRID_ROWS + 1] + added_rows.astype(F32)).astype(BF16)
    sent = [jnp.where(leads, rows[BAND:], rows[:BAND]) for rows in (final, grad_input)]
    swapped = swap_pair(jnp.stack(sent))
    leader_share = BAND * row_bands[device - parity]
    return (
        place_rows(final, swapped[0], leads, leader_share),
        place_rows(grad_input, swapped[1], leads, leader_share),
    )


def solution(mesh):
    return jax.shard_map(
        on_device,
        mesh=mesh,
        in_specs=(
            P(("parts", "row"), None, None),
            P("parts"),
            P(),
            P(),
            P(),
            P(),
            P(),
            P(("parts", "row"), None, None),
        ),
        out_specs=(P(("parts", "row"), None, None), P(("parts", "row"), None, None)),
        check_vma=False,
    )
```

```python
import math

import jax
import jax.numpy as jnp
import numpy as np
from jax import lax
from jax.experimental import pallas as pl
from jax.experimental.pallas import tpu as pltpu
from jax.sharding import PartitionSpec as P

HEADS = 16
GRID_ROWS = 16
BAND = 8
RIM = 2
EPSILON = 1e-06
CHUNK = 512
LANES = 128
WIDE = 256
ROOT = math.sqrt(2.0 / math.pi)
CUBIC = 0.044715
F32 = jnp.float32
BF16 = jnp.bfloat16
VMEM_LIMIT = 56 * 1024 * 1024


def nt_dot(left, right):
    return lax.dot_general(left, right, (((1,), (1,)), ((), ())), preferred_element_type=F32)


def tn_dot(left, right):
    return lax.dot_general(left, right, (((0,), (0,)), ((), ())), preferred_element_type=F32)


def nn_dot(left, right):
    return jnp.dot(left, right, preferred_element_type=F32)


def rms_scale(values):
    return lax.rsqrt(jnp.mean(values * values, -1, keepdims=True) + EPSILON)


def gelu_and_slope(v):
    square = v * v
    cdf = 0.5 + 0.5 * jnp.tanh(v * (ROOT + (ROOT * CUBIC) * square))
    value = v * cdf
    slope = cdf + (value - value * cdf) * (2.0 * ROOT + (6.0 * ROOT * CUBIC) * square)
    return value, slope


def whole(shape, space=None):
    zeros = (0,) * len(shape)
    return pl.BlockSpec(shape, lambda *_: zeros)


def params():
    return pltpu.CompilerParams(vmem_limit_bytes=VMEM_LIMIT)


def anywhere():
    return pl.BlockSpec(memory_space=pl.ANY)


def in_scalars():
    return pl.BlockSpec(memory_space=pltpu.SMEM)


def shares(bands_ref):
    device = lax.axis_index("row")
    parity = lax.rem(device, 2)
    return parity, BAND * bands_ref[device - parity], BAND * bands_ref[device]


def place(bands_ref, first):
    parity, leader_share, _ = shares(bands_ref)
    row = first + GRID_ROWS * parity
    beyond = (row < 0) | (row >= 2 * GRID_ROWS)
    in_leader = row < leader_share
    in_own = in_leader == (parity == 0)
    source = jnp.where(beyond, 2, jnp.where(in_own, 0, 1))
    return source, jnp.where(beyond, 0, jnp.where(in_leader, row, row - leader_share))


def start_pull(bands_ref, first, sources, rows, target, sem, rim_row=0):
    where, row = place(bands_ref, first)
    row = jnp.where(where == 2, rim_row, row)
    for number, source in enumerate(sources):

        @pl.when(where == number)
        def _():
            pltpu.make_async_copy(source.at[pl.ds(row, rows)], target, sem).start()


def wait_pull(sources, rows, target, sem):
    pltpu.make_async_copy(sources[0].at[pl.ds(0, rows)], target, sem).wait()


def even_body(bands_ref, own_ref, other_ref, out_ref, sems):
    sources = (own_ref, other_ref)
    targets = [out_ref.at[pl.ds(BAND * half, BAND)] for half in range(2)]
    for half in range(2):
        start_pull(bands_ref, BAND * half, sources, BAND, targets[half], sems.at[half])
    for half in range(2):
        wait_pull(sources, BAND, targets[half], sems.at[half])


def even_rows(bands, own, other):
    capacity, cols, width = own.shape
    shape = (GRID_ROWS, cols, width)
    return pl.pallas_call(
        even_body,
        grid=(1,),
        in_specs=[in_scalars(), anywhere(), anywhere()],
        out_specs=whole(shape),
        out_shape=jax.ShapeDtypeStruct(shape, own.dtype),
        scratch_shapes=[pltpu.SemaphoreType.DMA((2,))],
        compiler_params=params(),
        name="even_rows",
    )(bands, own, other)


def rim_body(bands_ref, features_ref, cotangent_ref, out_ref, sems):
    parity, _, share = shares(bands_ref)
    leads = parity == 0
    copies = [
        pltpu.make_async_copy(
            features_ref.at[pl.ds(jnp.where(leads, 0, share - RIM), RIM)], out_ref.at[pl.ds(0, RIM)], sems.at[0]
        ),
        pltpu.make_async_copy(
            cotangent_ref.at[pl.ds(jnp.where(leads, 0, share - 1), 1)], out_ref.at[pl.ds(RIM, 1)], sems.at[1]
        ),
    ]
    for copy in copies:
        copy.start()
    for copy in copies:
        copy.wait()


def rim_rows(bands, features, cotangent):
    capacity, cols, width = features.shape
    shape = (RIM + 1, cols, width)
    return pl.pallas_call(
        rim_body,
        grid=(1,),
        in_specs=[in_scalars(), anywhere(), anywhere()],
        out_specs=whole(shape),
        out_shape=jax.ShapeDtypeStruct(shape, features.dtype),
        scratch_shapes=[pltpu.SemaphoreType.DMA((2,))],
        compiler_params=params(),
        name="rim_rows",
    )(bands, features, cotangent)


def column_sums(left, mid, right, column, last):
    from_left = jnp.where(column == 0, 0.0, pltpu.roll(left, 1, 0))
    from_right = jnp.where(column == last, 0.0, pltpu.roll(right, last, 0))
    return mid + from_left + from_right


def spread_taps(taps_ref, lanes, cols):
    taps = taps_ref[...].astype(F32)
    return [jnp.broadcast_to(taps[i : i + 1, lanes], (cols, LANES)) for i in range(9)]


def forward_body(bands_ref, features_ref, other_ref, rim_ref, expand_ref, taps_ref, project_ref, first_ref,
                 normed_ref, slab_ref, slope_one_ref, slope_two_ref, slab, normed_one, expanded, hidden, hidden_two,
                 total, sems):
    step = pl.program_id(0)
    rows, cols, width = slab.shape
    own = rows - 2 * RIM
    chunk = expand_ref.shape[1]

    @pl.when(step == 0)
    def _():
        sources = (features_ref, other_ref, rim_ref)
        pieces = [(0, RIM), (RIM, BAND), (RIM + BAND, BAND), (RIM + 2 * BAND, RIM)]
        for index, (first, count) in enumerate(pieces):
            start_pull(bands_ref, first - RIM, sources, count, slab.at[pl.ds(first, count)], sems.at[index])
        for index, (first, count) in enumerate(pieces):
            wait_pull(sources, count, slab.at[pl.ds(first, count)], sems.at[index])
        slab_ref[...] = slab[RIM : RIM + own]
        for row in range(0, rows, 2):
            at = slice(row * cols, (row + 2) * cols)
            values = slab[row : row + 2].astype(F32).reshape(2 * cols, width)
            normed_one[at] = (values * rms_scale(values)).astype(BF16)
        total[...] = slab[1 : rows - 1].astype(F32).reshape((rows - 2) * cols, width)

    column = lax.broadcasted_iota(jnp.int32, (cols, LANES), 0)
    for lane in range(0, chunk, LANES):
        lanes = slice(lane, lane + LANES)
        if lane % WIDE == 0:
            wide = slice(lane, lane + WIDE)
            expanded[:, :, wide] = nn_dot(normed_one[...], expand_ref[:, wide]).reshape(rows, cols, WIDE)
        for row in range(rows):
            value, slope = gelu_and_slope(expanded[row, :, lanes])
            hidden[row, :, lanes] = value.astype(BF16).astype(F32)
            if RIM <= row < RIM + own:
                slope_one_ref[row - RIM, :, lanes] = slope.astype(BF16)
        taps = spread_taps(taps_ref, lanes, cols)
        for row in range(rows - 2):
            near = [hidden[row + a, :, lanes] for a in range(3)]
            sums = [
                taps[b] * near[0] + taps[3 + b] * near[1] + taps[6 + b] * near[2] for b in range(3)
            ]
            mixed = column_sums(sums[0], sums[1], sums[2], column, cols - 1)
            value, slope = gelu_and_slope(mixed)
            hidden_two[row * cols : (row + 1) * cols, lanes] = value.astype(BF16)
            slope_two_ref[row, :, lanes] = slope.astype(BF16)
    total[...] += nn_dot(hidden_two[...], project_ref[...])

    @pl.when(step == pl.num_programs(0) - 1)
    def _():
        for row in range(rows - 2):
            first = total[row * cols : (row + 1) * cols]
            first_ref[row] = first
            if 1 <= row <= own:
                normed_ref[row - 1] = (first * rms_scale(first)).astype(BF16)


def forward(bands, features, other, rim, w_expand, kernel, w_project):
    capacity, cols, width = features.shape
    own, rows = GRID_ROWS, GRID_ROWS + 2 * RIM
    hidden_width = w_expand.shape[1]
    return pl.pallas_call(
        forward_body,
        grid=(hidden_width // CHUNK,),
        in_specs=[
            in_scalars(),
            anywhere(),
            anywhere(),
            anywhere(),
            pl.BlockSpec((width, CHUNK), lambda j: (0, j)),
            pl.BlockSpec((9, CHUNK), lambda j: (0, j)),
            pl.BlockSpec((CHUNK, width), lambda j: (j, 0)),
        ],
        out_specs=[
            whole((rows - 2, cols, width)),
            whole((own, cols, width)),
            whole((own, cols, width)),
            pl.BlockSpec((own, cols, CHUNK), lambda j: (0, 0, j)),
            pl.BlockSpec((rows - 2, cols, CHUNK), lambda j: (0, 0, j)),
        ],
        out_shape=[
            jax.ShapeDtypeStruct((rows - 2, cols, width), F32),
            jax.ShapeDtypeStruct((own, cols, width), BF16),
            jax.ShapeDtypeStruct((own, cols, width), BF16),
            jax.ShapeDtypeStruct((own, cols, hidden_width), BF16),
            jax.ShapeDtypeStruct((rows - 2, cols, hidden_width), BF16),
        ],
        scratch_shapes=[
            pltpu.VMEM((rows, cols, width), BF16),
            pltpu.VMEM((rows * cols, width), BF16),
            pltpu.VMEM((rows, cols, CHUNK), F32),
            pltpu.VMEM((rows, cols, CHUNK), F32),
            pltpu.VMEM(((rows - 2) * cols, CHUNK), BF16),
            pltpu.VMEM(((rows - 2) * cols, width), F32),
            pltpu.SemaphoreType.DMA((4,)),
        ],
        compiler_params=params(),
        cost_estimate=pl.CostEstimate(
            flops=4 * rows * cols * width * hidden_width,
            bytes_accessed=12 * 1024 * 1024,
            transcendentals=2 * rows * cols * hidden_width,
        ),
        name="bottleneck_forward",
    )(bands, features, other, rim, w_expand, kernel, w_project)


def head_mask(span, head_dim):
    heads = LANES // head_dim
    row_head = np.arange(heads * span)[:, None] // span
    return (row_head == np.arange(LANES)[None, :] // head_dim).astype(np.float32)


def attention_body(normed_ref, cotangent_ref, mask_ref, qkv_ref, out_ref, added_ref, grad_ref,
                   rows_wide, in_windows, projected, grad_attended, grad_projected, attended):
    groups, own, cols, width = normed_ref.shape
    windows = cols // 8
    span = groups * 8
    head_dim = width // HEADS
    heads = LANES // head_dim
    scale = 1.0 / math.sqrt(head_dim)
    steepness = scale * math.log2(math.e)
    places = [(r, q) for r in range(own) for q in range(windows)]

    tiles = [slice(at, at + LANES) for at in range(0, width, LANES)]

    def to_windows(source_ref):
        for tile, lanes in enumerate(tiles):
            for group in range(groups):
                rows_wide[tile, group] = source_ref[group, :, :, lanes].astype(F32)
            for index, (r, q) in enumerate(places):
                pieces = [
                    rows_wide[tile, group, r, pl.ds(q, 8, stride=windows), :] for group in range(groups)
                ]
                rows = slice(index * span, (index + 1) * span)
                in_windows[rows, lanes] = jnp.concatenate(pieces, axis=0).astype(BF16)

    def to_rows(values, target_ref):
        for tile, lanes in enumerate(tiles):
            for index, (r, q) in enumerate(places):
                for group in range(groups):
                    first = index * span + group * 8
                    rows_wide[tile, group, r, pl.ds(q, 8, stride=windows), :] = values[first : first + 8, lanes]
            for group in range(groups):
                target_ref[group, :, :, lanes] = rows_wide[tile, group].astype(BF16)

    to_windows(cotangent_ref)
    grad_attended[...] = nt_dot(in_windows[...], out_ref[...]).astype(BF16)
    to_windows(normed_ref)
    projected[...] = nn_dot(in_windows[...], qkv_ref[...]).astype(BF16)

    lane_head = lax.broadcasted_iota(jnp.int32, (span, LANES), 1) // head_dim

    def spread(values):
        return jnp.concatenate([values] * heads, axis=0) * mask_ref[...]

    def per_query(values, weights):
        wide = nn_dot(values.T, weights)
        half = LANES // 2
        own = jnp.concatenate([wide[:half, :LANES], wide[half:, LANES:]], axis=0).T
        return jnp.where(lane_head % 2 == 0, own[:span], own[span:])

    def window(index, carry):
        rows = pl.ds(pl.multiple_of(index * span, span), span)
        for part in range(width // LANES):
            q_at, k_at, v_at = (
                slice(t * width + part * LANES, t * width + (part + 1) * LANES) for t in range(3)
            )
            q, k, v = projected[rows, q_at], projected[rows, k_at], projected[rows, v_at]
            q_wide = spread(q)
            g_wide = spread(grad_attended[rows, q_at])
            scores = nt_dot(k, q_wide)
            powers = jnp.exp2((scores - jnp.max(scores, axis=0, keepdims=True)) * steepness)
            weights = powers * (1.0 / jnp.sum(powers, axis=0, keepdims=True))
            half = weights.astype(BF16)
            grad_weights = nt_dot(v, g_wide)
            row_dot = jnp.sum(weights * grad_weights, axis=0, keepdims=True)
            grad_scores = (weights * (grad_weights - row_dot)).astype(BF16)
            attended[rows, q_at] = per_query(v, half).astype(BF16)
            grad_projected[rows, q_at] = (per_query(k, grad_scores) * scale).astype(BF16)
            grad_projected[rows, k_at] = (nn_dot(grad_scores, q_wide) * scale).astype(BF16)
            grad_projected[rows, v_at] = nn_dot(half, g_wide).astype(BF16)
        return carry

    lax.fori_loop(0, len(places), window, 0, unroll=4)

    to_rows(nt_dot(grad_projected[...], qkv_ref[...]), grad_ref)
    to_rows(nn_dot(attended[...], out_ref[...]), added_ref)


def attention(normed, cotangent, w_qkv, w_out):
    groups, own, cols, width = normed.shape
    tokens = groups * own * cols
    mask = head_mask(groups * 8, width // HEADS)
    out = jax.ShapeDtypeStruct(normed.shape, BF16)
    return pl.pallas_call(
        attention_body,
        grid=(1,),
        in_specs=[
            whole(normed.shape),
            whole(normed.shape),
            whole(mask.shape),
            whole(w_qkv.shape),
            whole(w_out.shape),
        ],
        out_specs=[whole(normed.shape)] * 2,
        out_shape=[out, out],
        scratch_shapes=[
            pltpu.VMEM((width // LANES, groups, own, cols, LANES), F32),
            pltpu.VMEM((tokens, width), BF16),
            pltpu.VMEM((tokens, 3 * width), BF16),
            pltpu.VMEM((tokens, width), BF16),
            pltpu.VMEM((tokens, 3 * width), BF16),
            pltpu.VMEM((tokens, width), BF16),
        ],
        compiler_params=params(),
        cost_estimate=pl.CostEstimate(
            flops=20 * tokens * width * width,
            bytes_accessed=4 * 1024 * 1024,
            transcendentals=tokens * 64 * HEADS,
        ),
        name="window_attention",
    )(normed, cotangent, jnp.asarray(mask, BF16), w_qkv, w_out)


def backward_body(bands_ref, cotangent_ref, other_ref, rim_ref, slab_ref, first_ref, grad_slab_ref, grad_ref,
                  pair_ref, next_ref, slope_one_ref, slope_two_ref, expand_ref, taps_ref, project_ref,
                  out_ref, rims, grad_first, grad_rows, grads, mixed, expanded, total, sems):
    step = pl.program_id(0)
    own, cols, width = slab_ref.shape
    chunk = expand_ref.shape[1]

    @pl.when(step == 0)
    def _():
        sources = (cotangent_ref, other_ref, rim_ref)
        for side, first in enumerate((-1, own)):
            start_pull(bands_ref, first, sources, 1, rims.at[pl.ds(side, 1)], sems.at[side], RIM)
        total[...] = jnp.zeros_like(total)

        def through_norm(cotangent, grad, first):
            rms = rms_scale(first)
            normed = first * rms
            grad = grad.astype(F32)
            inner = jnp.mean(grad * normed, -1, keepdims=True)
            return cotangent.astype(F32) + rms * (grad - normed * inner)

        for row in range(own):
            result = through_norm(grad_slab_ref[row], grad_ref[row], first_ref[row + 1])
            grad_first[row * cols : (row + 1) * cols] = result
            grad_rows[(row + 1) * cols : (row + 2) * cols] = result.astype(BF16)
        for side in range(2):
            wait_pull(sources, 1, rims.at[pl.ds(side, 1)], sems.at[side])
        leads = lax.rem(lax.axis_index("row"), 2) == 0
        above = jnp.where(leads, next_ref[0].astype(F32), pair_ref[0].astype(F32))
        below = jnp.where(leads, pair_ref[0].astype(F32), next_ref[0].astype(F32))
        grad_rows[0:cols] = through_norm(rims[0], above, first_ref[0]).astype(BF16)
        grad_rows[(own + 1) * cols :] = through_norm(rims[1], below, first_ref[own + 1]).astype(BF16)

    column = lax.broadcasted_iota(jnp.int32, (cols, LANES), 0)
    for lane in range(0, chunk, LANES):
        lanes = slice(lane, lane + LANES)
        if lane % WIDE == 0:
            wide = slice(lane, lane + WIDE)
            grads[:, :, wide] = nt_dot(grad_rows[...], project_ref[wide, :]).reshape(own + 2, cols, WIDE)
        for row in range(own + 2):
            slope = slope_two_ref[row, :, lanes].astype(F32)
            mixed[row, :, lanes] = (grads[row, :, lanes] * slope).astype(BF16).astype(F32)
        taps = spread_taps(taps_ref, lanes, cols)
        for row in range(own):
            near = [mixed[row + a, :, lanes] for a in range(3)]
            sums = [
                taps[8 - b] * near[0] + taps[5 - b] * near[1] + taps[2 - b] * near[2] for b in range(3)
            ]
            grad = column_sums(sums[0], sums[1], sums[2], column, cols - 1)
            slope = slope_one_ref[row, :, lanes].astype(F32)
            expanded[row * cols : (row + 1) * cols, lanes] = (grad * slope).astype(BF16)
    total[...] += nt_dot(expanded[...], expand_ref[...])

    @pl.when(step == pl.num_programs(0) - 1)
    def _():
        for row in range(own):
            at = slice(row * cols, (row + 1) * cols)
            values = slab_ref[row].astype(F32)
            rms = rms_scale(values)
            normed = values * rms
            grad = total[at]
            inner = jnp.mean(grad * normed, -1, keepdims=True)
            out_ref[row] = (grad_first[at] + rms * (grad - normed * inner)).astype(BF16)


def backward(bands, cotangent, other, rim, slab, first, grad_slab, grad, pair_row, next_row, slope_one,
             slope_two, w_expand, kernel, w_project):
    own, cols, width = slab.shape
    hidden_width = w_expand.shape[1]
    return pl.pallas_call(
        backward_body,
        grid=(hidden_width // CHUNK,),
        in_specs=[
            in_scalars(),
            anywhere(),
            anywhere(),
            anywhere(),
            whole(slab.shape),
            whole(first.shape),
            whole(grad_slab.shape),
            whole(grad.shape),
            whole(pair_row.shape),
            whole(next_row.shape),
            pl.BlockSpec((own, cols, CHUNK), lambda j: (0, 0, j)),
            pl.BlockSpec((own + 2, cols, CHUNK), lambda j: (0, 0, j)),
            pl.BlockSpec((width, CHUNK), lambda j: (0, j)),
            pl.BlockSpec((9, CHUNK), lambda j: (0, j)),
            pl.BlockSpec((CHUNK, width), lambda j: (j, 0)),
        ],
        out_specs=whole((own, cols, width)),
        out_shape=jax.ShapeDtypeStruct((own, cols, width), BF16),
        scratch_shapes=[
            pltpu.VMEM((2, cols, width), BF16),
            pltpu.VMEM((own * cols, width), F32),
            pltpu.VMEM(((own + 2) * cols, width), BF16),
            pltpu.VMEM((own + 2, cols, CHUNK), F32),
            pltpu.VMEM((own + 2, cols, CHUNK), F32),
            pltpu.VMEM((own * cols, CHUNK), BF16),
            pltpu.VMEM((own * cols, width), F32),
            pltpu.SemaphoreType.DMA((2,)),
        ],
        compiler_params=params(),
        cost_estimate=pl.CostEstimate(
            flops=4 * (own + 2) * cols * width * hidden_width,
            bytes_accessed=12 * 1024 * 1024,
            transcendentals=0,
        ),
        name="bottleneck_backward",
    )(bands, cotangent, other, rim, slab, first, grad_slab, grad, pair_row, next_row, slope_one,
      slope_two, w_expand, kernel, w_project)


def window_groups(size):
    stride = size // 8
    return [[first + stride * k for k in range(8)] for first in range(stride)]


def exchange_windows(rows):
    groups = window_groups(lax.axis_size("row"))
    return lax.all_to_all(
        rows, "row", split_axis=0, concat_axis=0, tiled=True, axis_index_groups=groups
    )


def swap_pair(rows):
    size = lax.axis_size("row")
    return lax.ppermute(rows, "row", [(i, i ^ 1) for i in range(size)])


def swap_next(rows):
    size = lax.axis_size("row")
    pairs = [(i, i + 1) for i in range(1, size - 1, 2)]
    return lax.ppermute(rows, "row", pairs + [(j, i) for i, j in pairs])


def place_rows(even, other, leads, leader_share):
    size = GRID_ROWS
    first, second = even[:BAND], even[BAND:]
    share = jnp.where(leads, leader_share, 2 * size - leader_share)
    zeros = jnp.zeros_like(first)
    low = jnp.where(leads | (share == size), first, jnp.where(share < size, second, other))
    mid = jnp.where(share < size, zeros, jnp.where(leads | (share == size), second, first))
    high = jnp.where(share > size, jnp.where(leads, other, second), zeros)
    return jnp.concatenate([low, mid, high], 0)


def on_device(features, row_bands, w_expand, kernel, w_project, w_qkv, w_out, cotangent):
    capacity, cols, width = features.shape
    device = lax.axis_index("row")
    parity = device % 2
    leads = parity == 0

    rim = swap_next(rim_rows(row_bands, features, cotangent))
    other_cotangent = swap_pair(cotangent)
    other_features = swap_pair(features)
    grad_slab = even_rows(row_bands, cotangent, other_cotangent)
    rim, grad_slab = lax.optimization_barrier((rim, grad_slab))

    grad_windows = exchange_windows(grad_slab)
    first, normed, slab, slope_one, slope_two = forward(
        row_bands, features, other_features, rim, w_expand, kernel, w_project
    )
    normed, grad_windows = lax.optimization_barrier((normed, grad_windows))
    normed_windows = exchange_windows(normed)
    shape = (8, GRID_ROWS // 8, cols, width)
    added, grad_normed = attention(
        normed_windows.reshape(shape), grad_windows.reshape(shape), w_qkv, w_out
    )
    grad_rows = exchange_windows(grad_normed.reshape(GRID_ROWS, cols, width))
    top, bottom = grad_rows[:1], grad_rows[GRID_ROWS - 1 :]
    pair_row = swap_pair(jnp.where(leads, bottom, top))
    next_row = swap_next(jnp.where(leads, top, bottom))
    added, pair_row, next_row = lax.optimization_barrier((added, pair_row, next_row))
    added_rows = exchange_windows(added.reshape(GRID_ROWS, cols, width))
    grad_input = backward(
        row_bands, cotangent, other_cotangent, rim, slab, first, grad_slab, grad_rows, pair_row, next_row,
        slope_one, slope_two, w_expand, kernel, w_project,
    )
    grad_input, added_rows = lax.optimization_barrier((grad_input, added_rows))
    final = (first[1 : GRID_ROWS + 1] + added_rows.astype(F32)).astype(BF16)
    sent = [jnp.where(leads, rows[BAND:], rows[:BAND]) for rows in (final, grad_input)]
    swapped = swap_pair(jnp.stack(sent))
    leader_share = BAND * row_bands[device - parity]
    return (
        place_rows(final, swapped[0], leads, leader_share),
        place_rows(grad_input, swapped[1], leads, leader_share),
    )


def solution(mesh):
    return jax.shard_map(
        on_device,
        mesh=mesh,
        in_specs=(
            P(("parts", "row"), None, None),
            P("parts"),
            P(),
            P(),
            P(),
            P(),
            P(),
            P(("parts", "row"), None, None),
        ),
        out_specs=(P(("parts", "row"), None, None), P(("parts", "row"), None, None)),
        check_vma=False,
    )
```

```python
import math

import jax
import jax.numpy as jnp
import numpy as np
from jax import lax
from jax.experimental import pallas as pl
from jax.experimental.pallas import tpu as pltpu
from jax.sharding import PartitionSpec as P

HEADS = 16
GRID_ROWS = 16
BAND = 8
RIM = 2
EPSILON = 1e-06
CHUNK = 512
LANES = 128
WIDE = 256
ROOT = math.sqrt(2.0 / math.pi)
CUBIC = 0.044715
F32 = jnp.float32
BF16 = jnp.bfloat16
VMEM_LIMIT = 56 * 1024 * 1024


def nt_dot(left, right):
    return lax.dot_general(left, right, (((1,), (1,)), ((), ())), preferred_element_type=F32)


def tn_dot(left, right):
    return lax.dot_general(left, right, (((0,), (0,)), ((), ())), preferred_element_type=F32)


def nn_dot(left, right):
    return jnp.dot(left, right, preferred_element_type=F32)


def rms_scale(values):
    return lax.rsqrt(jnp.mean(values * values, -1, keepdims=True) + EPSILON)


def gelu_and_slope(v):
    square = v * v
    cdf = 0.5 + 0.5 * jnp.tanh(v * (ROOT + (ROOT * CUBIC) * square))
    value = v * cdf
    slope = cdf + (value - value * cdf) * (2.0 * ROOT + (6.0 * ROOT * CUBIC) * square)
    return value, slope


def whole(shape, space=None):
    zeros = (0,) * len(shape)
    return pl.BlockSpec(shape, lambda *_: zeros)


def params():
    return pltpu.CompilerParams(vmem_limit_bytes=VMEM_LIMIT)


def anywhere():
    return pl.BlockSpec(memory_space=pl.ANY)


def in_scalars():
    return pl.BlockSpec(memory_space=pltpu.SMEM)


def shares(bands_ref):
    device = lax.axis_index("row")
    parity = lax.rem(device, 2)
    return parity, BAND * bands_ref[device - parity], BAND * bands_ref[device]


def place(bands_ref, first):
    parity, leader_share, _ = shares(bands_ref)
    row = first + GRID_ROWS * parity
    beyond = (row < 0) | (row >= 2 * GRID_ROWS)
    in_leader = row < leader_share
    in_own = in_leader == (parity == 0)
    source = jnp.where(beyond, 2, jnp.where(in_own, 0, 1))
    return source, jnp.where(beyond, 0, jnp.where(in_leader, row, row - leader_share))


def start_pull(bands_ref, first, sources, rows, target, sem, rim_row=0):
    where, row = place(bands_ref, first)
    row = jnp.where(where == 2, rim_row, row)
    for number, source in enumerate(sources):

        @pl.when(where == number)
        def _():
            pltpu.make_async_copy(source.at[pl.ds(row, rows)], target, sem).start()


def wait_pull(sources, rows, target, sem):
    pltpu.make_async_copy(sources[0].at[pl.ds(0, rows)], target, sem).wait()


def even_body(bands_ref, own_ref, other_ref, out_ref, sems):
    sources = (own_ref, other_ref)
    targets = [out_ref.at[pl.ds(BAND * half, BAND)] for half in range(2)]
    for half in range(2):
        start_pull(bands_ref, BAND * half, sources, BAND, targets[half], sems.at[half])
    for half in range(2):
        wait_pull(sources, BAND, targets[half], sems.at[half])


def even_rows(bands, own, other):
    capacity, cols, width = own.shape
    shape = (GRID_ROWS, cols, width)
    return pl.pallas_call(
        even_body,
        grid=(1,),
        in_specs=[in_scalars(), anywhere(), anywhere()],
        out_specs=whole(shape),
        out_shape=jax.ShapeDtypeStruct(shape, own.dtype),
        scratch_shapes=[pltpu.SemaphoreType.DMA((2,))],
        compiler_params=params(),
        name="even_rows",
    )(bands, own, other)


def rim_body(bands_ref, features_ref, cotangent_ref, out_ref, sems):
    parity, _, share = shares(bands_ref)
    leads = parity == 0
    copies = [
        pltpu.make_async_copy(
            features_ref.at[pl.ds(jnp.where(leads, 0, share - RIM), RIM)], out_ref.at[pl.ds(0, RIM)], sems.at[0]
        ),
        pltpu.make_async_copy(
            cotangent_ref.at[pl.ds(jnp.where(leads, 0, share - 1), 1)], out_ref.at[pl.ds(RIM, 1)], sems.at[1]
        ),
    ]
    for copy in copies:
        copy.start()
    for copy in copies:
        copy.wait()


def rim_rows(bands, features, cotangent):
    capacity, cols, width = features.shape
    shape = (RIM + 1, cols, width)
    return pl.pallas_call(
        rim_body,
        grid=(1,),
        in_specs=[in_scalars(), anywhere(), anywhere()],
        out_specs=whole(shape),
        out_shape=jax.ShapeDtypeStruct(shape, features.dtype),
        scratch_shapes=[pltpu.SemaphoreType.DMA((2,))],
        compiler_params=params(),
        name="rim_rows",
    )(bands, features, cotangent)


def column_sums(left, mid, right, column, last):
    from_left = jnp.where(column == 0, 0.0, pltpu.roll(left, 1, 0))
    from_right = jnp.where(column == last, 0.0, pltpu.roll(right, last, 0))
    return mid + from_left + from_right


def loop_rows(first, stop, body):
    def step(row, carry):
        body(row)
        return carry

    lax.fori_loop(first, stop, step, 0, unroll=2)


def spread_taps(taps_ref, lanes, cols):
    taps = taps_ref[...].astype(F32)
    return [jnp.broadcast_to(taps[i : i + 1, lanes], (cols, LANES)) for i in range(9)]


def forward_body(bands_ref, features_ref, other_ref, rim_ref, expand_ref, taps_ref, project_ref, first_ref,
                 normed_ref, slab_ref, slope_one_ref, slope_two_ref, slab, normed_one, expanded, hidden, hidden_two,
                 total, sems):
    step = pl.program_id(0)
    rows, cols, width = slab.shape
    own = rows - 2 * RIM
    chunk = expand_ref.shape[1]

    @pl.when(step == 0)
    def _():
        sources = (features_ref, other_ref, rim_ref)
        pieces = [(0, RIM), (RIM, BAND), (RIM + BAND, BAND), (RIM + 2 * BAND, RIM)]
        for index, (first, count) in enumerate(pieces):
            start_pull(bands_ref, first - RIM, sources, count, slab.at[pl.ds(first, count)], sems.at[index])
        for index, (first, count) in enumerate(pieces):
            wait_pull(sources, count, slab.at[pl.ds(first, count)], sems.at[index])
        slab_ref[...] = slab[RIM : RIM + own]
        for row in range(0, rows, 2):
            at = slice(row * cols, (row + 2) * cols)
            values = slab[row : row + 2].astype(F32).reshape(2 * cols, width)
            normed_one[at] = (values * rms_scale(values)).astype(BF16)
        total[...] = slab[1 : rows - 1].astype(F32).reshape((rows - 2) * cols, width)

    column = lax.broadcasted_iota(jnp.int32, (cols, LANES), 0)
    for start in range(0, chunk, WIDE):
        wide = slice(start, start + WIDE)
        pieces = [slice(lane, lane + LANES) for lane in range(start, start + WIDE, LANES)]
        expanded[:, :, wide] = nn_dot(normed_one[...], expand_ref[:, wide]).reshape(rows, cols, WIDE)

        def activate(row, keep):
            for lanes in pieces:
                value, slope = gelu_and_slope(expanded[row, :, lanes])
                hidden[row, :, lanes] = value.astype(BF16).astype(F32)
                if keep:
                    slope_one_ref[row - RIM, :, lanes] = slope.astype(BF16)

        for row in (0, 1, rows - 2, rows - 1):
            activate(row, False)
        loop_rows(RIM, RIM + own, lambda row: activate(row, True))
        taps = [spread_taps(taps_ref, lanes, cols) for lanes in pieces]

        def mix(row):
            for lanes, tap in zip(pieces, taps):
                near = [hidden[row + a, :, lanes] for a in range(3)]
                sums = [
                    tap[b] * near[0] + tap[3 + b] * near[1] + tap[6 + b] * near[2] for b in range(3)
                ]
                mixed = column_sums(sums[0], sums[1], sums[2], column, cols - 1)
                value, slope = gelu_and_slope(mixed)
                hidden_two[pl.ds(pl.multiple_of(row * cols, cols), cols), lanes] = value.astype(BF16)
                slope_two_ref[row, :, lanes] = slope.astype(BF16)

        loop_rows(0, rows - 2, mix)
    total[...] += nn_dot(hidden_two[...], project_ref[...])

    @pl.when(step == pl.num_programs(0) - 1)
    def _():
        for row in range(rows - 2):
            first = total[row * cols : (row + 1) * cols]
            first_ref[row] = first
            if 1 <= row <= own:
                normed_ref[row - 1] = (first * rms_scale(first)).astype(BF16)


def forward(bands, features, other, rim, w_expand, kernel, w_project):
    capacity, cols, width = features.shape
    own, rows = GRID_ROWS, GRID_ROWS + 2 * RIM
    hidden_width = w_expand.shape[1]
    return pl.pallas_call(
        forward_body,
        grid=(hidden_width // CHUNK,),
        in_specs=[
            in_scalars(),
            anywhere(),
            anywhere(),
            anywhere(),
            pl.BlockSpec((width, CHUNK), lambda j: (0, j)),
            pl.BlockSpec((9, CHUNK), lambda j: (0, j)),
            pl.BlockSpec((CHUNK, width), lambda j: (j, 0)),
        ],
        out_specs=[
            whole((rows - 2, cols, width)),
            whole((own, cols, width)),
            whole((own, cols, width)),
            pl.BlockSpec((own, cols, CHUNK), lambda j: (0, 0, j)),
            pl.BlockSpec((rows - 2, cols, CHUNK), lambda j: (0, 0, j)),
        ],
        out_shape=[
            jax.ShapeDtypeStruct((rows - 2, cols, width), F32),
            jax.ShapeDtypeStruct((own, cols, width), BF16),
            jax.ShapeDtypeStruct((own, cols, width), BF16),
            jax.ShapeDtypeStruct((own, cols, hidden_width), BF16),
            jax.ShapeDtypeStruct((rows - 2, cols, hidden_width), BF16),
        ],
        scratch_shapes=[
            pltpu.VMEM((rows, cols, width), BF16),
            pltpu.VMEM((rows * cols, width), BF16),
            pltpu.VMEM((rows, cols, CHUNK), F32),
            pltpu.VMEM((rows, cols, CHUNK), F32),
            pltpu.VMEM(((rows - 2) * cols, CHUNK), BF16),
            pltpu.VMEM(((rows - 2) * cols, width), F32),
            pltpu.SemaphoreType.DMA((4,)),
        ],
        compiler_params=params(),
        cost_estimate=pl.CostEstimate(
            flops=4 * rows * cols * width * hidden_width,
            bytes_accessed=12 * 1024 * 1024,
            transcendentals=2 * rows * cols * hidden_width,
        ),
        name="bottleneck_forward",
    )(bands, features, other, rim, w_expand, kernel, w_project)


def head_mask(span, head_dim):
    heads = LANES // head_dim
    row_head = np.arange(heads * span)[:, None] // span
    return (row_head == np.arange(LANES)[None, :] // head_dim).astype(np.float32)


def attention_body(normed_ref, cotangent_ref, mask_ref, qkv_ref, out_ref, added_ref, grad_ref,
                   rows_wide, in_windows, projected, grad_attended, grad_projected, attended):
    groups, own, cols, width = normed_ref.shape
    windows = cols // 8
    span = groups * 8
    head_dim = width // HEADS
    heads = LANES // head_dim
    scale = 1.0 / math.sqrt(head_dim)
    steepness = scale * math.log2(math.e)
    places = [(r, q) for r in range(own) for q in range(windows)]

    tiles = [slice(at, at + LANES) for at in range(0, width, LANES)]

    def to_windows(source_ref):
        for tile, lanes in enumerate(tiles):
            for group in range(groups):
                rows_wide[tile, group] = source_ref[group, :, :, lanes].astype(F32)
            for index, (r, q) in enumerate(places):
                pieces = [
                    rows_wide[tile, group, r, pl.ds(q, 8, stride=windows), :] for group in range(groups)
                ]
                rows = slice(index * span, (index + 1) * span)
                in_windows[rows, lanes] = jnp.concatenate(pieces, axis=0).astype(BF16)

    def to_rows(values, target_ref):
        for tile, lanes in enumerate(tiles):
            for index, (r, q) in enumerate(places):
                for group in range(groups):
                    first = index * span + group * 8
                    rows_wide[tile, group, r, pl.ds(q, 8, stride=windows), :] = values[first : first + 8, lanes]
            for group in range(groups):
                target_ref[group, :, :, lanes] = rows_wide[tile, group].astype(BF16)

    to_windows(cotangent_ref)
    grad_attended[...] = nt_dot(in_windows[...], out_ref[...]).astype(BF16)
    to_windows(normed_ref)
    projected[...] = nn_dot(in_windows[...], qkv_ref[...]).astype(BF16)

    lane_head = lax.broadcasted_iota(jnp.int32, (span, LANES), 1) // head_dim

    def spread(values):
        return jnp.concatenate([values] * heads, axis=0) * mask_ref[...]

    def per_query(values, weights):
        wide = nn_dot(values.T, weights)
        half = LANES // 2
        own = jnp.concatenate([wide[:half, :LANES], wide[half:, LANES:]], axis=0).T
        return jnp.where(lane_head % 2 == 0, own[:span], own[span:])

    def window(index, carry):
        rows = pl.ds(pl.multiple_of(index * span, span), span)
        for part in range(width // LANES):
            q_at, k_at, v_at = (
                slice(t * width + part * LANES, t * width + (part + 1) * LANES) for t in range(3)
            )
            q, k, v = projected[rows, q_at], projected[rows, k_at], projected[rows, v_at]
            q_wide = spread(q)
            g_wide = spread(grad_attended[rows, q_at])
            scores = nt_dot(k, q_wide)
            powers = jnp.exp2((scores - jnp.max(scores, axis=0, keepdims=True)) * steepness)
            weights = powers * (1.0 / jnp.sum(powers, axis=0, keepdims=True))
            half = weights.astype(BF16)
            grad_weights = nt_dot(v, g_wide)
            row_dot = jnp.sum(weights * grad_weights, axis=0, keepdims=True)
            grad_scores = (weights * (grad_weights - row_dot)).astype(BF16)
            attended[rows, q_at] = per_query(v, half).astype(BF16)
            grad_projected[rows, q_at] = (per_query(k, grad_scores) * scale).astype(BF16)
            grad_projected[rows, k_at] = (nn_dot(grad_scores, q_wide) * scale).astype(BF16)
            grad_projected[rows, v_at] = nn_dot(half, g_wide).astype(BF16)
        return carry

    lax.fori_loop(0, len(places), window, 0, unroll=2)

    to_rows(nt_dot(grad_projected[...], qkv_ref[...]), grad_ref)
    to_rows(nn_dot(attended[...], out_ref[...]), added_ref)


def attention(normed, cotangent, w_qkv, w_out):
    groups, own, cols, width = normed.shape
    tokens = groups * own * cols
    mask = head_mask(groups * 8, width // HEADS)
    out = jax.ShapeDtypeStruct(normed.shape, BF16)
    return pl.pallas_call(
        attention_body,
        grid=(1,),
        in_specs=[
            whole(normed.shape),
            whole(normed.shape),
            whole(mask.shape),
            whole(w_qkv.shape),
            whole(w_out.shape),
        ],
        out_specs=[whole(normed.shape)] * 2,
        out_shape=[out, out],
        scratch_shapes=[
            pltpu.VMEM((width // LANES, groups, own, cols, LANES), F32),
            pltpu.VMEM((tokens, width), BF16),
            pltpu.VMEM((tokens, 3 * width), BF16),
            pltpu.VMEM((tokens, width), BF16),
            pltpu.VMEM((tokens, 3 * width), BF16),
            pltpu.VMEM((tokens, width), BF16),
        ],
        compiler_params=params(),
        cost_estimate=pl.CostEstimate(
            flops=20 * tokens * width * width,
            bytes_accessed=4 * 1024 * 1024,
            transcendentals=tokens * 64 * HEADS,
        ),
        name="window_attention",
    )(normed, cotangent, jnp.asarray(mask, BF16), w_qkv, w_out)


def backward_body(bands_ref, cotangent_ref, other_ref, rim_ref, slab_ref, first_ref, grad_slab_ref, grad_ref,
                  pair_ref, next_ref, slope_one_ref, slope_two_ref, expand_ref, taps_ref, project_ref,
                  out_ref, rims, grad_first, grad_rows, grads, mixed, expanded, total, sems):
    step = pl.program_id(0)
    own, cols, width = slab_ref.shape
    chunk = expand_ref.shape[1]

    @pl.when(step == 0)
    def _():
        sources = (cotangent_ref, other_ref, rim_ref)
        for side, first in enumerate((-1, own)):
            start_pull(bands_ref, first, sources, 1, rims.at[pl.ds(side, 1)], sems.at[side], RIM)
        total[...] = jnp.zeros_like(total)

        def through_norm(cotangent, grad, first):
            rms = rms_scale(first)
            normed = first * rms
            grad = grad.astype(F32)
            inner = jnp.mean(grad * normed, -1, keepdims=True)
            return cotangent.astype(F32) + rms * (grad - normed * inner)

        for row in range(own):
            result = through_norm(grad_slab_ref[row], grad_ref[row], first_ref[row + 1])
            grad_first[row * cols : (row + 1) * cols] = result
            grad_rows[(row + 1) * cols : (row + 2) * cols] = result.astype(BF16)
        for side in range(2):
            wait_pull(sources, 1, rims.at[pl.ds(side, 1)], sems.at[side])
        leads = lax.rem(lax.axis_index("row"), 2) == 0
        above = jnp.where(leads, next_ref[0].astype(F32), pair_ref[0].astype(F32))
        below = jnp.where(leads, pair_ref[0].astype(F32), next_ref[0].astype(F32))
        grad_rows[0:cols] = through_norm(rims[0], above, first_ref[0]).astype(BF16)
        grad_rows[(own + 1) * cols :] = through_norm(rims[1], below, first_ref[own + 1]).astype(BF16)

    column = lax.broadcasted_iota(jnp.int32, (cols, LANES), 0)
    for start in range(0, chunk, WIDE):
        wide = slice(start, start + WIDE)
        pieces = [slice(lane, lane + LANES) for lane in range(start, start + WIDE, LANES)]
        grads[:, :, wide] = nt_dot(grad_rows[...], project_ref[wide, :]).reshape(own + 2, cols, WIDE)

        def through_gelu(row):
            for lanes in pieces:
                slope = slope_two_ref[row, :, lanes].astype(F32)
                mixed[row, :, lanes] = (grads[row, :, lanes] * slope).astype(BF16).astype(F32)

        loop_rows(0, own + 2, through_gelu)
        taps = [spread_taps(taps_ref, lanes, cols) for lanes in pieces]

        def unmix(row):
            for lanes, tap in zip(pieces, taps):
                near = [mixed[row + a, :, lanes] for a in range(3)]
                sums = [
                    tap[8 - b] * near[0] + tap[5 - b] * near[1] + tap[2 - b] * near[2] for b in range(3)
                ]
                grad = column_sums(sums[0], sums[1], sums[2], column, cols - 1)
                slope = slope_one_ref[row, :, lanes].astype(F32)
                expanded[pl.ds(pl.multiple_of(row * cols, cols), cols), lanes] = (grad * slope).astype(BF16)

        loop_rows(0, own, unmix)
    total[...] += nt_dot(expanded[...], expand_ref[...])

    @pl.when(step == pl.num_programs(0) - 1)
    def _():
        for row in range(own):
            at = slice(row * cols, (row + 1) * cols)
            values = slab_ref[row].astype(F32)
            rms = rms_scale(values)
            normed = values * rms
            grad = total[at]
            inner = jnp.mean(grad * normed, -1, keepdims=True)
            out_ref[row] = (grad_first[at] + rms * (grad - normed * inner)).astype(BF16)


def backward(bands, cotangent, other, rim, slab, first, grad_slab, grad, pair_row, next_row, slope_one,
             slope_two, w_expand, kernel, w_project):
    own, cols, width = slab.shape
    hidden_width = w_expand.shape[1]
    return pl.pallas_call(
        backward_body,
        grid=(hidden_width // CHUNK,),
        in_specs=[
            in_scalars(),
            anywhere(),
            anywhere(),
            anywhere(),
            whole(slab.shape),
            whole(first.shape),
            whole(grad_slab.shape),
            whole(grad.shape),
            whole(pair_row.shape),
            whole(next_row.shape),
            pl.BlockSpec((own, cols, CHUNK), lambda j: (0, 0, j)),
            pl.BlockSpec((own + 2, cols, CHUNK), lambda j: (0, 0, j)),
            pl.BlockSpec((width, CHUNK), lambda j: (0, j)),
            pl.BlockSpec((9, CHUNK), lambda j: (0, j)),
            pl.BlockSpec((CHUNK, width), lambda j: (j, 0)),
        ],
        out_specs=whole((own, cols, width)),
        out_shape=jax.ShapeDtypeStruct((own, cols, width), BF16),
        scratch_shapes=[
            pltpu.VMEM((2, cols, width), BF16),
            pltpu.VMEM((own * cols, width), F32),
            pltpu.VMEM(((own + 2) * cols, width), BF16),
            pltpu.VMEM((own + 2, cols, CHUNK), F32),
            pltpu.VMEM((own + 2, cols, CHUNK), F32),
            pltpu.VMEM((own * cols, CHUNK), BF16),
            pltpu.VMEM((own * cols, width), F32),
            pltpu.SemaphoreType.DMA((2,)),
        ],
        compiler_params=params(),
        cost_estimate=pl.CostEstimate(
            flops=4 * (own + 2) * cols * width * hidden_width,
            bytes_accessed=12 * 1024 * 1024,
            transcendentals=0,
        ),
        name="bottleneck_backward",
    )(bands, cotangent, other, rim, slab, first, grad_slab, grad, pair_row, next_row, slope_one,
      slope_two, w_expand, kernel, w_project)


def window_groups(size):
    stride = size // 8
    return [[first + stride * k for k in range(8)] for first in range(stride)]


def exchange_windows(rows):
    groups = window_groups(lax.axis_size("row"))
    return lax.all_to_all(
        rows, "row", split_axis=0, concat_axis=0, tiled=True, axis_index_groups=groups
    )


def swap_pair(rows):
    size = lax.axis_size("row")
    return lax.ppermute(rows, "row", [(i, i ^ 1) for i in range(size)])


def swap_next(rows):
    size = lax.axis_size("row")
    pairs = [(i, i + 1) for i in range(1, size - 1, 2)]
    return lax.ppermute(rows, "row", pairs + [(j, i) for i, j in pairs])


def place_rows(even, other, leads, leader_share):
    size = GRID_ROWS
    first, second = even[:BAND], even[BAND:]
    share = jnp.where(leads, leader_share, 2 * size - leader_share)
    zeros = jnp.zeros_like(first)
    low = jnp.where(leads | (share == size), first, jnp.where(share < size, second, other))
    mid = jnp.where(share < size, zeros, jnp.where(leads | (share == size), second, first))
    high = jnp.where(share > size, jnp.where(leads, other, second), zeros)
    return jnp.concatenate([low, mid, high], 0)


def on_device(features, row_bands, w_expand, kernel, w_project, w_qkv, w_out, cotangent):
    capacity, cols, width = features.shape
    device = lax.axis_index("row")
    parity = device % 2
    leads = parity == 0

    rim = swap_next(rim_rows(row_bands, features, cotangent))
    other_cotangent = swap_pair(cotangent)
    other_features = swap_pair(features)
    grad_slab = even_rows(row_bands, cotangent, other_cotangent)
    rim, grad_slab = lax.optimization_barrier((rim, grad_slab))

    grad_windows = exchange_windows(grad_slab)
    first, normed, slab, slope_one, slope_two = forward(
        row_bands, features, other_features, rim, w_expand, kernel, w_project
    )
    normed, grad_windows = lax.optimization_barrier((normed, grad_windows))
    normed_windows = exchange_windows(normed)
    shape = (8, GRID_ROWS // 8, cols, width)
    added, grad_normed = attention(
        normed_windows.reshape(shape), grad_windows.reshape(shape), w_qkv, w_out
    )
    grad_rows = exchange_windows(grad_normed.reshape(GRID_ROWS, cols, width))
    top, bottom = grad_rows[:1], grad_rows[GRID_ROWS - 1 :]
    pair_row = swap_pair(jnp.where(leads, bottom, top))
    next_row = swap_next(jnp.where(leads, top, bottom))
    added, pair_row, next_row = lax.optimization_barrier((added, pair_row, next_row))
    added_rows = exchange_windows(added.reshape(GRID_ROWS, cols, width))
    grad_input = backward(
        row_bands, cotangent, other_cotangent, rim, slab, first, grad_slab, grad_rows, pair_row, next_row,
        slope_one, slope_two, w_expand, kernel, w_project,
    )
    grad_input, added_rows = lax.optimization_barrier((grad_input, added_rows))
    final = (first[1 : GRID_ROWS + 1] + added_rows.astype(F32)).astype(BF16)
    sent = [jnp.where(leads, rows[BAND:], rows[:BAND]) for rows in (final, grad_input)]
    swapped = swap_pair(jnp.stack(sent))
    leader_share = BAND * row_bands[device - parity]
    return (
        place_rows(final, swapped[0], leads, leader_share),
        place_rows(grad_input, swapped[1], leads, leader_share),
    )


def solution(mesh):
    return jax.shard_map(
        on_device,
        mesh=mesh,
        in_specs=(
            P(("parts", "row"), None, None),
            P("parts"),
            P(),
            P(),
            P(),
            P(),
            P(),
            P(("parts", "row"), None, None),
        ),
        out_specs=(P(("parts", "row"), None, None), P(("parts", "row"), None, None)),
        check_vma=False,
    )
```

```python
import math

import jax
import jax.numpy as jnp
import numpy as np
from jax import lax
from jax.experimental import pallas as pl
from jax.experimental.pallas import tpu as pltpu
from jax.sharding import PartitionSpec as P

HEADS = 16
GRID_ROWS = 16
BAND = 8
RIM = 2
EPSILON = 1e-06
CHUNK = 512
LANES = 128
ROOT = math.sqrt(2.0 / math.pi)
CUBIC = 0.044715
F32 = jnp.float32
BF16 = jnp.bfloat16
VMEM_LIMIT = 56 * 1024 * 1024


def nt_dot(left, right):
    return lax.dot_general(left, right, (((1,), (1,)), ((), ())), preferred_element_type=F32)


def tn_dot(left, right):
    return lax.dot_general(left, right, (((0,), (0,)), ((), ())), preferred_element_type=F32)


def nn_dot(left, right):
    return jnp.dot(left, right, preferred_element_type=F32)


def rms_scale(values):
    return lax.rsqrt(jnp.mean(values * values, -1, keepdims=True) + EPSILON)


def gelu_parts(v):
    square = v * v
    cdf = 0.5 + 0.5 * jnp.tanh(v * (ROOT + (ROOT * CUBIC) * square))
    return square, cdf, v * cdf


def gelu(v):
    return gelu_parts(v)[2]


def gelu_slope(v):
    square, cdf, value = gelu_parts(v)
    return cdf + (value - value * cdf) * (2.0 * ROOT + (6.0 * ROOT * CUBIC) * square)


def whole(shape, space=None):
    zeros = (0,) * len(shape)
    return pl.BlockSpec(shape, lambda *_: zeros)


def params():
    return pltpu.CompilerParams(vmem_limit_bytes=VMEM_LIMIT)


def anywhere():
    return pl.BlockSpec(memory_space=pl.ANY)


def in_scalars():
    return pl.BlockSpec(memory_space=pltpu.SMEM)


def shares(bands_ref):
    device = lax.axis_index("row")
    parity = lax.rem(device, 2)
    return parity, BAND * bands_ref[device - parity], BAND * bands_ref[device]


def place(bands_ref, first):
    parity, leader_share, _ = shares(bands_ref)
    row = first + GRID_ROWS * parity
    beyond = (row < 0) | (row >= 2 * GRID_ROWS)
    in_leader = row < leader_share
    in_own = in_leader == (parity == 0)
    source = jnp.where(beyond, 2, jnp.where(in_own, 0, 1))
    return source, jnp.where(beyond, 0, jnp.where(in_leader, row, row - leader_share))


def start_pull(bands_ref, first, sources, rows, target, sem, rim_row=0):
    where, row = place(bands_ref, first)
    row = jnp.where(where == 2, rim_row, row)
    for number, source in enumerate(sources):

        @pl.when(where == number)
        def _():
            pltpu.make_async_copy(source.at[pl.ds(row, rows)], target, sem).start()


def wait_pull(sources, rows, target, sem):
    pltpu.make_async_copy(sources[0].at[pl.ds(0, rows)], target, sem).wait()


def even_body(bands_ref, own_ref, other_ref, out_ref, sems):
    sources = (own_ref, other_ref)
    targets = [out_ref.at[pl.ds(BAND * half, BAND)] for half in range(2)]
    for half in range(2):
        start_pull(bands_ref, BAND * half, sources, BAND, targets[half], sems.at[half])
    for half in range(2):
        wait_pull(sources, BAND, targets[half], sems.at[half])


def even_rows(bands, own, other):
    capacity, cols, width = own.shape
    shape = (GRID_ROWS, cols, width)
    return pl.pallas_call(
        even_body,
        grid=(1,),
        in_specs=[in_scalars(), anywhere(), anywhere()],
        out_specs=whole(shape),
        out_shape=jax.ShapeDtypeStruct(shape, own.dtype),
        scratch_shapes=[pltpu.SemaphoreType.DMA((2,))],
        compiler_params=params(),
        name="even_rows",
    )(bands, own, other)


def rim_body(bands_ref, features_ref, cotangent_ref, out_ref, sems):
    parity, _, share = shares(bands_ref)
    leads = parity == 0
    copies = [
        pltpu.make_async_copy(
            features_ref.at[pl.ds(jnp.where(leads, 0, share - RIM), RIM)], out_ref.at[pl.ds(0, RIM)], sems.at[0]
        ),
        pltpu.make_async_copy(
            cotangent_ref.at[pl.ds(jnp.where(leads, 0, share - 1), 1)], out_ref.at[pl.ds(RIM, 1)], sems.at[1]
        ),
    ]
    for copy in copies:
        copy.start()
    for copy in copies:
        copy.wait()


def rim_rows(bands, features, cotangent):
    capacity, cols, width = features.shape
    shape = (RIM + 1, cols, width)
    return pl.pallas_call(
        rim_body,
        grid=(1,),
        in_specs=[in_scalars(), anywhere(), anywhere()],
        out_specs=whole(shape),
        out_shape=jax.ShapeDtypeStruct(shape, features.dtype),
        scratch_shapes=[pltpu.SemaphoreType.DMA((2,))],
        compiler_params=params(),
        name="rim_rows",
    )(bands, features, cotangent)


def column_sums(left, mid, right, column, last):
    from_left = jnp.where(column == 0, 0.0, pltpu.roll(left, 1, 0))
    from_right = jnp.where(column == last, 0.0, pltpu.roll(right, last, 0))
    return mid + from_left + from_right


def spread_taps(taps_ref, lanes, cols):
    taps = taps_ref[...].astype(F32)
    return [jnp.broadcast_to(taps[i : i + 1, lanes], (cols, LANES)) for i in range(9)]


def forward_body(bands_ref, features_ref, other_ref, rim_ref, expand_ref, taps_ref, project_ref, first_ref,
                 normed_ref, slab_ref, expanded_ref, mixed_ref, slab, normed_one, hidden, hidden_two,
                 total, sems):
    step = pl.program_id(0)
    rows, cols, width = slab.shape
    own = rows - 2 * RIM
    chunk = expand_ref.shape[1]

    @pl.when(step == 0)
    def _():
        sources = (features_ref, other_ref, rim_ref)
        pieces = [(0, RIM), (RIM, BAND), (RIM + BAND, BAND), (RIM + 2 * BAND, RIM)]
        for index, (first, count) in enumerate(pieces):
            start_pull(bands_ref, first - RIM, sources, count, slab.at[pl.ds(first, count)], sems.at[index])
        for index, (first, count) in enumerate(pieces):
            wait_pull(sources, count, slab.at[pl.ds(first, count)], sems.at[index])
        slab_ref[...] = slab[RIM : RIM + own]
        for row in range(0, rows, 2):
            at = slice(row * cols, (row + 2) * cols)
            values = slab[row : row + 2].astype(F32).reshape(2 * cols, width)
            normed_one[at] = (values * rms_scale(values)).astype(BF16)
        total[...] = slab[1 : rows - 1].astype(F32).reshape((rows - 2) * cols, width)

    for row in range(0, rows, 4):
        expanded = nn_dot(normed_one[row * cols : (row + 4) * cols, :], expand_ref[...])
        for inner in range(4):
            for lane in range(0, chunk, LANES):
                lanes = slice(lane, lane + LANES)
                values = expanded[inner * cols : (inner + 1) * cols, lanes]
                hidden[row + inner, :, lanes] = gelu(values).astype(BF16).astype(F32)
                if RIM <= row + inner < RIM + own:
                    expanded_ref[row + inner - RIM, :, lanes] = values

    column = lax.broadcasted_iota(jnp.int32, (cols, LANES), 0)
    for lane in range(0, chunk, LANES):
        lanes = slice(lane, lane + LANES)
        taps = spread_taps(taps_ref, lanes, cols)
        for row in range(rows - 2):
            near = [hidden[row + a, :, lanes] for a in range(3)]
            sums = [
                taps[b] * near[0] + taps[3 + b] * near[1] + taps[6 + b] * near[2] for b in range(3)
            ]
            mixed = column_sums(sums[0], sums[1], sums[2], column, cols - 1)
            hidden_two[row * cols : (row + 1) * cols, lanes] = gelu(mixed).astype(BF16)
            mixed_ref[row, :, lanes] = mixed
    total[...] += nn_dot(hidden_two[...], project_ref[...])

    @pl.when(step == pl.num_programs(0) - 1)
    def _():
        for row in range(rows - 2):
            first = total[row * cols : (row + 1) * cols]
            first_ref[row] = first
            if 1 <= row <= own:
                normed_ref[row - 1] = (first * rms_scale(first)).astype(BF16)


def forward(bands, features, other, rim, w_expand, kernel, w_project):
    capacity, cols, width = features.shape
    own, rows = GRID_ROWS, GRID_ROWS + 2 * RIM
    hidden_width = w_expand.shape[1]
    return pl.pallas_call(
        forward_body,
        grid=(hidden_width // CHUNK,),
        in_specs=[
            in_scalars(),
            anywhere(),
            anywhere(),
            anywhere(),
            pl.BlockSpec((width, CHUNK), lambda j: (0, j)),
            pl.BlockSpec((9, CHUNK), lambda j: (0, j)),
            pl.BlockSpec((CHUNK, width), lambda j: (j, 0)),
        ],
        out_specs=[
            whole((rows - 2, cols, width)),
            whole((own, cols, width)),
            whole((own, cols, width)),
            pl.BlockSpec((own, cols, CHUNK), lambda j: (0, 0, j)),
            pl.BlockSpec((rows - 2, cols, CHUNK), lambda j: (0, 0, j)),
        ],
        out_shape=[
            jax.ShapeDtypeStruct((rows - 2, cols, width), F32),
            jax.ShapeDtypeStruct((own, cols, width), BF16),
            jax.ShapeDtypeStruct((own, cols, width), BF16),
            jax.ShapeDtypeStruct((own, cols, hidden_width), F32),
            jax.ShapeDtypeStruct((rows - 2, cols, hidden_width), F32),
        ],
        scratch_shapes=[
            pltpu.VMEM((rows, cols, width), BF16),
            pltpu.VMEM((rows * cols, width), BF16),
            pltpu.VMEM((rows, cols, CHUNK), F32),
            pltpu.VMEM(((rows - 2) * cols, CHUNK), BF16),
            pltpu.VMEM(((rows - 2) * cols, width), F32),
            pltpu.SemaphoreType.DMA((4,)),
        ],
        compiler_params=params(),
        cost_estimate=pl.CostEstimate(
            flops=4 * rows * cols * width * hidden_width,
            bytes_accessed=12 * 1024 * 1024,
            transcendentals=2 * rows * cols * hidden_width,
        ),
        name="bottleneck_forward",
    )(bands, features, other, rim, w_expand, kernel, w_project)


def slopes_body(expanded_ref, mixed_ref, slope_one_ref, slope_two_ref):
    for source, target in ((expanded_ref, slope_one_ref), (mixed_ref, slope_two_ref)):
        rows, _, chunk = source.shape
        for row in range(rows):
            for lane in range(0, chunk, LANES):
                lanes = slice(lane, lane + LANES)
                target[row, :, lanes] = gelu_slope(source[row, :, lanes]).astype(BF16)


def slopes(expanded, mixed):
    hidden_width = expanded.shape[2]
    blocks = [
        pl.BlockSpec(values.shape[:2] + (CHUNK,), lambda j: (0, 0, j)) for values in (expanded, mixed)
    ]
    return pl.pallas_call(
        slopes_body,
        grid=(hidden_width // CHUNK,),
        in_specs=blocks,
        out_specs=blocks,
        out_shape=[jax.ShapeDtypeStruct(values.shape, BF16) for values in (expanded, mixed)],
        compiler_params=params(),
        cost_estimate=pl.CostEstimate(
            flops=15 * (expanded.size + mixed.size),
            bytes_accessed=6 * (expanded.size + mixed.size),
            transcendentals=expanded.size + mixed.size,
        ),
        name="gelu_slopes",
    )(expanded, mixed)


def head_mask(span, head_dim):
    heads = LANES // head_dim
    row_head = np.arange(heads * span)[:, None] // span
    return (row_head == np.arange(LANES)[None, :] // head_dim).astype(np.float32)


def lane_tiles(width):
    return [slice(at, at + LANES) for at in range(0, width, LANES)]


def window_places(own, cols):
    return [(r, q) for r in range(own) for q in range(cols // 8)]


def to_windows(source_ref, rows_wide, target):
    groups, own, cols, width = source_ref.shape
    span = groups * 8
    for tile, lanes in enumerate(lane_tiles(width)):
        for group in range(groups):
            rows_wide[tile, group] = source_ref[group, :, :, lanes].astype(F32)
        for index, (r, q) in enumerate(window_places(own, cols)):
            pieces = [
                rows_wide[tile, group, r, pl.ds(q, 8, stride=cols // 8), :] for group in range(groups)
            ]
            rows = slice(index * span, (index + 1) * span)
            target[rows, lanes] = jnp.concatenate(pieces, axis=0).astype(BF16)


def to_rows(values, rows_wide, target_ref):
    groups, own, cols, width = target_ref.shape
    span = groups * 8
    for tile, lanes in enumerate(lane_tiles(width)):
        for index, (r, q) in enumerate(window_places(own, cols)):
            for group in range(groups):
                first = index * span + group * 8
                rows_wide[tile, group, r, pl.ds(q, 8, stride=cols // 8), :] = values[first : first + 8, lanes]
        for group in range(groups):
            target_ref[group, :, :, lanes] = rows_wide[tile, group].astype(BF16)


def wide_scratch(shape):
    groups, own, cols, width = shape
    return pltpu.VMEM((width // LANES, groups, own, cols, LANES), F32)


def grad_attended_body(cotangent_ref, out_ref, grad_ref, rows_wide, in_windows):
    to_windows(cotangent_ref, rows_wide, in_windows)
    grad_ref[...] = nt_dot(in_windows[...], out_ref[...]).astype(BF16)


def attended_gradient(cotangent, w_out):
    groups, own, cols, width = cotangent.shape
    shape = (groups * own * cols, width)
    return pl.pallas_call(
        grad_attended_body,
        grid=(1,),
        in_specs=[whole(cotangent.shape), whole(w_out.shape)],
        out_specs=whole(shape),
        out_shape=jax.ShapeDtypeStruct(shape, BF16),
        scratch_shapes=[wide_scratch(cotangent.shape), pltpu.VMEM(shape, BF16)],
        compiler_params=params(),
        cost_estimate=pl.CostEstimate(
            flops=2 * shape[0] * width * width, bytes_accessed=2 * 1024 * 1024, transcendentals=0
        ),
        name="attended_gradient",
    )(cotangent, w_out)


def per_query(values, weights, span, head_dim):
    wide = nn_dot(values.T, weights)
    half = LANES // 2
    own = jnp.concatenate([wide[:half, :LANES], wide[half:, LANES:]], axis=0).T
    lane_head = lax.broadcasted_iota(jnp.int32, (span, LANES), 1) // head_dim
    return jnp.where(lane_head % 2 == 0, own[:span], own[span:])


def attention_body(normed_ref, grad_attended_ref, mask_ref, qkv_ref, grad_ref, weights_ref, values_ref,
                   rows_wide, in_windows, projected, grad_projected):
    groups, own, cols, width = normed_ref.shape
    span = groups * 8
    head_dim = width // HEADS
    heads = LANES // head_dim
    scale = 1.0 / math.sqrt(head_dim)
    steepness = scale * math.log2(math.e)

    to_windows(normed_ref, rows_wide, in_windows)
    projected[...] = nn_dot(in_windows[...], qkv_ref[...]).astype(BF16)
    values_ref[...] = projected[:, 2 * width :]

    def spread(values):
        return jnp.concatenate([values] * heads, axis=0) * mask_ref[...]

    def window(index, carry):
        rows = pl.ds(pl.multiple_of(index * span, span), span)
        for part in range(width // LANES):
            q_at, k_at, v_at = (
                slice(t * width + part * LANES, t * width + (part + 1) * LANES) for t in range(3)
            )
            q, k, v = projected[rows, q_at], projected[rows, k_at], projected[rows, v_at]
            q_wide = spread(q)
            g_wide = spread(grad_attended_ref[rows, q_at])
            scores = nt_dot(k, q_wide)
            powers = jnp.exp2((scores - jnp.max(scores, axis=0, keepdims=True)) * steepness)
            weights = powers * (1.0 / jnp.sum(powers, axis=0, keepdims=True))
            half = weights.astype(BF16)
            weights_ref[index, :, part * heads * span : (part + 1) * heads * span] = half
            grad_weights = nt_dot(v, g_wide)
            row_dot = jnp.sum(weights * grad_weights, axis=0, keepdims=True)
            grad_scores = (weights * (grad_weights - row_dot)).astype(BF16)
            grad_projected[rows, q_at] = (per_query(k, grad_scores, span, head_dim) * scale).astype(BF16)
            grad_projected[rows, k_at] = (nn_dot(grad_scores, q_wide) * scale).astype(BF16)
            grad_projected[rows, v_at] = nn_dot(half, g_wide).astype(BF16)
        return carry

    lax.fori_loop(0, own * cols // 8, window, 0, unroll=4)
    to_rows(nt_dot(grad_projected[...], qkv_ref[...]), rows_wide, grad_ref)


def attention(normed, grad_attended, w_qkv):
    groups, own, cols, width = normed.shape
    span = groups * 8
    tokens = groups * own * cols
    windows = tokens // span
    mask = head_mask(span, width // HEADS)
    out_shapes = [normed.shape, (windows, span, HEADS * span), (tokens, width)]
    return pl.pallas_call(
        attention_body,
        grid=(1,),
        in_specs=[
            whole(normed.shape),
            whole(grad_attended.shape),
            whole(mask.shape),
            whole(w_qkv.shape),
        ],
        out_specs=[whole(shape) for shape in out_shapes],
        out_shape=[jax.ShapeDtypeStruct(shape, BF16) for shape in out_shapes],
        scratch_shapes=[
            wide_scratch(normed.shape),
            pltpu.VMEM((tokens, width), BF16),
            pltpu.VMEM((tokens, 3 * width), BF16),
            pltpu.VMEM((tokens, 3 * width), BF16),
        ],
        compiler_params=params(),
        cost_estimate=pl.CostEstimate(
            flops=16 * tokens * width * width,
            bytes_accessed=4 * 1024 * 1024,
            transcendentals=tokens * span * HEADS,
        ),
        name="window_attention",
    )(normed, grad_attended, jnp.asarray(mask, BF16), w_qkv)


def attended_body(weights_ref, values_ref, out_ref, added_ref, rows_wide, attended):
    windows, span, wide = weights_ref.shape
    width = values_ref.shape[1]
    heads = LANES * HEADS // width
    for index in range(windows):
        rows = slice(index * span, (index + 1) * span)
        for part, lanes in enumerate(lane_tiles(width)):
            weights = weights_ref[index, :, part * heads * span : (part + 1) * heads * span]
            attended[rows, lanes] = per_query(values_ref[rows, lanes], weights, span, width // HEADS).astype(BF16)
    to_rows(nn_dot(attended[...], out_ref[...]), rows_wide, added_ref)


def attend(weights, values, w_out, shape):
    return pl.pallas_call(
        attended_body,
        grid=(1,),
        in_specs=[whole(weights.shape), whole(values.shape), whole(w_out.shape)],
        out_specs=whole(shape),
        out_shape=jax.ShapeDtypeStruct(shape, BF16),
        scratch_shapes=[wide_scratch(shape), pltpu.VMEM(values.shape, BF16)],
        compiler_params=params(),
        cost_estimate=pl.CostEstimate(
            flops=4 * values.size * values.shape[1], bytes_accessed=3 * 1024 * 1024, transcendentals=0
        ),
        name="attended_output",
    )(weights, values, w_out)


def backward_body(bands_ref, cotangent_ref, other_ref, rim_ref, slab_ref, first_ref, grad_slab_ref, grad_ref,
                  pair_ref, next_ref, slope_one_ref, slope_two_ref, expand_ref, taps_ref, project_ref,
                  out_ref, rims, grad_first, grad_rows, mixed, expanded, total, sems):
    step = pl.program_id(0)
    own, cols, width = slab_ref.shape
    chunk = expand_ref.shape[1]

    @pl.when(step == 0)
    def _():
        sources = (cotangent_ref, other_ref, rim_ref)
        for side, first in enumerate((-1, own)):
            start_pull(bands_ref, first, sources, 1, rims.at[pl.ds(side, 1)], sems.at[side], RIM)
        total[...] = jnp.zeros_like(total)

        def through_norm(cotangent, grad, first):
            rms = rms_scale(first)
            normed = first * rms
            grad = grad.astype(F32)
            inner = jnp.mean(grad * normed, -1, keepdims=True)
            return cotangent.astype(F32) + rms * (grad - normed * inner)

        for row in range(own):
            result = through_norm(grad_slab_ref[row], grad_ref[row], first_ref[row + 1])
            grad_first[row * cols : (row + 1) * cols] = result
            grad_rows[(row + 1) * cols : (row + 2) * cols] = result.astype(BF16)
        for side in range(2):
            wait_pull(sources, 1, rims.at[pl.ds(side, 1)], sems.at[side])
        leads = lax.rem(lax.axis_index("row"), 2) == 0
        above = jnp.where(leads, next_ref[0].astype(F32), pair_ref[0].astype(F32))
        below = jnp.where(leads, pair_ref[0].astype(F32), next_ref[0].astype(F32))
        grad_rows[0:cols] = through_norm(rims[0], above, first_ref[0]).astype(BF16)
        grad_rows[(own + 1) * cols :] = through_norm(rims[1], below, first_ref[own + 1]).astype(BF16)

    for row in range(0, own + 2, 6):
        grad = nt_dot(grad_rows[row * cols : (row + 6) * cols, :], project_ref[...])
        for inner in range(6):
            for lane in range(0, chunk, LANES):
                lanes = slice(lane, lane + LANES)
                slope = slope_two_ref[row + inner, :, lanes].astype(F32)
                value = grad[inner * cols : (inner + 1) * cols, lanes] * slope
                mixed[row + inner, :, lanes] = value.astype(BF16).astype(F32)

    column = lax.broadcasted_iota(jnp.int32, (cols, LANES), 0)
    for lane in range(0, chunk, LANES):
        lanes = slice(lane, lane + LANES)
        taps = spread_taps(taps_ref, lanes, cols)
        for row in range(own):
            near = [mixed[row + a, :, lanes] for a in range(3)]
            sums = [
                taps[8 - b] * near[0] + taps[5 - b] * near[1] + taps[2 - b] * near[2] for b in range(3)
            ]
            grad = column_sums(sums[0], sums[1], sums[2], column, cols - 1)
            slope = slope_one_ref[row, :, lanes].astype(F32)
            expanded[row * cols : (row + 1) * cols, lanes] = (grad * slope).astype(BF16)
    total[...] += nt_dot(expanded[...], expand_ref[...])

    @pl.when(step == pl.num_programs(0) - 1)
    def _():
        for row in range(own):
            at = slice(row * cols, (row + 1) * cols)
            values = slab_ref[row].astype(F32)
            rms = rms_scale(values)
            normed = values * rms
            grad = total[at]
            inner = jnp.mean(grad * normed, -1, keepdims=True)
            out_ref[row] = (grad_first[at] + rms * (grad - normed * inner)).astype(BF16)


def backward(bands, cotangent, other, rim, slab, first, grad_slab, grad, pair_row, next_row, slope_one,
             slope_two, w_expand, kernel, w_project):
    own, cols, width = slab.shape
    hidden_width = w_expand.shape[1]
    return pl.pallas_call(
        backward_body,
        grid=(hidden_width // CHUNK,),
        in_specs=[
            in_scalars(),
            anywhere(),
            anywhere(),
            anywhere(),
            whole(slab.shape),
            whole(first.shape),
            whole(grad_slab.shape),
            whole(grad.shape),
            whole(pair_row.shape),
            whole(next_row.shape),
            pl.BlockSpec((own, cols, CHUNK), lambda j: (0, 0, j)),
            pl.BlockSpec((own + 2, cols, CHUNK), lambda j: (0, 0, j)),
            pl.BlockSpec((width, CHUNK), lambda j: (0, j)),
            pl.BlockSpec((9, CHUNK), lambda j: (0, j)),
            pl.BlockSpec((CHUNK, width), lambda j: (j, 0)),
        ],
        out_specs=whole((own, cols, width)),
        out_shape=jax.ShapeDtypeStruct((own, cols, width), BF16),
        scratch_shapes=[
            pltpu.VMEM((2, cols, width), BF16),
            pltpu.VMEM((own * cols, width), F32),
            pltpu.VMEM(((own + 2) * cols, width), BF16),
            pltpu.VMEM((own + 2, cols, CHUNK), F32),
            pltpu.VMEM((own * cols, CHUNK), BF16),
            pltpu.VMEM((own * cols, width), F32),
            pltpu.SemaphoreType.DMA((2,)),
        ],
        compiler_params=params(),
        cost_estimate=pl.CostEstimate(
            flops=4 * (own + 2) * cols * width * hidden_width,
            bytes_accessed=12 * 1024 * 1024,
            transcendentals=0,
        ),
        name="bottleneck_backward",
    )(bands, cotangent, other, rim, slab, first, grad_slab, grad, pair_row, next_row, slope_one,
      slope_two, w_expand, kernel, w_project)


def window_groups(size):
    stride = size // 8
    return [[first + stride * k for k in range(8)] for first in range(stride)]


def exchange_windows(rows):
    groups = window_groups(lax.axis_size("row"))
    return lax.all_to_all(
        rows, "row", split_axis=0, concat_axis=0, tiled=True, axis_index_groups=groups
    )


def swap_pair(rows):
    size = lax.axis_size("row")
    return lax.ppermute(rows, "row", [(i, i ^ 1) for i in range(size)])


def swap_next(rows):
    size = lax.axis_size("row")
    pairs = [(i, i + 1) for i in range(1, size - 1, 2)]
    return lax.ppermute(rows, "row", pairs + [(j, i) for i, j in pairs])


def place_rows(even, other, leads, leader_share):
    size = GRID_ROWS
    first, second = even[:BAND], even[BAND:]
    share = jnp.where(leads, leader_share, 2 * size - leader_share)
    zeros = jnp.zeros_like(first)
    low = jnp.where(leads | (share == size), first, jnp.where(share < size, second, other))
    mid = jnp.where(share < size, zeros, jnp.where(leads | (share == size), second, first))
    high = jnp.where(share > size, jnp.where(leads, other, second), zeros)
    return jnp.concatenate([low, mid, high], 0)


def on_device(features, row_bands, w_expand, kernel, w_project, w_qkv, w_out, cotangent):
    capacity, cols, width = features.shape
    device = lax.axis_index("row")
    parity = device % 2
    leads = parity == 0

    rim = swap_next(rim_rows(row_bands, features, cotangent))
    other_cotangent = swap_pair(cotangent)
    other_features = swap_pair(features)
    grad_slab = even_rows(row_bands, cotangent, other_cotangent)
    rim, grad_slab = lax.optimization_barrier((rim, grad_slab))

    grad_windows = exchange_windows(grad_slab)
    first, normed, slab, expanded, mixed = forward(
        row_bands, features, other_features, rim, w_expand, kernel, w_project
    )
    normed, grad_windows = lax.optimization_barrier((normed, grad_windows))
    normed_windows = exchange_windows(normed)
    shape = (8, GRID_ROWS // 8, cols, width)
    slope_one, slope_two = slopes(expanded, mixed)
    grad_attended = attended_gradient(grad_windows.reshape(shape), w_out)
    normed_windows, slope_one, slope_two, grad_attended = lax.optimization_barrier(
        (normed_windows, slope_one, slope_two, grad_attended)
    )
    grad_normed, weights, values = attention(normed_windows.reshape(shape), grad_attended, w_qkv)
    grad_rows = exchange_windows(grad_normed.reshape(GRID_ROWS, cols, width))
    added = attend(weights, values, w_out, shape)
    grad_rows, added = lax.optimization_barrier((grad_rows, added))
    top, bottom = grad_rows[:1], grad_rows[GRID_ROWS - 1 :]
    pair_row = swap_pair(jnp.where(leads, bottom, top))
    next_row = swap_next(jnp.where(leads, top, bottom))
    added, pair_row, next_row = lax.optimization_barrier((added, pair_row, next_row))
    added_rows = exchange_windows(added.reshape(GRID_ROWS, cols, width))
    grad_input = backward(
        row_bands, cotangent, other_cotangent, rim, slab, first, grad_slab, grad_rows, pair_row, next_row,
        slope_one, slope_two, w_expand, kernel, w_project,
    )
    grad_input, added_rows = lax.optimization_barrier((grad_input, added_rows))
    final = (first[1 : GRID_ROWS + 1] + added_rows.astype(F32)).astype(BF16)
    sent = [jnp.where(leads, rows[BAND:], rows[:BAND]) for rows in (final, grad_input)]
    swapped = swap_pair(jnp.stack(sent))
    leader_share = BAND * row_bands[device - parity]
    return (
        place_rows(final, swapped[0], leads, leader_share),
        place_rows(grad_input, swapped[1], leads, leader_share),
    )


def solution(mesh):
    return jax.shard_map(
        on_device,
        mesh=mesh,
        in_specs=(
            P(("parts", "row"), None, None),
            P("parts"),
            P(),
            P(),
            P(),
            P(),
            P(),
            P(("parts", "row"), None, None),
        ),
        out_specs=(P(("parts", "row"), None, None), P(("parts", "row"), None, None)),
        check_vma=False,
    )
```

```python
import math

import jax
import jax.numpy as jnp
import numpy as np
from jax import lax
from jax.experimental import pallas as pl
from jax.experimental.pallas import tpu as pltpu
from jax.sharding import PartitionSpec as P

HEADS = 16
GRID_ROWS = 16
BAND = 8
RIM = 2
EPSILON = 1e-06
CHUNK = 512
LANES = 128
ROOT = math.sqrt(2.0 / math.pi)
CUBIC = 0.044715
F32 = jnp.float32
BF16 = jnp.bfloat16
VMEM_LIMIT = 20 * 1024 * 1024


def nt_dot(left, right):
    return lax.dot_general(left, right, (((1,), (1,)), ((), ())), preferred_element_type=F32)


def tn_dot(left, right):
    return lax.dot_general(left, right, (((0,), (0,)), ((), ())), preferred_element_type=F32)


def nn_dot(left, right):
    return jnp.dot(left, right, preferred_element_type=F32)


def rms_scale(values):
    return lax.rsqrt(jnp.mean(values * values, -1, keepdims=True) + EPSILON)


def gelu_parts(v):
    square = v * v
    cdf = 0.5 + 0.5 * jnp.tanh(v * (ROOT + (ROOT * CUBIC) * square))
    return square, cdf, v * cdf


def gelu(v):
    return gelu_parts(v)[2]


def gelu_slope(v):
    square, cdf, value = gelu_parts(v)
    return cdf + (value - value * cdf) * (2.0 * ROOT + (6.0 * ROOT * CUBIC) * square)


def in_vmem():
    return pl.BlockSpec(memory_space=pltpu.VMEM)


def params():
    return pltpu.CompilerParams(vmem_limit_bytes=VMEM_LIMIT)


def in_scalars():
    return pl.BlockSpec(memory_space=pltpu.SMEM)


def shares(bands_ref):
    device = lax.axis_index("row")
    parity = lax.rem(device, 2)
    return parity, BAND * bands_ref[device - parity], BAND * bands_ref[device]


def place(bands_ref, first):
    parity, leader_share, _ = shares(bands_ref)
    row = first + GRID_ROWS * parity
    beyond = (row < 0) | (row >= 2 * GRID_ROWS)
    in_leader = row < leader_share
    in_own = in_leader == (parity == 0)
    source = jnp.where(beyond, 2, jnp.where(in_own, 0, 1))
    return source, jnp.where(beyond, 0, jnp.where(in_leader, row, row - leader_share))


def pull(bands_ref, first, sources, rows, target, at, rim_row=0):
    where, row = place(bands_ref, first)
    row = jnp.where(where == 2, rim_row, row)
    for number, source in enumerate(sources):

        @pl.when(where == number)
        def _():
            target[at : at + rows] = source[pl.ds(row, rows)]


def even_body(bands_ref, own_ref, other_ref, out_ref):
    for half in range(2):
        pull(bands_ref, BAND * half, (own_ref, other_ref), BAND, out_ref, BAND * half)


def even_rows(bands, own, other):
    shape = (GRID_ROWS,) + own.shape[1:]
    return pl.pallas_call(
        even_body,
        in_specs=[in_scalars(), in_vmem(), in_vmem()],
        out_specs=in_vmem(),
        out_shape=jax.ShapeDtypeStruct(shape, own.dtype),
        compiler_params=params(),
        name="even_rows",
    )(bands, own, other)


def rim_body(bands_ref, features_ref, cotangent_ref, out_ref):
    parity, _, share = shares(bands_ref)
    leads = parity == 0
    out_ref[0:RIM] = features_ref[pl.ds(jnp.where(leads, 0, share - RIM), RIM)]
    out_ref[RIM : RIM + 1] = cotangent_ref[pl.ds(jnp.where(leads, 0, share - 1), 1)]


def rim_rows(bands, features, cotangent):
    shape = (RIM + 1,) + features.shape[1:]
    return pl.pallas_call(
        rim_body,
        in_specs=[in_scalars(), in_vmem(), in_vmem()],
        out_specs=in_vmem(),
        out_shape=jax.ShapeDtypeStruct(shape, features.dtype),
        compiler_params=params(),
        name="rim_rows",
    )(bands, features, cotangent)


def column_sums(left, mid, right, column, last):
    from_left = jnp.where(column == 0, 0.0, pltpu.roll(left, 1, 0))
    from_right = jnp.where(column == last, 0.0, pltpu.roll(right, last, 0))
    return mid + from_left + from_right


def spread_taps(taps_ref, lanes, cols):
    taps = taps_ref[:, lanes].astype(F32)
    return [jnp.broadcast_to(taps[i : i + 1], (cols, LANES)) for i in range(9)]


def hidden_lanes(step, lane=0, count=CHUNK):
    return pl.ds(pl.multiple_of(step * CHUNK + lane, LANES), count)


def forward_body(bands_ref, features_ref, other_ref, rim_ref, expand_ref, taps_ref, project_ref, first_ref,
                 normed_ref, slab_ref, expanded_ref, mixed_ref, slab, normed_one, hidden, hidden_two, total):
    rows, cols, width = slab.shape
    own = rows - 2 * RIM

    sources = (features_ref, other_ref, rim_ref)
    for first, count in ((0, RIM), (RIM, BAND), (RIM + BAND, BAND), (RIM + 2 * BAND, RIM)):
        pull(bands_ref, first - RIM, sources, count, slab, first)
    slab_ref[...] = slab[RIM : RIM + own]
    for row in range(0, rows, 2):
        at = slice(row * cols, (row + 2) * cols)
        values = slab[row : row + 2].astype(F32).reshape(2 * cols, width)
        normed_one[at] = (values * rms_scale(values)).astype(BF16)
    total[...] = slab[1 : rows - 1].astype(F32).reshape((rows - 2) * cols, width)
    column = lax.broadcasted_iota(jnp.int32, (cols, LANES), 0)

    def step(index, carry):
        weights = expand_ref[:, hidden_lanes(index)]
        for row in range(0, rows, 4):
            expanded = nn_dot(normed_one[row * cols : (row + 4) * cols, :], weights)
            for inner in range(4):
                for lane in range(0, CHUNK, LANES):
                    lanes = slice(lane, lane + LANES)
                    values = expanded[inner * cols : (inner + 1) * cols, lanes]
                    hidden[row + inner, :, lanes] = gelu(values).astype(BF16).astype(F32)
                    if RIM <= row + inner < RIM + own:
                        expanded_ref[row + inner - RIM, :, hidden_lanes(index, lane, LANES)] = values

        for lane in range(0, CHUNK, LANES):
            lanes = slice(lane, lane + LANES)
            taps = spread_taps(taps_ref, hidden_lanes(index, lane, LANES), cols)
            for row in range(rows - 2):
                near = [hidden[row + a, :, lanes] for a in range(3)]
                sums = [
                    taps[b] * near[0] + taps[3 + b] * near[1] + taps[6 + b] * near[2] for b in range(3)
                ]
                mixed = column_sums(sums[0], sums[1], sums[2], column, cols - 1)
                hidden_two[row * cols : (row + 1) * cols, lanes] = gelu(mixed).astype(BF16)
                mixed_ref[row, :, hidden_lanes(index, lane, LANES)] = mixed
        total[...] += nn_dot(hidden_two[...], project_ref[hidden_lanes(index), :])
        return carry

    lax.fori_loop(0, expand_ref.shape[1] // CHUNK, step, 0)
    for row in range(rows - 2):
        first = total[row * cols : (row + 1) * cols]
        first_ref[row] = first
        if 1 <= row <= own:
            normed_ref[row - 1] = (first * rms_scale(first)).astype(BF16)


def forward(bands, features, other, rim, w_expand, kernel, w_project):
    capacity, cols, width = features.shape
    own, rows = GRID_ROWS, GRID_ROWS + 2 * RIM
    hidden_width = w_expand.shape[1]
    return pl.pallas_call(
        forward_body,
        in_specs=[in_scalars()] + [in_vmem()] * 6,
        out_specs=[in_vmem()] * 5,
        out_shape=[
            jax.ShapeDtypeStruct((rows - 2, cols, width), F32),
            jax.ShapeDtypeStruct((own, cols, width), BF16),
            jax.ShapeDtypeStruct((own, cols, width), BF16),
            jax.ShapeDtypeStruct((own, cols, hidden_width), F32),
            jax.ShapeDtypeStruct((rows - 2, cols, hidden_width), F32),
        ],
        scratch_shapes=[
            pltpu.VMEM((rows, cols, width), BF16),
            pltpu.VMEM((rows * cols, width), BF16),
            pltpu.VMEM((rows, cols, CHUNK), F32),
            pltpu.VMEM(((rows - 2) * cols, CHUNK), BF16),
            pltpu.VMEM(((rows - 2) * cols, width), F32),
        ],
        compiler_params=params(),
        cost_estimate=pl.CostEstimate(
            flops=4 * rows * cols * width * hidden_width,
            bytes_accessed=12 * 1024 * 1024,
            transcendentals=2 * rows * cols * hidden_width,
        ),
        name="bottleneck_forward",
    )(bands, features, other, rim, w_expand, kernel, w_project)


def slopes_body(expanded_ref, mixed_ref, slope_one_ref, slope_two_ref):
    for source, target in ((expanded_ref, slope_one_ref), (mixed_ref, slope_two_ref)):

        def step(row, carry):
            for lane in range(0, source.shape[2], LANES):
                lanes = slice(lane, lane + LANES)
                target[row, :, lanes] = gelu_slope(source[row, :, lanes]).astype(BF16)
            return carry

        lax.fori_loop(0, source.shape[0], step, 0)


def slopes(expanded, mixed):
    return pl.pallas_call(
        slopes_body,
        in_specs=[in_vmem()] * 2,
        out_specs=[in_vmem()] * 2,
        out_shape=[jax.ShapeDtypeStruct(values.shape, BF16) for values in (expanded, mixed)],
        compiler_params=params(),
        cost_estimate=pl.CostEstimate(
            flops=15 * (expanded.size + mixed.size),
            bytes_accessed=6 * (expanded.size + mixed.size),
            transcendentals=expanded.size + mixed.size,
        ),
        name="gelu_slopes",
    )(expanded, mixed)


def head_mask(span, head_dim):
    heads = LANES // head_dim
    row_head = np.arange(heads * span)[:, None] // span
    return (row_head == np.arange(LANES)[None, :] // head_dim).astype(np.float32)


def lane_tiles(width):
    return [slice(at, at + LANES) for at in range(0, width, LANES)]


def window_places(own, cols):
    return [(r, q) for r in range(own) for q in range(cols // 8)]


def to_windows(source_ref, rows_wide, target):
    groups, own, cols, width = source_ref.shape
    span = groups * 8
    for tile, lanes in enumerate(lane_tiles(width)):
        for group in range(groups):
            rows_wide[tile, group] = source_ref[group, :, :, lanes].astype(F32)
        for index, (r, q) in enumerate(window_places(own, cols)):
            pieces = [
                rows_wide[tile, group, r, pl.ds(q, 8, stride=cols // 8), :] for group in range(groups)
            ]
            rows = slice(index * span, (index + 1) * span)
            target[rows, lanes] = jnp.concatenate(pieces, axis=0).astype(BF16)


def to_rows(values, rows_wide, target_ref):
    groups, own, cols, width = target_ref.shape
    span = groups * 8
    for tile, lanes in enumerate(lane_tiles(width)):
        for index, (r, q) in enumerate(window_places(own, cols)):
            for group in range(groups):
                first = index * span + group * 8
                rows_wide[tile, group, r, pl.ds(q, 8, stride=cols // 8), :] = values[first : first + 8, lanes]
        for group in range(groups):
            target_ref[group, :, :, lanes] = rows_wide[tile, group].astype(BF16)


def wide_scratch(shape):
    groups, own, cols, width = shape
    return pltpu.VMEM((width // LANES, groups, own, cols, LANES), F32)


def grad_attended_body(cotangent_ref, out_ref, grad_ref, rows_wide, in_windows):
    to_windows(cotangent_ref, rows_wide, in_windows)
    grad_ref[...] = nt_dot(in_windows[...], out_ref[...]).astype(BF16)


def attended_gradient(cotangent, w_out):
    groups, own, cols, width = cotangent.shape
    shape = (groups * own * cols, width)
    return pl.pallas_call(
        grad_attended_body,
        in_specs=[in_vmem()] * 2,
        out_specs=in_vmem(),
        out_shape=jax.ShapeDtypeStruct(shape, BF16),
        scratch_shapes=[wide_scratch(cotangent.shape), pltpu.VMEM(shape, BF16)],
        compiler_params=params(),
        cost_estimate=pl.CostEstimate(
            flops=2 * shape[0] * width * width, bytes_accessed=2 * 1024 * 1024, transcendentals=0
        ),
        name="attended_gradient",
    )(cotangent, w_out)


def per_query(values, weights, span, head_dim):
    wide = nn_dot(values.T, weights)
    half = LANES // 2
    own = jnp.concatenate([wide[:half, :LANES], wide[half:, LANES:]], axis=0).T
    lane_head = lax.broadcasted_iota(jnp.int32, (span, LANES), 1) // head_dim
    return jnp.where(lane_head % 2 == 0, own[:span], own[span:])


def attention_body(normed_ref, grad_attended_ref, mask_ref, qkv_ref, grad_ref, weights_ref, values_ref,
                   rows_wide, in_windows, projected, grad_projected):
    groups, own, cols, width = normed_ref.shape
    span = groups * 8
    head_dim = width // HEADS
    heads = LANES // head_dim
    scale = 1.0 / math.sqrt(head_dim)
    steepness = scale * math.log2(math.e)

    to_windows(normed_ref, rows_wide, in_windows)
    projected[...] = nn_dot(in_windows[...], qkv_ref[...]).astype(BF16)
    values_ref[...] = projected[:, 2 * width :]

    def spread(values):
        return jnp.concatenate([values] * heads, axis=0) * mask_ref[...]

    def window(index, carry):
        rows = pl.ds(pl.multiple_of(index * span, span), span)
        for part in range(width // LANES):
            q_at, k_at, v_at = (
                slice(t * width + part * LANES, t * width + (part + 1) * LANES) for t in range(3)
            )
            q, k, v = projected[rows, q_at], projected[rows, k_at], projected[rows, v_at]
            q_wide = spread(q)
            g_wide = spread(grad_attended_ref[rows, q_at])
            scores = nt_dot(k, q_wide)
            powers = jnp.exp2((scores - jnp.max(scores, axis=0, keepdims=True)) * steepness)
            weights = powers * (1.0 / jnp.sum(powers, axis=0, keepdims=True))
            half = weights.astype(BF16)
            weights_ref[index, :, part * heads * span : (part + 1) * heads * span] = half
            grad_weights = nt_dot(v, g_wide)
            row_dot = jnp.sum(weights * grad_weights, axis=0, keepdims=True)
            grad_scores = (weights * (grad_weights - row_dot)).astype(BF16)
            grad_projected[rows, q_at] = (per_query(k, grad_scores, span, head_dim) * scale).astype(BF16)
            grad_projected[rows, k_at] = (nn_dot(grad_scores, q_wide) * scale).astype(BF16)
            grad_projected[rows, v_at] = nn_dot(half, g_wide).astype(BF16)
        return carry

    lax.fori_loop(0, own * cols // 8, window, 0, unroll=4)
    to_rows(nt_dot(grad_projected[...], qkv_ref[...]), rows_wide, grad_ref)


def attention(normed, grad_attended, w_qkv):
    groups, own, cols, width = normed.shape
    span = groups * 8
    tokens = groups * own * cols
    windows = tokens // span
    mask = head_mask(span, width // HEADS)
    out_shapes = [normed.shape, (windows, span, HEADS * span), (tokens, width)]
    return pl.pallas_call(
        attention_body,
        in_specs=[in_vmem()] * 4,
        out_specs=[in_vmem()] * 3,
        out_shape=[jax.ShapeDtypeStruct(shape, BF16) for shape in out_shapes],
        scratch_shapes=[
            wide_scratch(normed.shape),
            pltpu.VMEM((tokens, width), BF16),
            pltpu.VMEM((tokens, 3 * width), BF16),
            pltpu.VMEM((tokens, 3 * width), BF16),
        ],
        compiler_params=params(),
        cost_estimate=pl.CostEstimate(
            flops=16 * tokens * width * width,
            bytes_accessed=4 * 1024 * 1024,
            transcendentals=tokens * span * HEADS,
        ),
        name="window_attention",
    )(normed, grad_attended, jnp.asarray(mask, BF16), w_qkv)


def attended_body(weights_ref, values_ref, out_ref, added_ref, rows_wide, attended):
    windows, span, wide = weights_ref.shape
    width = values_ref.shape[1]
    heads = LANES * HEADS // width
    for index in range(windows):
        rows = slice(index * span, (index + 1) * span)
        for part, lanes in enumerate(lane_tiles(width)):
            weights = weights_ref[index, :, part * heads * span : (part + 1) * heads * span]
            attended[rows, lanes] = per_query(values_ref[rows, lanes], weights, span, width // HEADS).astype(BF16)
    to_rows(nn_dot(attended[...], out_ref[...]), rows_wide, added_ref)


def attend(weights, values, w_out, shape):
    return pl.pallas_call(
        attended_body,
        in_specs=[in_vmem()] * 3,
        out_specs=in_vmem(),
        out_shape=jax.ShapeDtypeStruct(shape, BF16),
        scratch_shapes=[wide_scratch(shape), pltpu.VMEM(values.shape, BF16)],
        compiler_params=params(),
        cost_estimate=pl.CostEstimate(
            flops=4 * values.size * values.shape[1], bytes_accessed=3 * 1024 * 1024, transcendentals=0
        ),
        name="attended_output",
    )(weights, values, w_out)


def backward_body(bands_ref, cotangent_ref, other_ref, rim_ref, slab_ref, first_ref, grad_slab_ref, grad_ref,
                  pair_ref, next_ref, slope_one_ref, slope_two_ref, expand_ref, taps_ref, project_ref,
                  out_ref, rims, grad_first, grad_rows, mixed, expanded, total):
    own, cols, width = slab_ref.shape

    def through_norm(cotangent, grad, first):
        rms = rms_scale(first)
        normed = first * rms
        grad = grad.astype(F32)
        inner = jnp.mean(grad * normed, -1, keepdims=True)
        return cotangent.astype(F32) + rms * (grad - normed * inner)

    for side, first in enumerate((-1, own)):
        pull(bands_ref, first, (cotangent_ref, other_ref, rim_ref), 1, rims, side, RIM)
    for row in range(own):
        result = through_norm(grad_slab_ref[row], grad_ref[row], first_ref[row + 1])
        grad_first[row * cols : (row + 1) * cols] = result
        grad_rows[(row + 1) * cols : (row + 2) * cols] = result.astype(BF16)
    leads = lax.rem(lax.axis_index("row"), 2) == 0
    above = jnp.where(leads, next_ref[0].astype(F32), pair_ref[0].astype(F32))
    below = jnp.where(leads, pair_ref[0].astype(F32), next_ref[0].astype(F32))
    grad_rows[0:cols] = through_norm(rims[0], above, first_ref[0]).astype(BF16)
    grad_rows[(own + 1) * cols :] = through_norm(rims[1], below, first_ref[own + 1]).astype(BF16)
    total[...] = jnp.zeros_like(total)
    column = lax.broadcasted_iota(jnp.int32, (cols, LANES), 0)

    def step(index, carry):
        weights = project_ref[hidden_lanes(index), :]
        for row in range(0, own + 2, 6):
            grad = nt_dot(grad_rows[row * cols : (row + 6) * cols, :], weights)
            for inner in range(6):
                for lane in range(0, CHUNK, LANES):
                    lanes = slice(lane, lane + LANES)
                    slope = slope_two_ref[row + inner, :, hidden_lanes(index, lane, LANES)].astype(F32)
                    value = grad[inner * cols : (inner + 1) * cols, lanes] * slope
                    mixed[row + inner, :, lanes] = value.astype(BF16).astype(F32)

        for lane in range(0, CHUNK, LANES):
            lanes = slice(lane, lane + LANES)
            taps = spread_taps(taps_ref, hidden_lanes(index, lane, LANES), cols)
            for row in range(own):
                near = [mixed[row + a, :, lanes] for a in range(3)]
                sums = [
                    taps[8 - b] * near[0] + taps[5 - b] * near[1] + taps[2 - b] * near[2] for b in range(3)
                ]
                grad = column_sums(sums[0], sums[1], sums[2], column, cols - 1)
                slope = slope_one_ref[row, :, hidden_lanes(index, lane, LANES)].astype(F32)
                expanded[row * cols : (row + 1) * cols, lanes] = (grad * slope).astype(BF16)
        total[...] += nt_dot(expanded[...], expand_ref[:, hidden_lanes(index)])
        return carry

    lax.fori_loop(0, expand_ref.shape[1] // CHUNK, step, 0)
    for row in range(own):
        at = slice(row * cols, (row + 1) * cols)
        values = slab_ref[row].astype(F32)
        rms = rms_scale(values)
        normed = values * rms
        grad = total[at]
        inner = jnp.mean(grad * normed, -1, keepdims=True)
        out_ref[row] = (grad_first[at] + rms * (grad - normed * inner)).astype(BF16)


def backward(bands, cotangent, other, rim, slab, first, grad_slab, grad, pair_row, next_row, slope_one,
             slope_two, w_expand, kernel, w_project):
    own, cols, width = slab.shape
    hidden_width = w_expand.shape[1]
    return pl.pallas_call(
        backward_body,
        in_specs=[in_scalars()] + [in_vmem()] * 14,
        out_specs=in_vmem(),
        out_shape=jax.ShapeDtypeStruct((own, cols, width), BF16),
        scratch_shapes=[
            pltpu.VMEM((2, cols, width), BF16),
            pltpu.VMEM((own * cols, width), F32),
            pltpu.VMEM(((own + 2) * cols, width), BF16),
            pltpu.VMEM((own + 2, cols, CHUNK), F32),
            pltpu.VMEM((own * cols, CHUNK), BF16),
            pltpu.VMEM((own * cols, width), F32),
        ],
        compiler_params=params(),
        cost_estimate=pl.CostEstimate(
            flops=4 * (own + 2) * cols * width * hidden_width,
            bytes_accessed=12 * 1024 * 1024,
            transcendentals=0,
        ),
        name="bottleneck_backward",
    )(bands, cotangent, other, rim, slab, first, grad_slab, grad, pair_row, next_row, slope_one,
      slope_two, w_expand, kernel, w_project)


def window_groups(size):
    stride = size // 8
    return [[first + stride * k for k in range(8)] for first in range(stride)]


def exchange_windows(rows):
    groups = window_groups(lax.axis_size("row"))
    return lax.all_to_all(
        rows, "row", split_axis=0, concat_axis=0, tiled=True, axis_index_groups=groups
    )


def swap_pair(rows):
    size = lax.axis_size("row")
    return lax.ppermute(rows, "row", [(i, i ^ 1) for i in range(size)])


def swap_next(rows):
    size = lax.axis_size("row")
    pairs = [(i, i + 1) for i in range(1, size - 1, 2)]
    return lax.ppermute(rows, "row", pairs + [(j, i) for i, j in pairs])


def place_rows(even, other, leads, leader_share):
    size = GRID_ROWS
    first, second = even[:BAND], even[BAND:]
    share = jnp.where(leads, leader_share, 2 * size - leader_share)
    zeros = jnp.zeros_like(first)
    low = jnp.where(leads | (share == size), first, jnp.where(share < size, second, other))
    mid = jnp.where(share < size, zeros, jnp.where(leads | (share == size), second, first))
    high = jnp.where(share > size, jnp.where(leads, other, second), zeros)
    return jnp.concatenate([low, mid, high], 0)


def on_device(features, row_bands, w_expand, kernel, w_project, w_qkv, w_out, cotangent):
    capacity, cols, width = features.shape
    device = lax.axis_index("row")
    parity = device % 2
    leads = parity == 0

    rim = swap_next(rim_rows(row_bands, features, cotangent))
    other_cotangent = swap_pair(cotangent)
    other_features = swap_pair(features)
    grad_slab = even_rows(row_bands, cotangent, other_cotangent)
    rim, grad_slab = lax.optimization_barrier((rim, grad_slab))

    grad_windows = exchange_windows(grad_slab)
    first, normed, slab, expanded, mixed = forward(
        row_bands, features, other_features, rim, w_expand, kernel, w_project
    )
    normed, grad_windows = lax.optimization_barrier((normed, grad_windows))
    normed_windows = exchange_windows(normed)
    shape = (8, GRID_ROWS // 8, cols, width)
    slope_one, slope_two = slopes(expanded, mixed)
    grad_attended = attended_gradient(grad_windows.reshape(shape), w_out)
    normed_windows, slope_one, slope_two, grad_attended = lax.optimization_barrier(
        (normed_windows, slope_one, slope_two, grad_attended)
    )
    grad_normed, weights, values = attention(normed_windows.reshape(shape), grad_attended, w_qkv)
    grad_rows = exchange_windows(grad_normed.reshape(GRID_ROWS, cols, width))
    added = attend(weights, values, w_out, shape)
    grad_rows, added = lax.optimization_barrier((grad_rows, added))
    top, bottom = grad_rows[:1], grad_rows[GRID_ROWS - 1 :]
    pair_row = swap_pair(jnp.where(leads, bottom, top))
    next_row = swap_next(jnp.where(leads, top, bottom))
    added, pair_row, next_row = lax.optimization_barrier((added, pair_row, next_row))
    added_rows = exchange_windows(added.reshape(GRID_ROWS, cols, width))
    grad_input = backward(
        row_bands, cotangent, other_cotangent, rim, slab, first, grad_slab, grad_rows, pair_row, next_row,
        slope_one, slope_two, w_expand, kernel, w_project,
    )
    grad_input, added_rows = lax.optimization_barrier((grad_input, added_rows))
    final = (first[1 : GRID_ROWS + 1] + added_rows.astype(F32)).astype(BF16)
    sent = [jnp.where(leads, rows[BAND:], rows[:BAND]) for rows in (final, grad_input)]
    swapped = swap_pair(jnp.stack(sent))
    leader_share = BAND * row_bands[device - parity]
    return (
        place_rows(final, swapped[0], leads, leader_share),
        place_rows(grad_input, swapped[1], leads, leader_share),
    )


def solution(mesh):
    return jax.shard_map(
        on_device,
        mesh=mesh,
        in_specs=(
            P(("parts", "row"), None, None),
            P("parts"),
            P(),
            P(),
            P(),
            P(),
            P(),
            P(("parts", "row"), None, None),
        ),
        out_specs=(P(("parts", "row"), None, None), P(("parts", "row"), None, None)),
        check_vma=False,
    )
```

```python
import math

import jax
import jax.numpy as jnp
import numpy as np
from jax import lax
from jax.experimental import pallas as pl
from jax.experimental.pallas import tpu as pltpu
from jax.sharding import PartitionSpec as P

HEADS = 16
GRID_ROWS = 16
BAND = 8
RIM = 2
EPSILON = 1e-06
CHUNK = 512
LANES = 128
WIDE = 256
ROOT = math.sqrt(2.0 / math.pi)
CUBIC = 0.044715
F32 = jnp.float32
BF16 = jnp.bfloat16
VMEM_LIMIT = 56 * 1024 * 1024


def nt_dot(left, right):
    return lax.dot_general(left, right, (((1,), (1,)), ((), ())), preferred_element_type=F32)


def tn_dot(left, right):
    return lax.dot_general(left, right, (((0,), (0,)), ((), ())), preferred_element_type=F32)


def nn_dot(left, right):
    return jnp.dot(left, right, preferred_element_type=F32)


def rms_scale(values):
    return lax.rsqrt(jnp.mean(values * values, -1, keepdims=True) + EPSILON)


def gelu_parts(v):
    square = v * v
    cdf = 0.5 + 0.5 * jnp.tanh(v * (ROOT + (ROOT * CUBIC) * square))
    return square, cdf, v * cdf


def gelu(v):
    return gelu_parts(v)[2]


def gelu_slope(v):
    square, cdf, value = gelu_parts(v)
    return cdf + (value - value * cdf) * (2.0 * ROOT + (6.0 * ROOT * CUBIC) * square)


def whole(shape, space=None):
    zeros = (0,) * len(shape)
    return pl.BlockSpec(shape, lambda *_: zeros)


def params():
    return pltpu.CompilerParams(vmem_limit_bytes=VMEM_LIMIT)


def in_vmem():
    return pl.BlockSpec(memory_space=pltpu.VMEM)


def in_hbm():
    return pl.BlockSpec(memory_space=pltpu.HBM)


def in_scalars():
    return pl.BlockSpec(memory_space=pltpu.SMEM)


def shares(bands_ref):
    device = lax.axis_index("row")
    parity = lax.rem(device, 2)
    return parity, BAND * bands_ref[device - parity], BAND * bands_ref[device]


def place(bands_ref, first):
    parity, leader_share, _ = shares(bands_ref)
    row = first + GRID_ROWS * parity
    beyond = (row < 0) | (row >= 2 * GRID_ROWS)
    in_leader = row < leader_share
    in_own = in_leader == (parity == 0)
    source = jnp.where(beyond, 2, jnp.where(in_own, 0, 1))
    return source, jnp.where(beyond, 0, jnp.where(in_leader, row, row - leader_share))


def start_pull(bands_ref, first, sources, rows, target, sem, rim_row=0):
    where, row = place(bands_ref, first)
    row = jnp.where(where == 2, rim_row, row)
    for number, source in enumerate(sources):

        @pl.when(where == number)
        def _():
            pltpu.make_async_copy(source.at[pl.ds(row, rows)], target, sem).start()


def wait_pull(sources, rows, target, sem):
    pltpu.make_async_copy(sources[0].at[pl.ds(0, rows)], target, sem).wait()


def even_body(bands_ref, own_ref, other_ref, out_ref, held, sems):
    halves = [pl.ds(BAND * half, BAND) for half in range(2)]
    places = [place(bands_ref, BAND * half) for half in range(2)]

    def copies(half):
        row = places[half][1]
        return (
            pltpu.make_async_copy(own_ref.at[pl.ds(row, BAND)], held.at[halves[half]], sems.at[half]),
            pltpu.make_async_copy(other_ref.at[pl.ds(row, BAND)], out_ref.at[halves[half]], sems.at[2 + half]),
            pltpu.make_async_copy(held.at[halves[half]], out_ref.at[halves[half]], sems.at[2 + half]),
        )

    for half in range(2):
        fetch, direct, store = copies(half)
        pl.when(places[half][0] == 0)(fetch.start)
        pl.when(places[half][0] == 1)(direct.start)
    for half in range(2):
        fetch, direct, store = copies(half)

        @pl.when(places[half][0] == 0)
        def _():
            fetch.wait()
            store.start()

    for half in range(2):
        copies(half)[2].wait()


def even_rows(bands, own, other):
    shape = (GRID_ROWS,) + own.shape[1:]
    return pl.pallas_call(
        even_body,
        in_specs=[in_scalars(), in_hbm(), in_vmem()],
        out_specs=in_hbm(),
        out_shape=jax.ShapeDtypeStruct(shape, own.dtype),
        scratch_shapes=[pltpu.VMEM(shape, own.dtype), pltpu.SemaphoreType.DMA((4,))],
        compiler_params=params(),
        name="even_rows",
    )(bands, own, other)


def rim_body(bands_ref, features_ref, cotangent_ref, out_ref, sems):
    parity, _, share = shares(bands_ref)
    leads = parity == 0
    copies = [
        pltpu.make_async_copy(
            features_ref.at[pl.ds(jnp.where(leads, 0, share - RIM), RIM)], out_ref.at[pl.ds(0, RIM)], sems.at[0]
        ),
        pltpu.make_async_copy(
            cotangent_ref.at[pl.ds(jnp.where(leads, 0, share - 1), 1)], out_ref.at[pl.ds(RIM, 1)], sems.at[1]
        ),
    ]
    for copy in copies:
        copy.start()
    for copy in copies:
        copy.wait()


def rim_rows(bands, features, cotangent):
    shape = (RIM + 1,) + features.shape[1:]
    return pl.pallas_call(
        rim_body,
        in_specs=[in_scalars(), in_hbm(), in_hbm()],
        out_specs=in_vmem(),
        out_shape=jax.ShapeDtypeStruct(shape, features.dtype),
        scratch_shapes=[pltpu.SemaphoreType.DMA((2,))],
        compiler_params=params(),
        name="rim_rows",
    )(bands, features, cotangent)


def column_sums(left, mid, right, column, last):
    from_left = jnp.where(column == 0, 0.0, pltpu.roll(left, 1, 0))
    from_right = jnp.where(column == last, 0.0, pltpu.roll(right, last, 0))
    return mid + from_left + from_right


def spread_taps(taps_ref, lanes, cols):
    taps = taps_ref[:, lanes].astype(F32)
    return [jnp.broadcast_to(taps[i : i + 1], (cols, LANES)) for i in range(9)]


def chunk_lanes(index):
    return pl.ds(index * CHUNK, CHUNK)


def lane_pieces(first, count):
    return [slice(at, at + LANES) for at in range(first, first + count, LANES)]


def forward_body(bands_ref, features_ref, other_ref, rim_ref, expand_ref, taps_ref, project_ref, first_ref,
                 normed_ref, slab_ref, expanded_ref, mixed_ref, slab, normed_one, expand, project, expanded,
                 hidden, mixed, hidden_two, total, normed, row_sems, weight_sems, out_sems):
    rows, cols, width = slab.shape
    own = rows - 2 * RIM
    chunks = expand_ref.shape[1] // CHUNK

    sources = (features_ref, other_ref, rim_ref)
    pieces = [(0, RIM), (RIM, BAND), (RIM + BAND, BAND), (RIM + 2 * BAND, RIM)]
    for index, (first, count) in enumerate(pieces):
        start_pull(bands_ref, first - RIM, sources, count, slab.at[pl.ds(first, count)], row_sems.at[index])
    fetches = []
    for index in range(chunks):
        lanes = chunk_lanes(index)
        fetches.append(pltpu.make_async_copy(expand_ref.at[:, lanes], expand.at[index], weight_sems.at[2 * index]))
        fetches.append(pltpu.make_async_copy(project_ref.at[lanes], project.at[index], weight_sems.at[2 * index + 1]))
    for fetch in fetches:
        fetch.start()
    for index, (first, count) in enumerate(pieces):
        wait_pull(sources, count, slab.at[pl.ds(first, count)], row_sems.at[index])

    stores = [pltpu.make_async_copy(slab.at[pl.ds(RIM, own)], slab_ref, out_sems.at[0])]
    stores[0].start()
    for row in range(0, rows, 2):
        at = slice(row * cols, (row + 2) * cols)
        values = slab[row : row + 2].astype(F32).reshape(2 * cols, width)
        normed_one[at] = (values * rms_scale(values)).astype(BF16)
    total[...] = slab[1 : rows - 1].astype(F32).reshape((rows - 2) * cols, width)
    column = lax.broadcasted_iota(jnp.int32, (cols, LANES), 0)

    def expand_chunk(index):
        fetches[2 * index].wait()
        for lane in range(0, CHUNK, WIDE):
            product = nn_dot(normed_one[...], expand[index, :, lane : lane + WIDE])
            expanded[:, :, index * CHUNK + lane : index * CHUNK + lane + WIDE] = product.reshape(rows, cols, WIDE)

    def project_chunk(index):
        fetches[2 * index + 1].wait()
        total[...] += nn_dot(hidden_two[index % 2], project[index])

    expand_chunk(0)
    for index in range(chunks):
        if index + 1 < chunks:
            expand_chunk(index + 1)
        if index > 0:
            project_chunk(index - 1)
        for lanes in lane_pieces(0, CHUNK):
            at = slice(index * CHUNK + lanes.start, index * CHUNK + lanes.stop)
            for row in range(rows):
                hidden[row, :, lanes] = gelu(expanded[row, :, at]).astype(BF16).astype(F32)
            taps = spread_taps(taps_ref, at, cols)
            for row in range(rows - 2):
                near = [hidden[row + a, :, lanes] for a in range(3)]
                sums = [
                    taps[b] * near[0] + taps[3 + b] * near[1] + taps[6 + b] * near[2] for b in range(3)
                ]
                values = column_sums(sums[0], sums[1], sums[2], column, cols - 1)
                hidden_two[index % 2, row * cols : (row + 1) * cols, lanes] = gelu(values).astype(BF16)
                mixed[row, :, at] = values
        lanes = chunk_lanes(index)
        stores.append(
            pltpu.make_async_copy(
                expanded.at[pl.ds(RIM, own), :, lanes], expanded_ref.at[:, :, lanes], out_sems.at[1 + 2 * index]
            )
        )
        stores.append(
            pltpu.make_async_copy(mixed.at[:, :, lanes], mixed_ref.at[:, :, lanes], out_sems.at[2 + 2 * index])
        )
        for store in stores[-2:]:
            store.start()
    project_chunk(chunks - 1)

    for row in range(1, own + 1):
        first = total[row * cols : (row + 1) * cols]
        normed[row - 1] = (first * rms_scale(first)).astype(BF16)
    stores.append(pltpu.make_async_copy(normed, normed_ref, out_sems.at[1 + 2 * chunks]))
    stores.append(pltpu.make_async_copy(total, first_ref, out_sems.at[2 + 2 * chunks]))
    for store in stores[-2:]:
        store.start()
    for store in stores:
        store.wait()


def forward(bands, features, other, rim, w_expand, kernel, w_project):
    capacity, cols, width = features.shape
    own, rows = GRID_ROWS, GRID_ROWS + 2 * RIM
    hidden_width = w_expand.shape[1]
    chunks = hidden_width // CHUNK
    return pl.pallas_call(
        forward_body,
        in_specs=[in_scalars()] + [in_hbm()] * 4 + [in_vmem(), in_hbm()],
        out_specs=[in_hbm()] * 5,
        out_shape=[
            jax.ShapeDtypeStruct(((rows - 2) * cols, width), F32),
            jax.ShapeDtypeStruct((own, cols, width), BF16),
            jax.ShapeDtypeStruct((own, cols, width), BF16),
            jax.ShapeDtypeStruct((own, cols, hidden_width), F32),
            jax.ShapeDtypeStruct((rows - 2, cols, hidden_width), F32),
        ],
        scratch_shapes=[
            pltpu.VMEM((rows, cols, width), BF16),
            pltpu.VMEM((rows * cols, width), BF16),
            pltpu.VMEM((chunks, width, CHUNK), BF16),
            pltpu.VMEM((chunks, CHUNK, width), BF16),
            pltpu.VMEM((rows, cols, hidden_width), F32),
            pltpu.VMEM((rows, cols, CHUNK), F32),
            pltpu.VMEM((rows - 2, cols, hidden_width), F32),
            pltpu.VMEM((2, (rows - 2) * cols, CHUNK), BF16),
            pltpu.VMEM(((rows - 2) * cols, width), F32),
            pltpu.VMEM((own, cols, width), BF16),
            pltpu.SemaphoreType.DMA((4,)),
            pltpu.SemaphoreType.DMA((2 * chunks,)),
            pltpu.SemaphoreType.DMA((2 * chunks + 3,)),
        ],
        compiler_params=params(),
        cost_estimate=pl.CostEstimate(
            flops=4 * rows * cols * width * hidden_width,
            bytes_accessed=12 * 1024 * 1024,
            transcendentals=2 * rows * cols * hidden_width,
        ),
        name="bottleneck_forward",
    )(bands, features, other, rim, w_expand, kernel, w_project)


def slopes_body(expanded_ref, mixed_ref, slope_one_ref, slope_two_ref):
    for source, target in ((expanded_ref, slope_one_ref), (mixed_ref, slope_two_ref)):
        rows, _, chunk = source.shape
        for row in range(rows):
            for lane in range(0, chunk, LANES):
                lanes = slice(lane, lane + LANES)
                target[row, :, lanes] = gelu_slope(source[row, :, lanes]).astype(BF16)


def slopes(expanded, mixed):
    hidden_width = expanded.shape[2]
    blocks = [
        pl.BlockSpec(values.shape[:2] + (CHUNK,), lambda j: (0, 0, j)) for values in (expanded, mixed)
    ]
    return pl.pallas_call(
        slopes_body,
        grid=(hidden_width // CHUNK,),
        in_specs=blocks,
        out_specs=blocks,
        out_shape=[jax.ShapeDtypeStruct(values.shape, BF16) for values in (expanded, mixed)],
        compiler_params=params(),
        cost_estimate=pl.CostEstimate(
            flops=15 * (expanded.size + mixed.size),
            bytes_accessed=6 * (expanded.size + mixed.size),
            transcendentals=expanded.size + mixed.size,
        ),
        name="gelu_slopes",
    )(expanded, mixed)


def head_mask(span, head_dim):
    heads = LANES // head_dim
    row_head = np.arange(heads * span)[:, None] // span
    return (row_head == np.arange(LANES)[None, :] // head_dim).astype(np.float32)


def lane_tiles(width):
    return [slice(at, at + LANES) for at in range(0, width, LANES)]


def window_places(own, cols):
    return [(r, q) for r in range(own) for q in range(cols // 8)]


def to_windows(source_ref, rows_wide, target):
    groups, own, cols, width = source_ref.shape
    span = groups * 8
    for tile, lanes in enumerate(lane_tiles(width)):
        for group in range(groups):
            rows_wide[tile, group] = source_ref[group, :, :, lanes].astype(F32)
        for index, (r, q) in enumerate(window_places(own, cols)):
            pieces = [
                rows_wide[tile, group, r, pl.ds(q, 8, stride=cols // 8), :] for group in range(groups)
            ]
            rows = slice(index * span, (index + 1) * span)
            target[rows, lanes] = jnp.concatenate(pieces, axis=0).astype(BF16)


def to_rows(values, rows_wide, target_ref):
    groups, own, cols, width = target_ref.shape
    span = groups * 8
    for tile, lanes in enumerate(lane_tiles(width)):
        for index, (r, q) in enumerate(window_places(own, cols)):
            for group in range(groups):
                first = index * span + group * 8
                rows_wide[tile, group, r, pl.ds(q, 8, stride=cols // 8), :] = values[first : first + 8, lanes]
        for group in range(groups):
            target_ref[group, :, :, lanes] = rows_wide[tile, group].astype(BF16)


def wide_scratch(shape):
    groups, own, cols, width = shape
    return pltpu.VMEM((width // LANES, groups, own, cols, LANES), F32)


def grad_attended_body(cotangent_ref, out_ref, grad_ref, rows_wide, in_windows):
    to_windows(cotangent_ref, rows_wide, in_windows)
    grad_ref[...] = nt_dot(in_windows[...], out_ref[...]).astype(BF16)


def attended_gradient(cotangent, w_out):
    groups, own, cols, width = cotangent.shape
    shape = (groups * own * cols, width)
    return pl.pallas_call(
        grad_attended_body,
        grid=(1,),
        in_specs=[whole(cotangent.shape), whole(w_out.shape)],
        out_specs=whole(shape),
        out_shape=jax.ShapeDtypeStruct(shape, BF16),
        scratch_shapes=[wide_scratch(cotangent.shape), pltpu.VMEM(shape, BF16)],
        compiler_params=params(),
        cost_estimate=pl.CostEstimate(
            flops=2 * shape[0] * width * width, bytes_accessed=2 * 1024 * 1024, transcendentals=0
        ),
        name="attended_gradient",
    )(cotangent, w_out)


def per_query(values, weights, span, head_dim):
    wide = nn_dot(values.T, weights)
    half = LANES // 2
    own = jnp.concatenate([wide[:half, :LANES], wide[half:, LANES:]], axis=0).T
    lane_head = lax.broadcasted_iota(jnp.int32, (span, LANES), 1) // head_dim
    return jnp.where(lane_head % 2 == 0, own[:span], own[span:])


def attention_body(normed_ref, grad_attended_ref, mask_ref, qkv_ref, grad_ref, weights_ref, values_ref,
                   rows_wide, in_windows, projected, grad_projected):
    groups, own, cols, width = normed_ref.shape
    span = groups * 8
    head_dim = width // HEADS
    heads = LANES // head_dim
    scale = 1.0 / math.sqrt(head_dim)
    steepness = scale * math.log2(math.e)

    to_windows(normed_ref, rows_wide, in_windows)
    projected[...] = nn_dot(in_windows[...], qkv_ref[...]).astype(BF16)
    values_ref[...] = projected[:, 2 * width :]

    def spread(values):
        return jnp.concatenate([values] * heads, axis=0) * mask_ref[...]

    def window(index, carry):
        rows = pl.ds(pl.multiple_of(index * span, span), span)
        for part in range(width // LANES):
            q_at, k_at, v_at = (
                slice(t * width + part * LANES, t * width + (part + 1) * LANES) for t in range(3)
            )
            q, k, v = projected[rows, q_at], projected[rows, k_at], projected[rows, v_at]
            q_wide = spread(q)
            g_wide = spread(grad_attended_ref[rows, q_at])
            scores = nt_dot(k, q_wide)
            powers = jnp.exp2((scores - jnp.max(scores, axis=0, keepdims=True)) * steepness)
            weights = powers * (1.0 / jnp.sum(powers, axis=0, keepdims=True))
            half = weights.astype(BF16)
            weights_ref[index, :, part * heads * span : (part + 1) * heads * span] = half
            grad_weights = nt_dot(v, g_wide)
            row_dot = jnp.sum(weights * grad_weights, axis=0, keepdims=True)
            grad_scores = (weights * (grad_weights - row_dot)).astype(BF16)
            grad_projected[rows, q_at] = (per_query(k, grad_scores, span, head_dim) * scale).astype(BF16)
            grad_projected[rows, k_at] = (nn_dot(grad_scores, q_wide) * scale).astype(BF16)
            grad_projected[rows, v_at] = nn_dot(half, g_wide).astype(BF16)
        return carry

    lax.fori_loop(0, own * cols // 8, window, 0, unroll=4)
    to_rows(nt_dot(grad_projected[...], qkv_ref[...]), rows_wide, grad_ref)


def attention(normed, grad_attended, w_qkv):
    groups, own, cols, width = normed.shape
    span = groups * 8
    tokens = groups * own * cols
    windows = tokens // span
    mask = head_mask(span, width // HEADS)
    out_shapes = [normed.shape, (windows, span, HEADS * span), (tokens, width)]
    return pl.pallas_call(
        attention_body,
        grid=(1,),
        in_specs=[
            whole(normed.shape),
            whole(grad_attended.shape),
            whole(mask.shape),
            whole(w_qkv.shape),
        ],
        out_specs=[whole(shape) for shape in out_shapes],
        out_shape=[jax.ShapeDtypeStruct(shape, BF16) for shape in out_shapes],
        scratch_shapes=[
            wide_scratch(normed.shape),
            pltpu.VMEM((tokens, width), BF16),
            pltpu.VMEM((tokens, 3 * width), BF16),
            pltpu.VMEM((tokens, 3 * width), BF16),
        ],
        compiler_params=params(),
        cost_estimate=pl.CostEstimate(
            flops=16 * tokens * width * width,
            bytes_accessed=4 * 1024 * 1024,
            transcendentals=tokens * span * HEADS,
        ),
        name="window_attention",
    )(normed, grad_attended, jnp.asarray(mask, BF16), w_qkv)


def attended_body(weights_ref, values_ref, out_ref, added_ref, rows_wide, attended):
    windows, span, wide = weights_ref.shape
    width = values_ref.shape[1]
    heads = LANES * HEADS // width
    for index in range(windows):
        rows = slice(index * span, (index + 1) * span)
        for part, lanes in enumerate(lane_tiles(width)):
            weights = weights_ref[index, :, part * heads * span : (part + 1) * heads * span]
            attended[rows, lanes] = per_query(values_ref[rows, lanes], weights, span, width // HEADS).astype(BF16)
    to_rows(nn_dot(attended[...], out_ref[...]), rows_wide, added_ref)


def attend(weights, values, w_out, shape):
    return pl.pallas_call(
        attended_body,
        grid=(1,),
        in_specs=[whole(weights.shape), whole(values.shape), whole(w_out.shape)],
        out_specs=whole(shape),
        out_shape=jax.ShapeDtypeStruct(shape, BF16),
        scratch_shapes=[wide_scratch(shape), pltpu.VMEM(values.shape, BF16)],
        compiler_params=params(),
        cost_estimate=pl.CostEstimate(
            flops=4 * values.size * values.shape[1], bytes_accessed=3 * 1024 * 1024, transcendentals=0
        ),
        name="attended_output",
    )(weights, values, w_out)


def backward_body(bands_ref, cotangent_ref, other_ref, rim_ref, slab_ref, first_ref, grad_slab_ref, grad_ref,
                  pair_ref, next_ref, slope_one_ref, slope_two_ref, expand_ref, taps_ref, project_ref,
                  out_ref, rims, slab, first, grad_slab, grad_in, slope_one, slope_two, expand, project,
                  grad_first, grad_rows, grads, mixed, expanded, total, row_sems, in_sems, chunk_sems):
    own, cols, width = slab.shape
    chunks = expand_ref.shape[1] // CHUNK

    sources = (cotangent_ref, other_ref, rim_ref)
    sides = list(enumerate((-1, own)))
    for side, place_first in sides:
        start_pull(bands_ref, place_first, sources, 1, rims.at[pl.ds(side, 1)], row_sems.at[side], RIM)
    inputs = [
        pltpu.make_async_copy(source, target, in_sems.at[index])
        for index, (source, target) in enumerate(
            ((first_ref, first), (grad_ref, grad_in), (grad_slab_ref, grad_slab), (slab_ref, slab))
        )
    ]
    for copy in inputs:
        copy.start()
    fetches = []
    for index in range(chunks):
        lanes = chunk_lanes(index)
        pairs = (
            (project_ref.at[lanes], project.at[index]),
            (slope_two_ref.at[:, :, lanes], slope_two.at[:, :, lanes]),
            (slope_one_ref.at[:, :, lanes], slope_one.at[:, :, lanes]),
            (expand_ref.at[:, lanes], expand.at[index]),
        )
        fetches.append(
            [
                pltpu.make_async_copy(source, target, chunk_sems.at[4 * index + number])
                for number, (source, target) in enumerate(pairs)
            ]
        )
        for copy in fetches[-1]:
            copy.start()

    def through_norm(cotangent, grad, first):
        rms = rms_scale(first)
        normed = first * rms
        grad = grad.astype(F32)
        inner = jnp.mean(grad * normed, -1, keepdims=True)
        return cotangent.astype(F32) + rms * (grad - normed * inner)

    for copy in inputs[:3]:
        copy.wait()
    for row in range(own):
        below = first[(row + 1) * cols : (row + 2) * cols]
        result = through_norm(grad_slab[row], grad_in[row], below)
        grad_first[row * cols : (row + 1) * cols] = result
        grad_rows[(row + 1) * cols : (row + 2) * cols] = result.astype(BF16)
    for side, place_first in sides:
        wait_pull(sources, 1, rims.at[pl.ds(side, 1)], row_sems.at[side])
    leads = lax.rem(lax.axis_index("row"), 2) == 0
    above = jnp.where(leads, next_ref[0].astype(F32), pair_ref[0].astype(F32))
    below = jnp.where(leads, pair_ref[0].astype(F32), next_ref[0].astype(F32))
    last = (own + 1) * cols
    grad_rows[0:cols] = through_norm(rims[0], above, first[0:cols]).astype(BF16)
    grad_rows[last:] = through_norm(rims[1], below, first[last:]).astype(BF16)
    column = lax.broadcasted_iota(jnp.int32, (cols, LANES), 0)

    def project_chunk(index):
        fetches[index][0].wait()
        for lane in range(0, CHUNK, WIDE):
            wide = slice(lane, lane + WIDE)
            product = nt_dot(grad_rows[...], project[index, wide, :])
            grads[index % 2, :, :, wide] = product.reshape(own + 2, cols, WIDE)

    def expand_chunk(index):
        fetches[index][3].wait()
        product = nt_dot(expanded[index % 2], expand[index])
        total[...] = product if index == 0 else total[...] + product

    project_chunk(0)
    for index in range(chunks):
        if index + 1 < chunks:
            project_chunk(index + 1)
        if index > 0:
            expand_chunk(index - 1)
        for copy in fetches[index][1:3]:
            copy.wait()
        for lanes in lane_pieces(0, CHUNK):
            at = slice(index * CHUNK + lanes.start, index * CHUNK + lanes.stop)
            for row in range(own + 2):
                value = grads[index % 2, row, :, lanes] * slope_two[row, :, at].astype(F32)
                mixed[row, :, lanes] = value.astype(BF16).astype(F32)
            taps = spread_taps(taps_ref, at, cols)
            for row in range(own):
                near = [mixed[row + a, :, lanes] for a in range(3)]
                sums = [
                    taps[8 - b] * near[0] + taps[5 - b] * near[1] + taps[2 - b] * near[2] for b in range(3)
                ]
                value = column_sums(sums[0], sums[1], sums[2], column, cols - 1)
                value = value * slope_one[row, :, at].astype(F32)
                expanded[index % 2, row * cols : (row + 1) * cols, lanes] = value.astype(BF16)
    expand_chunk(chunks - 1)

    inputs[3].wait()
    for row in range(own):
        at = slice(row * cols, (row + 1) * cols)
        values = slab[row].astype(F32)
        rms = rms_scale(values)
        normed = values * rms
        grad = total[at]
        inner = jnp.mean(grad * normed, -1, keepdims=True)
        out_ref[row] = (grad_first[at] + rms * (grad - normed * inner)).astype(BF16)


def backward(bands, cotangent, other, rim, slab, first, grad_slab, grad, pair_row, next_row, slope_one,
             slope_two, w_expand, kernel, w_project):
    own, cols, width = slab.shape
    hidden_width = w_expand.shape[1]
    chunks = hidden_width // CHUNK
    return pl.pallas_call(
        backward_body,
        in_specs=[in_scalars()] + [in_hbm()] * 7 + [in_vmem()] * 2 + [in_hbm()] * 3 + [in_vmem(), in_hbm()],
        out_specs=in_vmem(),
        out_shape=jax.ShapeDtypeStruct((own, cols, width), BF16),
        scratch_shapes=[
            pltpu.VMEM((2, cols, width), BF16),
            pltpu.VMEM((own, cols, width), BF16),
            pltpu.VMEM(((own + 2) * cols, width), F32),
            pltpu.VMEM((own, cols, width), BF16),
            pltpu.VMEM((own, cols, width), BF16),
            pltpu.VMEM((own, cols, hidden_width), BF16),
            pltpu.VMEM((own + 2, cols, hidden_width), BF16),
            pltpu.VMEM((chunks, width, CHUNK), BF16),
            pltpu.VMEM((chunks, CHUNK, width), BF16),
            pltpu.VMEM((own * cols, width), F32),
            pltpu.VMEM(((own + 2) * cols, width), BF16),
            pltpu.VMEM((2, own + 2, cols, CHUNK), F32),
            pltpu.VMEM((own + 2, cols, CHUNK), F32),
            pltpu.VMEM((2, own * cols, CHUNK), BF16),
            pltpu.VMEM((own * cols, width), F32),
            pltpu.SemaphoreType.DMA((2,)),
            pltpu.SemaphoreType.DMA((4,)),
            pltpu.SemaphoreType.DMA((4 * chunks,)),
        ],
        compiler_params=params(),
        cost_estimate=pl.CostEstimate(
            flops=4 * (own + 2) * cols * width * hidden_width,
            bytes_accessed=12 * 1024 * 1024,
            transcendentals=0,
        ),
        name="bottleneck_backward",
    )(bands, cotangent, other, rim, slab, first, grad_slab, grad, pair_row, next_row, slope_one,
      slope_two, w_expand, kernel, w_project)


def window_groups(size):
    stride = size // 8
    return [[first + stride * k for k in range(8)] for first in range(stride)]


def exchange_windows(rows):
    groups = window_groups(lax.axis_size("row"))
    return lax.all_to_all(
        rows, "row", split_axis=0, concat_axis=0, tiled=True, axis_index_groups=groups
    )


def swap_pair(rows):
    size = lax.axis_size("row")
    return lax.ppermute(rows, "row", [(i, i ^ 1) for i in range(size)])


def swap_next(rows):
    size = lax.axis_size("row")
    pairs = [(i, i + 1) for i in range(1, size - 1, 2)]
    return lax.ppermute(rows, "row", pairs + [(j, i) for i, j in pairs])


def place_rows(even, other, leads, leader_share):
    size = GRID_ROWS
    first, second = even[:BAND], even[BAND:]
    share = jnp.where(leads, leader_share, 2 * size - leader_share)
    zeros = jnp.zeros_like(first)
    low = jnp.where(leads | (share == size), first, jnp.where(share < size, second, other))
    mid = jnp.where(share < size, zeros, jnp.where(leads | (share == size), second, first))
    high = jnp.where(share > size, jnp.where(leads, other, second), zeros)
    return jnp.concatenate([low, mid, high], 0)


def on_device(features, row_bands, w_expand, kernel, w_project, w_qkv, w_out, cotangent):
    capacity, cols, width = features.shape
    device = lax.axis_index("row")
    parity = device % 2
    leads = parity == 0

    rim = swap_next(rim_rows(row_bands, features, cotangent))
    other_cotangent = swap_pair(cotangent)
    other_features = swap_pair(features)
    grad_slab = even_rows(row_bands, cotangent, other_cotangent)
    rim, grad_slab = lax.optimization_barrier((rim, grad_slab))

    grad_windows = exchange_windows(grad_slab)
    first, normed, slab, expanded, mixed = forward(
        row_bands, features, other_features, rim, w_expand, kernel, w_project
    )
    normed, grad_windows = lax.optimization_barrier((normed, grad_windows))
    normed_windows = exchange_windows(normed)
    shape = (8, GRID_ROWS // 8, cols, width)
    slope_one, slope_two = slopes(expanded, mixed)
    grad_attended = attended_gradient(grad_windows.reshape(shape), w_out)
    normed_windows, slope_one, slope_two, grad_attended = lax.optimization_barrier(
        (normed_windows, slope_one, slope_two, grad_attended)
    )
    grad_normed, weights, values = attention(normed_windows.reshape(shape), grad_attended, w_qkv)
    grad_rows = exchange_windows(grad_normed.reshape(GRID_ROWS, cols, width))
    added = attend(weights, values, w_out, shape)
    grad_rows, added = lax.optimization_barrier((grad_rows, added))
    top, bottom = grad_rows[:1], grad_rows[GRID_ROWS - 1 :]
    pair_row = swap_pair(jnp.where(leads, bottom, top))
    next_row = swap_next(jnp.where(leads, top, bottom))
    added, pair_row, next_row = lax.optimization_barrier((added, pair_row, next_row))
    added_rows = exchange_windows(added.reshape(GRID_ROWS, cols, width))
    grad_input = backward(
        row_bands, cotangent, other_cotangent, rim, slab, first, grad_slab, grad_rows, pair_row, next_row,
        slope_one, slope_two, w_expand, kernel, w_project,
    )
    grad_input, added_rows = lax.optimization_barrier((grad_input, added_rows))
    first = first.reshape(GRID_ROWS + 2, cols, width)[1 : GRID_ROWS + 1]
    final = (first + added_rows.astype(F32)).astype(BF16)
    sent = [jnp.where(leads, rows[BAND:], rows[:BAND]) for rows in (final, grad_input)]
    swapped = swap_pair(jnp.stack(sent))
    leader_share = BAND * row_bands[device - parity]
    return (
        place_rows(final, swapped[0], leads, leader_share),
        place_rows(grad_input, swapped[1], leads, leader_share),
    )


def solution(mesh):
    return jax.shard_map(
        on_device,
        mesh=mesh,
        in_specs=(
            P(("parts", "row"), None, None),
            P("parts"),
            P(),
            P(),
            P(),
            P(),
            P(),
            P(("parts", "row"), None, None),
        ),
        out_specs=(P(("parts", "row"), None, None), P(("parts", "row"), None, None)),
        check_vma=False,
    )
```

```python
import math

import jax
import jax.numpy as jnp
from jax import lax
from jax.experimental import pallas as pl
from jax.experimental.pallas import tpu as pltpu
from jax.sharding import PartitionSpec as P

HEADS = 16
GRID_ROWS = 16
BAND = 8
RIM = 2
EPSILON = 1e-06
CHUNK = 512
LANES = 128
ROOT = math.sqrt(2.0 / math.pi)
CUBIC = 0.044715
F32 = jnp.float32
BF16 = jnp.bfloat16
MIB = 1024 * 1024


def nt_dot(left, right):
    return lax.dot_general(left, right, (((1,), (1,)), ((), ())), preferred_element_type=F32)


def tn_dot(left, right):
    return lax.dot_general(left, right, (((0,), (0,)), ((), ())), preferred_element_type=F32)


def nn_dot(left, right):
    return jnp.dot(left, right, preferred_element_type=F32)


def rms_scale(values):
    return lax.rsqrt(jnp.mean(values * values, -1, keepdims=True) + EPSILON)


def gelu_parts(v):
    square = v * v
    cdf = 0.5 + 0.5 * jnp.tanh(v * (ROOT + (ROOT * CUBIC) * square))
    return square, cdf, v * cdf


def gelu(v):
    return gelu_parts(v)[2]


def gelu_slope(v):
    square, cdf, value = gelu_parts(v)
    return cdf + (value - value * cdf) * (2.0 * ROOT + (6.0 * ROOT * CUBIC) * square)


def whole(shape, space=None):
    zeros = (0,) * len(shape)
    return pl.BlockSpec(shape, lambda *_: zeros)


def params(mebibytes=56):
    return pltpu.CompilerParams(vmem_limit_bytes=mebibytes * MIB)


def in_vmem():
    return pl.BlockSpec(memory_space=pltpu.VMEM)


def in_hbm():
    return pl.BlockSpec(memory_space=pltpu.HBM)


def held(array):
    return pltpu.with_memory_space_constraint(array, pltpu.HBM)


def near(array):
    return pltpu.with_memory_space_constraint(array, pltpu.VMEM)


def in_scalars():
    return pl.BlockSpec(memory_space=pltpu.SMEM)


def shares(bands_ref):
    device = lax.axis_index("row")
    parity = lax.rem(device, 2)
    return parity, BAND * bands_ref[device - parity], BAND * bands_ref[device]


def place(bands_ref, first):
    parity, leader_share, _ = shares(bands_ref)
    row = first + GRID_ROWS * parity
    beyond = (row < 0) | (row >= 2 * GRID_ROWS)
    in_leader = row < leader_share
    in_own = in_leader == (parity == 0)
    source = jnp.where(beyond, 2, jnp.where(in_own, 0, 1))
    return source, jnp.where(beyond, 0, jnp.where(in_leader, row, row - leader_share))


def start_pull(bands_ref, first, sources, rows, target, sem, rim_row=0):
    where, row = place(bands_ref, first)
    row = jnp.where(where == 2, rim_row, row)
    for number, source in enumerate(sources):

        @pl.when(where == number)
        def _():
            pltpu.make_async_copy(source.at[pl.ds(row, rows)], target, sem).start()


def wait_pull(sources, rows, target, sem):
    pltpu.make_async_copy(sources[0].at[pl.ds(0, rows)], target, sem).wait()


def even_body(bands_ref, own_ref, other_ref, out_ref):
    for half in range(2):
        where, row = place(bands_ref, BAND * half)
        for number, source in enumerate((own_ref, other_ref)):

            @pl.when(where == number)
            def _():
                out_ref[BAND * half : BAND * half + BAND] = source[pl.ds(row, BAND)]


def even_rows(bands, own, other):
    shape = (GRID_ROWS,) + own.shape[1:]
    return pl.pallas_call(
        even_body,
        in_specs=[in_scalars(), in_vmem(), in_vmem()],
        out_specs=in_vmem(),
        out_shape=jax.ShapeDtypeStruct(shape, own.dtype),
        compiler_params=params(8),
        name="even_rows",
    )(bands, near(own), near(other))


def rim_body(bands_ref, features_ref, cotangent_ref, out_ref, sems):
    parity, _, share = shares(bands_ref)
    leads = parity == 0
    copies = [
        pltpu.make_async_copy(
            features_ref.at[pl.ds(jnp.where(leads, 0, share - RIM), RIM)], out_ref.at[pl.ds(0, RIM)], sems.at[0]
        ),
        pltpu.make_async_copy(
            cotangent_ref.at[pl.ds(jnp.where(leads, 0, share - 1), 1)], out_ref.at[pl.ds(RIM, 1)], sems.at[1]
        ),
    ]
    for copy in copies:
        copy.start()
    for copy in copies:
        copy.wait()


def rim_rows(bands, features, cotangent):
    shape = (RIM + 1,) + features.shape[1:]
    return pl.pallas_call(
        rim_body,
        in_specs=[in_scalars(), in_hbm(), in_hbm()],
        out_specs=in_vmem(),
        out_shape=jax.ShapeDtypeStruct(shape, features.dtype),
        scratch_shapes=[pltpu.SemaphoreType.DMA((2,))],
        compiler_params=params(8),
        name="rim_rows",
    )(bands, held(features), held(cotangent))


def column_sums(left, mid, right, column, last):
    from_left = jnp.where(column == 0, 0.0, pltpu.roll(left, 1, 0))
    from_right = jnp.where(column == last, 0.0, pltpu.roll(right, last, 0))
    return mid + from_left + from_right


def spread_taps(taps_ref, lanes, cols):
    taps = taps_ref[:, lanes].astype(F32)
    return [jnp.broadcast_to(taps[i : i + 1], (cols, LANES)) for i in range(9)]


def chunk_lanes(index, lane=0, count=CHUNK):
    return pl.ds(pl.multiple_of(index * CHUNK + lane, LANES), count)


def forward_body(bands_ref, features_ref, other_ref, rim_ref, expand_ref, taps_ref, project_ref, first_ref,
                 normed_ref, slab_ref, expanded_ref, mixed_ref, slab, normed_one, expand, project, expanded,
                 hidden, mixed, hidden_two, total, normed, row_sems, weight_sems, chunk_sems, out_sems):
    rows, cols, width = slab.shape
    own = rows - 2 * RIM
    chunks = expand_ref.shape[1] // CHUNK

    sources = (features_ref, other_ref, rim_ref)
    pieces = [(0, RIM), (RIM, BAND), (RIM + BAND, BAND), (RIM + 2 * BAND, RIM)]
    for index, (first, count) in enumerate(pieces):
        start_pull(bands_ref, first - RIM, sources, count, slab.at[pl.ds(first, count)], row_sems.at[index])

    def fetch_expand(index):
        lanes = chunk_lanes(index)
        return pltpu.make_async_copy(expand_ref.at[:, lanes], expand.at[:, lanes], weight_sems.at[0, index])

    def fetch_project(index):
        lanes = chunk_lanes(index)
        return pltpu.make_async_copy(project_ref.at[lanes], project.at[lanes], weight_sems.at[1, index])

    def store_expanded(index):
        lanes = chunk_lanes(index)
        return pltpu.make_async_copy(
            expanded.at[:, :, lanes], expanded_ref.at[:, :, lanes], chunk_sems.at[0, index]
        )

    def store_mixed(index):
        lanes = chunk_lanes(index)
        return pltpu.make_async_copy(mixed.at[:, :, lanes], mixed_ref.at[:, :, lanes], chunk_sems.at[1, index])

    for index in range(chunks):
        fetch_expand(index).start()
        fetch_project(index).start()
    for index, (first, count) in enumerate(pieces):
        wait_pull(sources, count, slab.at[pl.ds(first, count)], row_sems.at[index])
    store_slab = pltpu.make_async_copy(slab.at[pl.ds(RIM, own)], slab_ref, out_sems.at[0])
    store_slab.start()
    for row in range(0, rows, 2):
        at = slice(row * cols, (row + 2) * cols)
        values = slab[row : row + 2].astype(F32).reshape(2 * cols, width)
        normed_one[at] = (values * rms_scale(values)).astype(BF16)
    total[...] = slab[1 : rows - 1].astype(F32).reshape((rows - 2) * cols, width)
    column = lax.broadcasted_iota(jnp.int32, (cols, LANES), 0)

    def step(index, carry):
        fetch_expand(index).wait()
        weights = expand[:, chunk_lanes(index)]
        for row in range(0, rows, 4):
            product = nn_dot(normed_one[row * cols : (row + 4) * cols, :], weights)
            for inner in range(4):
                for lane in range(0, CHUNK, LANES):
                    lanes = slice(lane, lane + LANES)
                    values = product[inner * cols : (inner + 1) * cols, lanes]
                    hidden[row + inner, :, lanes] = gelu(values).astype(BF16).astype(F32)
                    if RIM <= row + inner < RIM + own:
                        expanded[row + inner - RIM, :, chunk_lanes(index, lane, LANES)] = values
        store_expanded(index).start()

        for lane in range(0, CHUNK, LANES):
            lanes = slice(lane, lane + LANES)
            taps = spread_taps(taps_ref, chunk_lanes(index, lane, LANES), cols)
            for row in range(rows - 2):
                rows_near = [hidden[row + a, :, lanes] for a in range(3)]
                sums = [
                    taps[b] * rows_near[0] + taps[3 + b] * rows_near[1] + taps[6 + b] * rows_near[2] for b in range(3)
                ]
                values = column_sums(sums[0], sums[1], sums[2], column, cols - 1)
                hidden_two[row * cols : (row + 1) * cols, lanes] = gelu(values).astype(BF16)
                mixed[row, :, chunk_lanes(index, lane, LANES)] = values
        store_mixed(index).start()
        fetch_project(index).wait()
        total[...] += nn_dot(hidden_two[...], project[chunk_lanes(index), :])
        return carry

    lax.fori_loop(0, chunks, step, 0)
    for row in range(1, own + 1):
        first = total[row * cols : (row + 1) * cols]
        normed[row - 1] = (first * rms_scale(first)).astype(BF16)
    store_normed = pltpu.make_async_copy(normed, normed_ref, out_sems.at[1])
    store_first = pltpu.make_async_copy(total, first_ref, out_sems.at[2])
    store_normed.start()
    store_first.start()
    for index in range(chunks):
        store_expanded(index).wait()
        store_mixed(index).wait()
    store_slab.wait()
    store_normed.wait()
    store_first.wait()


def forward(bands, features, other, rim, w_expand, kernel, w_project):
    capacity, cols, width = features.shape
    own, rows = GRID_ROWS, GRID_ROWS + 2 * RIM
    hidden_width = w_expand.shape[1]
    chunks = hidden_width // CHUNK
    return pl.pallas_call(
        forward_body,
        in_specs=[in_scalars(), in_hbm(), in_vmem(), in_vmem(), in_hbm(), in_vmem(), in_hbm()],
        out_specs=[in_hbm()] * 5,
        out_shape=[
            pltpu.HBM(((rows - 2) * cols, width), F32),
            pltpu.HBM((own, cols, width), BF16),
            pltpu.HBM((own, cols, width), BF16),
            pltpu.HBM((own, cols, hidden_width), F32),
            pltpu.HBM((rows - 2, cols, hidden_width), F32),
        ],
        scratch_shapes=[
            pltpu.VMEM((rows, cols, width), BF16),
            pltpu.VMEM((rows * cols, width), BF16),
            pltpu.VMEM((width, hidden_width), BF16),
            pltpu.VMEM((hidden_width, width), BF16),
            pltpu.VMEM((own, cols, hidden_width), F32),
            pltpu.VMEM((rows, cols, CHUNK), F32),
            pltpu.VMEM((rows - 2, cols, hidden_width), F32),
            pltpu.VMEM(((rows - 2) * cols, CHUNK), BF16),
            pltpu.VMEM(((rows - 2) * cols, width), F32),
            pltpu.VMEM((own, cols, width), BF16),
            pltpu.SemaphoreType.DMA((4,)),
            pltpu.SemaphoreType.DMA((2, chunks)),
            pltpu.SemaphoreType.DMA((2, chunks)),
            pltpu.SemaphoreType.DMA((3,)),
        ],
        compiler_params=params(26),
        cost_estimate=pl.CostEstimate(
            flops=4 * rows * cols * width * hidden_width,
            bytes_accessed=12 * 1024 * 1024,
            transcendentals=2 * rows * cols * hidden_width,
        ),
        name="bottleneck_forward",
    )(bands, held(features), near(other), near(rim), held(w_expand), near(kernel), held(w_project))


def slopes_body(expanded_ref, mixed_ref, slope_one_ref, slope_two_ref):
    for source, target in ((expanded_ref, slope_one_ref), (mixed_ref, slope_two_ref)):
        rows, _, chunk = source.shape
        for row in range(rows):
            for lane in range(0, chunk, LANES):
                lanes = slice(lane, lane + LANES)
                target[row, :, lanes] = gelu_slope(source[row, :, lanes]).astype(BF16)


def slopes(expanded, mixed):
    hidden_width = expanded.shape[2]
    blocks = [
        pl.BlockSpec(values.shape[:2] + (CHUNK,), lambda j: (0, 0, j)) for values in (expanded, mixed)
    ]
    return pl.pallas_call(
        slopes_body,
        grid=(hidden_width // CHUNK,),
        in_specs=blocks,
        out_specs=blocks,
        out_shape=[jax.ShapeDtypeStruct(values.shape, BF16) for values in (expanded, mixed)],
        compiler_params=params(),
        cost_estimate=pl.CostEstimate(
            flops=15 * (expanded.size + mixed.size),
            bytes_accessed=6 * (expanded.size + mixed.size),
            transcendentals=expanded.size + mixed.size,
        ),
        name="gelu_slopes",
    )(expanded, mixed)


def lane_tiles(width):
    return [slice(at, at + LANES) for at in range(0, width, LANES)]


def window_places(own, cols):
    return [(r, q) for r in range(own) for q in range(cols // 8)]


def to_windows(source_ref, rows_wide, target):
    groups, own, cols, width = source_ref.shape
    span = groups * 8
    for tile, lanes in enumerate(lane_tiles(width)):
        for group in range(groups):
            rows_wide[tile, group] = source_ref[group, :, :, lanes].astype(F32)
        for index, (r, q) in enumerate(window_places(own, cols)):
            pieces = [
                rows_wide[tile, group, r, pl.ds(q, 8, stride=cols // 8), :] for group in range(groups)
            ]
            rows = slice(index * span, (index + 1) * span)
            target[rows, lanes] = jnp.concatenate(pieces, axis=0).astype(BF16)


def to_rows(values, rows_wide, target_ref):
    groups, own, cols, width = target_ref.shape
    span = groups * 8
    for tile, lanes in enumerate(lane_tiles(width)):
        for index, (r, q) in enumerate(window_places(own, cols)):
            for group in range(groups):
                first = index * span + group * 8
                rows_wide[tile, group, r, pl.ds(q, 8, stride=cols // 8), :] = values[first : first + 8, lanes]
        for group in range(groups):
            target_ref[group, :, :, lanes] = rows_wide[tile, group].astype(BF16)


def wide_scratch(shape):
    groups, own, cols, width = shape
    return pltpu.VMEM((width // LANES, groups, own, cols, LANES), F32)


def grad_attended_body(cotangent_ref, out_ref, grad_ref, rows_wide, in_windows):
    to_windows(cotangent_ref, rows_wide, in_windows)
    grad_ref[...] = nt_dot(in_windows[...], out_ref[...]).astype(BF16)


def attended_gradient(cotangent, w_out):
    groups, own, cols, width = cotangent.shape
    shape = (groups * own * cols, width)
    return pl.pallas_call(
        grad_attended_body,
        grid=(1,),
        in_specs=[whole(cotangent.shape), whole(w_out.shape)],
        out_specs=whole(shape),
        out_shape=jax.ShapeDtypeStruct(shape, BF16),
        scratch_shapes=[wide_scratch(cotangent.shape), pltpu.VMEM(shape, BF16)],
        compiler_params=params(),
        cost_estimate=pl.CostEstimate(
            flops=2 * shape[0] * width * width, bytes_accessed=2 * 1024 * 1024, transcendentals=0
        ),
        name="attended_gradient",
    )(cotangent, w_out)


def per_query(values, weights, span, head_dim):
    wide = nn_dot(values.T, weights)
    half = LANES // 2
    own = jnp.concatenate([wide[:half, :LANES], wide[half:, LANES:]], axis=0).T
    lane_head = lax.broadcasted_iota(jnp.int32, (span, LANES), 1) // head_dim
    return jnp.where(lane_head % 2 == 0, own[:span], own[span:])


def attention_body(normed_ref, grad_attended_ref, qkv_ref, grad_ref, weights_ref, values_ref, rows_wide,
                   in_windows, projected, grad_projected, grad_attended, qkv, grad, weights, in_sems, out_sems):
    groups, own, cols, width = normed_ref.shape
    span = groups * 8
    windows = own * cols // 8
    head_dim = width // HEADS
    heads = LANES // head_dim
    scale = 1.0 / math.sqrt(head_dim)
    steepness = scale * math.log2(math.e)

    fetch_qkv = pltpu.make_async_copy(qkv_ref, qkv, in_sems.at[0])
    fetch_grad = pltpu.make_async_copy(grad_attended_ref, grad_attended, in_sems.at[1])
    fetch_qkv.start()
    fetch_grad.start()
    to_windows(normed_ref, rows_wide, in_windows)
    fetch_qkv.wait()
    projected[...] = nn_dot(in_windows[...], qkv[...]).astype(BF16)
    store_values = pltpu.make_async_copy(projected.at[:, pl.ds(2 * width, width)], values_ref, out_sems.at[0])
    store_values.start()
    fetch_grad.wait()

    row_head = lax.broadcasted_iota(jnp.int32, (heads * span, LANES), 0) // span
    lane_head = lax.broadcasted_iota(jnp.int32, (heads * span, LANES), 1) // head_dim
    mask = (row_head == lane_head).astype(F32).astype(BF16)

    def spread(values):
        return jnp.concatenate([values] * heads, axis=0) * mask

    def window(index, carry):
        rows = pl.ds(pl.multiple_of(index * span, span), span)
        for part in range(width // LANES):
            q_at, k_at, v_at = (
                slice(t * width + part * LANES, t * width + (part + 1) * LANES) for t in range(3)
            )
            q, k, v = projected[rows, q_at], projected[rows, k_at], projected[rows, v_at]
            q_wide = spread(q)
            g_wide = spread(grad_attended[rows, q_at])
            scores = nt_dot(k, q_wide)
            powers = jnp.exp2((scores - jnp.max(scores, axis=0, keepdims=True)) * steepness)
            shares = powers * (1.0 / jnp.sum(powers, axis=0, keepdims=True))
            half = shares.astype(BF16)
            weights[index, :, part * heads * span : (part + 1) * heads * span] = half
            grad_weights = nt_dot(v, g_wide)
            row_dot = jnp.sum(shares * grad_weights, axis=0, keepdims=True)
            grad_scores = (shares * (grad_weights - row_dot)).astype(BF16)
            grad_projected[rows, q_at] = (per_query(k, grad_scores, span, head_dim) * scale).astype(BF16)
            grad_projected[rows, k_at] = (nn_dot(grad_scores, q_wide) * scale).astype(BF16)
            grad_projected[rows, v_at] = nn_dot(half, g_wide).astype(BF16)
        return carry

    lax.fori_loop(0, windows, window, 0, unroll=4)
    store_weights = pltpu.make_async_copy(weights, weights_ref, out_sems.at[1])
    store_weights.start()
    to_rows(nt_dot(grad_projected[...], qkv[...]), rows_wide, grad)
    store_grad = pltpu.make_async_copy(grad, grad_ref, out_sems.at[2])
    store_grad.start()
    store_values.wait()
    store_weights.wait()
    store_grad.wait()


def attention(normed, grad_attended, w_qkv):
    groups, own, cols, width = normed.shape
    span = groups * 8
    tokens = groups * own * cols
    out_shapes = [normed.shape, (tokens // span, span, HEADS * span), (tokens, width)]
    return pl.pallas_call(
        attention_body,
        in_specs=[in_vmem(), in_hbm(), in_hbm()],
        out_specs=[in_hbm()] * 3,
        out_shape=[pltpu.HBM(shape, BF16) for shape in out_shapes],
        scratch_shapes=[
            wide_scratch(normed.shape),
            pltpu.VMEM((tokens, width), BF16),
            pltpu.VMEM((tokens, 3 * width), BF16),
            pltpu.VMEM((tokens, 3 * width), BF16),
            pltpu.VMEM((tokens, width), BF16),
            pltpu.VMEM(w_qkv.shape, BF16),
            pltpu.VMEM(normed.shape, BF16),
            pltpu.VMEM(out_shapes[1], BF16),
            pltpu.SemaphoreType.DMA((2,)),
            pltpu.SemaphoreType.DMA((3,)),
        ],
        compiler_params=params(18),
        cost_estimate=pl.CostEstimate(
            flops=16 * tokens * width * width,
            bytes_accessed=4 * 1024 * 1024,
            transcendentals=tokens * span * HEADS,
        ),
        name="window_attention",
    )(near(normed), held(grad_attended), held(w_qkv))


def attended_body(weights_ref, values_ref, out_ref, added_ref, rows_wide, attended):
    windows, span, wide = weights_ref.shape
    width = values_ref.shape[1]
    heads = LANES * HEADS // width
    for index in range(windows):
        rows = slice(index * span, (index + 1) * span)
        for part, lanes in enumerate(lane_tiles(width)):
            weights = weights_ref[index, :, part * heads * span : (part + 1) * heads * span]
            attended[rows, lanes] = per_query(values_ref[rows, lanes], weights, span, width // HEADS).astype(BF16)
    to_rows(nn_dot(attended[...], out_ref[...]), rows_wide, added_ref)


def attend(weights, values, w_out, shape):
    return pl.pallas_call(
        attended_body,
        grid=(1,),
        in_specs=[whole(weights.shape), whole(values.shape), whole(w_out.shape)],
        out_specs=whole(shape),
        out_shape=jax.ShapeDtypeStruct(shape, BF16),
        scratch_shapes=[wide_scratch(shape), pltpu.VMEM(values.shape, BF16)],
        compiler_params=params(),
        cost_estimate=pl.CostEstimate(
            flops=4 * values.size * values.shape[1], bytes_accessed=3 * 1024 * 1024, transcendentals=0
        ),
        name="attended_output",
    )(weights, values, w_out)


def backward_body(bands_ref, cotangent_ref, other_ref, rim_ref, slab_ref, first_ref, grad_slab_ref, grad_ref,
                  pair_ref, next_ref, slope_one_ref, slope_two_ref, expand_ref, taps_ref, project_ref,
                  out_ref, rims, slab, first, grad_slab, grad_in, slope_one, slope_two, expand, project,
                  grad_first, grad_rows, mixed, expanded, total, row_sems, in_sems, chunk_sems):
    own, cols, width = slab.shape
    chunks = expand_ref.shape[1] // CHUNK

    sources = (cotangent_ref, other_ref, rim_ref)
    sides = list(enumerate((-1, own)))
    for side, place_first in sides:
        start_pull(bands_ref, place_first, sources, 1, rims.at[pl.ds(side, 1)], row_sems.at[side], RIM)
    inputs = [
        pltpu.make_async_copy(source, target, in_sems.at[index])
        for index, (source, target) in enumerate(
            ((first_ref, first), (grad_ref, grad_in), (grad_slab_ref, grad_slab), (slab_ref, slab))
        )
    ]
    for copy in inputs:
        copy.start()

    def fetches(index):
        lanes = chunk_lanes(index)
        pairs = (
            (project_ref.at[lanes], project.at[lanes]),
            (slope_two_ref.at[:, :, lanes], slope_two.at[:, :, lanes]),
            (slope_one_ref.at[:, :, lanes], slope_one.at[:, :, lanes]),
            (expand_ref.at[:, lanes], expand.at[:, lanes]),
        )
        return [
            pltpu.make_async_copy(source, target, chunk_sems.at[number, index])
            for number, (source, target) in enumerate(pairs)
        ]

    for index in range(chunks):
        for copy in fetches(index):
            copy.start()

    def through_norm(cotangent, grad, first):
        rms = rms_scale(first)
        normed = first * rms
        grad = grad.astype(F32)
        inner = jnp.mean(grad * normed, -1, keepdims=True)
        return cotangent.astype(F32) + rms * (grad - normed * inner)

    for copy in inputs[:3]:
        copy.wait()
    for row in range(own):
        below = first[(row + 1) * cols : (row + 2) * cols]
        result = through_norm(grad_slab[row], grad_in[row], below)
        grad_first[row * cols : (row + 1) * cols] = result
        grad_rows[(row + 1) * cols : (row + 2) * cols] = result.astype(BF16)
    for side, place_first in sides:
        wait_pull(sources, 1, rims.at[pl.ds(side, 1)], row_sems.at[side])
    leads = lax.rem(lax.axis_index("row"), 2) == 0
    above = jnp.where(leads, next_ref[0].astype(F32), pair_ref[0].astype(F32))
    below = jnp.where(leads, pair_ref[0].astype(F32), next_ref[0].astype(F32))
    last = (own + 1) * cols
    grad_rows[0:cols] = through_norm(rims[0], above, first[0:cols]).astype(BF16)
    grad_rows[last:] = through_norm(rims[1], below, first[last:]).astype(BF16)
    column = lax.broadcasted_iota(jnp.int32, (cols, LANES), 0)

    total[...] = jnp.zeros_like(total)

    def step(index, carry):
        for copy in fetches(index):
            copy.wait()
        weights = project[chunk_lanes(index), :]
        for row in range(0, own + 2, 6):
            grad = nt_dot(grad_rows[row * cols : (row + 6) * cols, :], weights)
            for inner in range(6):
                for lane in range(0, CHUNK, LANES):
                    lanes = slice(lane, lane + LANES)
                    slope = slope_two[row + inner, :, chunk_lanes(index, lane, LANES)].astype(F32)
                    value = grad[inner * cols : (inner + 1) * cols, lanes] * slope
                    mixed[row + inner, :, lanes] = value.astype(BF16).astype(F32)

        for lane in range(0, CHUNK, LANES):
            lanes = slice(lane, lane + LANES)
            taps = spread_taps(taps_ref, chunk_lanes(index, lane, LANES), cols)
            for row in range(own):
                rows_near = [mixed[row + a, :, lanes] for a in range(3)]
                sums = [
                    taps[8 - b] * rows_near[0] + taps[5 - b] * rows_near[1] + taps[2 - b] * rows_near[2] for b in range(3)
                ]
                value = column_sums(sums[0], sums[1], sums[2], column, cols - 1)
                value = value * slope_one[row, :, chunk_lanes(index, lane, LANES)].astype(F32)
                expanded[row * cols : (row + 1) * cols, lanes] = value.astype(BF16)
        total[...] += nt_dot(expanded[...], expand[:, chunk_lanes(index)])
        return carry

    lax.fori_loop(0, chunks, step, 0)
    inputs[3].wait()
    for row in range(own):
        at = slice(row * cols, (row + 1) * cols)
        values = slab[row].astype(F32)
        rms = rms_scale(values)
        normed = values * rms
        grad = total[at]
        inner = jnp.mean(grad * normed, -1, keepdims=True)
        out_ref[row] = (grad_first[at] + rms * (grad - normed * inner)).astype(BF16)


def backward(bands, cotangent, other, rim, slab, first, grad_slab, grad, pair_row, next_row, slope_one,
             slope_two, w_expand, kernel, w_project):
    own, cols, width = slab.shape
    hidden_width = w_expand.shape[1]
    chunks = hidden_width // CHUNK
    return pl.pallas_call(
        backward_body,
        in_specs=[in_scalars()] + [in_hbm()] * 7 + [in_vmem()] * 2 + [in_hbm()] * 3 + [in_vmem(), in_hbm()],
        out_specs=in_vmem(),
        out_shape=jax.ShapeDtypeStruct((own, cols, width), BF16),
        scratch_shapes=[
            pltpu.VMEM((2, cols, width), BF16),
            pltpu.VMEM((own, cols, width), BF16),
            pltpu.VMEM(((own + 2) * cols, width), F32),
            pltpu.VMEM((own, cols, width), BF16),
            pltpu.VMEM((own, cols, width), BF16),
            pltpu.VMEM((own, cols, hidden_width), BF16),
            pltpu.VMEM((own + 2, cols, hidden_width), BF16),
            pltpu.VMEM((width, hidden_width), BF16),
            pltpu.VMEM((hidden_width, width), BF16),
            pltpu.VMEM((own * cols, width), F32),
            pltpu.VMEM(((own + 2) * cols, width), BF16),
            pltpu.VMEM((own + 2, cols, CHUNK), F32),
            pltpu.VMEM((own * cols, CHUNK), BF16),
            pltpu.VMEM((own * cols, width), F32),
            pltpu.SemaphoreType.DMA((2,)),
            pltpu.SemaphoreType.DMA((4,)),
            pltpu.SemaphoreType.DMA((4, chunks)),
        ],
        compiler_params=params(26),
        cost_estimate=pl.CostEstimate(
            flops=4 * (own + 2) * cols * width * hidden_width,
            bytes_accessed=12 * 1024 * 1024,
            transcendentals=0,
        ),
        name="bottleneck_backward",
    )(bands, held(cotangent), held(other), held(rim), held(slab), held(first), held(grad_slab), held(grad),
      near(pair_row), near(next_row), held(slope_one), held(slope_two), held(w_expand), near(kernel),
      held(w_project))


def window_groups(size):
    stride = size // 8
    return [[first + stride * k for k in range(8)] for first in range(stride)]


def exchange_windows(rows):
    groups = window_groups(lax.axis_size("row"))
    return lax.all_to_all(
        rows, "row", split_axis=0, concat_axis=0, tiled=True, axis_index_groups=groups
    )


def swap_pair(rows):
    size = lax.axis_size("row")
    return lax.ppermute(rows, "row", [(i, i ^ 1) for i in range(size)])


def swap_next(rows):
    size = lax.axis_size("row")
    pairs = [(i, i + 1) for i in range(1, size - 1, 2)]
    return lax.ppermute(rows, "row", pairs + [(j, i) for i, j in pairs])


def place_rows(even, other, leads, leader_share):
    size = GRID_ROWS
    first, second = even[:BAND], even[BAND:]
    share = jnp.where(leads, leader_share, 2 * size - leader_share)
    zeros = jnp.zeros_like(first)
    low = jnp.where(leads | (share == size), first, jnp.where(share < size, second, other))
    mid = jnp.where(share < size, zeros, jnp.where(leads | (share == size), second, first))
    high = jnp.where(share > size, jnp.where(leads, other, second), zeros)
    return jnp.concatenate([low, mid, high], 0)


def on_device(features, row_bands, w_expand, kernel, w_project, w_qkv, w_out, cotangent):
    capacity, cols, width = features.shape
    device = lax.axis_index("row")
    parity = device % 2
    leads = parity == 0

    rim = swap_next(rim_rows(row_bands, features, cotangent))
    other_cotangent = swap_pair(cotangent)
    other_features = swap_pair(features)
    grad_slab = even_rows(row_bands, cotangent, other_cotangent)
    rim, grad_slab = lax.optimization_barrier((rim, grad_slab))

    grad_windows = exchange_windows(grad_slab)
    first, normed, slab, expanded, mixed = forward(
        row_bands, features, other_features, rim, w_expand, kernel, w_project
    )
    normed, grad_windows = lax.optimization_barrier((normed, grad_windows))
    normed_windows = exchange_windows(normed)
    shape = (8, GRID_ROWS // 8, cols, width)
    slope_one, slope_two = slopes(expanded, mixed)
    grad_attended = attended_gradient(grad_windows.reshape(shape), w_out)
    normed_windows, slope_one, slope_two, grad_attended = lax.optimization_barrier(
        (normed_windows, slope_one, slope_two, grad_attended)
    )
    grad_normed, weights, values = attention(normed_windows.reshape(shape), grad_attended, w_qkv)
    grad_rows = exchange_windows(grad_normed.reshape(GRID_ROWS, cols, width))
    added = attend(weights, values, w_out, shape)
    grad_rows, added = lax.optimization_barrier((grad_rows, added))
    top, bottom = grad_rows[:1], grad_rows[GRID_ROWS - 1 :]
    pair_row = swap_pair(jnp.where(leads, bottom, top))
    next_row = swap_next(jnp.where(leads, top, bottom))
    added, pair_row, next_row = lax.optimization_barrier((added, pair_row, next_row))
    added_rows = exchange_windows(added.reshape(GRID_ROWS, cols, width))
    grad_input = backward(
        row_bands, cotangent, other_cotangent, rim, slab, first, grad_slab, grad_rows, pair_row, next_row,
        slope_one, slope_two, w_expand, kernel, w_project,
    )
    grad_input, added_rows = lax.optimization_barrier((grad_input, added_rows))
    first = first.reshape(GRID_ROWS + 2, cols, width)[1 : GRID_ROWS + 1]
    final = (first + added_rows.astype(F32)).astype(BF16)
    sent = [jnp.where(leads, rows[BAND:], rows[:BAND]) for rows in (final, grad_input)]
    swapped = swap_pair(jnp.stack(sent))
    leader_share = BAND * row_bands[device - parity]
    return (
        place_rows(final, swapped[0], leads, leader_share),
        place_rows(grad_input, swapped[1], leads, leader_share),
    )


def solution(mesh):
    return jax.shard_map(
        on_device,
        mesh=mesh,
        in_specs=(
            P(("parts", "row"), None, None),
            P("parts"),
            P(),
            P(),
            P(),
            P(),
            P(),
            P(("parts", "row"), None, None),
        ),
        out_specs=(P(("parts", "row"), None, None), P(("parts", "row"), None, None)),
        check_vma=False,
    )
```

```python
import math

import jax
import jax.numpy as jnp
from jax import lax
from jax.experimental import pallas as pl
from jax.experimental.pallas import tpu as pltpu
from jax.sharding import PartitionSpec as P

HEADS = 16
GRID_ROWS = 16
BAND = 8
RIM = 2
EPSILON = 1e-06
CHUNK = 512
HALF = 256
LANES = 128
ROOT = math.sqrt(2.0 / math.pi)
CUBIC = 0.044715
F32 = jnp.float32
BF16 = jnp.bfloat16
MIB = 1024 * 1024


def nt_dot(left, right):
    return lax.dot_general(left, right, (((1,), (1,)), ((), ())), preferred_element_type=F32)


def tn_dot(left, right):
    return lax.dot_general(left, right, (((0,), (0,)), ((), ())), preferred_element_type=F32)


def nn_dot(left, right):
    return jnp.dot(left, right, preferred_element_type=F32)


def rms_scale(values):
    return lax.rsqrt(jnp.mean(values * values, -1, keepdims=True) + EPSILON)


def gelu_parts(v):
    square = v * v
    cdf = 0.5 + 0.5 * jnp.tanh(v * (ROOT + (ROOT * CUBIC) * square))
    return square, cdf, v * cdf


def gelu(v):
    return gelu_parts(v)[2]


def gelu_slope(v):
    square, cdf, value = gelu_parts(v)
    return cdf + (value - value * cdf) * (2.0 * ROOT + (6.0 * ROOT * CUBIC) * square)


def whole(shape, space=None):
    zeros = (0,) * len(shape)
    return pl.BlockSpec(shape, lambda *_: zeros)


def params(mebibytes=56):
    return pltpu.CompilerParams(vmem_limit_bytes=mebibytes * MIB)


def in_vmem():
    return pl.BlockSpec(memory_space=pltpu.VMEM)


def in_hbm():
    return pl.BlockSpec(memory_space=pltpu.HBM)


def held(array):
    return pltpu.with_memory_space_constraint(array, pltpu.HBM)


def near(array):
    return pltpu.with_memory_space_constraint(array, pltpu.VMEM)


def in_scalars():
    return pl.BlockSpec(memory_space=pltpu.SMEM)


def shares(bands_ref):
    device = lax.axis_index("row")
    parity = lax.rem(device, 2)
    return parity, BAND * bands_ref[device - parity], BAND * bands_ref[device]


def place(bands_ref, first):
    parity, leader_share, _ = shares(bands_ref)
    row = first + GRID_ROWS * parity
    beyond = (row < 0) | (row >= 2 * GRID_ROWS)
    in_leader = row < leader_share
    in_own = in_leader == (parity == 0)
    source = jnp.where(beyond, 2, jnp.where(in_own, 0, 1))
    return source, jnp.where(beyond, 0, jnp.where(in_leader, row, row - leader_share))


def start_pull(bands_ref, first, sources, rows, target, sem, rim_row=0):
    where, row = place(bands_ref, first)
    row = jnp.where(where == 2, rim_row, row)
    for number, source in enumerate(sources):

        @pl.when(where == number)
        def _():
            pltpu.make_async_copy(source.at[pl.ds(row, rows)], target, sem).start()


def wait_pull(sources, rows, target, sem):
    pltpu.make_async_copy(sources[0].at[pl.ds(0, rows)], target, sem).wait()


def even_body(bands_ref, own_ref, other_ref, out_ref):
    for half in range(2):
        where, row = place(bands_ref, BAND * half)
        for number, source in enumerate((own_ref, other_ref)):

            @pl.when(where == number)
            def _():
                out_ref[BAND * half : BAND * half + BAND] = source[pl.ds(row, BAND)]


def even_rows(bands, own, other):
    shape = (GRID_ROWS,) + own.shape[1:]
    return pl.pallas_call(
        even_body,
        in_specs=[in_scalars(), in_vmem(), in_vmem()],
        out_specs=in_vmem(),
        out_shape=jax.ShapeDtypeStruct(shape, own.dtype),
        compiler_params=params(8),
        name="even_rows",
    )(bands, near(own), near(other))


def rim_body(bands_ref, features_ref, cotangent_ref, out_ref, sems):
    parity, _, share = shares(bands_ref)
    leads = parity == 0
    copies = [
        pltpu.make_async_copy(
            features_ref.at[pl.ds(jnp.where(leads, 0, share - RIM), RIM)], out_ref.at[pl.ds(0, RIM)], sems.at[0]
        ),
        pltpu.make_async_copy(
            cotangent_ref.at[pl.ds(jnp.where(leads, 0, share - 1), 1)], out_ref.at[pl.ds(RIM, 1)], sems.at[1]
        ),
    ]
    for copy in copies:
        copy.start()
    for copy in copies:
        copy.wait()


def rim_rows(bands, features, cotangent):
    shape = (RIM + 1,) + features.shape[1:]
    return pl.pallas_call(
        rim_body,
        in_specs=[in_scalars(), in_hbm(), in_hbm()],
        out_specs=in_vmem(),
        out_shape=jax.ShapeDtypeStruct(shape, features.dtype),
        scratch_shapes=[pltpu.SemaphoreType.DMA((2,))],
        compiler_params=params(8),
        name="rim_rows",
    )(bands, held(features), held(cotangent))


def column_sums(left, mid, right, column, last):
    from_left = jnp.where(column == 0, 0.0, pltpu.roll(left, 1, 0))
    from_right = jnp.where(column == last, 0.0, pltpu.roll(right, last, 0))
    return mid + from_left + from_right


def spread_taps(taps_ref, lanes, cols):
    taps = taps_ref[:, lanes].astype(F32)
    return [jnp.broadcast_to(taps[i : i + 1], (cols, LANES)) for i in range(9)]


def chunk_lanes(index, lane=0, count=CHUNK):
    return pl.ds(pl.multiple_of(index * CHUNK + lane, LANES), count)


def forward_body(bands_ref, features_ref, other_ref, rim_ref, expand_ref, taps_ref, project_ref, first_ref,
                 own_first_ref, normed_ref, slab_ref, expanded_ref, mixed_ref, slab, normed_one, expand, project,
                 expanded, hidden, mixed, product_a, product_b, hidden_a, hidden_b, total, normed, row_sems,
                 weight_sems, chunk_sems, out_sems):
    rows, cols, width = slab.shape
    own = rows - 2 * RIM
    chunks = expand_ref.shape[1] // CHUNK

    sources = (features_ref, other_ref, rim_ref)
    pieces = [(0, RIM), (RIM, BAND), (RIM + BAND, BAND), (RIM + 2 * BAND, RIM)]
    for index, (first, count) in enumerate(pieces):
        start_pull(bands_ref, first - RIM, sources, count, slab.at[pl.ds(first, count)], row_sems.at[index])

    def fetch_expand(index):
        lanes = chunk_lanes(index)
        return pltpu.make_async_copy(expand_ref.at[:, lanes], expand.at[:, lanes], weight_sems.at[0, index])

    def fetch_project(index):
        lanes = chunk_lanes(index)
        return pltpu.make_async_copy(project_ref.at[lanes], project.at[lanes], weight_sems.at[1, index])

    def store_expanded(index):
        lanes = chunk_lanes(index)
        return pltpu.make_async_copy(
            expanded.at[:, :, lanes], expanded_ref.at[:, :, lanes], chunk_sems.at[0, index]
        )

    def store_mixed(index):
        lanes = chunk_lanes(index)
        return pltpu.make_async_copy(mixed.at[:, :, lanes], mixed_ref.at[:, :, lanes], chunk_sems.at[1, index])

    fetch_expand(0).start()
    fetch_project(0).start()
    for index, (first, count) in enumerate(pieces):
        wait_pull(sources, count, slab.at[pl.ds(first, count)], row_sems.at[index])
    store_slab = pltpu.make_async_copy(slab.at[pl.ds(RIM, own)], slab_ref, out_sems.at[0])
    store_slab.start()
    for row in range(0, rows, 2):
        at = slice(row * cols, (row + 2) * cols)
        values = slab[row : row + 2].astype(F32).reshape(2 * cols, width)
        normed_one[at] = (values * rms_scale(values)).astype(BF16)
    total[...] = slab[1 : rows - 1].astype(F32).reshape((rows - 2) * cols, width)
    column = lax.broadcasted_iota(jnp.int32, (cols, LANES), 0)

    def step(index, carry):
        @pl.when(index + 1 < chunks)
        def _():
            fetch_expand(index + 1).start()
            fetch_project(index + 1).start()

        def expand_half(half, product):
            weights = expand[:, chunk_lanes(index, half * HALF, HALF)]
            product[...] = nn_dot(normed_one[...], weights).reshape(rows, cols, HALF)

        def project_half(half, hidden_two):
            total[...] += nn_dot(hidden_two[...], project[chunk_lanes(index, half * HALF, HALF), :])

        def mix_half(half, product, hidden_two):
            for lane in range(0, HALF, LANES):
                lanes = slice(lane, lane + LANES)
                at = chunk_lanes(index, half * HALF + lane, LANES)
                for row in range(rows):
                    values = product[row, :, lanes]
                    hidden[row, :, lanes] = gelu(values).astype(BF16).astype(F32)
                    if RIM <= row < RIM + own:
                        expanded[row - RIM, :, at] = values
                taps = spread_taps(taps_ref, at, cols)
                for row in range(rows - 2):
                    rows_near = [hidden[row + a, :, lanes] for a in range(3)]
                    sums = [
                        taps[b] * rows_near[0] + taps[3 + b] * rows_near[1] + taps[6 + b] * rows_near[2]
                        for b in range(3)
                    ]
                    values = column_sums(sums[0], sums[1], sums[2], column, cols - 1)
                    hidden_two[row * cols : (row + 1) * cols, lanes] = gelu(values).astype(BF16)
                    mixed[row, :, at] = values

        fetch_expand(index).wait()
        expand_half(0, product_a)
        expand_half(1, product_b)
        mix_half(0, product_a, hidden_a)
        fetch_project(index).wait()
        project_half(0, hidden_a)
        mix_half(1, product_b, hidden_b)
        project_half(1, hidden_b)
        store_expanded(index).start()
        store_mixed(index).start()
        return carry

    lax.fori_loop(0, chunks, step, 0)
    for row in range(1, own + 1):
        first = total[row * cols : (row + 1) * cols]
        normed[row - 1] = (first * rms_scale(first)).astype(BF16)
    store_normed = pltpu.make_async_copy(normed, normed_ref, out_sems.at[1])
    store_first = pltpu.make_async_copy(total, first_ref, out_sems.at[2])
    store_own = pltpu.make_async_copy(total.at[pl.ds(cols, own * cols)], own_first_ref, out_sems.at[3])
    store_normed.start()
    store_first.start()
    store_own.start()
    for index in range(chunks):
        store_expanded(index).wait()
        store_mixed(index).wait()
    store_slab.wait()
    store_normed.wait()
    store_first.wait()
    store_own.wait()


def forward(bands, features, other, rim, w_expand, kernel, w_project):
    capacity, cols, width = features.shape
    own, rows = GRID_ROWS, GRID_ROWS + 2 * RIM
    hidden_width = w_expand.shape[1]
    chunks = hidden_width // CHUNK
    return pl.pallas_call(
        forward_body,
        in_specs=[in_scalars(), in_hbm(), in_vmem(), in_vmem(), in_hbm(), in_vmem(), in_hbm()],
        out_specs=[in_hbm()] * 6,
        out_shape=[
            pltpu.HBM(((rows - 2) * cols, width), F32),
            pltpu.HBM((own * cols, width), F32),
            pltpu.HBM((own, cols, width), BF16),
            pltpu.HBM((own, cols, width), BF16),
            pltpu.HBM((own, cols, hidden_width), F32),
            pltpu.HBM((rows - 2, cols, hidden_width), F32),
        ],
        scratch_shapes=[
            pltpu.VMEM((rows, cols, width), BF16),
            pltpu.VMEM((rows * cols, width), BF16),
            pltpu.VMEM((width, hidden_width), BF16),
            pltpu.VMEM((hidden_width, width), BF16),
            pltpu.VMEM((own, cols, hidden_width), F32),
            pltpu.VMEM((rows, cols, HALF), F32),
            pltpu.VMEM((rows - 2, cols, hidden_width), F32),
            pltpu.VMEM((rows, cols, HALF), F32),
            pltpu.VMEM((rows, cols, HALF), F32),
            pltpu.VMEM(((rows - 2) * cols, HALF), BF16),
            pltpu.VMEM(((rows - 2) * cols, HALF), BF16),
            pltpu.VMEM(((rows - 2) * cols, width), F32),
            pltpu.VMEM((own, cols, width), BF16),
            pltpu.SemaphoreType.DMA((4,)),
            pltpu.SemaphoreType.DMA((2, chunks)),
            pltpu.SemaphoreType.DMA((2, chunks)),
            pltpu.SemaphoreType.DMA((4,)),
        ],
        compiler_params=params(28),
        cost_estimate=pl.CostEstimate(
            flops=4 * rows * cols * width * hidden_width,
            bytes_accessed=12 * 1024 * 1024,
            transcendentals=2 * rows * cols * hidden_width,
        ),
        name="bottleneck_forward",
    )(bands, held(features), near(other), near(rim), held(w_expand), near(kernel), held(w_project))


def slopes_body(expanded_ref, mixed_ref, slope_one_ref, slope_two_ref):
    for source, target in ((expanded_ref, slope_one_ref), (mixed_ref, slope_two_ref)):
        rows, _, chunk = source.shape
        for row in range(rows):
            for lane in range(0, chunk, LANES):
                lanes = slice(lane, lane + LANES)
                target[row, :, lanes] = gelu_slope(source[row, :, lanes]).astype(BF16)


def slopes(expanded, mixed):
    hidden_width = expanded.shape[2]
    blocks = [
        pl.BlockSpec(values.shape[:2] + (CHUNK,), lambda j: (0, 0, j)) for values in (expanded, mixed)
    ]
    return pl.pallas_call(
        slopes_body,
        grid=(hidden_width // CHUNK,),
        in_specs=blocks,
        out_specs=blocks,
        out_shape=[jax.ShapeDtypeStruct(values.shape, BF16) for values in (expanded, mixed)],
        compiler_params=params(),
        cost_estimate=pl.CostEstimate(
            flops=15 * (expanded.size + mixed.size),
            bytes_accessed=6 * (expanded.size + mixed.size),
            transcendentals=expanded.size + mixed.size,
        ),
        name="gelu_slopes",
    )(expanded, mixed)


def lane_tiles(width):
    return [slice(at, at + LANES) for at in range(0, width, LANES)]


def window_places(own, cols):
    return [(r, q) for r in range(own) for q in range(cols // 8)]


def to_windows(source_ref, rows_wide, target):
    groups, own, cols, width = source_ref.shape
    span = groups * 8
    for tile, lanes in enumerate(lane_tiles(width)):
        for group in range(groups):
            rows_wide[tile, group] = source_ref[group, :, :, lanes].astype(F32)
        for index, (r, q) in enumerate(window_places(own, cols)):
            pieces = [
                rows_wide[tile, group, r, pl.ds(q, 8, stride=cols // 8), :] for group in range(groups)
            ]
            rows = slice(index * span, (index + 1) * span)
            target[rows, lanes] = jnp.concatenate(pieces, axis=0).astype(BF16)


def to_rows(values, rows_wide, target_ref):
    groups, own, cols, width = target_ref.shape
    span = groups * 8
    for tile, lanes in enumerate(lane_tiles(width)):
        for index, (r, q) in enumerate(window_places(own, cols)):
            for group in range(groups):
                first = index * span + group * 8
                rows_wide[tile, group, r, pl.ds(q, 8, stride=cols // 8), :] = values[first : first + 8, lanes]
        for group in range(groups):
            target_ref[group, :, :, lanes] = rows_wide[tile, group].astype(BF16)


def wide_scratch(shape):
    groups, own, cols, width = shape
    return pltpu.VMEM((width // LANES, groups, own, cols, LANES), F32)


def grad_attended_body(cotangent_ref, out_ref, grad_ref, rows_wide, in_windows):
    to_windows(cotangent_ref, rows_wide, in_windows)
    grad_ref[...] = nt_dot(in_windows[...], out_ref[...]).astype(BF16)


def attended_gradient(cotangent, w_out):
    groups, own, cols, width = cotangent.shape
    shape = (groups * own * cols, width)
    return pl.pallas_call(
        grad_attended_body,
        grid=(1,),
        in_specs=[whole(cotangent.shape), whole(w_out.shape)],
        out_specs=whole(shape),
        out_shape=jax.ShapeDtypeStruct(shape, BF16),
        scratch_shapes=[wide_scratch(cotangent.shape), pltpu.VMEM(shape, BF16)],
        compiler_params=params(),
        cost_estimate=pl.CostEstimate(
            flops=2 * shape[0] * width * width, bytes_accessed=2 * 1024 * 1024, transcendentals=0
        ),
        name="attended_gradient",
    )(cotangent, w_out)


def per_query(values, weights, span, head_dim):
    wide = nn_dot(values.T, weights)
    half = LANES // 2
    own = jnp.concatenate([wide[:half, :LANES], wide[half:, LANES:]], axis=0).T
    lane_head = lax.broadcasted_iota(jnp.int32, (span, LANES), 1) // head_dim
    return jnp.where(lane_head % 2 == 0, own[:span], own[span:])


def attention_body(normed_ref, grad_attended_ref, qkv_ref, grad_ref, weights_ref, values_ref, rows_wide,
                   in_windows, projected, grad_projected, grad_attended, qkv, grad, weights, in_sems, out_sems):
    groups, own, cols, width = normed_ref.shape
    span = groups * 8
    windows = own * cols // 8
    head_dim = width // HEADS
    heads = LANES // head_dim
    scale = 1.0 / math.sqrt(head_dim)
    steepness = scale * math.log2(math.e)

    fetch_qkv = pltpu.make_async_copy(qkv_ref, qkv, in_sems.at[0])
    fetch_grad = pltpu.make_async_copy(grad_attended_ref, grad_attended, in_sems.at[1])
    fetch_qkv.start()
    fetch_grad.start()
    to_windows(normed_ref, rows_wide, in_windows)
    fetch_qkv.wait()
    projected[...] = nn_dot(in_windows[...], qkv[...]).astype(BF16)
    store_values = pltpu.make_async_copy(projected.at[:, pl.ds(2 * width, width)], values_ref, out_sems.at[0])
    store_values.start()
    fetch_grad.wait()

    row_head = lax.broadcasted_iota(jnp.int32, (heads * span, LANES), 0) // span
    lane_head = lax.broadcasted_iota(jnp.int32, (heads * span, LANES), 1) // head_dim
    mask = (row_head == lane_head).astype(F32).astype(BF16)

    def spread(values):
        return jnp.concatenate([values] * heads, axis=0) * mask

    def window(index, carry):
        rows = pl.ds(pl.multiple_of(index * span, span), span)
        for part in range(width // LANES):
            q_at, k_at, v_at = (
                slice(t * width + part * LANES, t * width + (part + 1) * LANES) for t in range(3)
            )
            q, k, v = projected[rows, q_at], projected[rows, k_at], projected[rows, v_at]
            q_wide = spread(q)
            g_wide = spread(grad_attended[rows, q_at])
            scores = nt_dot(k, q_wide)
            powers = jnp.exp2((scores - jnp.max(scores, axis=0, keepdims=True)) * steepness)
            shares = powers * (1.0 / jnp.sum(powers, axis=0, keepdims=True))
            half = shares.astype(BF16)
            weights[index, :, part * heads * span : (part + 1) * heads * span] = half
            grad_weights = nt_dot(v, g_wide)
            row_dot = jnp.sum(shares * grad_weights, axis=0, keepdims=True)
            grad_scores = (shares * (grad_weights - row_dot)).astype(BF16)
            grad_projected[rows, q_at] = (per_query(k, grad_scores, span, head_dim) * scale).astype(BF16)
            grad_projected[rows, k_at] = (nn_dot(grad_scores, q_wide) * scale).astype(BF16)
            grad_projected[rows, v_at] = nn_dot(half, g_wide).astype(BF16)
        return carry

    lax.fori_loop(0, windows, window, 0, unroll=4)
    store_weights = pltpu.make_async_copy(weights, weights_ref, out_sems.at[1])
    store_weights.start()
    to_rows(nt_dot(grad_projected[...], qkv[...]), rows_wide, grad)
    store_grad = pltpu.make_async_copy(grad, grad_ref, out_sems.at[2])
    store_grad.start()
    store_values.wait()
    store_weights.wait()
    store_grad.wait()


def attention(normed, grad_attended, w_qkv):
    groups, own, cols, width = normed.shape
    span = groups * 8
    tokens = groups * own * cols
    out_shapes = [normed.shape, (tokens // span, span, HEADS * span), (tokens, width)]
    return pl.pallas_call(
        attention_body,
        in_specs=[in_vmem(), in_hbm(), in_hbm()],
        out_specs=[in_hbm()] * 3,
        out_shape=[pltpu.HBM(shape, BF16) for shape in out_shapes],
        scratch_shapes=[
            wide_scratch(normed.shape),
            pltpu.VMEM((tokens, width), BF16),
            pltpu.VMEM((tokens, 3 * width), BF16),
            pltpu.VMEM((tokens, 3 * width), BF16),
            pltpu.VMEM((tokens, width), BF16),
            pltpu.VMEM(w_qkv.shape, BF16),
            pltpu.VMEM(normed.shape, BF16),
            pltpu.VMEM(out_shapes[1], BF16),
            pltpu.SemaphoreType.DMA((2,)),
            pltpu.SemaphoreType.DMA((3,)),
        ],
        compiler_params=params(18),
        cost_estimate=pl.CostEstimate(
            flops=16 * tokens * width * width,
            bytes_accessed=4 * 1024 * 1024,
            transcendentals=tokens * span * HEADS,
        ),
        name="window_attention",
    )(near(normed), held(grad_attended), held(w_qkv))


def attended_body(weights_ref, values_ref, out_ref, added_ref, rows_wide, attended):
    windows, span, wide = weights_ref.shape
    width = values_ref.shape[1]
    heads = LANES * HEADS // width
    for index in range(windows):
        rows = slice(index * span, (index + 1) * span)
        for part, lanes in enumerate(lane_tiles(width)):
            weights = weights_ref[index, :, part * heads * span : (part + 1) * heads * span]
            attended[rows, lanes] = per_query(values_ref[rows, lanes], weights, span, width // HEADS).astype(BF16)
    to_rows(nn_dot(attended[...], out_ref[...]), rows_wide, added_ref)


def attend(weights, values, w_out, shape):
    return pl.pallas_call(
        attended_body,
        grid=(1,),
        in_specs=[whole(weights.shape), whole(values.shape), whole(w_out.shape)],
        out_specs=whole(shape),
        out_shape=jax.ShapeDtypeStruct(shape, BF16),
        scratch_shapes=[wide_scratch(shape), pltpu.VMEM(values.shape, BF16)],
        compiler_params=params(),
        cost_estimate=pl.CostEstimate(
            flops=4 * values.size * values.shape[1], bytes_accessed=3 * 1024 * 1024, transcendentals=0
        ),
        name="attended_output",
    )(weights, values, w_out)


def backward_body(bands_ref, cotangent_ref, other_ref, rim_ref, slab_ref, first_ref, grad_slab_ref, grad_ref,
                  pair_ref, next_ref, slope_one_ref, slope_two_ref, expand_ref, taps_ref, project_ref,
                  out_ref, rims, slab, first, grad_slab, grad_in, slope_one, slope_two, expand, project,
                  grad_first, grad_rows, mixed, product_a, product_b, expanded_a, expanded_b, total, row_sems,
                  in_sems, chunk_sems):
    own, cols, width = slab.shape
    chunks = expand_ref.shape[1] // CHUNK

    sources = (cotangent_ref, other_ref, rim_ref)
    sides = list(enumerate((-1, own)))
    for side, place_first in sides:
        start_pull(bands_ref, place_first, sources, 1, rims.at[pl.ds(side, 1)], row_sems.at[side], RIM)
    inputs = [
        pltpu.make_async_copy(source, target, in_sems.at[index])
        for index, (source, target) in enumerate(
            ((first_ref, first), (grad_ref, grad_in), (grad_slab_ref, grad_slab), (slab_ref, slab))
        )
    ]
    for copy in inputs:
        copy.start()

    def fetches(index):
        lanes = chunk_lanes(index)
        pairs = (
            (project_ref.at[lanes], project.at[lanes]),
            (slope_two_ref.at[:, :, lanes], slope_two.at[:, :, lanes]),
            (slope_one_ref.at[:, :, lanes], slope_one.at[:, :, lanes]),
            (expand_ref.at[:, lanes], expand.at[:, lanes]),
        )
        return [
            pltpu.make_async_copy(source, target, chunk_sems.at[number, index])
            for number, (source, target) in enumerate(pairs)
        ]

    for copy in fetches(0):
        copy.start()

    def through_norm(cotangent, grad, first):
        rms = rms_scale(first)
        normed = first * rms
        grad = grad.astype(F32)
        inner = jnp.mean(grad * normed, -1, keepdims=True)
        return cotangent.astype(F32) + rms * (grad - normed * inner)

    for copy in inputs[:3]:
        copy.wait()
    for row in range(own):
        below = first[(row + 1) * cols : (row + 2) * cols]
        result = through_norm(grad_slab[row], grad_in[row], below)
        grad_first[row * cols : (row + 1) * cols] = result
        grad_rows[(row + 1) * cols : (row + 2) * cols] = result.astype(BF16)
    for side, place_first in sides:
        wait_pull(sources, 1, rims.at[pl.ds(side, 1)], row_sems.at[side])
    leads = lax.rem(lax.axis_index("row"), 2) == 0
    above = jnp.where(leads, next_ref[0].astype(F32), pair_ref[0].astype(F32))
    below = jnp.where(leads, pair_ref[0].astype(F32), next_ref[0].astype(F32))
    last = (own + 1) * cols
    grad_rows[0:cols] = through_norm(rims[0], above, first[0:cols]).astype(BF16)
    grad_rows[last:] = through_norm(rims[1], below, first[last:]).astype(BF16)
    column = lax.broadcasted_iota(jnp.int32, (cols, LANES), 0)

    total[...] = jnp.zeros_like(total)

    def step(index, carry):
        @pl.when(index + 1 < chunks)
        def _():
            for copy in fetches(index + 1):
                copy.start()

        def project_half(half, product):
            weights = project[chunk_lanes(index, half * HALF, HALF), :]
            product[...] = nt_dot(grad_rows[...], weights).reshape(own + 2, cols, HALF)

        def expand_half(half, expanded):
            total[...] += nt_dot(expanded[...], expand[:, chunk_lanes(index, half * HALF, HALF)])

        def unmix_half(half, product, expanded):
            for lane in range(0, HALF, LANES):
                lanes = slice(lane, lane + LANES)
                at = chunk_lanes(index, half * HALF + lane, LANES)
                for row in range(own + 2):
                    value = product[row, :, lanes] * slope_two[row, :, at].astype(F32)
                    mixed[row, :, lanes] = value.astype(BF16).astype(F32)
                taps = spread_taps(taps_ref, at, cols)
                for row in range(own):
                    rows_near = [mixed[row + a, :, lanes] for a in range(3)]
                    sums = [
                        taps[8 - b] * rows_near[0] + taps[5 - b] * rows_near[1] + taps[2 - b] * rows_near[2]
                        for b in range(3)
                    ]
                    value = column_sums(sums[0], sums[1], sums[2], column, cols - 1)
                    value = value * slope_one[row, :, at].astype(F32)
                    expanded[row * cols : (row + 1) * cols, lanes] = value.astype(BF16)

        for copy in fetches(index):
            copy.wait()
        project_half(0, product_a)
        project_half(1, product_b)
        unmix_half(0, product_a, expanded_a)
        expand_half(0, expanded_a)
        unmix_half(1, product_b, expanded_b)
        expand_half(1, expanded_b)
        return carry

    lax.fori_loop(0, chunks, step, 0)
    inputs[3].wait()
    for row in range(own):
        at = slice(row * cols, (row + 1) * cols)
        values = slab[row].astype(F32)
        rms = rms_scale(values)
        normed = values * rms
        grad = total[at]
        inner = jnp.mean(grad * normed, -1, keepdims=True)
        out_ref[row] = (grad_first[at] + rms * (grad - normed * inner)).astype(BF16)


def backward(bands, cotangent, other, rim, slab, first, grad_slab, grad, pair_row, next_row, slope_one,
             slope_two, w_expand, kernel, w_project):
    own, cols, width = slab.shape
    hidden_width = w_expand.shape[1]
    chunks = hidden_width // CHUNK
    return pl.pallas_call(
        backward_body,
        in_specs=[in_scalars()] + [in_hbm()] * 7 + [in_vmem()] * 2 + [in_hbm()] * 3 + [in_vmem(), in_hbm()],
        out_specs=in_vmem(),
        out_shape=jax.ShapeDtypeStruct((own, cols, width), BF16),
        scratch_shapes=[
            pltpu.VMEM((2, cols, width), BF16),
            pltpu.VMEM((own, cols, width), BF16),
            pltpu.VMEM(((own + 2) * cols, width), F32),
            pltpu.VMEM((own, cols, width), BF16),
            pltpu.VMEM((own, cols, width), BF16),
            pltpu.VMEM((own, cols, hidden_width), BF16),
            pltpu.VMEM((own + 2, cols, hidden_width), BF16),
            pltpu.VMEM((width, hidden_width), BF16),
            pltpu.VMEM((hidden_width, width), BF16),
            pltpu.VMEM((own * cols, width), F32),
            pltpu.VMEM(((own + 2) * cols, width), BF16),
            pltpu.VMEM((own + 2, cols, HALF), F32),
            pltpu.VMEM((own + 2, cols, HALF), F32),
            pltpu.VMEM((own + 2, cols, HALF), F32),
            pltpu.VMEM((own * cols, HALF), BF16),
            pltpu.VMEM((own * cols, HALF), BF16),
            pltpu.VMEM((own * cols, width), F32),
            pltpu.SemaphoreType.DMA((2,)),
            pltpu.SemaphoreType.DMA((4,)),
            pltpu.SemaphoreType.DMA((4, chunks)),
        ],
        compiler_params=params(26),
        cost_estimate=pl.CostEstimate(
            flops=4 * (own + 2) * cols * width * hidden_width,
            bytes_accessed=12 * 1024 * 1024,
            transcendentals=0,
        ),
        name="bottleneck_backward",
    )(bands, held(cotangent), held(other), held(rim), held(slab), held(first), held(grad_slab), held(grad),
      near(pair_row), near(next_row), held(slope_one), held(slope_two), held(w_expand), near(kernel),
      held(w_project))


def window_groups(size):
    stride = size // 8
    return [[first + stride * k for k in range(8)] for first in range(stride)]


def exchange_windows(rows):
    groups = window_groups(lax.axis_size("row"))
    return lax.all_to_all(
        rows, "row", split_axis=0, concat_axis=0, tiled=True, axis_index_groups=groups
    )


def swap_pair(rows):
    size = lax.axis_size("row")
    return lax.ppermute(rows, "row", [(i, i ^ 1) for i in range(size)])


def swap_next(rows):
    size = lax.axis_size("row")
    pairs = [(i, i + 1) for i in range(1, size - 1, 2)]
    return lax.ppermute(rows, "row", pairs + [(j, i) for i, j in pairs])


def place_rows(even, other, leads, leader_share):
    size = GRID_ROWS
    first, second = even[:BAND], even[BAND:]
    share = jnp.where(leads, leader_share, 2 * size - leader_share)
    zeros = jnp.zeros_like(first)
    low = jnp.where(leads | (share == size), first, jnp.where(share < size, second, other))
    mid = jnp.where(share < size, zeros, jnp.where(leads | (share == size), second, first))
    high = jnp.where(share > size, jnp.where(leads, other, second), zeros)
    return jnp.concatenate([low, mid, high], 0)


def on_device(features, row_bands, w_expand, kernel, w_project, w_qkv, w_out, cotangent):
    capacity, cols, width = features.shape
    device = lax.axis_index("row")
    parity = device % 2
    leads = parity == 0

    rim = swap_next(rim_rows(row_bands, features, cotangent))
    other_cotangent = swap_pair(cotangent)
    other_features = swap_pair(features)
    grad_slab = even_rows(row_bands, cotangent, other_cotangent)
    rim, grad_slab = lax.optimization_barrier((rim, grad_slab))

    grad_windows = exchange_windows(grad_slab)
    first, own_first, normed, slab, expanded, mixed = forward(
        row_bands, features, other_features, rim, w_expand, kernel, w_project
    )
    normed, grad_windows = lax.optimization_barrier((normed, grad_windows))
    normed_windows = exchange_windows(normed)
    shape = (8, GRID_ROWS // 8, cols, width)
    slope_one, slope_two = slopes(expanded, mixed)
    grad_attended = attended_gradient(grad_windows.reshape(shape), w_out)
    normed_windows, slope_one, slope_two, grad_attended = lax.optimization_barrier(
        (normed_windows, slope_one, slope_two, grad_attended)
    )
    grad_normed, weights, values = attention(normed_windows.reshape(shape), grad_attended, w_qkv)
    grad_rows = exchange_windows(grad_normed.reshape(GRID_ROWS, cols, width))
    added = attend(weights, values, w_out, shape)
    grad_rows, added = lax.optimization_barrier((grad_rows, added))
    top, bottom = grad_rows[:1], grad_rows[GRID_ROWS - 1 :]
    pair_row = swap_pair(jnp.where(leads, bottom, top))
    next_row = swap_next(jnp.where(leads, top, bottom))
    added, pair_row, next_row = lax.optimization_barrier((added, pair_row, next_row))
    added_rows = exchange_windows(added.reshape(GRID_ROWS, cols, width))
    grad_input = backward(
        row_bands, cotangent, other_cotangent, rim, slab, first, grad_slab, grad_rows, pair_row, next_row,
        slope_one, slope_two, w_expand, kernel, w_project,
    )
    grad_input, added_rows = lax.optimization_barrier((grad_input, added_rows))
    final = (own_first.reshape(GRID_ROWS, cols, width) + added_rows.astype(F32)).astype(BF16)
    sent = [jnp.where(leads, rows[BAND:], rows[:BAND]) for rows in (final, grad_input)]
    swapped = swap_pair(jnp.stack(sent))
    leader_share = BAND * row_bands[device - parity]
    return (
        place_rows(final, swapped[0], leads, leader_share),
        place_rows(grad_input, swapped[1], leads, leader_share),
    )


def solution(mesh):
    return jax.shard_map(
        on_device,
        mesh=mesh,
        in_specs=(
            P(("parts", "row"), None, None),
            P("parts"),
            P(),
            P(),
            P(),
            P(),
            P(),
            P(("parts", "row"), None, None),
        ),
        out_specs=(P(("parts", "row"), None, None), P(("parts", "row"), None, None)),
        check_vma=False,
    )
```

```python
import math

import jax
import jax.numpy as jnp
from jax import lax
from jax.experimental import pallas as pl
from jax.experimental.pallas import tpu as pltpu
from jax.sharding import PartitionSpec as P

HEADS = 16
GRID_ROWS = 16
BAND = 8
RIM = 2
EPSILON = 1e-06
CHUNK = 512
HALF = 256
LANES = 128
ROOT = math.sqrt(2.0 / math.pi)
CUBIC = 0.044715
F32 = jnp.float32
BF16 = jnp.bfloat16
MIB = 1024 * 1024


def nt_dot(left, right):
    return lax.dot_general(left, right, (((1,), (1,)), ((), ())), preferred_element_type=F32)


def tn_dot(left, right):
    return lax.dot_general(left, right, (((0,), (0,)), ((), ())), preferred_element_type=F32)


def nn_dot(left, right):
    return jnp.dot(left, right, preferred_element_type=F32)


def rms_scale(values):
    return lax.rsqrt(jnp.mean(values * values, -1, keepdims=True) + EPSILON)


def gelu_parts(v):
    square = v * v
    cdf = 0.5 + 0.5 * jnp.tanh(v * (ROOT + (ROOT * CUBIC) * square))
    return square, cdf, v * cdf


def gelu(v):
    return gelu_parts(v)[2]


def gelu_slope(v):
    square, cdf, value = gelu_parts(v)
    return cdf + (value - value * cdf) * (2.0 * ROOT + (6.0 * ROOT * CUBIC) * square)


def whole(shape, space=None):
    zeros = (0,) * len(shape)
    return pl.BlockSpec(shape, lambda *_: zeros)


def params(mebibytes=56):
    return pltpu.CompilerParams(vmem_limit_bytes=mebibytes * MIB)


def in_vmem():
    return pl.BlockSpec(memory_space=pltpu.VMEM)


def in_hbm():
    return pl.BlockSpec(memory_space=pltpu.HBM)


def held(array):
    return pltpu.with_memory_space_constraint(array, pltpu.HBM)


def near(array):
    return pltpu.with_memory_space_constraint(array, pltpu.VMEM)


def in_scalars():
    return pl.BlockSpec(memory_space=pltpu.SMEM)


def shares(bands_ref):
    device = lax.axis_index("row")
    parity = lax.rem(device, 2)
    return parity, BAND * bands_ref[device - parity], BAND * bands_ref[device]


def place(bands_ref, first):
    parity, leader_share, _ = shares(bands_ref)
    row = first + GRID_ROWS * parity
    beyond = (row < 0) | (row >= 2 * GRID_ROWS)
    in_leader = row < leader_share
    in_own = in_leader == (parity == 0)
    source = jnp.where(beyond, 2, jnp.where(in_own, 0, 1))
    return source, jnp.where(beyond, 0, jnp.where(in_leader, row, row - leader_share))


def start_pull(bands_ref, first, sources, rows, target, sem, rim_row=0):
    where, row = place(bands_ref, first)
    row = jnp.where(where == 2, rim_row, row)
    for number, source in enumerate(sources):

        @pl.when(where == number)
        def _():
            pltpu.make_async_copy(source.at[pl.ds(row, rows)], target, sem).start()


def wait_pull(sources, rows, target, sem):
    pltpu.make_async_copy(sources[0].at[pl.ds(0, rows)], target, sem).wait()


def even_body(bands_ref, own_ref, other_ref, out_ref):
    for half in range(2):
        where, row = place(bands_ref, BAND * half)
        for number, source in enumerate((own_ref, other_ref)):

            @pl.when(where == number)
            def _():
                out_ref[BAND * half : BAND * half + BAND] = source[pl.ds(row, BAND)]


def even_rows(bands, own, other):
    shape = (GRID_ROWS,) + own.shape[1:]
    return pl.pallas_call(
        even_body,
        in_specs=[in_scalars(), in_vmem(), in_vmem()],
        out_specs=in_vmem(),
        out_shape=jax.ShapeDtypeStruct(shape, own.dtype),
        compiler_params=params(8),
        name="even_rows",
    )(bands, near(own), near(other))


def rim_body(bands_ref, features_ref, cotangent_ref, out_ref, sems):
    parity, _, share = shares(bands_ref)
    leads = parity == 0
    copies = [
        pltpu.make_async_copy(
            features_ref.at[pl.ds(jnp.where(leads, 0, share - RIM), RIM)], out_ref.at[pl.ds(0, RIM)], sems.at[0]
        ),
        pltpu.make_async_copy(
            cotangent_ref.at[pl.ds(jnp.where(leads, 0, share - 1), 1)], out_ref.at[pl.ds(RIM, 1)], sems.at[1]
        ),
    ]
    for copy in copies:
        copy.start()
    for copy in copies:
        copy.wait()


def rim_rows(bands, features, cotangent):
    shape = (RIM + 1,) + features.shape[1:]
    return pl.pallas_call(
        rim_body,
        in_specs=[in_scalars(), in_hbm(), in_hbm()],
        out_specs=in_vmem(),
        out_shape=jax.ShapeDtypeStruct(shape, features.dtype),
        scratch_shapes=[pltpu.SemaphoreType.DMA((2,))],
        compiler_params=params(8),
        name="rim_rows",
    )(bands, held(features), held(cotangent))


def column_sums(left, mid, right, column, last):
    from_left = jnp.where(column == 0, 0.0, pltpu.roll(left, 1, 0))
    from_right = jnp.where(column == last, 0.0, pltpu.roll(right, last, 0))
    return mid + from_left + from_right


def spread_taps(taps_ref, lanes, cols):
    taps = taps_ref[:, lanes].astype(F32)
    return [jnp.broadcast_to(taps[i : i + 1], (cols, LANES)) for i in range(9)]


def chunk_lanes(index, lane=0, count=CHUNK):
    return pl.ds(pl.multiple_of(index * CHUNK + lane, LANES), count)


def forward_body(bands_ref, features_ref, other_ref, rim_ref, expand_ref, taps_ref, project_ref, first_ref,
                 own_first_ref, normed_ref, slab_ref, expanded_ref, mixed_ref, slab, normed_one, expand, project,
                 expanded, hidden, mixed, hidden_two, total, normed, row_sems,
                 weight_sems, chunk_sems, out_sems):
    rows, cols, width = slab.shape
    own = rows - 2 * RIM
    chunks = expand_ref.shape[1] // CHUNK

    sources = (features_ref, other_ref, rim_ref)
    pieces = [(0, RIM), (RIM, BAND), (RIM + BAND, BAND), (RIM + 2 * BAND, RIM)]
    for index, (first, count) in enumerate(pieces):
        start_pull(bands_ref, first - RIM, sources, count, slab.at[pl.ds(first, count)], row_sems.at[index])

    def fetch_expand(index):
        lanes = chunk_lanes(index)
        return pltpu.make_async_copy(expand_ref.at[:, lanes], expand.at[:, lanes], weight_sems.at[0, index])

    def fetch_project(index):
        lanes = chunk_lanes(index)
        return pltpu.make_async_copy(project_ref.at[lanes], project.at[lanes], weight_sems.at[1, index])

    def store_expanded(index):
        lanes = chunk_lanes(index)
        return pltpu.make_async_copy(
            expanded.at[:, :, lanes], expanded_ref.at[:, :, lanes], chunk_sems.at[0, index]
        )

    def store_mixed(index):
        lanes = chunk_lanes(index)
        return pltpu.make_async_copy(mixed.at[:, :, lanes], mixed_ref.at[:, :, lanes], chunk_sems.at[1, index])

    fetch_expand(0).start()
    fetch_project(0).start()
    for index, (first, count) in enumerate(pieces):
        wait_pull(sources, count, slab.at[pl.ds(first, count)], row_sems.at[index])
    store_slab = pltpu.make_async_copy(slab.at[pl.ds(RIM, own)], slab_ref, out_sems.at[0])
    store_slab.start()
    for row in range(0, rows, 2):
        at = slice(row * cols, (row + 2) * cols)
        values = slab[row : row + 2].astype(F32).reshape(2 * cols, width)
        normed_one[at] = (values * rms_scale(values)).astype(BF16)
    total[...] = slab[1 : rows - 1].astype(F32).reshape((rows - 2) * cols, width)
    column = lax.broadcasted_iota(jnp.int32, (cols, LANES), 0)

    def step(index, carry):
        @pl.when(index + 1 < chunks)
        def _():
            fetch_expand(index + 1).start()
            fetch_project(index + 1).start()

        fetch_expand(index).wait()
        weights = expand[:, chunk_lanes(index)]
        for row in range(0, rows, 4):
            product = nn_dot(normed_one[row * cols : (row + 4) * cols, :], weights)
            for inner in range(4):
                for lane in range(0, CHUNK, LANES):
                    lanes = slice(lane, lane + LANES)
                    values = product[inner * cols : (inner + 1) * cols, lanes]
                    hidden[row + inner, :, lanes] = gelu(values).astype(BF16).astype(F32)
                    if RIM <= row + inner < RIM + own:
                        expanded[row + inner - RIM, :, chunk_lanes(index, lane, LANES)] = values
        store_expanded(index).start()

        for lane in range(0, CHUNK, LANES):
            lanes = slice(lane, lane + LANES)
            taps = spread_taps(taps_ref, chunk_lanes(index, lane, LANES), cols)
            for row in range(rows - 2):
                rows_near = [hidden[row + a, :, lanes] for a in range(3)]
                sums = [
                    taps[b] * rows_near[0] + taps[3 + b] * rows_near[1] + taps[6 + b] * rows_near[2] for b in range(3)
                ]
                values = column_sums(sums[0], sums[1], sums[2], column, cols - 1)
                hidden_two[row * cols : (row + 1) * cols, lanes] = gelu(values).astype(BF16)
                mixed[row, :, chunk_lanes(index, lane, LANES)] = values
        store_mixed(index).start()
        fetch_project(index).wait()
        total[...] += nn_dot(hidden_two[...], project[chunk_lanes(index), :])
        return carry

    lax.fori_loop(0, chunks, step, 0)
    for row in range(1, own + 1):
        first = total[row * cols : (row + 1) * cols]
        normed[row - 1] = (first * rms_scale(first)).astype(BF16)
    store_normed = pltpu.make_async_copy(normed, normed_ref, out_sems.at[1])
    store_first = pltpu.make_async_copy(total, first_ref, out_sems.at[2])
    store_own = pltpu.make_async_copy(total.at[pl.ds(cols, own * cols)], own_first_ref, out_sems.at[3])
    store_normed.start()
    store_first.start()
    store_own.start()
    for index in range(chunks):
        store_expanded(index).wait()
        store_mixed(index).wait()
    store_slab.wait()
    store_normed.wait()
    store_first.wait()
    store_own.wait()


def forward(bands, features, other, rim, w_expand, kernel, w_project):
    capacity, cols, width = features.shape
    own, rows = GRID_ROWS, GRID_ROWS + 2 * RIM
    hidden_width = w_expand.shape[1]
    chunks = hidden_width // CHUNK
    return pl.pallas_call(
        forward_body,
        in_specs=[in_scalars(), in_hbm(), in_vmem(), in_vmem(), in_hbm(), in_vmem(), in_hbm()],
        out_specs=[in_hbm()] * 6,
        out_shape=[
            pltpu.HBM(((rows - 2) * cols, width), F32),
            pltpu.HBM((own * cols, width), F32),
            pltpu.HBM((own, cols, width), BF16),
            pltpu.HBM((own, cols, width), BF16),
            pltpu.HBM((own, cols, hidden_width), F32),
            pltpu.HBM((rows - 2, cols, hidden_width), F32),
        ],
        scratch_shapes=[
            pltpu.VMEM((rows, cols, width), BF16),
            pltpu.VMEM((rows * cols, width), BF16),
            pltpu.VMEM((width, hidden_width), BF16),
            pltpu.VMEM((hidden_width, width), BF16),
            pltpu.VMEM((own, cols, hidden_width), F32),
            pltpu.VMEM((rows, cols, CHUNK), F32),
            pltpu.VMEM((rows - 2, cols, hidden_width), F32),
            pltpu.VMEM(((rows - 2) * cols, CHUNK), BF16),
            pltpu.VMEM(((rows - 2) * cols, width), F32),
            pltpu.VMEM((own, cols, width), BF16),
            pltpu.SemaphoreType.DMA((4,)),
            pltpu.SemaphoreType.DMA((2, chunks)),
            pltpu.SemaphoreType.DMA((2, chunks)),
            pltpu.SemaphoreType.DMA((4,)),
        ],
        compiler_params=params(28),
        cost_estimate=pl.CostEstimate(
            flops=4 * rows * cols * width * hidden_width,
            bytes_accessed=12 * 1024 * 1024,
            transcendentals=2 * rows * cols * hidden_width,
        ),
        name="bottleneck_forward",
    )(bands, held(features), near(other), near(rim), held(w_expand), near(kernel), held(w_project))


def slopes_body(expanded_ref, mixed_ref, slope_one_ref, slope_two_ref):
    for source, target in ((expanded_ref, slope_one_ref), (mixed_ref, slope_two_ref)):
        rows, _, chunk = source.shape
        for row in range(rows):
            for lane in range(0, chunk, LANES):
                lanes = slice(lane, lane + LANES)
                target[row, :, lanes] = gelu_slope(source[row, :, lanes]).astype(BF16)


def slopes(expanded, mixed):
    hidden_width = expanded.shape[2]
    blocks = [
        pl.BlockSpec(values.shape[:2] + (CHUNK,), lambda j: (0, 0, j)) for values in (expanded, mixed)
    ]
    return pl.pallas_call(
        slopes_body,
        grid=(hidden_width // CHUNK,),
        in_specs=blocks,
        out_specs=blocks,
        out_shape=[jax.ShapeDtypeStruct(values.shape, BF16) for values in (expanded, mixed)],
        compiler_params=params(),
        cost_estimate=pl.CostEstimate(
            flops=15 * (expanded.size + mixed.size),
            bytes_accessed=6 * (expanded.size + mixed.size),
            transcendentals=expanded.size + mixed.size,
        ),
        name="gelu_slopes",
    )(expanded, mixed)


def lane_tiles(width):
    return [slice(at, at + LANES) for at in range(0, width, LANES)]


def window_places(own, cols):
    return [(r, q) for r in range(own) for q in range(cols // 8)]


def to_windows(source_ref, rows_wide, target):
    groups, own, cols, width = source_ref.shape
    span = groups * 8
    for tile, lanes in enumerate(lane_tiles(width)):
        for group in range(groups):
            rows_wide[tile, group] = source_ref[group, :, :, lanes].astype(F32)
        for index, (r, q) in enumerate(window_places(own, cols)):
            pieces = [
                rows_wide[tile, group, r, pl.ds(q, 8, stride=cols // 8), :] for group in range(groups)
            ]
            rows = slice(index * span, (index + 1) * span)
            target[rows, lanes] = jnp.concatenate(pieces, axis=0).astype(BF16)


def to_rows(values, rows_wide, target_ref):
    groups, own, cols, width = target_ref.shape
    span = groups * 8
    for tile, lanes in enumerate(lane_tiles(width)):
        for index, (r, q) in enumerate(window_places(own, cols)):
            for group in range(groups):
                first = index * span + group * 8
                rows_wide[tile, group, r, pl.ds(q, 8, stride=cols // 8), :] = values[first : first + 8, lanes]
        for group in range(groups):
            target_ref[group, :, :, lanes] = rows_wide[tile, group].astype(BF16)


def wide_scratch(shape):
    groups, own, cols, width = shape
    return pltpu.VMEM((width // LANES, groups, own, cols, LANES), F32)


def grad_attended_body(cotangent_ref, out_ref, grad_ref, rows_wide, in_windows):
    to_windows(cotangent_ref, rows_wide, in_windows)
    grad_ref[...] = nt_dot(in_windows[...], out_ref[...]).astype(BF16)


def attended_gradient(cotangent, w_out):
    groups, own, cols, width = cotangent.shape
    shape = (groups * own * cols, width)
    return pl.pallas_call(
        grad_attended_body,
        grid=(1,),
        in_specs=[whole(cotangent.shape), whole(w_out.shape)],
        out_specs=whole(shape),
        out_shape=jax.ShapeDtypeStruct(shape, BF16),
        scratch_shapes=[wide_scratch(cotangent.shape), pltpu.VMEM(shape, BF16)],
        compiler_params=params(),
        cost_estimate=pl.CostEstimate(
            flops=2 * shape[0] * width * width, bytes_accessed=2 * 1024 * 1024, transcendentals=0
        ),
        name="attended_gradient",
    )(cotangent, w_out)


def per_query(values, weights, span, head_dim):
    wide = nn_dot(values.T, weights)
    half = LANES // 2
    own = jnp.concatenate([wide[:half, :LANES], wide[half:, LANES:]], axis=0).T
    lane_head = lax.broadcasted_iota(jnp.int32, (span, LANES), 1) // head_dim
    return jnp.where(lane_head % 2 == 0, own[:span], own[span:])


def attention_body(normed_ref, grad_attended_ref, qkv_ref, grad_ref, weights_ref, values_ref, rows_wide,
                   in_windows, projected, grad_projected, grad_attended, qkv, grad, weights, in_sems, out_sems):
    groups, own, cols, width = normed_ref.shape
    span = groups * 8
    windows = own * cols // 8
    head_dim = width // HEADS
    heads = LANES // head_dim
    scale = 1.0 / math.sqrt(head_dim)
    steepness = scale * math.log2(math.e)

    fetch_qkv = pltpu.make_async_copy(qkv_ref, qkv, in_sems.at[0])
    fetch_grad = pltpu.make_async_copy(grad_attended_ref, grad_attended, in_sems.at[1])
    fetch_qkv.start()
    fetch_grad.start()
    to_windows(normed_ref, rows_wide, in_windows)
    fetch_qkv.wait()
    projected[...] = nn_dot(in_windows[...], qkv[...]).astype(BF16)
    store_values = pltpu.make_async_copy(projected.at[:, pl.ds(2 * width, width)], values_ref, out_sems.at[0])
    store_values.start()
    fetch_grad.wait()

    row_head = lax.broadcasted_iota(jnp.int32, (heads * span, LANES), 0) // span
    lane_head = lax.broadcasted_iota(jnp.int32, (heads * span, LANES), 1) // head_dim
    mask = (row_head == lane_head).astype(F32).astype(BF16)

    def spread(values):
        return jnp.concatenate([values] * heads, axis=0) * mask

    def window(index, carry):
        rows = pl.ds(pl.multiple_of(index * span, span), span)
        for part in range(width // LANES):
            q_at, k_at, v_at = (
                slice(t * width + part * LANES, t * width + (part + 1) * LANES) for t in range(3)
            )
            q, k, v = projected[rows, q_at], projected[rows, k_at], projected[rows, v_at]
            q_wide = spread(q)
            g_wide = spread(grad_attended[rows, q_at])
            scores = nt_dot(k, q_wide)
            powers = jnp.exp2((scores - jnp.max(scores, axis=0, keepdims=True)) * steepness)
            shares = powers * (1.0 / jnp.sum(powers, axis=0, keepdims=True))
            half = shares.astype(BF16)
            weights[index, :, part * heads * span : (part + 1) * heads * span] = half
            grad_weights = nt_dot(v, g_wide)
            row_dot = jnp.sum(shares * grad_weights, axis=0, keepdims=True)
            grad_scores = (shares * (grad_weights - row_dot)).astype(BF16)
            grad_projected[rows, q_at] = (per_query(k, grad_scores, span, head_dim) * scale).astype(BF16)
            grad_projected[rows, k_at] = (nn_dot(grad_scores, q_wide) * scale).astype(BF16)
            grad_projected[rows, v_at] = nn_dot(half, g_wide).astype(BF16)
        return carry

    lax.fori_loop(0, windows, window, 0, unroll=4)
    store_weights = pltpu.make_async_copy(weights, weights_ref, out_sems.at[1])
    store_weights.start()
    to_rows(nt_dot(grad_projected[...], qkv[...]), rows_wide, grad)
    store_grad = pltpu.make_async_copy(grad, grad_ref, out_sems.at[2])
    store_grad.start()
    store_values.wait()
    store_weights.wait()
    store_grad.wait()


def attention(normed, grad_attended, w_qkv):
    groups, own, cols, width = normed.shape
    span = groups * 8
    tokens = groups * own * cols
    out_shapes = [normed.shape, (tokens // span, span, HEADS * span), (tokens, width)]
    return pl.pallas_call(
        attention_body,
        in_specs=[in_vmem(), in_hbm(), in_hbm()],
        out_specs=[in_hbm()] * 3,
        out_shape=[pltpu.HBM(shape, BF16) for shape in out_shapes],
        scratch_shapes=[
            wide_scratch(normed.shape),
            pltpu.VMEM((tokens, width), BF16),
            pltpu.VMEM((tokens, 3 * width), BF16),
            pltpu.VMEM((tokens, 3 * width), BF16),
            pltpu.VMEM((tokens, width), BF16),
            pltpu.VMEM(w_qkv.shape, BF16),
            pltpu.VMEM(normed.shape, BF16),
            pltpu.VMEM(out_shapes[1], BF16),
            pltpu.SemaphoreType.DMA((2,)),
            pltpu.SemaphoreType.DMA((3,)),
        ],
        compiler_params=params(18),
        cost_estimate=pl.CostEstimate(
            flops=16 * tokens * width * width,
            bytes_accessed=4 * 1024 * 1024,
            transcendentals=tokens * span * HEADS,
        ),
        name="window_attention",
    )(near(normed), held(grad_attended), held(w_qkv))


def attended_body(weights_ref, values_ref, out_ref, added_ref, rows_wide, attended):
    windows, span, wide = weights_ref.shape
    width = values_ref.shape[1]
    heads = LANES * HEADS // width
    for index in range(windows):
        rows = slice(index * span, (index + 1) * span)
        for part, lanes in enumerate(lane_tiles(width)):
            weights = weights_ref[index, :, part * heads * span : (part + 1) * heads * span]
            attended[rows, lanes] = per_query(values_ref[rows, lanes], weights, span, width // HEADS).astype(BF16)
    to_rows(nn_dot(attended[...], out_ref[...]), rows_wide, added_ref)


def attend(weights, values, w_out, shape):
    return pl.pallas_call(
        attended_body,
        grid=(1,),
        in_specs=[whole(weights.shape), whole(values.shape), whole(w_out.shape)],
        out_specs=whole(shape),
        out_shape=jax.ShapeDtypeStruct(shape, BF16),
        scratch_shapes=[wide_scratch(shape), pltpu.VMEM(values.shape, BF16)],
        compiler_params=params(),
        cost_estimate=pl.CostEstimate(
            flops=4 * values.size * values.shape[1], bytes_accessed=3 * 1024 * 1024, transcendentals=0
        ),
        name="attended_output",
    )(weights, values, w_out)


def backward_body(bands_ref, cotangent_ref, other_ref, rim_ref, slab_ref, first_ref, grad_slab_ref, grad_ref,
                  pair_ref, next_ref, slope_one_ref, slope_two_ref, expand_ref, taps_ref, project_ref,
                  out_ref, rims, slab, first, grad_slab, grad_in, slope_one, slope_two, expand, project,
                  grad_first, grad_rows, mixed, product_a, product_b, expanded_a, expanded_b, total, row_sems,
                  in_sems, chunk_sems):
    own, cols, width = slab.shape
    chunks = expand_ref.shape[1] // CHUNK

    sources = (cotangent_ref, other_ref, rim_ref)
    sides = list(enumerate((-1, own)))
    for side, place_first in sides:
        start_pull(bands_ref, place_first, sources, 1, rims.at[pl.ds(side, 1)], row_sems.at[side], RIM)
    inputs = [
        pltpu.make_async_copy(source, target, in_sems.at[index])
        for index, (source, target) in enumerate(
            ((first_ref, first), (grad_ref, grad_in), (grad_slab_ref, grad_slab), (slab_ref, slab))
        )
    ]
    for copy in inputs:
        copy.start()

    def fetches(index):
        lanes = chunk_lanes(index)
        pairs = (
            (project_ref.at[lanes], project.at[lanes]),
            (slope_two_ref.at[:, :, lanes], slope_two.at[:, :, lanes]),
            (slope_one_ref.at[:, :, lanes], slope_one.at[:, :, lanes]),
            (expand_ref.at[:, lanes], expand.at[:, lanes]),
        )
        return [
            pltpu.make_async_copy(source, target, chunk_sems.at[number, index])
            for number, (source, target) in enumerate(pairs)
        ]

    for copy in fetches(0):
        copy.start()

    def through_norm(cotangent, grad, first):
        rms = rms_scale(first)
        normed = first * rms
        grad = grad.astype(F32)
        inner = jnp.mean(grad * normed, -1, keepdims=True)
        return cotangent.astype(F32) + rms * (grad - normed * inner)

    for copy in inputs[:3]:
        copy.wait()
    for row in range(own):
        below = first[(row + 1) * cols : (row + 2) * cols]
        result = through_norm(grad_slab[row], grad_in[row], below)
        grad_first[row * cols : (row + 1) * cols] = result
        grad_rows[(row + 1) * cols : (row + 2) * cols] = result.astype(BF16)
    for side, place_first in sides:
        wait_pull(sources, 1, rims.at[pl.ds(side, 1)], row_sems.at[side])
    leads = lax.rem(lax.axis_index("row"), 2) == 0
    above = jnp.where(leads, next_ref[0].astype(F32), pair_ref[0].astype(F32))
    below = jnp.where(leads, pair_ref[0].astype(F32), next_ref[0].astype(F32))
    last = (own + 1) * cols
    grad_rows[0:cols] = through_norm(rims[0], above, first[0:cols]).astype(BF16)
    grad_rows[last:] = through_norm(rims[1], below, first[last:]).astype(BF16)
    column = lax.broadcasted_iota(jnp.int32, (cols, LANES), 0)

    total[...] = jnp.zeros_like(total)

    def step(index, carry):
        @pl.when(index + 1 < chunks)
        def _():
            for copy in fetches(index + 1):
                copy.start()

        def project_half(half, product):
            weights = project[chunk_lanes(index, half * HALF, HALF), :]
            product[...] = nt_dot(grad_rows[...], weights).reshape(own + 2, cols, HALF)

        def expand_half(half, expanded):
            total[...] += nt_dot(expanded[...], expand[:, chunk_lanes(index, half * HALF, HALF)])

        def unmix_half(half, product, expanded):
            for lane in range(0, HALF, LANES):
                lanes = slice(lane, lane + LANES)
                at = chunk_lanes(index, half * HALF + lane, LANES)
                for row in range(own + 2):
                    value = product[row, :, lanes] * slope_two[row, :, at].astype(F32)
                    mixed[row, :, lanes] = value.astype(BF16).astype(F32)
                taps = spread_taps(taps_ref, at, cols)
                for row in range(own):
                    rows_near = [mixed[row + a, :, lanes] for a in range(3)]
                    sums = [
                        taps[8 - b] * rows_near[0] + taps[5 - b] * rows_near[1] + taps[2 - b] * rows_near[2]
                        for b in range(3)
                    ]
                    value = column_sums(sums[0], sums[1], sums[2], column, cols - 1)
                    value = value * slope_one[row, :, at].astype(F32)
                    expanded[row * cols : (row + 1) * cols, lanes] = value.astype(BF16)

        for copy in fetches(index):
            copy.wait()
        project_half(0, product_a)
        project_half(1, product_b)
        unmix_half(0, product_a, expanded_a)
        expand_half(0, expanded_a)
        unmix_half(1, product_b, expanded_b)
        expand_half(1, expanded_b)
        return carry

    lax.fori_loop(0, chunks, step, 0)
    inputs[3].wait()
    for row in range(own):
        at = slice(row * cols, (row + 1) * cols)
        values = slab[row].astype(F32)
        rms = rms_scale(values)
        normed = values * rms
        grad = total[at]
        inner = jnp.mean(grad * normed, -1, keepdims=True)
        out_ref[row] = (grad_first[at] + rms * (grad - normed * inner)).astype(BF16)


def backward(bands, cotangent, other, rim, slab, first, grad_slab, grad, pair_row, next_row, slope_one,
             slope_two, w_expand, kernel, w_project):
    own, cols, width = slab.shape
    hidden_width = w_expand.shape[1]
    chunks = hidden_width // CHUNK
    return pl.pallas_call(
        backward_body,
        in_specs=[in_scalars()] + [in_hbm()] * 7 + [in_vmem()] * 2 + [in_hbm()] * 3 + [in_vmem(), in_hbm()],
        out_specs=in_vmem(),
        out_shape=jax.ShapeDtypeStruct((own, cols, width), BF16),
        scratch_shapes=[
            pltpu.VMEM((2, cols, width), BF16),
            pltpu.VMEM((own, cols, width), BF16),
            pltpu.VMEM(((own + 2) * cols, width), F32),
            pltpu.VMEM((own, cols, width), BF16),
            pltpu.VMEM((own, cols, width), BF16),
            pltpu.VMEM((own, cols, hidden_width), BF16),
            pltpu.VMEM((own + 2, cols, hidden_width), BF16),
            pltpu.VMEM((width, hidden_width), BF16),
            pltpu.VMEM((hidden_width, width), BF16),
            pltpu.VMEM((own * cols, width), F32),
            pltpu.VMEM(((own + 2) * cols, width), BF16),
            pltpu.VMEM((own + 2, cols, HALF), F32),
            pltpu.VMEM((own + 2, cols, HALF), F32),
            pltpu.VMEM((own + 2, cols, HALF), F32),
            pltpu.VMEM((own * cols, HALF), BF16),
            pltpu.VMEM((own * cols, HALF), BF16),
            pltpu.VMEM((own * cols, width), F32),
            pltpu.SemaphoreType.DMA((2,)),
            pltpu.SemaphoreType.DMA((4,)),
            pltpu.SemaphoreType.DMA((4, chunks)),
        ],
        compiler_params=params(26),
        cost_estimate=pl.CostEstimate(
            flops=4 * (own + 2) * cols * width * hidden_width,
            bytes_accessed=12 * 1024 * 1024,
            transcendentals=0,
        ),
        name="bottleneck_backward",
    )(bands, held(cotangent), held(other), held(rim), held(slab), held(first), held(grad_slab), held(grad),
      near(pair_row), near(next_row), held(slope_one), held(slope_two), held(w_expand), near(kernel),
      held(w_project))


def window_groups(size):
    stride = size // 8
    return [[first + stride * k for k in range(8)] for first in range(stride)]


def exchange_windows(rows):
    groups = window_groups(lax.axis_size("row"))
    return lax.all_to_all(
        rows, "row", split_axis=0, concat_axis=0, tiled=True, axis_index_groups=groups
    )


def swap_pair(rows):
    size = lax.axis_size("row")
    return lax.ppermute(rows, "row", [(i, i ^ 1) for i in range(size)])


def swap_next(rows):
    size = lax.axis_size("row")
    pairs = [(i, i + 1) for i in range(1, size - 1, 2)]
    return lax.ppermute(rows, "row", pairs + [(j, i) for i, j in pairs])


def place_rows(even, other, leads, leader_share):
    size = GRID_ROWS
    first, second = even[:BAND], even[BAND:]
    share = jnp.where(leads, leader_share, 2 * size - leader_share)
    zeros = jnp.zeros_like(first)
    low = jnp.where(leads | (share == size), first, jnp.where(share < size, second, other))
    mid = jnp.where(share < size, zeros, jnp.where(leads | (share == size), second, first))
    high = jnp.where(share > size, jnp.where(leads, other, second), zeros)
    return jnp.concatenate([low, mid, high], 0)


def on_device(features, row_bands, w_expand, kernel, w_project, w_qkv, w_out, cotangent):
    capacity, cols, width = features.shape
    device = lax.axis_index("row")
    parity = device % 2
    leads = parity == 0

    rim = swap_next(rim_rows(row_bands, features, cotangent))
    other_cotangent = swap_pair(cotangent)
    other_features = swap_pair(features)
    grad_slab = even_rows(row_bands, cotangent, other_cotangent)
    rim, grad_slab = lax.optimization_barrier((rim, grad_slab))

    grad_windows = exchange_windows(grad_slab)
    first, own_first, normed, slab, expanded, mixed = forward(
        row_bands, features, other_features, rim, w_expand, kernel, w_project
    )
    normed, grad_windows = lax.optimization_barrier((normed, grad_windows))
    normed_windows = exchange_windows(normed)
    shape = (8, GRID_ROWS // 8, cols, width)
    slope_one, slope_two = slopes(expanded, mixed)
    grad_attended = attended_gradient(grad_windows.reshape(shape), w_out)
    normed_windows, slope_one, slope_two, grad_attended = lax.optimization_barrier(
        (normed_windows, slope_one, slope_two, grad_attended)
    )
    grad_normed, weights, values = attention(normed_windows.reshape(shape), grad_attended, w_qkv)
    grad_rows = exchange_windows(grad_normed.reshape(GRID_ROWS, cols, width))
    added = attend(weights, values, w_out, shape)
    grad_rows, added = lax.optimization_barrier((grad_rows, added))
    top, bottom = grad_rows[:1], grad_rows[GRID_ROWS - 1 :]
    pair_row = swap_pair(jnp.where(leads, bottom, top))
    next_row = swap_next(jnp.where(leads, top, bottom))
    added, pair_row, next_row = lax.optimization_barrier((added, pair_row, next_row))
    added_rows = exchange_windows(added.reshape(GRID_ROWS, cols, width))
    grad_input = backward(
        row_bands, cotangent, other_cotangent, rim, slab, first, grad_slab, grad_rows, pair_row, next_row,
        slope_one, slope_two, w_expand, kernel, w_project,
    )
    grad_input, added_rows = lax.optimization_barrier((grad_input, added_rows))
    final = (own_first.reshape(GRID_ROWS, cols, width) + added_rows.astype(F32)).astype(BF16)
    sent = [jnp.where(leads, rows[BAND:], rows[:BAND]) for rows in (final, grad_input)]
    swapped = swap_pair(jnp.stack(sent))
    leader_share = BAND * row_bands[device - parity]
    return (
        place_rows(final, swapped[0], leads, leader_share),
        place_rows(grad_input, swapped[1], leads, leader_share),
    )


def solution(mesh):
    return jax.shard_map(
        on_device,
        mesh=mesh,
        in_specs=(
            P(("parts", "row"), None, None),
            P("parts"),
            P(),
            P(),
            P(),
            P(),
            P(),
            P(("parts", "row"), None, None),
        ),
        out_specs=(P(("parts", "row"), None, None), P(("parts", "row"), None, None)),
        check_vma=False,
    )
```

```python
import math

import jax
import jax.numpy as jnp
from jax import lax
from jax.experimental import pallas as pl
from jax.experimental.pallas import tpu as pltpu
from jax.sharding import PartitionSpec as P

HEADS = 16
GRID_ROWS = 16
BAND = 8
RIM = 2
EPSILON = 1e-06
CHUNK = 512
HALF = 256
GROUP_FORWARD = 10
GROUP_BACKWARD = 9
LANES = 128
ROOT = math.sqrt(2.0 / math.pi)
CUBIC = 0.044715
F32 = jnp.float32
BF16 = jnp.bfloat16
MIB = 1024 * 1024


def nt_dot(left, right):
    return lax.dot_general(left, right, (((1,), (1,)), ((), ())), preferred_element_type=F32)


def tn_dot(left, right):
    return lax.dot_general(left, right, (((0,), (0,)), ((), ())), preferred_element_type=F32)


def nn_dot(left, right):
    return jnp.dot(left, right, preferred_element_type=F32)


def rms_scale(values):
    return lax.rsqrt(jnp.mean(values * values, -1, keepdims=True) + EPSILON)


def gelu_parts(v):
    square = v * v
    cdf = 0.5 + 0.5 * jnp.tanh(v * (ROOT + (ROOT * CUBIC) * square))
    return square, cdf, v * cdf


def gelu(v):
    return gelu_parts(v)[2]


def gelu_slope(v):
    square, cdf, value = gelu_parts(v)
    return cdf + (value - value * cdf) * (2.0 * ROOT + (6.0 * ROOT * CUBIC) * square)


def whole(shape, space=None):
    zeros = (0,) * len(shape)
    return pl.BlockSpec(shape, lambda *_: zeros)


def params(mebibytes=56):
    return pltpu.CompilerParams(vmem_limit_bytes=mebibytes * MIB)


def in_vmem():
    return pl.BlockSpec(memory_space=pltpu.VMEM)


def in_hbm():
    return pl.BlockSpec(memory_space=pltpu.HBM)


def held(array):
    return pltpu.with_memory_space_constraint(array, pltpu.HBM)


def near(array):
    return pltpu.with_memory_space_constraint(array, pltpu.VMEM)


def in_scalars():
    return pl.BlockSpec(memory_space=pltpu.SMEM)


def shares(bands_ref):
    device = lax.axis_index("row")
    parity = lax.rem(device, 2)
    return parity, BAND * bands_ref[device - parity], BAND * bands_ref[device]


def place(bands_ref, first):
    parity, leader_share, _ = shares(bands_ref)
    row = first + GRID_ROWS * parity
    beyond = (row < 0) | (row >= 2 * GRID_ROWS)
    in_leader = row < leader_share
    in_own = in_leader == (parity == 0)
    source = jnp.where(beyond, 2, jnp.where(in_own, 0, 1))
    return source, jnp.where(beyond, 0, jnp.where(in_leader, row, row - leader_share))


def start_pull(bands_ref, first, sources, rows, target, sem, rim_row=0):
    where, row = place(bands_ref, first)
    row = jnp.where(where == 2, rim_row, row)
    for number, source in enumerate(sources):

        @pl.when(where == number)
        def _():
            pltpu.make_async_copy(source.at[pl.ds(row, rows)], target, sem).start()


def wait_pull(sources, rows, target, sem):
    pltpu.make_async_copy(sources[0].at[pl.ds(0, rows)], target, sem).wait()


def even_body(bands_ref, own_ref, other_ref, out_ref):
    for half in range(2):
        where, row = place(bands_ref, BAND * half)
        for number, source in enumerate((own_ref, other_ref)):

            @pl.when(where == number)
            def _():
                out_ref[BAND * half : BAND * half + BAND] = source[pl.ds(row, BAND)]


def even_rows(bands, own, other):
    shape = (GRID_ROWS,) + own.shape[1:]
    return pl.pallas_call(
        even_body,
        in_specs=[in_scalars(), in_vmem(), in_vmem()],
        out_specs=in_vmem(),
        out_shape=jax.ShapeDtypeStruct(shape, own.dtype),
        compiler_params=params(8),
        name="even_rows",
    )(bands, near(own), near(other))


def rim_body(bands_ref, features_ref, cotangent_ref, out_ref, sems):
    parity, _, share = shares(bands_ref)
    leads = parity == 0
    copies = [
        pltpu.make_async_copy(
            features_ref.at[pl.ds(jnp.where(leads, 0, share - RIM), RIM)], out_ref.at[pl.ds(0, RIM)], sems.at[0]
        ),
        pltpu.make_async_copy(
            cotangent_ref.at[pl.ds(jnp.where(leads, 0, share - 1), 1)], out_ref.at[pl.ds(RIM, 1)], sems.at[1]
        ),
    ]
    for copy in copies:
        copy.start()
    for copy in copies:
        copy.wait()


def rim_rows(bands, features, cotangent):
    shape = (RIM + 1,) + features.shape[1:]
    return pl.pallas_call(
        rim_body,
        in_specs=[in_scalars(), in_hbm(), in_hbm()],
        out_specs=in_vmem(),
        out_shape=jax.ShapeDtypeStruct(shape, features.dtype),
        scratch_shapes=[pltpu.SemaphoreType.DMA((2,))],
        compiler_params=params(8),
        name="rim_rows",
    )(bands, held(features), held(cotangent))


def column_sums(left, mid, right, column, last):
    from_left = jnp.where(column == 0, 0.0, pltpu.roll(left, 1, 0))
    from_right = jnp.where(column == last, 0.0, pltpu.roll(right, last, 0))
    return mid + from_left + from_right


def spread_taps(taps_ref, lanes, cols):
    taps = taps_ref[:, lanes].astype(F32)
    return [jnp.broadcast_to(taps[i : i + 1], (cols, LANES)) for i in range(9)]


def chunk_lanes(index, lane=0, count=CHUNK):
    return pl.ds(pl.multiple_of(index * CHUNK + lane, LANES), count)


def forward_body(bands_ref, features_ref, other_ref, rim_ref, expand_ref, taps_ref, project_ref, first_ref,
                 own_first_ref, normed_ref, slab_ref, expanded_ref, mixed_ref, slab, normed_one, expand, project,
                 expanded, hidden, mixed, hidden_two, total, normed, row_sems,
                 weight_sems, chunk_sems, out_sems):
    rows, cols, width = slab.shape
    own = rows - 2 * RIM
    chunks = expand_ref.shape[1] // CHUNK

    sources = (features_ref, other_ref, rim_ref)
    pieces = [(0, RIM), (RIM, BAND), (RIM + BAND, BAND), (RIM + 2 * BAND, RIM)]
    for index, (first, count) in enumerate(pieces):
        start_pull(bands_ref, first - RIM, sources, count, slab.at[pl.ds(first, count)], row_sems.at[index])

    def fetch_expand(index):
        lanes = chunk_lanes(index)
        return pltpu.make_async_copy(expand_ref.at[:, lanes], expand.at[:, lanes], weight_sems.at[0, index])

    def fetch_project(index):
        lanes = chunk_lanes(index)
        return pltpu.make_async_copy(project_ref.at[lanes], project.at[lanes], weight_sems.at[1, index])

    def store_expanded(index):
        lanes = chunk_lanes(index)
        return pltpu.make_async_copy(
            expanded.at[:, :, lanes], expanded_ref.at[:, :, lanes], chunk_sems.at[0, index]
        )

    def store_mixed(index):
        lanes = chunk_lanes(index)
        return pltpu.make_async_copy(mixed.at[:, :, lanes], mixed_ref.at[:, :, lanes], chunk_sems.at[1, index])

    fetch_expand(0).start()
    fetch_project(0).start()
    for index, (first, count) in enumerate(pieces):
        wait_pull(sources, count, slab.at[pl.ds(first, count)], row_sems.at[index])
    store_slab = pltpu.make_async_copy(slab.at[pl.ds(RIM, own)], slab_ref, out_sems.at[0])
    store_slab.start()
    for row in range(0, rows, 2):
        at = slice(row * cols, (row + 2) * cols)
        values = slab[row : row + 2].astype(F32).reshape(2 * cols, width)
        normed_one[at] = (values * rms_scale(values)).astype(BF16)
    total[...] = slab[1 : rows - 1].astype(F32).reshape((rows - 2) * cols, width)
    column = lax.broadcasted_iota(jnp.int32, (cols, LANES), 0)

    def step(index, carry):
        @pl.when(index + 1 < chunks)
        def _():
            fetch_expand(index + 1).start()
            fetch_project(index + 1).start()

        fetch_expand(index).wait()
        for start in range(0, CHUNK, HALF):
            weights = expand[:, chunk_lanes(index, start, HALF)]
            for row in range(0, rows, GROUP_FORWARD):
                product = nn_dot(normed_one[row * cols : (row + GROUP_FORWARD) * cols, :], weights)
                for inner in range(GROUP_FORWARD):
                    for lane in range(0, HALF, LANES):
                        values = product[inner * cols : (inner + 1) * cols, lane : lane + LANES]
                        at = slice(start + lane, start + lane + LANES)
                        hidden[row + inner, :, at] = gelu(values).astype(BF16).astype(F32)
                        if RIM <= row + inner < RIM + own:
                            expanded[row + inner - RIM, :, chunk_lanes(index, start + lane, LANES)] = values
        store_expanded(index).start()

        for lane in range(0, CHUNK, LANES):
            lanes = slice(lane, lane + LANES)
            taps = spread_taps(taps_ref, chunk_lanes(index, lane, LANES), cols)
            for row in range(rows - 2):
                rows_near = [hidden[row + a, :, lanes] for a in range(3)]
                sums = [
                    taps[b] * rows_near[0] + taps[3 + b] * rows_near[1] + taps[6 + b] * rows_near[2] for b in range(3)
                ]
                values = column_sums(sums[0], sums[1], sums[2], column, cols - 1)
                hidden_two[row * cols : (row + 1) * cols, lanes] = gelu(values).astype(BF16)
                mixed[row, :, chunk_lanes(index, lane, LANES)] = values
        store_mixed(index).start()
        fetch_project(index).wait()
        total[...] += nn_dot(hidden_two[...], project[chunk_lanes(index), :])
        return carry

    lax.fori_loop(0, chunks, step, 0)
    for row in range(1, own + 1):
        first = total[row * cols : (row + 1) * cols]
        normed[row - 1] = (first * rms_scale(first)).astype(BF16)
    store_normed = pltpu.make_async_copy(normed, normed_ref, out_sems.at[1])
    store_first = pltpu.make_async_copy(total, first_ref, out_sems.at[2])
    store_own = pltpu.make_async_copy(total.at[pl.ds(cols, own * cols)], own_first_ref, out_sems.at[3])
    store_normed.start()
    store_first.start()
    store_own.start()
    for index in range(chunks):
        store_expanded(index).wait()
        store_mixed(index).wait()
    store_slab.wait()
    store_normed.wait()
    store_first.wait()
    store_own.wait()


def forward(bands, features, other, rim, w_expand, kernel, w_project):
    capacity, cols, width = features.shape
    own, rows = GRID_ROWS, GRID_ROWS + 2 * RIM
    hidden_width = w_expand.shape[1]
    chunks = hidden_width // CHUNK
    return pl.pallas_call(
        forward_body,
        in_specs=[in_scalars(), in_hbm(), in_vmem(), in_vmem(), in_hbm(), in_vmem(), in_hbm()],
        out_specs=[in_hbm()] * 6,
        out_shape=[
            pltpu.HBM(((rows - 2) * cols, width), F32),
            pltpu.HBM((own * cols, width), F32),
            pltpu.HBM((own, cols, width), BF16),
            pltpu.HBM((own, cols, width), BF16),
            pltpu.HBM((own, cols, hidden_width), F32),
            pltpu.HBM((rows - 2, cols, hidden_width), F32),
        ],
        scratch_shapes=[
            pltpu.VMEM((rows, cols, width), BF16),
            pltpu.VMEM((rows * cols, width), BF16),
            pltpu.VMEM((width, hidden_width), BF16),
            pltpu.VMEM((hidden_width, width), BF16),
            pltpu.VMEM((own, cols, hidden_width), F32),
            pltpu.VMEM((rows, cols, CHUNK), F32),
            pltpu.VMEM((rows - 2, cols, hidden_width), F32),
            pltpu.VMEM(((rows - 2) * cols, CHUNK), BF16),
            pltpu.VMEM(((rows - 2) * cols, width), F32),
            pltpu.VMEM((own, cols, width), BF16),
            pltpu.SemaphoreType.DMA((4,)),
            pltpu.SemaphoreType.DMA((2, chunks)),
            pltpu.SemaphoreType.DMA((2, chunks)),
            pltpu.SemaphoreType.DMA((4,)),
        ],
        compiler_params=params(28),
        cost_estimate=pl.CostEstimate(
            flops=4 * rows * cols * width * hidden_width,
            bytes_accessed=12 * 1024 * 1024,
            transcendentals=2 * rows * cols * hidden_width,
        ),
        name="bottleneck_forward",
    )(bands, held(features), near(other), near(rim), held(w_expand), near(kernel), held(w_project))


def slopes_body(expanded_ref, mixed_ref, slope_one_ref, slope_two_ref):
    for source, target in ((expanded_ref, slope_one_ref), (mixed_ref, slope_two_ref)):
        rows, _, chunk = source.shape
        for row in range(rows):
            for lane in range(0, chunk, LANES):
                lanes = slice(lane, lane + LANES)
                target[row, :, lanes] = gelu_slope(source[row, :, lanes]).astype(BF16)


def slopes(expanded, mixed):
    hidden_width = expanded.shape[2]
    blocks = [
        pl.BlockSpec(values.shape[:2] + (CHUNK,), lambda j: (0, 0, j)) for values in (expanded, mixed)
    ]
    return pl.pallas_call(
        slopes_body,
        grid=(hidden_width // CHUNK,),
        in_specs=blocks,
        out_specs=blocks,
        out_shape=[jax.ShapeDtypeStruct(values.shape, BF16) for values in (expanded, mixed)],
        compiler_params=params(),
        cost_estimate=pl.CostEstimate(
            flops=15 * (expanded.size + mixed.size),
            bytes_accessed=6 * (expanded.size + mixed.size),
            transcendentals=expanded.size + mixed.size,
        ),
        name="gelu_slopes",
    )(expanded, mixed)


def lane_tiles(width):
    return [slice(at, at + LANES) for at in range(0, width, LANES)]


def window_places(own, cols):
    return [(r, q) for r in range(own) for q in range(cols // 8)]


def to_windows(source_ref, rows_wide, target):
    groups, own, cols, width = source_ref.shape
    span = groups * 8
    for tile, lanes in enumerate(lane_tiles(width)):
        for group in range(groups):
            rows_wide[tile, group] = source_ref[group, :, :, lanes].astype(F32)
        for index, (r, q) in enumerate(window_places(own, cols)):
            pieces = [
                rows_wide[tile, group, r, pl.ds(q, 8, stride=cols // 8), :] for group in range(groups)
            ]
            rows = slice(index * span, (index + 1) * span)
            target[rows, lanes] = jnp.concatenate(pieces, axis=0).astype(BF16)


def to_rows(values, rows_wide, target_ref):
    groups, own, cols, width = target_ref.shape
    span = groups * 8
    for tile, lanes in enumerate(lane_tiles(width)):
        for index, (r, q) in enumerate(window_places(own, cols)):
            for group in range(groups):
                first = index * span + group * 8
                rows_wide[tile, group, r, pl.ds(q, 8, stride=cols // 8), :] = values[first : first + 8, lanes]
        for group in range(groups):
            target_ref[group, :, :, lanes] = rows_wide[tile, group].astype(BF16)


def wide_scratch(shape):
    groups, own, cols, width = shape
    return pltpu.VMEM((width // LANES, groups, own, cols, LANES), F32)


def grad_attended_body(cotangent_ref, out_ref, grad_ref, rows_wide, in_windows):
    to_windows(cotangent_ref, rows_wide, in_windows)
    grad_ref[...] = nt_dot(in_windows[...], out_ref[...]).astype(BF16)


def attended_gradient(cotangent, w_out):
    groups, own, cols, width = cotangent.shape
    shape = (groups * own * cols, width)
    return pl.pallas_call(
        grad_attended_body,
        grid=(1,),
        in_specs=[whole(cotangent.shape), whole(w_out.shape)],
        out_specs=whole(shape),
        out_shape=jax.ShapeDtypeStruct(shape, BF16),
        scratch_shapes=[wide_scratch(cotangent.shape), pltpu.VMEM(shape, BF16)],
        compiler_params=params(),
        cost_estimate=pl.CostEstimate(
            flops=2 * shape[0] * width * width, bytes_accessed=2 * 1024 * 1024, transcendentals=0
        ),
        name="attended_gradient",
    )(cotangent, w_out)


def per_query(values, weights, span, head_dim):
    wide = nn_dot(values.T, weights)
    half = LANES // 2
    own = jnp.concatenate([wide[:half, :LANES], wide[half:, LANES:]], axis=0).T
    lane_head = lax.broadcasted_iota(jnp.int32, (span, LANES), 1) // head_dim
    return jnp.where(lane_head % 2 == 0, own[:span], own[span:])


def attention_body(normed_ref, grad_attended_ref, qkv_ref, grad_ref, weights_ref, values_ref, rows_wide,
                   in_windows, projected, grad_projected, grad_attended, qkv, grad, weights, in_sems, out_sems):
    groups, own, cols, width = normed_ref.shape
    span = groups * 8
    windows = own * cols // 8
    head_dim = width // HEADS
    heads = LANES // head_dim
    scale = 1.0 / math.sqrt(head_dim)
    steepness = scale * math.log2(math.e)

    fetch_qkv = pltpu.make_async_copy(qkv_ref, qkv, in_sems.at[0])
    fetch_grad = pltpu.make_async_copy(grad_attended_ref, grad_attended, in_sems.at[1])
    fetch_qkv.start()
    fetch_grad.start()
    to_windows(normed_ref, rows_wide, in_windows)
    fetch_qkv.wait()
    projected[...] = nn_dot(in_windows[...], qkv[...]).astype(BF16)
    store_values = pltpu.make_async_copy(projected.at[:, pl.ds(2 * width, width)], values_ref, out_sems.at[0])
    store_values.start()
    fetch_grad.wait()

    row_head = lax.broadcasted_iota(jnp.int32, (heads * span, LANES), 0) // span
    lane_head = lax.broadcasted_iota(jnp.int32, (heads * span, LANES), 1) // head_dim
    mask = (row_head == lane_head).astype(F32).astype(BF16)

    def spread(values):
        return jnp.concatenate([values] * heads, axis=0) * mask

    def window(index, carry):
        rows = pl.ds(pl.multiple_of(index * span, span), span)
        for part in range(width // LANES):
            q_at, k_at, v_at = (
                slice(t * width + part * LANES, t * width + (part + 1) * LANES) for t in range(3)
            )
            q, k, v = projected[rows, q_at], projected[rows, k_at], projected[rows, v_at]
            q_wide = spread(q)
            g_wide = spread(grad_attended[rows, q_at])
            scores = nt_dot(k, q_wide)
            powers = jnp.exp2((scores - jnp.max(scores, axis=0, keepdims=True)) * steepness)
            shares = powers * (1.0 / jnp.sum(powers, axis=0, keepdims=True))
            half = shares.astype(BF16)
            weights[index, :, part * heads * span : (part + 1) * heads * span] = half
            grad_weights = nt_dot(v, g_wide)
            row_dot = jnp.sum(shares * grad_weights, axis=0, keepdims=True)
            grad_scores = (shares * (grad_weights - row_dot)).astype(BF16)
            grad_projected[rows, q_at] = (per_query(k, grad_scores, span, head_dim) * scale).astype(BF16)
            grad_projected[rows, k_at] = (nn_dot(grad_scores, q_wide) * scale).astype(BF16)
            grad_projected[rows, v_at] = nn_dot(half, g_wide).astype(BF16)
        return carry

    lax.fori_loop(0, windows, window, 0, unroll=4)
    store_weights = pltpu.make_async_copy(weights, weights_ref, out_sems.at[1])
    store_weights.start()
    to_rows(nt_dot(grad_projected[...], qkv[...]), rows_wide, grad)
    store_grad = pltpu.make_async_copy(grad, grad_ref, out_sems.at[2])
    store_grad.start()
    store_values.wait()
    store_weights.wait()
    store_grad.wait()


def attention(normed, grad_attended, w_qkv):
    groups, own, cols, width = normed.shape
    span = groups * 8
    tokens = groups * own * cols
    out_shapes = [normed.shape, (tokens // span, span, HEADS * span), (tokens, width)]
    return pl.pallas_call(
        attention_body,
        in_specs=[in_vmem(), in_hbm(), in_hbm()],
        out_specs=[in_hbm()] * 3,
        out_shape=[pltpu.HBM(shape, BF16) for shape in out_shapes],
        scratch_shapes=[
            wide_scratch(normed.shape),
            pltpu.VMEM((tokens, width), BF16),
            pltpu.VMEM((tokens, 3 * width), BF16),
            pltpu.VMEM((tokens, 3 * width), BF16),
            pltpu.VMEM((tokens, width), BF16),
            pltpu.VMEM(w_qkv.shape, BF16),
            pltpu.VMEM(normed.shape, BF16),
            pltpu.VMEM(out_shapes[1], BF16),
            pltpu.SemaphoreType.DMA((2,)),
            pltpu.SemaphoreType.DMA((3,)),
        ],
        compiler_params=params(18),
        cost_estimate=pl.CostEstimate(
            flops=16 * tokens * width * width,
            bytes_accessed=4 * 1024 * 1024,
            transcendentals=tokens * span * HEADS,
        ),
        name="window_attention",
    )(near(normed), held(grad_attended), held(w_qkv))


def attended_body(weights_ref, values_ref, out_ref, added_ref, rows_wide, attended):
    windows, span, wide = weights_ref.shape
    width = values_ref.shape[1]
    heads = LANES * HEADS // width
    for index in range(windows):
        rows = slice(index * span, (index + 1) * span)
        for part, lanes in enumerate(lane_tiles(width)):
            weights = weights_ref[index, :, part * heads * span : (part + 1) * heads * span]
            attended[rows, lanes] = per_query(values_ref[rows, lanes], weights, span, width // HEADS).astype(BF16)
    to_rows(nn_dot(attended[...], out_ref[...]), rows_wide, added_ref)


def attend(weights, values, w_out, shape):
    return pl.pallas_call(
        attended_body,
        grid=(1,),
        in_specs=[whole(weights.shape), whole(values.shape), whole(w_out.shape)],
        out_specs=whole(shape),
        out_shape=jax.ShapeDtypeStruct(shape, BF16),
        scratch_shapes=[wide_scratch(shape), pltpu.VMEM(values.shape, BF16)],
        compiler_params=params(),
        cost_estimate=pl.CostEstimate(
            flops=4 * values.size * values.shape[1], bytes_accessed=3 * 1024 * 1024, transcendentals=0
        ),
        name="attended_output",
    )(weights, values, w_out)


def backward_body(bands_ref, cotangent_ref, other_ref, rim_ref, slab_ref, first_ref, grad_slab_ref, grad_ref,
                  pair_ref, next_ref, slope_one_ref, slope_two_ref, expand_ref, taps_ref, project_ref,
                  out_ref, rims, slab, first, grad_slab, grad_in, slope_one, slope_two, expand, project,
                  grad_first, grad_rows, mixed, expanded, total, row_sems,
                  in_sems, chunk_sems):
    own, cols, width = slab.shape
    chunks = expand_ref.shape[1] // CHUNK

    sources = (cotangent_ref, other_ref, rim_ref)
    sides = list(enumerate((-1, own)))
    for side, place_first in sides:
        start_pull(bands_ref, place_first, sources, 1, rims.at[pl.ds(side, 1)], row_sems.at[side], RIM)
    inputs = [
        pltpu.make_async_copy(source, target, in_sems.at[index])
        for index, (source, target) in enumerate(
            ((first_ref, first), (grad_ref, grad_in), (grad_slab_ref, grad_slab), (slab_ref, slab))
        )
    ]
    for copy in inputs:
        copy.start()

    def fetches(index):
        lanes = chunk_lanes(index)
        pairs = (
            (project_ref.at[lanes], project.at[lanes]),
            (slope_two_ref.at[:, :, lanes], slope_two.at[:, :, lanes]),
            (slope_one_ref.at[:, :, lanes], slope_one.at[:, :, lanes]),
            (expand_ref.at[:, lanes], expand.at[:, lanes]),
        )
        return [
            pltpu.make_async_copy(source, target, chunk_sems.at[number, index])
            for number, (source, target) in enumerate(pairs)
        ]

    for copy in fetches(0):
        copy.start()

    def through_norm(cotangent, grad, first):
        rms = rms_scale(first)
        normed = first * rms
        grad = grad.astype(F32)
        inner = jnp.mean(grad * normed, -1, keepdims=True)
        return cotangent.astype(F32) + rms * (grad - normed * inner)

    for copy in inputs[:3]:
        copy.wait()
    for row in range(own):
        below = first[(row + 1) * cols : (row + 2) * cols]
        result = through_norm(grad_slab[row], grad_in[row], below)
        grad_first[row * cols : (row + 1) * cols] = result
        grad_rows[(row + 1) * cols : (row + 2) * cols] = result.astype(BF16)
    for side, place_first in sides:
        wait_pull(sources, 1, rims.at[pl.ds(side, 1)], row_sems.at[side])
    leads = lax.rem(lax.axis_index("row"), 2) == 0
    above = jnp.where(leads, next_ref[0].astype(F32), pair_ref[0].astype(F32))
    below = jnp.where(leads, pair_ref[0].astype(F32), next_ref[0].astype(F32))
    last = (own + 1) * cols
    grad_rows[0:cols] = through_norm(rims[0], above, first[0:cols]).astype(BF16)
    grad_rows[last:] = through_norm(rims[1], below, first[last:]).astype(BF16)
    column = lax.broadcasted_iota(jnp.int32, (cols, LANES), 0)

    total[...] = jnp.zeros_like(total)

    def step(index, carry):
        @pl.when(index + 1 < chunks)
        def _():
            for copy in fetches(index + 1):
                copy.start()

        for copy in fetches(index):
            copy.wait()
        for start in range(0, CHUNK, HALF):
            weights = project[chunk_lanes(index, start, HALF), :]
            for row in range(0, own + 2, GROUP_BACKWARD):
                product = nt_dot(grad_rows[row * cols : (row + GROUP_BACKWARD) * cols, :], weights)
                for inner in range(GROUP_BACKWARD):
                    for lane in range(0, HALF, LANES):
                        slope = slope_two[row + inner, :, chunk_lanes(index, start + lane, LANES)].astype(F32)
                        value = product[inner * cols : (inner + 1) * cols, lane : lane + LANES] * slope
                        at = slice(start + lane, start + lane + LANES)
                        mixed[row + inner, :, at] = value.astype(BF16).astype(F32)

        for lane in range(0, CHUNK, LANES):
            lanes = slice(lane, lane + LANES)
            taps = spread_taps(taps_ref, chunk_lanes(index, lane, LANES), cols)
            for row in range(own):
                rows_near = [mixed[row + a, :, lanes] for a in range(3)]
                sums = [
                    taps[8 - b] * rows_near[0] + taps[5 - b] * rows_near[1] + taps[2 - b] * rows_near[2]
                    for b in range(3)
                ]
                value = column_sums(sums[0], sums[1], sums[2], column, cols - 1)
                value = value * slope_one[row, :, chunk_lanes(index, lane, LANES)].astype(F32)
                expanded[row * cols : (row + 1) * cols, lanes] = value.astype(BF16)
        total[...] += nt_dot(expanded[...], expand[:, chunk_lanes(index)])
        return carry

    lax.fori_loop(0, chunks, step, 0)
    inputs[3].wait()
    for row in range(own):
        at = slice(row * cols, (row + 1) * cols)
        values = slab[row].astype(F32)
        rms = rms_scale(values)
        normed = values * rms
        grad = total[at]
        inner = jnp.mean(grad * normed, -1, keepdims=True)
        out_ref[row] = (grad_first[at] + rms * (grad - normed * inner)).astype(BF16)


def backward(bands, cotangent, other, rim, slab, first, grad_slab, grad, pair_row, next_row, slope_one,
             slope_two, w_expand, kernel, w_project):
    own, cols, width = slab.shape
    hidden_width = w_expand.shape[1]
    chunks = hidden_width // CHUNK
    return pl.pallas_call(
        backward_body,
        in_specs=[in_scalars()] + [in_hbm()] * 7 + [in_vmem()] * 2 + [in_hbm()] * 3 + [in_vmem(), in_hbm()],
        out_specs=in_vmem(),
        out_shape=jax.ShapeDtypeStruct((own, cols, width), BF16),
        scratch_shapes=[
            pltpu.VMEM((2, cols, width), BF16),
            pltpu.VMEM((own, cols, width), BF16),
            pltpu.VMEM(((own + 2) * cols, width), F32),
            pltpu.VMEM((own, cols, width), BF16),
            pltpu.VMEM((own, cols, width), BF16),
            pltpu.VMEM((own, cols, hidden_width), BF16),
            pltpu.VMEM((own + 2, cols, hidden_width), BF16),
            pltpu.VMEM((width, hidden_width), BF16),
            pltpu.VMEM((hidden_width, width), BF16),
            pltpu.VMEM((own * cols, width), F32),
            pltpu.VMEM(((own + 2) * cols, width), BF16),
            pltpu.VMEM((own + 2, cols, CHUNK), F32),
            pltpu.VMEM((own * cols, CHUNK), BF16),
            pltpu.VMEM((own * cols, width), F32),
            pltpu.SemaphoreType.DMA((2,)),
            pltpu.SemaphoreType.DMA((4,)),
            pltpu.SemaphoreType.DMA((4, chunks)),
        ],
        compiler_params=params(26),
        cost_estimate=pl.CostEstimate(
            flops=4 * (own + 2) * cols * width * hidden_width,
            bytes_accessed=12 * 1024 * 1024,
            transcendentals=0,
        ),
        name="bottleneck_backward",
    )(bands, held(cotangent), held(other), held(rim), held(slab), held(first), held(grad_slab), held(grad),
      near(pair_row), near(next_row), held(slope_one), held(slope_two), held(w_expand), near(kernel),
      held(w_project))


def window_groups(size):
    stride = size // 8
    return [[first + stride * k for k in range(8)] for first in range(stride)]


def exchange_windows(rows):
    groups = window_groups(lax.axis_size("row"))
    return lax.all_to_all(
        rows, "row", split_axis=0, concat_axis=0, tiled=True, axis_index_groups=groups
    )


def swap_pair(rows):
    size = lax.axis_size("row")
    return lax.ppermute(rows, "row", [(i, i ^ 1) for i in range(size)])


def swap_next(rows):
    size = lax.axis_size("row")
    pairs = [(i, i + 1) for i in range(1, size - 1, 2)]
    return lax.ppermute(rows, "row", pairs + [(j, i) for i, j in pairs])


def place_rows(even, other, leads, leader_share):
    size = GRID_ROWS
    first, second = even[:BAND], even[BAND:]
    share = jnp.where(leads, leader_share, 2 * size - leader_share)
    zeros = jnp.zeros_like(first)
    low = jnp.where(leads | (share == size), first, jnp.where(share < size, second, other))
    mid = jnp.where(share < size, zeros, jnp.where(leads | (share == size), second, first))
    high = jnp.where(share > size, jnp.where(leads, other, second), zeros)
    return jnp.concatenate([low, mid, high], 0)


def on_device(features, row_bands, w_expand, kernel, w_project, w_qkv, w_out, cotangent):
    capacity, cols, width = features.shape
    device = lax.axis_index("row")
    parity = device % 2
    leads = parity == 0

    rim = swap_next(rim_rows(row_bands, features, cotangent))
    other_cotangent = swap_pair(cotangent)
    other_features = swap_pair(features)
    grad_slab = even_rows(row_bands, cotangent, other_cotangent)
    rim, grad_slab = lax.optimization_barrier((rim, grad_slab))

    grad_windows = exchange_windows(grad_slab)
    first, own_first, normed, slab, expanded, mixed = forward(
        row_bands, features, other_features, rim, w_expand, kernel, w_project
    )
    normed, grad_windows = lax.optimization_barrier((normed, grad_windows))
    normed_windows = exchange_windows(normed)
    shape = (8, GRID_ROWS // 8, cols, width)
    slope_one, slope_two = slopes(expanded, mixed)
    grad_attended = attended_gradient(grad_windows.reshape(shape), w_out)
    normed_windows, slope_one, slope_two, grad_attended = lax.optimization_barrier(
        (normed_windows, slope_one, slope_two, grad_attended)
    )
    grad_normed, weights, values = attention(normed_windows.reshape(shape), grad_attended, w_qkv)
    grad_rows = exchange_windows(grad_normed.reshape(GRID_ROWS, cols, width))
    added = attend(weights, values, w_out, shape)
    grad_rows, added = lax.optimization_barrier((grad_rows, added))
    top, bottom = grad_rows[:1], grad_rows[GRID_ROWS - 1 :]
    pair_row = swap_pair(jnp.where(leads, bottom, top))
    next_row = swap_next(jnp.where(leads, top, bottom))
    added, pair_row, next_row = lax.optimization_barrier((added, pair_row, next_row))
    added_rows = exchange_windows(added.reshape(GRID_ROWS, cols, width))
    grad_input = backward(
        row_bands, cotangent, other_cotangent, rim, slab, first, grad_slab, grad_rows, pair_row, next_row,
        slope_one, slope_two, w_expand, kernel, w_project,
    )
    def sent(rows):
        return jnp.where(leads, rows[BAND:], rows[:BAND])

    other_grad = swap_pair(sent(grad_input))
    grad_input, added_rows = lax.optimization_barrier((grad_input, added_rows))
    final = (own_first.reshape(GRID_ROWS, cols, width) + added_rows.astype(F32)).astype(BF16)
    other_final = swap_pair(sent(final))
    leader_share = BAND * row_bands[device - parity]
    return (
        place_rows(final, other_final, leads, leader_share),
        place_rows(grad_input, other_grad, leads, leader_share),
    )


def solution(mesh):
    return jax.shard_map(
        on_device,
        mesh=mesh,
        in_specs=(
            P(("parts", "row"), None, None),
            P("parts"),
            P(),
            P(),
            P(),
            P(),
            P(),
            P(("parts", "row"), None, None),
        ),
        out_specs=(P(("parts", "row"), None, None), P(("parts", "row"), None, None)),
        check_vma=False,
    )
```

```python
import math

import jax
import jax.numpy as jnp
from jax import lax
from jax.experimental import pallas as pl
from jax.experimental.pallas import tpu as pltpu
from jax.sharding import PartitionSpec as P

HEADS = 16
GRID_ROWS = 16
BAND = 8
RIM = 2
EPSILON = 1e-06
CHUNK = 512
HALF = 256
GROUP_FORWARD = 10
GROUP_BACKWARD = 9
LANES = 128
ROOT = math.sqrt(2.0 / math.pi)
CUBIC = 0.044715
F32 = jnp.float32
BF16 = jnp.bfloat16
MIB = 1024 * 1024


def nt_dot(left, right):
    return lax.dot_general(left, right, (((1,), (1,)), ((), ())), preferred_element_type=F32)


def tn_dot(left, right):
    return lax.dot_general(left, right, (((0,), (0,)), ((), ())), preferred_element_type=F32)


def nn_dot(left, right):
    return jnp.dot(left, right, preferred_element_type=F32)


def rms_scale(values):
    return lax.rsqrt(jnp.mean(values * values, -1, keepdims=True) + EPSILON)


def gelu_parts(v):
    square = v * v
    cdf = 0.5 + 0.5 * jnp.tanh(v * (ROOT + (ROOT * CUBIC) * square))
    return square, cdf, v * cdf


def gelu(v):
    return gelu_parts(v)[2]


def gelu_slope(v):
    square, cdf, value = gelu_parts(v)
    return cdf + (value - value * cdf) * (2.0 * ROOT + (6.0 * ROOT * CUBIC) * square)


def whole(shape, space=None):
    zeros = (0,) * len(shape)
    return pl.BlockSpec(shape, lambda *_: zeros)


def params(mebibytes=56):
    return pltpu.CompilerParams(vmem_limit_bytes=mebibytes * MIB)


def in_vmem():
    return pl.BlockSpec(memory_space=pltpu.VMEM)


def in_hbm():
    return pl.BlockSpec(memory_space=pltpu.HBM)


def held(array):
    return pltpu.with_memory_space_constraint(array, pltpu.HBM)


def near(array):
    return pltpu.with_memory_space_constraint(array, pltpu.VMEM)


def in_scalars():
    return pl.BlockSpec(memory_space=pltpu.SMEM)


def shares(bands_ref):
    device = lax.axis_index("row")
    parity = lax.rem(device, 2)
    return parity, BAND * bands_ref[device - parity], BAND * bands_ref[device]


def place(bands_ref, first):
    parity, leader_share, _ = shares(bands_ref)
    row = first + GRID_ROWS * parity
    beyond = (row < 0) | (row >= 2 * GRID_ROWS)
    in_leader = row < leader_share
    in_own = in_leader == (parity == 0)
    source = jnp.where(beyond, 2, jnp.where(in_own, 0, 1))
    return source, jnp.where(beyond, 0, jnp.where(in_leader, row, row - leader_share))


def start_pull(bands_ref, first, sources, rows, target, sem, rim_row=0):
    where, row = place(bands_ref, first)
    row = jnp.where(where == 2, rim_row, row)
    for number, source in enumerate(sources):

        @pl.when(where == number)
        def _():
            pltpu.make_async_copy(source.at[pl.ds(row, rows)], target, sem).start()


def wait_pull(sources, rows, target, sem):
    pltpu.make_async_copy(sources[0].at[pl.ds(0, rows)], target, sem).wait()


def even_body(bands_ref, own_ref, other_ref, out_ref):
    for half in range(2):
        where, row = place(bands_ref, BAND * half)
        for number, source in enumerate((own_ref, other_ref)):

            @pl.when(where == number)
            def _():
                out_ref[BAND * half : BAND * half + BAND] = source[pl.ds(row, BAND)]


def even_rows(bands, own, other):
    shape = (GRID_ROWS,) + own.shape[1:]
    return pl.pallas_call(
        even_body,
        in_specs=[in_scalars(), in_vmem(), in_vmem()],
        out_specs=in_vmem(),
        out_shape=jax.ShapeDtypeStruct(shape, own.dtype),
        compiler_params=params(8),
        name="even_rows",
    )(bands, near(own), near(other))


def rim_body(bands_ref, features_ref, cotangent_ref, out_ref, sems):
    parity, _, share = shares(bands_ref)
    leads = parity == 0
    copies = [
        pltpu.make_async_copy(
            features_ref.at[pl.ds(jnp.where(leads, 0, share - RIM), RIM)], out_ref.at[pl.ds(0, RIM)], sems.at[0]
        ),
        pltpu.make_async_copy(
            cotangent_ref.at[pl.ds(jnp.where(leads, 0, share - 1), 1)], out_ref.at[pl.ds(RIM, 1)], sems.at[1]
        ),
    ]
    for copy in copies:
        copy.start()
    for copy in copies:
        copy.wait()


def rim_rows(bands, features, cotangent):
    shape = (RIM + 1,) + features.shape[1:]
    return pl.pallas_call(
        rim_body,
        in_specs=[in_scalars(), in_hbm(), in_hbm()],
        out_specs=in_vmem(),
        out_shape=jax.ShapeDtypeStruct(shape, features.dtype),
        scratch_shapes=[pltpu.SemaphoreType.DMA((2,))],
        compiler_params=params(8),
        name="rim_rows",
    )(bands, held(features), held(cotangent))


def column_sums(left, mid, right, column, last):
    from_left = jnp.where(column == 0, 0.0, pltpu.roll(left, 1, 0))
    from_right = jnp.where(column == last, 0.0, pltpu.roll(right, last, 0))
    return mid + from_left + from_right


def spread_taps(taps_ref, lanes, cols):
    taps = taps_ref[:, lanes].astype(F32)
    return [jnp.broadcast_to(taps[i : i + 1], (cols, LANES)) for i in range(9)]


def chunk_lanes(index, lane=0, count=CHUNK):
    return pl.ds(pl.multiple_of(index * CHUNK + lane, LANES), count)


def forward_body(bands_ref, features_ref, other_ref, rim_ref, expand_ref, taps_ref, project_ref, first_ref,
                 own_first_ref, normed_ref, slab_ref, expanded_ref, mixed_ref, slab, normed_one, expand, project,
                 expanded, hidden, mixed, hidden_two, total, normed, row_sems,
                 weight_sems, chunk_sems, out_sems):
    rows, cols, width = slab.shape
    own = rows - 2 * RIM
    chunks = expand_ref.shape[1] // CHUNK

    sources = (features_ref, other_ref, rim_ref)
    pieces = [(0, RIM), (RIM, BAND), (RIM + BAND, BAND), (RIM + 2 * BAND, RIM)]
    for index, (first, count) in enumerate(pieces):
        start_pull(bands_ref, first - RIM, sources, count, slab.at[pl.ds(first, count)], row_sems.at[index])

    def fetch_expand(index):
        lanes = chunk_lanes(index)
        return pltpu.make_async_copy(expand_ref.at[:, lanes], expand.at[:, lanes], weight_sems.at[0, index])

    def fetch_project(index):
        lanes = chunk_lanes(index)
        return pltpu.make_async_copy(project_ref.at[lanes], project.at[lanes], weight_sems.at[1, index])

    def store_expanded(index):
        lanes = chunk_lanes(index)
        return pltpu.make_async_copy(
            expanded.at[:, :, lanes], expanded_ref.at[:, :, lanes], chunk_sems.at[0, index]
        )

    def store_mixed(index):
        lanes = chunk_lanes(index)
        return pltpu.make_async_copy(mixed.at[:, :, lanes], mixed_ref.at[:, :, lanes], chunk_sems.at[1, index])

    fetch_expand(0).start()
    fetch_project(0).start()
    for index, (first, count) in enumerate(pieces):
        wait_pull(sources, count, slab.at[pl.ds(first, count)], row_sems.at[index])
    store_slab = pltpu.make_async_copy(slab.at[pl.ds(RIM, own)], slab_ref, out_sems.at[0])
    store_slab.start()
    for row in range(0, rows, 2):
        at = slice(row * cols, (row + 2) * cols)
        values = slab[row : row + 2].astype(F32).reshape(2 * cols, width)
        normed_one[at] = (values * rms_scale(values)).astype(BF16)
    total[...] = slab[1 : rows - 1].astype(F32).reshape((rows - 2) * cols, width)
    column = lax.broadcasted_iota(jnp.int32, (cols, LANES), 0)

    def step(index, carry):
        @pl.when(index + 1 < chunks)
        def _():
            fetch_expand(index + 1).start()
            fetch_project(index + 1).start()

        fetch_expand(index).wait()
        for start in range(0, CHUNK, HALF):
            weights = expand[:, chunk_lanes(index, start, HALF)]
            for row in range(0, rows, GROUP_FORWARD):
                product = nn_dot(normed_one[row * cols : (row + GROUP_FORWARD) * cols, :], weights)
                for inner in range(GROUP_FORWARD):
                    for lane in range(0, HALF, LANES):
                        values = product[inner * cols : (inner + 1) * cols, lane : lane + LANES]
                        at = slice(start + lane, start + lane + LANES)
                        hidden[row + inner, :, at] = gelu(values).astype(BF16).astype(F32)
                        if RIM <= row + inner < RIM + own:
                            expanded[row + inner - RIM, :, chunk_lanes(index, start + lane, LANES)] = values.astype(BF16)
        store_expanded(index).start()

        for lane in range(0, CHUNK, LANES):
            lanes = slice(lane, lane + LANES)
            taps = spread_taps(taps_ref, chunk_lanes(index, lane, LANES), cols)
            for row in range(rows - 2):
                rows_near = [hidden[row + a, :, lanes] for a in range(3)]
                sums = [
                    taps[b] * rows_near[0] + taps[3 + b] * rows_near[1] + taps[6 + b] * rows_near[2] for b in range(3)
                ]
                values = column_sums(sums[0], sums[1], sums[2], column, cols - 1)
                hidden_two[row * cols : (row + 1) * cols, lanes] = gelu(values).astype(BF16)
                mixed[row, :, chunk_lanes(index, lane, LANES)] = values.astype(BF16)
        store_mixed(index).start()
        fetch_project(index).wait()
        total[...] += nn_dot(hidden_two[...], project[chunk_lanes(index), :])
        return carry

    lax.fori_loop(0, chunks, step, 0)
    for row in range(1, own + 1):
        first = total[row * cols : (row + 1) * cols]
        normed[row - 1] = (first * rms_scale(first)).astype(BF16)
    store_normed = pltpu.make_async_copy(normed, normed_ref, out_sems.at[1])
    store_above = pltpu.make_async_copy(total.at[pl.ds(0, cols)], first_ref.at[pl.ds(0, cols)], out_sems.at[2])
    store_below = pltpu.make_async_copy(
        total.at[pl.ds((own + 1) * cols, cols)], first_ref.at[pl.ds(cols, cols)], out_sems.at[3]
    )
    store_own = pltpu.make_async_copy(total.at[pl.ds(cols, own * cols)], own_first_ref, out_sems.at[4])
    store_normed.start()
    store_above.start()
    store_below.start()
    store_own.start()
    for index in range(chunks):
        store_expanded(index).wait()
        store_mixed(index).wait()
    store_slab.wait()
    store_normed.wait()
    store_above.wait()
    store_below.wait()
    store_own.wait()


def forward(bands, features, other, rim, w_expand, kernel, w_project):
    capacity, cols, width = features.shape
    own, rows = GRID_ROWS, GRID_ROWS + 2 * RIM
    hidden_width = w_expand.shape[1]
    chunks = hidden_width // CHUNK
    return pl.pallas_call(
        forward_body,
        in_specs=[in_scalars(), in_hbm(), in_vmem(), in_vmem(), in_hbm(), in_vmem(), in_hbm()],
        out_specs=[in_hbm()] * 6,
        out_shape=[
            pltpu.HBM((2 * cols, width), F32),
            pltpu.HBM((own * cols, width), F32),
            pltpu.HBM((own, cols, width), BF16),
            pltpu.HBM((own, cols, width), BF16),
            pltpu.HBM((own, cols, hidden_width), BF16),
            pltpu.HBM((rows - 2, cols, hidden_width), BF16),
        ],
        scratch_shapes=[
            pltpu.VMEM((rows, cols, width), BF16),
            pltpu.VMEM((rows * cols, width), BF16),
            pltpu.VMEM((width, hidden_width), BF16),
            pltpu.VMEM((hidden_width, width), BF16),
            pltpu.VMEM((own, cols, hidden_width), BF16),
            pltpu.VMEM((rows, cols, CHUNK), F32),
            pltpu.VMEM((rows - 2, cols, hidden_width), BF16),
            pltpu.VMEM(((rows - 2) * cols, CHUNK), BF16),
            pltpu.VMEM(((rows - 2) * cols, width), F32),
            pltpu.VMEM((own, cols, width), BF16),
            pltpu.SemaphoreType.DMA((4,)),
            pltpu.SemaphoreType.DMA((2, chunks)),
            pltpu.SemaphoreType.DMA((2, chunks)),
            pltpu.SemaphoreType.DMA((5,)),
        ],
        compiler_params=params(24),
        cost_estimate=pl.CostEstimate(
            flops=4 * rows * cols * width * hidden_width,
            bytes_accessed=12 * 1024 * 1024,
            transcendentals=2 * rows * cols * hidden_width,
        ),
        name="bottleneck_forward",
    )(bands, held(features), near(other), near(rim), held(w_expand), near(kernel), held(w_project))


def slopes_body(expanded_ref, mixed_ref, slope_one_ref, slope_two_ref):
    for source, target in ((expanded_ref, slope_one_ref), (mixed_ref, slope_two_ref)):
        rows, _, chunk = source.shape
        for row in range(rows):
            for lane in range(0, chunk, LANES):
                lanes = slice(lane, lane + LANES)
                target[row, :, lanes] = gelu_slope(source[row, :, lanes].astype(F32)).astype(BF16)


def slopes(expanded, mixed):
    hidden_width = expanded.shape[2]
    blocks = [
        pl.BlockSpec(values.shape[:2] + (CHUNK,), lambda j: (0, 0, j)) for values in (expanded, mixed)
    ]
    return pl.pallas_call(
        slopes_body,
        grid=(hidden_width // CHUNK,),
        in_specs=blocks,
        out_specs=blocks,
        out_shape=[jax.ShapeDtypeStruct(values.shape, BF16) for values in (expanded, mixed)],
        compiler_params=params(),
        cost_estimate=pl.CostEstimate(
            flops=15 * (expanded.size + mixed.size),
            bytes_accessed=6 * (expanded.size + mixed.size),
            transcendentals=expanded.size + mixed.size,
        ),
        name="gelu_slopes",
    )(expanded, mixed)


def lane_tiles(width):
    return [slice(at, at + LANES) for at in range(0, width, LANES)]


def window_places(own, cols):
    return [(r, q) for r in range(own) for q in range(cols // 8)]


def to_windows(source_ref, rows_wide, target):
    groups, own, cols, width = source_ref.shape
    span = groups * 8
    for tile, lanes in enumerate(lane_tiles(width)):
        for group in range(groups):
            rows_wide[tile, group] = source_ref[group, :, :, lanes].astype(F32)
        for index, (r, q) in enumerate(window_places(own, cols)):
            pieces = [
                rows_wide[tile, group, r, pl.ds(q, 8, stride=cols // 8), :] for group in range(groups)
            ]
            rows = slice(index * span, (index + 1) * span)
            target[rows, lanes] = jnp.concatenate(pieces, axis=0).astype(BF16)


def to_rows(values, rows_wide, target_ref):
    groups, own, cols, width = target_ref.shape
    span = groups * 8
    for tile, lanes in enumerate(lane_tiles(width)):
        for index, (r, q) in enumerate(window_places(own, cols)):
            for group in range(groups):
                first = index * span + group * 8
                rows_wide[tile, group, r, pl.ds(q, 8, stride=cols // 8), :] = values[first : first + 8, lanes]
        for group in range(groups):
            target_ref[group, :, :, lanes] = rows_wide[tile, group].astype(BF16)


def wide_scratch(shape):
    groups, own, cols, width = shape
    return pltpu.VMEM((width // LANES, groups, own, cols, LANES), F32)


def grad_attended_body(cotangent_ref, out_ref, grad_ref, rows_wide, in_windows):
    to_windows(cotangent_ref, rows_wide, in_windows)
    grad_ref[...] = nt_dot(in_windows[...], out_ref[...]).astype(BF16)


def attended_gradient(cotangent, w_out):
    groups, own, cols, width = cotangent.shape
    shape = (groups * own * cols, width)
    return pl.pallas_call(
        grad_attended_body,
        grid=(1,),
        in_specs=[whole(cotangent.shape), whole(w_out.shape)],
        out_specs=whole(shape),
        out_shape=jax.ShapeDtypeStruct(shape, BF16),
        scratch_shapes=[wide_scratch(cotangent.shape), pltpu.VMEM(shape, BF16)],
        compiler_params=params(),
        cost_estimate=pl.CostEstimate(
            flops=2 * shape[0] * width * width, bytes_accessed=2 * 1024 * 1024, transcendentals=0
        ),
        name="attended_gradient",
    )(cotangent, w_out)


def per_query(values, weights, span, head_dim, scale=1.0):
    wide = nn_dot(values.T, weights)
    half = LANES // 2
    own = jnp.concatenate([wide[:half, :LANES], wide[half:, LANES:]], axis=0) * scale
    own = own.astype(BF16).T
    lane_head = lax.broadcasted_iota(jnp.int32, (span, LANES), 1) // head_dim
    return jnp.where(lane_head % 2 == 0, own[:span].astype(F32), own[span:].astype(F32)).astype(BF16)


def attention_body(normed_ref, grad_attended_ref, qkv_ref, grad_ref, weights_ref, values_ref, rows_wide,
                   in_windows, projected, grad_projected, grad_attended, qkv, grad, weights, in_sems, out_sems):
    groups, own, cols, width = normed_ref.shape
    span = groups * 8
    windows = own * cols // 8
    head_dim = width // HEADS
    heads = LANES // head_dim
    scale = 1.0 / math.sqrt(head_dim)
    steepness = scale * math.log2(math.e)

    fetch_qkv = pltpu.make_async_copy(qkv_ref, qkv, in_sems.at[0])
    fetch_grad = pltpu.make_async_copy(grad_attended_ref, grad_attended, in_sems.at[1])
    fetch_qkv.start()
    fetch_grad.start()
    to_windows(normed_ref, rows_wide, in_windows)
    fetch_qkv.wait()
    projected[...] = nn_dot(in_windows[...], qkv[...]).astype(BF16)
    store_values = pltpu.make_async_copy(projected.at[:, pl.ds(2 * width, width)], values_ref, out_sems.at[0])
    store_values.start()
    fetch_grad.wait()

    row_head = lax.broadcasted_iota(jnp.int32, (heads * span, LANES), 0) // span
    lane_head = lax.broadcasted_iota(jnp.int32, (heads * span, LANES), 1) // head_dim
    mask = (row_head == lane_head).astype(F32).astype(BF16)

    def spread(values):
        return jnp.concatenate([values] * heads, axis=0) * mask

    def window(index, carry):
        rows = pl.ds(pl.multiple_of(index * span, span), span)
        for part in range(width // LANES):
            q_at, k_at, v_at = (
                slice(t * width + part * LANES, t * width + (part + 1) * LANES) for t in range(3)
            )
            q, k, v = projected[rows, q_at], projected[rows, k_at], projected[rows, v_at]
            q_wide = spread(q)
            g_wide = spread(grad_attended[rows, q_at])
            scores = nt_dot(k, q_wide)
            powers = jnp.exp2((scores - jnp.max(scores, axis=0, keepdims=True)) * steepness)
            shares = powers * (1.0 / jnp.sum(powers, axis=0, keepdims=True))
            half = shares.astype(BF16)
            weights[index, :, part * heads * span : (part + 1) * heads * span] = half
            grad_weights = nt_dot(v, g_wide)
            row_dot = jnp.sum(shares * grad_weights, axis=0, keepdims=True)
            grad_scores = (shares * (grad_weights - row_dot)).astype(BF16)
            grad_projected[rows, q_at] = per_query(k, grad_scores, span, head_dim, scale)
            grad_projected[rows, k_at] = (nn_dot(grad_scores, q_wide) * scale).astype(BF16)
            grad_projected[rows, v_at] = nn_dot(half, g_wide).astype(BF16)
        return carry

    lax.fori_loop(0, windows, window, 0, unroll=4)
    store_weights = pltpu.make_async_copy(weights, weights_ref, out_sems.at[1])
    store_weights.start()
    to_rows(nt_dot(grad_projected[...], qkv[...]), rows_wide, grad)
    store_grad = pltpu.make_async_copy(grad, grad_ref, out_sems.at[2])
    store_grad.start()
    store_values.wait()
    store_weights.wait()
    store_grad.wait()


def attention(normed, grad_attended, w_qkv):
    groups, own, cols, width = normed.shape
    span = groups * 8
    tokens = groups * own * cols
    out_shapes = [normed.shape, (tokens // span, span, HEADS * span), (tokens, width)]
    return pl.pallas_call(
        attention_body,
        in_specs=[in_vmem(), in_hbm(), in_hbm()],
        out_specs=[in_hbm()] * 3,
        out_shape=[pltpu.HBM(shape, BF16) for shape in out_shapes],
        scratch_shapes=[
            wide_scratch(normed.shape),
            pltpu.VMEM((tokens, width), BF16),
            pltpu.VMEM((tokens, 3 * width), BF16),
            pltpu.VMEM((tokens, 3 * width), BF16),
            pltpu.VMEM((tokens, width), BF16),
            pltpu.VMEM(w_qkv.shape, BF16),
            pltpu.VMEM(normed.shape, BF16),
            pltpu.VMEM(out_shapes[1], BF16),
            pltpu.SemaphoreType.DMA((2,)),
            pltpu.SemaphoreType.DMA((3,)),
        ],
        compiler_params=params(18),
        cost_estimate=pl.CostEstimate(
            flops=16 * tokens * width * width,
            bytes_accessed=4 * 1024 * 1024,
            transcendentals=tokens * span * HEADS,
        ),
        name="window_attention",
    )(near(normed), held(grad_attended), held(w_qkv))


def attended_body(weights_ref, values_ref, out_ref, added_ref, rows_wide, attended):
    windows, span, wide = weights_ref.shape
    width = values_ref.shape[1]
    heads = LANES * HEADS // width
    for index in range(windows):
        rows = slice(index * span, (index + 1) * span)
        for part, lanes in enumerate(lane_tiles(width)):
            weights = weights_ref[index, :, part * heads * span : (part + 1) * heads * span]
            attended[rows, lanes] = per_query(values_ref[rows, lanes], weights, span, width // HEADS)
    to_rows(nn_dot(attended[...], out_ref[...]), rows_wide, added_ref)


def attend(weights, values, w_out, shape):
    return pl.pallas_call(
        attended_body,
        grid=(1,),
        in_specs=[whole(weights.shape), whole(values.shape), whole(w_out.shape)],
        out_specs=whole(shape),
        out_shape=jax.ShapeDtypeStruct(shape, BF16),
        scratch_shapes=[wide_scratch(shape), pltpu.VMEM(values.shape, BF16)],
        compiler_params=params(),
        cost_estimate=pl.CostEstimate(
            flops=4 * values.size * values.shape[1], bytes_accessed=3 * 1024 * 1024, transcendentals=0
        ),
        name="attended_output",
    )(weights, values, w_out)


def backward_body(bands_ref, cotangent_ref, other_ref, rim_ref, slab_ref, first_ref, edges_ref, grad_slab_ref,
                  grad_ref, pair_ref, next_ref, slope_one_ref, slope_two_ref, expand_ref, taps_ref, project_ref,
                  out_ref, rims, slab, first, edges, grad_slab, grad_in, slope_one, slope_two, expand, project,
                  grad_first, grad_rows, mixed, expanded, total, row_sems,
                  in_sems, chunk_sems):
    own, cols, width = slab.shape
    chunks = expand_ref.shape[1] // CHUNK

    sources = (cotangent_ref, other_ref, rim_ref)
    sides = list(enumerate((-1, own)))
    for side, place_first in sides:
        start_pull(bands_ref, place_first, sources, 1, rims.at[pl.ds(side, 1)], row_sems.at[side], RIM)
    inputs = [
        pltpu.make_async_copy(source, target, in_sems.at[index])
        for index, (source, target) in enumerate(
            ((first_ref, first), (grad_ref, grad_in), (grad_slab_ref, grad_slab), (edges_ref, edges), (slab_ref, slab))
        )
    ]
    for copy in inputs:
        copy.start()

    def fetches(index):
        lanes = chunk_lanes(index)
        pairs = (
            (project_ref.at[lanes], project.at[lanes]),
            (slope_two_ref.at[:, :, lanes], slope_two.at[:, :, lanes]),
            (slope_one_ref.at[:, :, lanes], slope_one.at[:, :, lanes]),
            (expand_ref.at[:, lanes], expand.at[:, lanes]),
        )
        return [
            pltpu.make_async_copy(source, target, chunk_sems.at[number, index])
            for number, (source, target) in enumerate(pairs)
        ]

    for copy in fetches(0):
        copy.start()

    def through_norm(cotangent, grad, first):
        rms = rms_scale(first)
        normed = first * rms
        grad = grad.astype(F32)
        inner = jnp.mean(grad * normed, -1, keepdims=True)
        return cotangent.astype(F32) + rms * (grad - normed * inner)

    for copy in inputs[:4]:
        copy.wait()
    for row in range(own):
        at = slice(row * cols, (row + 1) * cols)
        result = through_norm(grad_slab[row], grad_in[row], first[at])
        grad_first[at] = result
        grad_rows[(row + 1) * cols : (row + 2) * cols] = result.astype(BF16)
    for side, place_first in sides:
        wait_pull(sources, 1, rims.at[pl.ds(side, 1)], row_sems.at[side])
    leads = lax.rem(lax.axis_index("row"), 2) == 0
    above = jnp.where(leads, next_ref[0].astype(F32), pair_ref[0].astype(F32))
    below = jnp.where(leads, pair_ref[0].astype(F32), next_ref[0].astype(F32))
    last = (own + 1) * cols
    grad_rows[0:cols] = through_norm(rims[0], above, edges[:cols]).astype(BF16)
    grad_rows[last:] = through_norm(rims[1], below, edges[cols:]).astype(BF16)
    column = lax.broadcasted_iota(jnp.int32, (cols, LANES), 0)

    total[...] = jnp.zeros_like(total)

    def step(index, carry):
        @pl.when(index + 1 < chunks)
        def _():
            for copy in fetches(index + 1):
                copy.start()

        for copy in fetches(index):
            copy.wait()
        for start in range(0, CHUNK, HALF):
            weights = project[chunk_lanes(index, start, HALF), :]
            for row in range(0, own + 2, GROUP_BACKWARD):
                product = nt_dot(grad_rows[row * cols : (row + GROUP_BACKWARD) * cols, :], weights)
                for inner in range(GROUP_BACKWARD):
                    for lane in range(0, HALF, LANES):
                        slope = slope_two[row + inner, :, chunk_lanes(index, start + lane, LANES)].astype(F32)
                        value = product[inner * cols : (inner + 1) * cols, lane : lane + LANES] * slope
                        at = slice(start + lane, start + lane + LANES)
                        mixed[row + inner, :, at] = value.astype(BF16).astype(F32)

        for lane in range(0, CHUNK, LANES):
            lanes = slice(lane, lane + LANES)
            taps = spread_taps(taps_ref, chunk_lanes(index, lane, LANES), cols)
            for row in range(own):
                rows_near = [mixed[row + a, :, lanes] for a in range(3)]
                sums = [
                    taps[8 - b] * rows_near[0] + taps[5 - b] * rows_near[1] + taps[2 - b] * rows_near[2]
                    for b in range(3)
                ]
                value = column_sums(sums[0], sums[1], sums[2], column, cols - 1)
                value = value * slope_one[row, :, chunk_lanes(index, lane, LANES)].astype(F32)
                expanded[row * cols : (row + 1) * cols, lanes] = value.astype(BF16)
        total[...] += nt_dot(expanded[...], expand[:, chunk_lanes(index)])
        return carry

    lax.fori_loop(0, chunks, step, 0)
    inputs[4].wait()
    for row in range(own):
        at = slice(row * cols, (row + 1) * cols)
        values = slab[row].astype(F32)
        rms = rms_scale(values)
        normed = values * rms
        grad = total[at]
        inner = jnp.mean(grad * normed, -1, keepdims=True)
        out_ref[row] = (grad_first[at] + rms * (grad - normed * inner)).astype(BF16)


def backward(bands, cotangent, other, rim, slab, first, edges, grad_slab, grad, pair_row, next_row, slope_one,
             slope_two, w_expand, kernel, w_project):
    own, cols, width = slab.shape
    hidden_width = w_expand.shape[1]
    chunks = hidden_width // CHUNK
    return pl.pallas_call(
        backward_body,
        in_specs=[in_scalars()] + [in_hbm()] * 8 + [in_vmem()] * 2 + [in_hbm()] * 3 + [in_vmem(), in_hbm()],
        out_specs=in_vmem(),
        out_shape=jax.ShapeDtypeStruct((own, cols, width), BF16),
        scratch_shapes=[
            pltpu.VMEM((2, cols, width), BF16),
            pltpu.VMEM((own, cols, width), BF16),
            pltpu.VMEM((own * cols, width), F32),
            pltpu.VMEM((2 * cols, width), F32),
            pltpu.VMEM((own, cols, width), BF16),
            pltpu.VMEM((own, cols, width), BF16),
            pltpu.VMEM((own, cols, hidden_width), BF16),
            pltpu.VMEM((own + 2, cols, hidden_width), BF16),
            pltpu.VMEM((width, hidden_width), BF16),
            pltpu.VMEM((hidden_width, width), BF16),
            pltpu.VMEM((own * cols, width), F32),
            pltpu.VMEM(((own + 2) * cols, width), BF16),
            pltpu.VMEM((own + 2, cols, CHUNK), F32),
            pltpu.VMEM((own * cols, CHUNK), BF16),
            pltpu.VMEM((own * cols, width), F32),
            pltpu.SemaphoreType.DMA((2,)),
            pltpu.SemaphoreType.DMA((5,)),
            pltpu.SemaphoreType.DMA((4, chunks)),
        ],
        compiler_params=params(26),
        cost_estimate=pl.CostEstimate(
            flops=4 * (own + 2) * cols * width * hidden_width,
            bytes_accessed=12 * 1024 * 1024,
            transcendentals=0,
        ),
        name="bottleneck_backward",
    )(bands, held(cotangent), held(other), held(rim), held(slab), held(first), held(edges), held(grad_slab), held(grad),
      near(pair_row), near(next_row), held(slope_one), held(slope_two), held(w_expand), near(kernel),
      held(w_project))


def window_groups(size):
    stride = size // 8
    return [[first + stride * k for k in range(8)] for first in range(stride)]


def exchange_windows(rows):
    groups = window_groups(lax.axis_size("row"))
    return lax.all_to_all(
        rows, "row", split_axis=0, concat_axis=0, tiled=True, axis_index_groups=groups
    )


def swap_pair(rows):
    size = lax.axis_size("row")
    return lax.ppermute(rows, "row", [(i, i ^ 1) for i in range(size)])


def swap_next(rows):
    size = lax.axis_size("row")
    pairs = [(i, i + 1) for i in range(1, size - 1, 2)]
    return lax.ppermute(rows, "row", pairs + [(j, i) for i, j in pairs])


def place_rows(even, other, leads, leader_share):
    size = GRID_ROWS
    first, second = even[:BAND], even[BAND:]
    share = jnp.where(leads, leader_share, 2 * size - leader_share)
    zeros = jnp.zeros_like(first)
    low = jnp.where(leads | (share == size), first, jnp.where(share < size, second, other))
    mid = jnp.where(share < size, zeros, jnp.where(leads | (share == size), second, first))
    high = jnp.where(share > size, jnp.where(leads, other, second), zeros)
    return jnp.concatenate([low, mid, high], 0)


def on_device(features, row_bands, w_expand, kernel, w_project, w_qkv, w_out, cotangent):
    capacity, cols, width = features.shape
    device = lax.axis_index("row")
    parity = device % 2
    leads = parity == 0

    rim = swap_next(rim_rows(row_bands, features, cotangent))
    other_cotangent = swap_pair(cotangent)
    other_features = swap_pair(features)
    grad_slab = even_rows(row_bands, cotangent, other_cotangent)
    rim, grad_slab = lax.optimization_barrier((rim, grad_slab))

    grad_windows = exchange_windows(grad_slab)
    edges, first, normed, slab, expanded, mixed = forward(
        row_bands, features, other_features, rim, w_expand, kernel, w_project
    )
    normed, grad_windows = lax.optimization_barrier((normed, grad_windows))
    normed_windows = exchange_windows(normed)
    shape = (8, GRID_ROWS // 8, cols, width)
    slope_one, slope_two = slopes(expanded, mixed)
    grad_attended = attended_gradient(grad_windows.reshape(shape), w_out)
    normed_windows, slope_one, slope_two, grad_attended = lax.optimization_barrier(
        (normed_windows, slope_one, slope_two, grad_attended)
    )
    grad_normed, weights, values = attention(normed_windows.reshape(shape), grad_attended, w_qkv)
    grad_rows = exchange_windows(grad_normed.reshape(GRID_ROWS, cols, width))
    added = attend(weights, values, w_out, shape)
    leader_share = BAND * row_bands[device - parity]
    grad_rows, added, leader_share = lax.optimization_barrier((grad_rows, added, leader_share))
    top, bottom = grad_rows[:1], grad_rows[GRID_ROWS - 1 :]
    pair_row = swap_pair(jnp.where(leads, bottom, top))
    next_row = swap_next(jnp.where(leads, top, bottom))
    added, pair_row, next_row = lax.optimization_barrier((added, pair_row, next_row))
    added_rows = exchange_windows(added.reshape(GRID_ROWS, cols, width))
    grad_input = backward(
        row_bands, cotangent, other_cotangent, rim, slab, first, edges, grad_slab, grad_rows, pair_row, next_row,
        slope_one, slope_two, w_expand, kernel, w_project,
    )
    def sent(rows):
        return jnp.where(leads, rows[BAND:], rows[:BAND])

    other_grad = swap_pair(sent(grad_input))
    grad_input, added_rows = lax.optimization_barrier((grad_input, added_rows))
    final = (first.reshape(GRID_ROWS, cols, width) + added_rows.astype(F32)).astype(BF16)
    other_final = swap_pair(sent(final))
    return (
        place_rows(final, other_final, leads, leader_share),
        place_rows(grad_input, other_grad, leads, leader_share),
    )


def solution(mesh):
    return jax.shard_map(
        on_device,
        mesh=mesh,
        in_specs=(
            P(("parts", "row"), None, None),
            P("parts"),
            P(),
            P(),
            P(),
            P(),
            P(),
            P(("parts", "row"), None, None),
        ),
        out_specs=(P(("parts", "row"), None, None), P(("parts", "row"), None, None)),
        check_vma=False,
    )
```

```python
import math

import jax
import jax.numpy as jnp
from jax import lax
from jax.experimental import pallas as pl
from jax.experimental.pallas import tpu as pltpu
from jax.sharding import PartitionSpec as P

HEADS = 16
GRID_ROWS = 16
BAND = 8
RIM = 2
EPSILON = 1e-06
CHUNK = 512
HALF = 256
GROUP_FORWARD = 10
GROUP_BACKWARD = 9
LANES = 128
ROOT = math.sqrt(2.0 / math.pi)
CUBIC = 0.044715
F32 = jnp.float32
BF16 = jnp.bfloat16
MIB = 1024 * 1024


def nt_dot(left, right):
    return lax.dot_general(left, right, (((1,), (1,)), ((), ())), preferred_element_type=F32)


def tn_dot(left, right):
    return lax.dot_general(left, right, (((0,), (0,)), ((), ())), preferred_element_type=F32)


def nn_dot(left, right):
    return jnp.dot(left, right, preferred_element_type=F32)


def rms_scale(values):
    return lax.rsqrt(jnp.mean(values * values, -1, keepdims=True) + EPSILON)


def gelu_parts(v):
    square = v * v
    cdf = 0.5 + 0.5 * jnp.tanh(v * (ROOT + (ROOT * CUBIC) * square))
    return square, cdf, v * cdf


def gelu(v):
    return gelu_parts(v)[2]


def gelu_slope(v):
    square, cdf, value = gelu_parts(v)
    return cdf + (value - value * cdf) * (2.0 * ROOT + (6.0 * ROOT * CUBIC) * square)


def whole(shape, space=None):
    zeros = (0,) * len(shape)
    return pl.BlockSpec(shape, lambda *_: zeros)


def params(mebibytes=56):
    return pltpu.CompilerParams(vmem_limit_bytes=mebibytes * MIB)


def in_vmem():
    return pl.BlockSpec(memory_space=pltpu.VMEM)


def in_hbm():
    return pl.BlockSpec(memory_space=pltpu.HBM)


def held(array):
    return pltpu.with_memory_space_constraint(array, pltpu.HBM)


def near(array):
    return pltpu.with_memory_space_constraint(array, pltpu.VMEM)


def in_scalars():
    return pl.BlockSpec(memory_space=pltpu.SMEM)


def shares(bands_ref):
    device = lax.axis_index("row")
    parity = lax.rem(device, 2)
    return parity, BAND * bands_ref[device - parity], BAND * bands_ref[device]


def place(bands_ref, first):
    parity, leader_share, _ = shares(bands_ref)
    row = first + GRID_ROWS * parity
    beyond = (row < 0) | (row >= 2 * GRID_ROWS)
    in_leader = row < leader_share
    in_own = in_leader == (parity == 0)
    source = jnp.where(beyond, 2, jnp.where(in_own, 0, 1))
    return source, jnp.where(beyond, 0, jnp.where(in_leader, row, row - leader_share))


def start_pull(bands_ref, first, sources, rows, target, sem, rim_row=0):
    where, row = place(bands_ref, first)
    row = jnp.where(where == 2, rim_row, row)
    for number, source in enumerate(sources):

        @pl.when(where == number)
        def _():
            pltpu.make_async_copy(source.at[pl.ds(row, rows)], target, sem).start()


def wait_pull(sources, rows, target, sem):
    pltpu.make_async_copy(sources[0].at[pl.ds(0, rows)], target, sem).wait()


def even_body(bands_ref, own_ref, other_ref, out_ref):
    for half in range(2):
        where, row = place(bands_ref, BAND * half)
        for number, source in enumerate((own_ref, other_ref)):

            @pl.when(where == number)
            def _():
                out_ref[BAND * half : BAND * half + BAND] = source[pl.ds(row, BAND)]


def even_rows(bands, own, other):
    shape = (GRID_ROWS,) + own.shape[1:]
    return pl.pallas_call(
        even_body,
        in_specs=[in_scalars(), in_vmem(), in_vmem()],
        out_specs=in_vmem(),
        out_shape=jax.ShapeDtypeStruct(shape, own.dtype),
        compiler_params=params(8),
        name="even_rows",
    )(bands, near(own), near(other))


def rim_body(bands_ref, features_ref, cotangent_ref, out_ref, sems):
    parity, _, share = shares(bands_ref)
    leads = parity == 0
    copies = [
        pltpu.make_async_copy(
            features_ref.at[pl.ds(jnp.where(leads, 0, share - RIM), RIM)], out_ref.at[pl.ds(0, RIM)], sems.at[0]
        ),
        pltpu.make_async_copy(
            cotangent_ref.at[pl.ds(jnp.where(leads, 0, share - 1), 1)], out_ref.at[pl.ds(RIM, 1)], sems.at[1]
        ),
    ]
    for copy in copies:
        copy.start()
    for copy in copies:
        copy.wait()


def rim_rows(bands, features, cotangent):
    shape = (RIM + 1,) + features.shape[1:]
    return pl.pallas_call(
        rim_body,
        in_specs=[in_scalars(), in_hbm(), in_hbm()],
        out_specs=in_vmem(),
        out_shape=jax.ShapeDtypeStruct(shape, features.dtype),
        scratch_shapes=[pltpu.SemaphoreType.DMA((2,))],
        compiler_params=params(8),
        name="rim_rows",
    )(bands, held(features), held(cotangent))


def column_sums(left, mid, right, column, last):
    from_left = jnp.where(column == 0, 0.0, pltpu.roll(left, 1, 0))
    from_right = jnp.where(column == last, 0.0, pltpu.roll(right, last, 0))
    return mid + from_left + from_right


def spread_taps(taps_ref, lanes, cols):
    taps = taps_ref[:, lanes].astype(F32)
    return [jnp.broadcast_to(taps[i : i + 1], (cols, LANES)) for i in range(9)]


def chunk_lanes(index, lane=0, count=CHUNK):
    return pl.ds(pl.multiple_of(index * CHUNK + lane, LANES), count)


def forward_body(bands_ref, features_ref, other_ref, rim_ref, expand_ref, taps_ref, project_ref, first_ref,
                 own_first_ref, normed_ref, slab_ref, expanded_ref, mixed_ref, slab, normed_one, expand, project,
                 expanded, hidden, mixed, hidden_two, total, normed, row_sems,
                 weight_sems, chunk_sems, out_sems):
    rows, cols, width = slab.shape
    own = rows - 2 * RIM
    chunks = expand_ref.shape[1] // CHUNK

    sources = (features_ref, other_ref, rim_ref)
    pieces = [(0, RIM), (RIM, BAND), (RIM + BAND, BAND), (RIM + 2 * BAND, RIM)]
    for index, (first, count) in enumerate(pieces):
        start_pull(bands_ref, first - RIM, sources, count, slab.at[pl.ds(first, count)], row_sems.at[index])

    def fetch_expand(index):
        lanes = chunk_lanes(index)
        return pltpu.make_async_copy(expand_ref.at[:, lanes], expand.at[:, lanes], weight_sems.at[0, index])

    def fetch_project(index):
        lanes = chunk_lanes(index)
        return pltpu.make_async_copy(project_ref.at[lanes], project.at[lanes], weight_sems.at[1, index])

    def store_expanded(index):
        lanes = chunk_lanes(index)
        return pltpu.make_async_copy(
            expanded.at[:, :, lanes], expanded_ref.at[:, :, lanes], chunk_sems.at[0, index]
        )

    def store_mixed(index):
        lanes = chunk_lanes(index)
        return pltpu.make_async_copy(mixed.at[:, :, lanes], mixed_ref.at[:, :, lanes], chunk_sems.at[1, index])

    fetch_expand(0).start()
    fetch_project(0).start()
    for index, (first, count) in enumerate(pieces):
        wait_pull(sources, count, slab.at[pl.ds(first, count)], row_sems.at[index])
    store_slab = pltpu.make_async_copy(slab.at[pl.ds(RIM, own)], slab_ref, out_sems.at[0])
    store_slab.start()
    for row in range(0, rows, 2):
        at = slice(row * cols, (row + 2) * cols)
        values = slab[row : row + 2].astype(F32).reshape(2 * cols, width)
        normed_one[at] = (values * rms_scale(values)).astype(BF16)
    total[...] = slab[1 : rows - 1].astype(F32).reshape((rows - 2) * cols, width)
    column = lax.broadcasted_iota(jnp.int32, (cols, LANES), 0)

    def step(index, carry):
        @pl.when(index + 1 < chunks)
        def _():
            fetch_expand(index + 1).start()
            fetch_project(index + 1).start()

        fetch_expand(index).wait()
        for start in range(0, CHUNK, HALF):
            weights = expand[:, chunk_lanes(index, start, HALF)]
            for row in range(0, rows, GROUP_FORWARD):
                product = nn_dot(normed_one[row * cols : (row + GROUP_FORWARD) * cols, :], weights)
                for inner in range(GROUP_FORWARD):
                    for lane in range(0, HALF, LANES):
                        values = product[inner * cols : (inner + 1) * cols, lane : lane + LANES]
                        at = slice(start + lane, start + lane + LANES)
                        hidden[row + inner, :, at] = gelu(values).astype(BF16).astype(F32)
                        if RIM <= row + inner < RIM + own:
                            expanded[row + inner - RIM, :, chunk_lanes(index, start + lane, LANES)] = values.astype(BF16)
        store_expanded(index).start()

        for lane in range(0, CHUNK, LANES):
            lanes = slice(lane, lane + LANES)
            taps = spread_taps(taps_ref, chunk_lanes(index, lane, LANES), cols)
            for row in range(rows - 2):
                rows_near = [hidden[row + a, :, lanes] for a in range(3)]
                sums = [
                    taps[b] * rows_near[0] + taps[3 + b] * rows_near[1] + taps[6 + b] * rows_near[2] for b in range(3)
                ]
                values = column_sums(sums[0], sums[1], sums[2], column, cols - 1)
                hidden_two[row * cols : (row + 1) * cols, lanes] = gelu(values).astype(BF16)
                mixed[row, :, chunk_lanes(index, lane, LANES)] = values.astype(BF16)
        store_mixed(index).start()
        fetch_project(index).wait()
        total[...] += nn_dot(hidden_two[...], project[chunk_lanes(index), :])
        return carry

    lax.fori_loop(0, chunks, step, 0)
    for row in range(1, own + 1):
        first = total[row * cols : (row + 1) * cols]
        normed[row - 1] = (first * rms_scale(first)).astype(BF16)
    store_normed = pltpu.make_async_copy(normed, normed_ref, out_sems.at[1])
    store_above = pltpu.make_async_copy(total.at[pl.ds(0, cols)], first_ref.at[pl.ds(0, cols)], out_sems.at[2])
    store_below = pltpu.make_async_copy(
        total.at[pl.ds((own + 1) * cols, cols)], first_ref.at[pl.ds(cols, cols)], out_sems.at[3]
    )
    store_own = pltpu.make_async_copy(total.at[pl.ds(cols, own * cols)], own_first_ref, out_sems.at[4])
    store_normed.start()
    store_above.start()
    store_below.start()
    store_own.start()
    for index in range(chunks):
        store_expanded(index).wait()
        store_mixed(index).wait()
    store_slab.wait()
    store_normed.wait()
    store_above.wait()
    store_below.wait()
    store_own.wait()


def forward(bands, features, other, rim, w_expand, kernel, w_project):
    capacity, cols, width = features.shape
    own, rows = GRID_ROWS, GRID_ROWS + 2 * RIM
    hidden_width = w_expand.shape[1]
    chunks = hidden_width // CHUNK
    return pl.pallas_call(
        forward_body,
        in_specs=[in_scalars(), in_hbm(), in_vmem(), in_vmem(), in_hbm(), in_vmem(), in_hbm()],
        out_specs=[in_hbm()] * 6,
        out_shape=[
            pltpu.HBM((2 * cols, width), F32),
            pltpu.HBM((own * cols, width), F32),
            pltpu.HBM((own, cols, width), BF16),
            pltpu.HBM((own, cols, width), BF16),
            pltpu.HBM((own, cols, hidden_width), BF16),
            pltpu.HBM((rows - 2, cols, hidden_width), BF16),
        ],
        scratch_shapes=[
            pltpu.VMEM((rows, cols, width), BF16),
            pltpu.VMEM((rows * cols, width), BF16),
            pltpu.VMEM((width, hidden_width), BF16),
            pltpu.VMEM((hidden_width, width), BF16),
            pltpu.VMEM((own, cols, hidden_width), BF16),
            pltpu.VMEM((rows, cols, CHUNK), F32),
            pltpu.VMEM((rows - 2, cols, hidden_width), BF16),
            pltpu.VMEM(((rows - 2) * cols, CHUNK), BF16),
            pltpu.VMEM(((rows - 2) * cols, width), F32),
            pltpu.VMEM((own, cols, width), BF16),
            pltpu.SemaphoreType.DMA((4,)),
            pltpu.SemaphoreType.DMA((2, chunks)),
            pltpu.SemaphoreType.DMA((2, chunks)),
            pltpu.SemaphoreType.DMA((5,)),
        ],
        compiler_params=params(24),
        cost_estimate=pl.CostEstimate(
            flops=16 * 10**9,
            bytes_accessed=48 * MIB,
            transcendentals=2 * rows * cols * hidden_width,
        ),
        name="bottleneck_forward",
    )(bands, held(features), near(other), near(rim), held(w_expand), near(kernel), held(w_project))


def slopes_body(expanded_ref, mixed_ref, slope_one_ref, slope_two_ref):
    for source, target in ((expanded_ref, slope_one_ref), (mixed_ref, slope_two_ref)):
        rows, _, chunk = source.shape
        for row in range(rows):
            for lane in range(0, chunk, LANES):
                lanes = slice(lane, lane + LANES)
                target[row, :, lanes] = gelu_slope(source[row, :, lanes].astype(F32)).astype(BF16)


def slopes(expanded, mixed):
    hidden_width = expanded.shape[2]
    blocks = [
        pl.BlockSpec(values.shape[:2] + (CHUNK,), lambda j: (0, 0, j)) for values in (expanded, mixed)
    ]
    return pl.pallas_call(
        slopes_body,
        grid=(hidden_width // CHUNK,),
        in_specs=blocks,
        out_specs=blocks,
        out_shape=[jax.ShapeDtypeStruct(values.shape, BF16) for values in (expanded, mixed)],
        compiler_params=params(),
        cost_estimate=pl.CostEstimate(
            flops=15 * (expanded.size + mixed.size),
            bytes_accessed=6 * (expanded.size + mixed.size),
            transcendentals=expanded.size + mixed.size,
        ),
        name="gelu_slopes",
    )(expanded, mixed)


def lane_tiles(width):
    return [slice(at, at + LANES) for at in range(0, width, LANES)]


def window_places(own, cols):
    return [(r, q) for r in range(own) for q in range(cols // 8)]


def to_windows(source_ref, rows_wide, target):
    groups, own, cols, width = source_ref.shape
    span = groups * 8
    for tile, lanes in enumerate(lane_tiles(width)):
        for group in range(groups):
            rows_wide[tile, group] = source_ref[group, :, :, lanes].astype(F32)
        for index, (r, q) in enumerate(window_places(own, cols)):
            pieces = [
                rows_wide[tile, group, r, pl.ds(q, 8, stride=cols // 8), :] for group in range(groups)
            ]
            rows = slice(index * span, (index + 1) * span)
            target[rows, lanes] = jnp.concatenate(pieces, axis=0).astype(BF16)


def to_rows(values, rows_wide, target_ref):
    groups, own, cols, width = target_ref.shape
    span = groups * 8
    for tile, lanes in enumerate(lane_tiles(width)):
        for index, (r, q) in enumerate(window_places(own, cols)):
            for group in range(groups):
                first = index * span + group * 8
                rows_wide[tile, group, r, pl.ds(q, 8, stride=cols // 8), :] = values[first : first + 8, lanes]
        for group in range(groups):
            target_ref[group, :, :, lanes] = rows_wide[tile, group].astype(BF16)


def wide_scratch(shape):
    groups, own, cols, width = shape
    return pltpu.VMEM((width // LANES, groups, own, cols, LANES), F32)


def grad_attended_body(cotangent_ref, out_ref, grad_ref, rows_wide, in_windows):
    to_windows(cotangent_ref, rows_wide, in_windows)
    grad_ref[...] = nt_dot(in_windows[...], out_ref[...]).astype(BF16)


def attended_gradient(cotangent, w_out):
    groups, own, cols, width = cotangent.shape
    shape = (groups * own * cols, width)
    return pl.pallas_call(
        grad_attended_body,
        grid=(1,),
        in_specs=[whole(cotangent.shape), whole(w_out.shape)],
        out_specs=whole(shape),
        out_shape=jax.ShapeDtypeStruct(shape, BF16),
        scratch_shapes=[wide_scratch(cotangent.shape), pltpu.VMEM(shape, BF16)],
        compiler_params=params(),
        cost_estimate=pl.CostEstimate(
            flops=2 * shape[0] * width * width, bytes_accessed=2 * 1024 * 1024, transcendentals=0
        ),
        name="attended_gradient",
    )(cotangent, w_out)


def per_query(values, weights, span, head_dim, scale=1.0):
    wide = nn_dot(values.T, weights)
    half = LANES // 2
    own = jnp.concatenate([wide[:half, :LANES], wide[half:, LANES:]], axis=0) * scale
    own = own.astype(BF16).T
    lane_head = lax.broadcasted_iota(jnp.int32, (span, LANES), 1) // head_dim
    return jnp.where(lane_head % 2 == 0, own[:span].astype(F32), own[span:].astype(F32)).astype(BF16)


def attention_body(normed_ref, grad_attended_ref, qkv_ref, grad_ref, weights_ref, values_ref, rows_wide,
                   in_windows, projected, grad_projected, grad_attended, qkv, grad, weights, in_sems, out_sems):
    groups, own, cols, width = normed_ref.shape
    span = groups * 8
    windows = own * cols // 8
    head_dim = width // HEADS
    heads = LANES // head_dim
    scale = 1.0 / math.sqrt(head_dim)
    steepness = scale * math.log2(math.e)

    fetch_qkv = pltpu.make_async_copy(qkv_ref, qkv, in_sems.at[0])
    fetch_grad = pltpu.make_async_copy(grad_attended_ref, grad_attended, in_sems.at[1])
    fetch_qkv.start()
    fetch_grad.start()
    to_windows(normed_ref, rows_wide, in_windows)
    fetch_qkv.wait()
    projected[...] = nn_dot(in_windows[...], qkv[...]).astype(BF16)
    store_values = pltpu.make_async_copy(projected.at[:, pl.ds(2 * width, width)], values_ref, out_sems.at[0])
    store_values.start()
    fetch_grad.wait()

    row_head = lax.broadcasted_iota(jnp.int32, (heads * span, LANES), 0) // span
    lane_head = lax.broadcasted_iota(jnp.int32, (heads * span, LANES), 1) // head_dim
    mask = (row_head == lane_head).astype(F32).astype(BF16)

    def spread(values):
        return jnp.concatenate([values] * heads, axis=0) * mask

    def window(index, carry):
        rows = pl.ds(pl.multiple_of(index * span, span), span)
        for part in range(width // LANES):
            q_at, k_at, v_at = (
                slice(t * width + part * LANES, t * width + (part + 1) * LANES) for t in range(3)
            )
            q, k, v = projected[rows, q_at], projected[rows, k_at], projected[rows, v_at]
            q_wide = spread(q)
            g_wide = spread(grad_attended[rows, q_at])
            scores = nt_dot(k, q_wide)
            powers = jnp.exp2((scores - jnp.max(scores, axis=0, keepdims=True)) * steepness)
            shares = powers * (1.0 / jnp.sum(powers, axis=0, keepdims=True))
            half = shares.astype(BF16)
            weights[index, :, part * heads * span : (part + 1) * heads * span] = half
            grad_weights = nt_dot(v, g_wide)
            row_dot = jnp.sum(shares * grad_weights, axis=0, keepdims=True)
            grad_scores = (shares * (grad_weights - row_dot)).astype(BF16)
            grad_projected[rows, q_at] = per_query(k, grad_scores, span, head_dim, scale)
            grad_projected[rows, k_at] = (nn_dot(grad_scores, q_wide) * scale).astype(BF16)
            grad_projected[rows, v_at] = nn_dot(half, g_wide).astype(BF16)
        return carry

    lax.fori_loop(0, windows, window, 0, unroll=4)
    store_weights = pltpu.make_async_copy(weights, weights_ref, out_sems.at[1])
    store_weights.start()
    to_rows(nt_dot(grad_projected[...], qkv[...]), rows_wide, grad)
    store_grad = pltpu.make_async_copy(grad, grad_ref, out_sems.at[2])
    store_grad.start()
    store_values.wait()
    store_weights.wait()
    store_grad.wait()


def attention(normed, grad_attended, w_qkv):
    groups, own, cols, width = normed.shape
    span = groups * 8
    tokens = groups * own * cols
    out_shapes = [normed.shape, (tokens // span, span, HEADS * span), (tokens, width)]
    return pl.pallas_call(
        attention_body,
        in_specs=[in_vmem(), in_hbm(), in_hbm()],
        out_specs=[in_hbm()] * 3,
        out_shape=[pltpu.HBM(shape, BF16) for shape in out_shapes],
        scratch_shapes=[
            wide_scratch(normed.shape),
            pltpu.VMEM((tokens, width), BF16),
            pltpu.VMEM((tokens, 3 * width), BF16),
            pltpu.VMEM((tokens, 3 * width), BF16),
            pltpu.VMEM((tokens, width), BF16),
            pltpu.VMEM(w_qkv.shape, BF16),
            pltpu.VMEM(normed.shape, BF16),
            pltpu.VMEM(out_shapes[1], BF16),
            pltpu.SemaphoreType.DMA((2,)),
            pltpu.SemaphoreType.DMA((3,)),
        ],
        compiler_params=params(18),
        cost_estimate=pl.CostEstimate(
            flops=16 * tokens * width * width,
            bytes_accessed=4 * 1024 * 1024,
            transcendentals=tokens * span * HEADS,
        ),
        name="window_attention",
    )(near(normed), held(grad_attended), held(w_qkv))


def attended_body(weights_ref, values_ref, out_ref, added_ref, rows_wide, attended):
    windows, span, wide = weights_ref.shape
    width = values_ref.shape[1]
    heads = LANES * HEADS // width
    for index in range(windows):
        rows = slice(index * span, (index + 1) * span)
        for part, lanes in enumerate(lane_tiles(width)):
            weights = weights_ref[index, :, part * heads * span : (part + 1) * heads * span]
            attended[rows, lanes] = per_query(values_ref[rows, lanes], weights, span, width // HEADS)
    to_rows(nn_dot(attended[...], out_ref[...]), rows_wide, added_ref)


def attend(weights, values, w_out, shape):
    return pl.pallas_call(
        attended_body,
        grid=(1,),
        in_specs=[whole(weights.shape), whole(values.shape), whole(w_out.shape)],
        out_specs=whole(shape),
        out_shape=jax.ShapeDtypeStruct(shape, BF16),
        scratch_shapes=[wide_scratch(shape), pltpu.VMEM(values.shape, BF16)],
        compiler_params=params(),
        cost_estimate=pl.CostEstimate(
            flops=4 * values.size * values.shape[1], bytes_accessed=3 * 1024 * 1024, transcendentals=0
        ),
        name="attended_output",
    )(weights, values, w_out)


def backward_body(bands_ref, cotangent_ref, other_ref, rim_ref, slab_ref, first_ref, edges_ref, grad_slab_ref,
                  grad_ref, pair_ref, next_ref, slope_one_ref, slope_two_ref, expand_ref, taps_ref, project_ref,
                  out_ref, rims, slab, first, edges, grad_slab, grad_in, slope_one, slope_two, expand, project,
                  grad_first, grad_rows, mixed, expanded, total, row_sems,
                  in_sems, chunk_sems):
    own, cols, width = slab.shape
    chunks = expand_ref.shape[1] // CHUNK

    sources = (cotangent_ref, other_ref, rim_ref)
    sides = list(enumerate((-1, own)))
    for side, place_first in sides:
        start_pull(bands_ref, place_first, sources, 1, rims.at[pl.ds(side, 1)], row_sems.at[side], RIM)
    inputs = [
        pltpu.make_async_copy(source, target, in_sems.at[index])
        for index, (source, target) in enumerate(
            ((first_ref, first), (grad_ref, grad_in), (grad_slab_ref, grad_slab), (edges_ref, edges), (slab_ref, slab))
        )
    ]
    for copy in inputs:
        copy.start()

    def fetches(index):
        lanes = chunk_lanes(index)
        pairs = (
            (project_ref.at[lanes], project.at[lanes]),
            (slope_two_ref.at[:, :, lanes], slope_two.at[:, :, lanes]),
            (slope_one_ref.at[:, :, lanes], slope_one.at[:, :, lanes]),
            (expand_ref.at[:, lanes], expand.at[:, lanes]),
        )
        return [
            pltpu.make_async_copy(source, target, chunk_sems.at[number, index])
            for number, (source, target) in enumerate(pairs)
        ]

    for copy in fetches(0):
        copy.start()

    def through_norm(cotangent, grad, first):
        rms = rms_scale(first)
        normed = first * rms
        grad = grad.astype(F32)
        inner = jnp.mean(grad * normed, -1, keepdims=True)
        return cotangent.astype(F32) + rms * (grad - normed * inner)

    for copy in inputs[:4]:
        copy.wait()
    for row in range(own):
        at = slice(row * cols, (row + 1) * cols)
        result = through_norm(grad_slab[row], grad_in[row], first[at])
        grad_first[at] = result
        grad_rows[(row + 1) * cols : (row + 2) * cols] = result.astype(BF16)
    for side, place_first in sides:
        wait_pull(sources, 1, rims.at[pl.ds(side, 1)], row_sems.at[side])
    leads = lax.rem(lax.axis_index("row"), 2) == 0
    above = jnp.where(leads, next_ref[0].astype(F32), pair_ref[0].astype(F32))
    below = jnp.where(leads, pair_ref[0].astype(F32), next_ref[0].astype(F32))
    last = (own + 1) * cols
    grad_rows[0:cols] = through_norm(rims[0], above, edges[:cols]).astype(BF16)
    grad_rows[last:] = through_norm(rims[1], below, edges[cols:]).astype(BF16)
    column = lax.broadcasted_iota(jnp.int32, (cols, LANES), 0)

    total[...] = jnp.zeros_like(total)

    def step(index, carry):
        @pl.when(index + 1 < chunks)
        def _():
            for copy in fetches(index + 1):
                copy.start()

        for copy in fetches(index):
            copy.wait()
        for start in range(0, CHUNK, HALF):
            weights = project[chunk_lanes(index, start, HALF), :]
            for row in range(0, own + 2, GROUP_BACKWARD):
                product = nt_dot(grad_rows[row * cols : (row + GROUP_BACKWARD) * cols, :], weights)
                for inner in range(GROUP_BACKWARD):
                    for lane in range(0, HALF, LANES):
                        slope = slope_two[row + inner, :, chunk_lanes(index, start + lane, LANES)].astype(F32)
                        value = product[inner * cols : (inner + 1) * cols, lane : lane + LANES] * slope
                        at = slice(start + lane, start + lane + LANES)
                        mixed[row + inner, :, at] = value.astype(BF16).astype(F32)

        for lane in range(0, CHUNK, LANES):
            lanes = slice(lane, lane + LANES)
            taps = spread_taps(taps_ref, chunk_lanes(index, lane, LANES), cols)
            for row in range(own):
                rows_near = [mixed[row + a, :, lanes] for a in range(3)]
                sums = [
                    taps[8 - b] * rows_near[0] + taps[5 - b] * rows_near[1] + taps[2 - b] * rows_near[2]
                    for b in range(3)
                ]
                value = column_sums(sums[0], sums[1], sums[2], column, cols - 1)
                value = value * slope_one[row, :, chunk_lanes(index, lane, LANES)].astype(F32)
                expanded[row * cols : (row + 1) * cols, lanes] = value.astype(BF16)
        total[...] += nt_dot(expanded[...], expand[:, chunk_lanes(index)])
        return carry

    lax.fori_loop(0, chunks, step, 0)
    inputs[4].wait()
    for row in range(own):
        at = slice(row * cols, (row + 1) * cols)
        values = slab[row].astype(F32)
        rms = rms_scale(values)
        normed = values * rms
        grad = total[at]
        inner = jnp.mean(grad * normed, -1, keepdims=True)
        out_ref[row] = (grad_first[at] + rms * (grad - normed * inner)).astype(BF16)


def backward(bands, cotangent, other, rim, slab, first, edges, grad_slab, grad, pair_row, next_row, slope_one,
             slope_two, w_expand, kernel, w_project):
    own, cols, width = slab.shape
    hidden_width = w_expand.shape[1]
    chunks = hidden_width // CHUNK
    return pl.pallas_call(
        backward_body,
        in_specs=[in_scalars()] + [in_hbm()] * 8 + [in_vmem()] * 2 + [in_hbm()] * 3 + [in_vmem(), in_hbm()],
        out_specs=in_vmem(),
        out_shape=jax.ShapeDtypeStruct((own, cols, width), BF16),
        scratch_shapes=[
            pltpu.VMEM((2, cols, width), BF16),
            pltpu.VMEM((own, cols, width), BF16),
            pltpu.VMEM((own * cols, width), F32),
            pltpu.VMEM((2 * cols, width), F32),
            pltpu.VMEM((own, cols, width), BF16),
            pltpu.VMEM((own, cols, width), BF16),
            pltpu.VMEM((own, cols, hidden_width), BF16),
            pltpu.VMEM((own + 2, cols, hidden_width), BF16),
            pltpu.VMEM((width, hidden_width), BF16),
            pltpu.VMEM((hidden_width, width), BF16),
            pltpu.VMEM((own * cols, width), F32),
            pltpu.VMEM(((own + 2) * cols, width), BF16),
            pltpu.VMEM((own + 2, cols, CHUNK), F32),
            pltpu.VMEM((own * cols, CHUNK), BF16),
            pltpu.VMEM((own * cols, width), F32),
            pltpu.SemaphoreType.DMA((2,)),
            pltpu.SemaphoreType.DMA((5,)),
            pltpu.SemaphoreType.DMA((4, chunks)),
        ],
        compiler_params=params(26),
        cost_estimate=pl.CostEstimate(
            flops=16 * 10**9,
            bytes_accessed=48 * MIB,
            transcendentals=0,
        ),
        name="bottleneck_backward",
    )(bands, held(cotangent), held(other), held(rim), held(slab), held(first), held(edges), held(grad_slab), held(grad),
      near(pair_row), near(next_row), held(slope_one), held(slope_two), held(w_expand), near(kernel),
      held(w_project))


def window_groups(size):
    stride = size // 8
    return [[first + stride * k for k in range(8)] for first in range(stride)]


def exchange_windows(rows):
    groups = window_groups(lax.axis_size("row"))
    return lax.all_to_all(
        rows, "row", split_axis=0, concat_axis=0, tiled=True, axis_index_groups=groups
    )


def swap_pair(rows):
    size = lax.axis_size("row")
    return lax.ppermute(rows, "row", [(i, i ^ 1) for i in range(size)])


def swap_next(rows):
    size = lax.axis_size("row")
    pairs = [(i, i + 1) for i in range(1, size - 1, 2)]
    return lax.ppermute(rows, "row", pairs + [(j, i) for i, j in pairs])


def place_rows(even, other, leads, leader_share):
    size = GRID_ROWS
    first, second = even[:BAND], even[BAND:]
    share = jnp.where(leads, leader_share, 2 * size - leader_share)
    zeros = jnp.zeros_like(first)
    low = jnp.where(leads | (share == size), first, jnp.where(share < size, second, other))
    mid = jnp.where(share < size, zeros, jnp.where(leads | (share == size), second, first))
    high = jnp.where(share > size, jnp.where(leads, other, second), zeros)
    return jnp.concatenate([low, mid, high], 0)


def on_device(features, row_bands, w_expand, kernel, w_project, w_qkv, w_out, cotangent):
    capacity, cols, width = features.shape
    device = lax.axis_index("row")
    parity = device % 2
    leads = parity == 0

    rim = swap_next(rim_rows(row_bands, features, cotangent))
    other_cotangent = swap_pair(cotangent)
    other_features = swap_pair(features)
    grad_slab = even_rows(row_bands, cotangent, other_cotangent)

    grad_windows = exchange_windows(grad_slab)
    edges, first, normed, slab, expanded, mixed = forward(
        row_bands, features, other_features, rim, w_expand, kernel, w_project
    )
    normed, grad_windows = lax.optimization_barrier((normed, grad_windows))
    normed_windows = exchange_windows(normed)
    shape = (8, GRID_ROWS // 8, cols, width)
    slope_one, slope_two = slopes(expanded, mixed)
    grad_attended = attended_gradient(grad_windows.reshape(shape), w_out)
    normed_windows, slope_one, slope_two, grad_attended = lax.optimization_barrier(
        (normed_windows, slope_one, slope_two, grad_attended)
    )
    grad_normed, weights, values = attention(normed_windows.reshape(shape), grad_attended, w_qkv)
    grad_rows = exchange_windows(grad_normed.reshape(GRID_ROWS, cols, width))
    added = attend(weights, values, w_out, shape)
    leader_share = BAND * row_bands[device - parity]
    grad_rows, added, leader_share = lax.optimization_barrier((grad_rows, added, leader_share))
    top, bottom = grad_rows[:1], grad_rows[GRID_ROWS - 1 :]
    sent_next, sent_pair = jnp.where(leads, top, bottom), jnp.where(leads, bottom, top)
    added, sent_next, sent_pair = lax.optimization_barrier((added, sent_next, sent_pair))
    next_row, pair_row = swap_next(sent_next), swap_pair(sent_pair)
    added_rows = exchange_windows(added.reshape(GRID_ROWS, cols, width))
    grad_input = backward(
        row_bands, cotangent, other_cotangent, rim, slab, first, edges, grad_slab, grad_rows, pair_row, next_row,
        slope_one, slope_two, w_expand, kernel, w_project,
    )
    def sent(rows):
        return jnp.where(leads, rows[BAND:], rows[:BAND])

    other_grad = swap_pair(sent(grad_input))
    grad_input, added_rows = lax.optimization_barrier((grad_input, added_rows))
    final = (first.reshape(GRID_ROWS, cols, width) + added_rows.astype(F32)).astype(BF16)
    other_final = swap_pair(sent(final))
    return (
        place_rows(final, other_final, leads, leader_share),
        place_rows(grad_input, other_grad, leads, leader_share),
    )


def solution(mesh):
    return jax.shard_map(
        on_device,
        mesh=mesh,
        in_specs=(
            P(("parts", "row"), None, None),
            P("parts"),
            P(),
            P(),
            P(),
            P(),
            P(),
            P(("parts", "row"), None, None),
        ),
        out_specs=(P(("parts", "row"), None, None), P(("parts", "row"), None, None)),
        check_vma=False,
    )
```

```python
import math

import jax
import jax.numpy as jnp
from jax import lax
from jax.experimental import pallas as pl
from jax.experimental.pallas import tpu as pltpu
from jax.sharding import PartitionSpec as P

HEADS = 16
GRID_ROWS = 16
BAND = 8
RIM = 2
EPSILON = 1e-06
CHUNK = 512
GROUP_FORWARD = 10
GROUP_BACKWARD = 9
LANES = 128
ROOT = math.sqrt(2.0 / math.pi)
CUBIC = 0.044715
F32 = jnp.float32
BF16 = jnp.bfloat16
MIB = 1024 * 1024


def nt_dot(left, right):
    return lax.dot_general(left, right, (((1,), (1,)), ((), ())), preferred_element_type=F32)


def tn_dot(left, right):
    return lax.dot_general(left, right, (((0,), (0,)), ((), ())), preferred_element_type=F32)


def nn_dot(left, right):
    return jnp.dot(left, right, preferred_element_type=F32)


def rms_scale(values):
    return lax.rsqrt(jnp.mean(values * values, -1, keepdims=True) + EPSILON)


def gelu_parts(v):
    square = v * v
    cdf = 0.5 + 0.5 * jnp.tanh(v * (ROOT + (ROOT * CUBIC) * square))
    return square, cdf, v * cdf


def gelu(v):
    return gelu_parts(v)[2]


def gelu_slope(v):
    square, cdf, value = gelu_parts(v)
    return cdf + (value - value * cdf) * (2.0 * ROOT + (6.0 * ROOT * CUBIC) * square)


def whole(shape, space=None):
    zeros = (0,) * len(shape)
    return pl.BlockSpec(shape, lambda *_: zeros)


def params(mebibytes=56):
    return pltpu.CompilerParams(vmem_limit_bytes=mebibytes * MIB)


def in_vmem():
    return pl.BlockSpec(memory_space=pltpu.VMEM)


def in_hbm():
    return pl.BlockSpec(memory_space=pltpu.HBM)


def held(array):
    return pltpu.with_memory_space_constraint(array, pltpu.HBM)


def near(array):
    return pltpu.with_memory_space_constraint(array, pltpu.VMEM)


def in_scalars():
    return pl.BlockSpec(memory_space=pltpu.SMEM)


def shares(bands_ref):
    device = lax.axis_index("row")
    parity = lax.rem(device, 2)
    return parity, BAND * bands_ref[device - parity], BAND * bands_ref[device]


def place(bands_ref, first):
    parity, leader_share, _ = shares(bands_ref)
    row = first + GRID_ROWS * parity
    beyond = (row < 0) | (row >= 2 * GRID_ROWS)
    in_leader = row < leader_share
    in_own = in_leader == (parity == 0)
    source = jnp.where(beyond, 2, jnp.where(in_own, 0, 1))
    return source, jnp.where(beyond, 0, jnp.where(in_leader, row, row - leader_share))


def start_pull(bands_ref, first, sources, rows, target, sem, rim_row=0):
    where, row = place(bands_ref, first)
    row = jnp.where(where == 2, rim_row, row)
    for number, source in enumerate(sources):

        @pl.when(where == number)
        def _():
            pltpu.make_async_copy(source.at[pl.ds(row, rows)], target, sem).start()


def wait_pull(sources, rows, target, sem):
    pltpu.make_async_copy(sources[0].at[pl.ds(0, rows)], target, sem).wait()


def even_body(bands_ref, own_ref, other_ref, out_ref):
    for half in range(2):
        where, row = place(bands_ref, BAND * half)
        for number, source in enumerate((own_ref, other_ref)):

            @pl.when(where == number)
            def _():
                out_ref[BAND * half : BAND * half + BAND] = source[pl.ds(row, BAND)]


def even_rows(bands, own, other):
    shape = (GRID_ROWS,) + own.shape[1:]
    return pl.pallas_call(
        even_body,
        in_specs=[in_scalars(), in_vmem(), in_vmem()],
        out_specs=in_vmem(),
        out_shape=jax.ShapeDtypeStruct(shape, own.dtype),
        compiler_params=params(8),
        name="even_rows",
    )(bands, near(own), near(other))


def rim_body(bands_ref, features_ref, cotangent_ref, out_ref, bands, choices, sems):
    fetch_bands = pltpu.make_async_copy(bands_ref, bands, sems.at[0])
    fetch_bands.start()
    copies = []
    for choice in range(4):
        first = max(0, BAND * choice - RIM)
        second = max(0, BAND * choice - 1)
        copies.append(
            pltpu.make_async_copy(
                features_ref.at[pl.ds(first, RIM)], choices.at[choice, pl.ds(0, RIM)], sems.at[1 + choice]
            )
        )
        copies.append(
            pltpu.make_async_copy(
                cotangent_ref.at[pl.ds(second, 1)], choices.at[choice, pl.ds(RIM, 1)], sems.at[5 + choice]
            )
        )
    for copy in copies:
        copy.start()
    fetch_bands.wait()
    device = lax.axis_index("row")
    choice = jnp.where(lax.rem(device, 2) == 0, 0, bands[device])
    for copy in copies:
        copy.wait()
    out_ref[...] = choices[choice]


def rim_rows(bands, features, cotangent):
    shape = (RIM + 1,) + features.shape[1:]
    return pl.pallas_call(
        rim_body,
        in_specs=[in_hbm(), in_hbm(), in_hbm()],
        out_specs=in_vmem(),
        out_shape=jax.ShapeDtypeStruct(shape, features.dtype),
        scratch_shapes=[
            pltpu.SMEM(bands.shape, bands.dtype),
            pltpu.VMEM((4,) + shape, features.dtype),
            pltpu.SemaphoreType.DMA((9,)),
        ],
        compiler_params=params(8),
        name="rim_rows",
    )(held(bands), held(features), held(cotangent))


def column_sums(left, mid, right, column, last):
    from_left = jnp.where(column == 0, 0.0, pltpu.roll(left, 1, 0))
    from_right = jnp.where(column == last, 0.0, pltpu.roll(right, last, 0))
    return mid + from_left + from_right


def spread_taps(taps_ref, lanes, cols):
    taps = taps_ref[:, lanes].astype(F32)
    return [jnp.broadcast_to(taps[i : i + 1], (cols, LANES)) for i in range(9)]


def chunk_lanes(index, lane=0, count=CHUNK):
    return pl.ds(pl.multiple_of(index * CHUNK + lane, LANES), count)


def forward_body(bands_ref, features_ref, other_ref, rim_ref, expand_ref, taps_ref, project_ref, first_ref,
                 own_first_ref, normed_ref, slab_ref, expanded_ref, mixed_ref, slab, normed_one, expand, project,
                 expanded, hidden, mixed, hidden_two, total, normed, row_sems,
                 weight_sems, chunk_sems, out_sems):
    rows, cols, width = slab.shape
    own = rows - 2 * RIM
    chunks = expand_ref.shape[1] // CHUNK

    sources = (features_ref, other_ref, rim_ref)
    pieces = [(0, RIM), (RIM, BAND), (RIM + BAND, BAND), (RIM + 2 * BAND, RIM)]
    for index, (first, count) in enumerate(pieces):
        start_pull(bands_ref, first - RIM, sources, count, slab.at[pl.ds(first, count)], row_sems.at[index])

    def fetch_expand(index):
        lanes = chunk_lanes(index)
        return pltpu.make_async_copy(expand_ref.at[:, lanes], expand.at[:, lanes], weight_sems.at[0, index])

    def fetch_project(index):
        lanes = chunk_lanes(index)
        return pltpu.make_async_copy(project_ref.at[lanes], project.at[lanes], weight_sems.at[1, index])

    def store_expanded(index):
        lanes = chunk_lanes(index)
        return pltpu.make_async_copy(
            expanded.at[:, :, lanes], expanded_ref.at[:, :, lanes], chunk_sems.at[0, index]
        )

    def store_mixed(index):
        lanes = chunk_lanes(index)
        return pltpu.make_async_copy(mixed.at[:, :, lanes], mixed_ref.at[:, :, lanes], chunk_sems.at[1, index])

    fetch_expand(0).start()
    fetch_project(0).start()
    for index, (first, count) in enumerate(pieces):
        wait_pull(sources, count, slab.at[pl.ds(first, count)], row_sems.at[index])
    store_slab = pltpu.make_async_copy(slab.at[pl.ds(RIM, own)], slab_ref, out_sems.at[0])
    store_slab.start()
    for row in range(0, rows, 2):
        at = slice(row * cols, (row + 2) * cols)
        values = slab[row : row + 2].astype(F32).reshape(2 * cols, width)
        normed_one[at] = (values * rms_scale(values)).astype(BF16)
    total[...] = slab[1 : rows - 1].astype(F32).reshape((rows - 2) * cols, width)
    column = lax.broadcasted_iota(jnp.int32, (cols, LANES), 0)

    def step(index, carry):
        @pl.when(index + 1 < chunks)
        def _():
            fetch_expand(index + 1).start()
            fetch_project(index + 1).start()

        fetch_expand(index).wait()
        weights = expand[:, chunk_lanes(index)]
        for row in range(0, rows, GROUP_FORWARD):
            product = nn_dot(normed_one[row * cols : (row + GROUP_FORWARD) * cols, :], weights)
            for inner in range(GROUP_FORWARD):
                for lane in range(0, CHUNK, LANES):
                    lanes = slice(lane, lane + LANES)
                    values = product[inner * cols : (inner + 1) * cols, lanes]
                    hidden[row + inner, :, lanes] = gelu(values).astype(BF16).astype(F32)
                    if RIM <= row + inner < RIM + own:
                        expanded[row + inner - RIM, :, chunk_lanes(index, lane, LANES)] = values.astype(BF16)
        store_expanded(index).start()

        for lane in range(0, CHUNK, LANES):
            lanes = slice(lane, lane + LANES)
            taps = spread_taps(taps_ref, chunk_lanes(index, lane, LANES), cols)
            for row in range(rows - 2):
                rows_near = [hidden[row + a, :, lanes] for a in range(3)]
                sums = [
                    taps[b] * rows_near[0] + taps[3 + b] * rows_near[1] + taps[6 + b] * rows_near[2] for b in range(3)
                ]
                values = column_sums(sums[0], sums[1], sums[2], column, cols - 1)
                hidden_two[row * cols : (row + 1) * cols, lanes] = gelu(values).astype(BF16)
                mixed[row, :, chunk_lanes(index, lane, LANES)] = values.astype(BF16)
        store_mixed(index).start()
        fetch_project(index).wait()
        total[...] += nn_dot(hidden_two[...], project[chunk_lanes(index), :])
        return carry

    lax.fori_loop(0, chunks, step, 0)
    for row in range(1, own + 1):
        first = total[row * cols : (row + 1) * cols]
        normed[row - 1] = (first * rms_scale(first)).astype(BF16)
    store_normed = pltpu.make_async_copy(normed, normed_ref, out_sems.at[1])
    store_above = pltpu.make_async_copy(total.at[pl.ds(0, cols)], first_ref.at[pl.ds(0, cols)], out_sems.at[2])
    store_below = pltpu.make_async_copy(
        total.at[pl.ds((own + 1) * cols, cols)], first_ref.at[pl.ds(cols, cols)], out_sems.at[3]
    )
    store_own = pltpu.make_async_copy(total.at[pl.ds(cols, own * cols)], own_first_ref, out_sems.at[4])
    store_normed.start()
    store_above.start()
    store_below.start()
    store_own.start()
    for index in range(chunks):
        store_expanded(index).wait()
        store_mixed(index).wait()
    store_slab.wait()
    store_normed.wait()
    store_above.wait()
    store_below.wait()
    store_own.wait()


def forward(bands, features, other, rim, w_expand, kernel, w_project):
    capacity, cols, width = features.shape
    own, rows = GRID_ROWS, GRID_ROWS + 2 * RIM
    hidden_width = w_expand.shape[1]
    chunks = hidden_width // CHUNK
    return pl.pallas_call(
        forward_body,
        in_specs=[in_scalars(), in_hbm(), in_vmem(), in_vmem(), in_hbm(), in_vmem(), in_hbm()],
        out_specs=[in_hbm()] * 6,
        out_shape=[
            pltpu.HBM((2 * cols, width), F32),
            pltpu.HBM((own * cols, width), F32),
            pltpu.HBM((own, cols, width), BF16),
            pltpu.HBM((own, cols, width), BF16),
            pltpu.HBM((own, cols, hidden_width), BF16),
            pltpu.HBM((rows - 2, cols, hidden_width), BF16),
        ],
        scratch_shapes=[
            pltpu.VMEM((rows, cols, width), BF16),
            pltpu.VMEM((rows * cols, width), BF16),
            pltpu.VMEM((width, hidden_width), BF16),
            pltpu.VMEM((hidden_width, width), BF16),
            pltpu.VMEM((own, cols, hidden_width), BF16),
            pltpu.VMEM((rows, cols, CHUNK), F32),
            pltpu.VMEM((rows - 2, cols, hidden_width), BF16),
            pltpu.VMEM(((rows - 2) * cols, CHUNK), BF16),
            pltpu.VMEM(((rows - 2) * cols, width), F32),
            pltpu.VMEM((own, cols, width), BF16),
            pltpu.SemaphoreType.DMA((4,)),
            pltpu.SemaphoreType.DMA((2, chunks)),
            pltpu.SemaphoreType.DMA((2, chunks)),
            pltpu.SemaphoreType.DMA((5,)),
        ],
        compiler_params=params(24),
        cost_estimate=pl.CostEstimate(
            flops=16 * 10**9,
            bytes_accessed=48 * MIB,
            transcendentals=2 * rows * cols * hidden_width,
        ),
        name="bottleneck_forward",
    )(bands, held(features), near(other), near(rim), held(w_expand), near(kernel), held(w_project))


def slopes_body(expanded_ref, mixed_ref, slope_one_ref, slope_two_ref):
    for source, target in ((expanded_ref, slope_one_ref), (mixed_ref, slope_two_ref)):
        rows, _, chunk = source.shape
        for row in range(rows):
            for lane in range(0, chunk, LANES):
                lanes = slice(lane, lane + LANES)
                target[row, :, lanes] = gelu_slope(source[row, :, lanes].astype(F32)).astype(BF16)


def slopes(expanded, mixed):
    hidden_width = expanded.shape[2]
    blocks = [
        pl.BlockSpec(values.shape[:2] + (CHUNK,), lambda j: (0, 0, j)) for values in (expanded, mixed)
    ]
    return pl.pallas_call(
        slopes_body,
        grid=(hidden_width // CHUNK,),
        in_specs=blocks,
        out_specs=blocks,
        out_shape=[jax.ShapeDtypeStruct(values.shape, BF16) for values in (expanded, mixed)],
        compiler_params=params(),
        cost_estimate=pl.CostEstimate(
            flops=15 * (expanded.size + mixed.size),
            bytes_accessed=6 * (expanded.size + mixed.size),
            transcendentals=expanded.size + mixed.size,
        ),
        name="gelu_slopes",
    )(expanded, mixed)


def lane_tiles(width):
    return [slice(at, at + LANES) for at in range(0, width, LANES)]


def window_places(own, cols):
    return [(r, q) for r in range(own) for q in range(cols // 8)]


def to_windows(source_ref, rows_wide, target):
    groups, own, cols, width = source_ref.shape
    span = groups * 8
    for tile, lanes in enumerate(lane_tiles(width)):
        for group in range(groups):
            rows_wide[tile, group] = source_ref[group, :, :, lanes].astype(F32)
        for index, (r, q) in enumerate(window_places(own, cols)):
            pieces = [
                rows_wide[tile, group, r, pl.ds(q, 8, stride=cols // 8), :] for group in range(groups)
            ]
            rows = slice(index * span, (index + 1) * span)
            target[rows, lanes] = jnp.concatenate(pieces, axis=0).astype(BF16)


def to_rows(values, rows_wide, target_ref):
    groups, own, cols, width = target_ref.shape
    span = groups * 8
    for tile, lanes in enumerate(lane_tiles(width)):
        for index, (r, q) in enumerate(window_places(own, cols)):
            for group in range(groups):
                first = index * span + group * 8
                rows_wide[tile, group, r, pl.ds(q, 8, stride=cols // 8), :] = values[first : first + 8, lanes]
        for group in range(groups):
            target_ref[group, :, :, lanes] = rows_wide[tile, group].astype(BF16)


def wide_scratch(shape):
    groups, own, cols, width = shape
    return pltpu.VMEM((width // LANES, groups, own, cols, LANES), F32)


def grad_attended_body(cotangent_ref, out_ref, grad_ref, rows_wide, in_windows):
    to_windows(cotangent_ref, rows_wide, in_windows)
    grad_ref[...] = nt_dot(in_windows[...], out_ref[...]).astype(BF16)


def attended_gradient(cotangent, w_out):
    groups, own, cols, width = cotangent.shape
    shape = (groups * own * cols, width)
    return pl.pallas_call(
        grad_attended_body,
        grid=(1,),
        in_specs=[whole(cotangent.shape), whole(w_out.shape)],
        out_specs=whole(shape),
        out_shape=jax.ShapeDtypeStruct(shape, BF16),
        scratch_shapes=[wide_scratch(cotangent.shape), pltpu.VMEM(shape, BF16)],
        compiler_params=params(),
        cost_estimate=pl.CostEstimate(
            flops=2 * shape[0] * width * width, bytes_accessed=2 * 1024 * 1024, transcendentals=0
        ),
        name="attended_gradient",
    )(cotangent, w_out)


def per_query(values, weights, span, head_dim, scale=1.0):
    wide = nn_dot(values.T, weights)
    half = LANES // 2
    own = jnp.concatenate([wide[:half, :LANES], wide[half:, LANES:]], axis=0) * scale
    own = own.astype(BF16).T
    lane_head = lax.broadcasted_iota(jnp.int32, (span, LANES), 1) // head_dim
    return jnp.where(lane_head % 2 == 0, own[:span].astype(F32), own[span:].astype(F32)).astype(BF16)


def attention_body(normed_ref, grad_attended_ref, qkv_ref, grad_ref, weights_ref, values_ref, rows_wide,
                   in_windows, projected, grad_projected, grad_attended, qkv, grad, weights, in_sems, out_sems):
    groups, own, cols, width = normed_ref.shape
    span = groups * 8
    windows = own * cols // 8
    head_dim = width // HEADS
    heads = LANES // head_dim
    scale = 1.0 / math.sqrt(head_dim)
    steepness = scale * math.log2(math.e)

    fetch_qkv = pltpu.make_async_copy(qkv_ref, qkv, in_sems.at[0])
    fetch_grad = pltpu.make_async_copy(grad_attended_ref, grad_attended, in_sems.at[1])
    fetch_qkv.start()
    fetch_grad.start()
    to_windows(normed_ref, rows_wide, in_windows)
    fetch_qkv.wait()
    projected[...] = nn_dot(in_windows[...], qkv[...]).astype(BF16)
    store_values = pltpu.make_async_copy(projected.at[:, pl.ds(2 * width, width)], values_ref, out_sems.at[0])
    store_values.start()
    fetch_grad.wait()

    row_head = lax.broadcasted_iota(jnp.int32, (heads * span, LANES), 0) // span
    lane_head = lax.broadcasted_iota(jnp.int32, (heads * span, LANES), 1) // head_dim
    mask = (row_head == lane_head).astype(F32).astype(BF16)

    def spread(values):
        return jnp.concatenate([values] * heads, axis=0) * mask

    def window(index, carry):
        rows = pl.ds(pl.multiple_of(index * span, span), span)
        for part in range(width // LANES):
            q_at, k_at, v_at = (
                slice(t * width + part * LANES, t * width + (part + 1) * LANES) for t in range(3)
            )
            q, k, v = projected[rows, q_at], projected[rows, k_at], projected[rows, v_at]
            q_wide = spread(q)
            g_wide = spread(grad_attended[rows, q_at])
            scores = nt_dot(k, q_wide)
            powers = jnp.exp2((scores - jnp.max(scores, axis=0, keepdims=True)) * steepness)
            shares = powers * (1.0 / jnp.sum(powers, axis=0, keepdims=True))
            half = shares.astype(BF16)
            weights[index, :, part * heads * span : (part + 1) * heads * span] = half
            grad_weights = nt_dot(v, g_wide)
            row_dot = jnp.sum(shares * grad_weights, axis=0, keepdims=True)
            grad_scores = (shares * (grad_weights - row_dot)).astype(BF16)
            grad_projected[rows, q_at] = per_query(k, grad_scores, span, head_dim, scale)
            grad_projected[rows, k_at] = (nn_dot(grad_scores, q_wide) * scale).astype(BF16)
            grad_projected[rows, v_at] = nn_dot(half, g_wide).astype(BF16)
        return carry

    lax.fori_loop(0, windows, window, 0, unroll=4)
    store_weights = pltpu.make_async_copy(weights, weights_ref, out_sems.at[1])
    store_weights.start()
    to_rows(nt_dot(grad_projected[...], qkv[...]), rows_wide, grad)
    store_grad = pltpu.make_async_copy(grad, grad_ref, out_sems.at[2])
    store_grad.start()
    store_values.wait()
    store_weights.wait()
    store_grad.wait()


def attention(normed, grad_attended, w_qkv):
    groups, own, cols, width = normed.shape
    span = groups * 8
    tokens = groups * own * cols
    out_shapes = [normed.shape, (tokens // span, span, HEADS * span), (tokens, width)]
    return pl.pallas_call(
        attention_body,
        in_specs=[in_vmem(), in_hbm(), in_hbm()],
        out_specs=[in_hbm()] * 3,
        out_shape=[pltpu.HBM(shape, BF16) for shape in out_shapes],
        scratch_shapes=[
            wide_scratch(normed.shape),
            pltpu.VMEM((tokens, width), BF16),
            pltpu.VMEM((tokens, 3 * width), BF16),
            pltpu.VMEM((tokens, 3 * width), BF16),
            pltpu.VMEM((tokens, width), BF16),
            pltpu.VMEM(w_qkv.shape, BF16),
            pltpu.VMEM(normed.shape, BF16),
            pltpu.VMEM(out_shapes[1], BF16),
            pltpu.SemaphoreType.DMA((2,)),
            pltpu.SemaphoreType.DMA((3,)),
        ],
        compiler_params=params(18),
        cost_estimate=pl.CostEstimate(
            flops=16 * tokens * width * width,
            bytes_accessed=4 * 1024 * 1024,
            transcendentals=tokens * span * HEADS,
        ),
        name="window_attention",
    )(near(normed), held(grad_attended), held(w_qkv))


def attended_body(weights_ref, values_ref, out_ref, added_ref, rows_wide, attended):
    windows, span, wide = weights_ref.shape
    width = values_ref.shape[1]
    heads = LANES * HEADS // width
    for index in range(windows):
        rows = slice(index * span, (index + 1) * span)
        for part, lanes in enumerate(lane_tiles(width)):
            weights = weights_ref[index, :, part * heads * span : (part + 1) * heads * span]
            attended[rows, lanes] = per_query(values_ref[rows, lanes], weights, span, width // HEADS)
    to_rows(nn_dot(attended[...], out_ref[...]), rows_wide, added_ref)


def attend(weights, values, w_out, shape):
    return pl.pallas_call(
        attended_body,
        grid=(1,),
        in_specs=[whole(weights.shape), whole(values.shape), whole(w_out.shape)],
        out_specs=whole(shape),
        out_shape=jax.ShapeDtypeStruct(shape, BF16),
        scratch_shapes=[wide_scratch(shape), pltpu.VMEM(values.shape, BF16)],
        compiler_params=params(),
        cost_estimate=pl.CostEstimate(
            flops=4 * values.size * values.shape[1], bytes_accessed=3 * 1024 * 1024, transcendentals=0
        ),
        name="attended_output",
    )(weights, values, w_out)


def backward_body(bands_ref, cotangent_ref, other_ref, rim_ref, slab_ref, first_ref, edges_ref, grad_slab_ref,
                  grad_ref, pair_ref, next_ref, slope_one_ref, slope_two_ref, expand_ref, taps_ref, project_ref,
                  out_ref, rims, slab, first, edges, grad_slab, grad_in, slope_one, slope_two, expand, project,
                  grad_first, grad_rows, mixed, expanded, total, row_sems,
                  in_sems, chunk_sems):
    own, cols, width = slab.shape
    chunks = expand_ref.shape[1] // CHUNK

    sources = (cotangent_ref, other_ref, rim_ref)
    sides = list(enumerate((-1, own)))
    for side, place_first in sides:
        start_pull(bands_ref, place_first, sources, 1, rims.at[pl.ds(side, 1)], row_sems.at[side], RIM)
    inputs = [
        pltpu.make_async_copy(source, target, in_sems.at[index])
        for index, (source, target) in enumerate(
            ((first_ref, first), (grad_ref, grad_in), (grad_slab_ref, grad_slab), (edges_ref, edges), (slab_ref, slab))
        )
    ]
    for copy in inputs:
        copy.start()

    def fetches(index):
        lanes = chunk_lanes(index)
        pairs = (
            (project_ref.at[lanes], project.at[lanes]),
            (slope_two_ref.at[:, :, lanes], slope_two.at[:, :, lanes]),
            (slope_one_ref.at[:, :, lanes], slope_one.at[:, :, lanes]),
            (expand_ref.at[:, lanes], expand.at[:, lanes]),
        )
        return [
            pltpu.make_async_copy(source, target, chunk_sems.at[number, index])
            for number, (source, target) in enumerate(pairs)
        ]

    for copy in fetches(0):
        copy.start()

    def through_norm(cotangent, grad, first):
        rms = rms_scale(first)
        normed = first * rms
        grad = grad.astype(F32)
        inner = jnp.mean(grad * normed, -1, keepdims=True)
        return cotangent.astype(F32) + rms * (grad - normed * inner)

    for copy in inputs[:4]:
        copy.wait()
    for row in range(own):
        at = slice(row * cols, (row + 1) * cols)
        result = through_norm(grad_slab[row], grad_in[row], first[at])
        grad_first[at] = result
        grad_rows[(row + 1) * cols : (row + 2) * cols] = result.astype(BF16)
    for side, place_first in sides:
        wait_pull(sources, 1, rims.at[pl.ds(side, 1)], row_sems.at[side])
    leads = lax.rem(lax.axis_index("row"), 2) == 0
    above = jnp.where(leads, next_ref[0].astype(F32), pair_ref[0].astype(F32))
    below = jnp.where(leads, pair_ref[0].astype(F32), next_ref[0].astype(F32))
    last = (own + 1) * cols
    grad_rows[0:cols] = through_norm(rims[0], above, edges[:cols]).astype(BF16)
    grad_rows[last:] = through_norm(rims[1], below, edges[cols:]).astype(BF16)
    column = lax.broadcasted_iota(jnp.int32, (cols, LANES), 0)

    total[...] = jnp.zeros_like(total)

    def step(index, carry):
        @pl.when(index + 1 < chunks)
        def _():
            for copy in fetches(index + 1):
                copy.start()

        for copy in fetches(index):
            copy.wait()
        weights = project[chunk_lanes(index), :]
        for row in range(0, own + 2, GROUP_BACKWARD):
            product = nt_dot(grad_rows[row * cols : (row + GROUP_BACKWARD) * cols, :], weights)
            for inner in range(GROUP_BACKWARD):
                for lane in range(0, CHUNK, LANES):
                    lanes = slice(lane, lane + LANES)
                    slope = slope_two[row + inner, :, chunk_lanes(index, lane, LANES)].astype(F32)
                    value = product[inner * cols : (inner + 1) * cols, lanes] * slope
                    mixed[row + inner, :, lanes] = value.astype(BF16).astype(F32)

        for lane in range(0, CHUNK, LANES):
            lanes = slice(lane, lane + LANES)
            taps = spread_taps(taps_ref, chunk_lanes(index, lane, LANES), cols)
            for row in range(own):
                rows_near = [mixed[row + a, :, lanes] for a in range(3)]
                sums = [
                    taps[8 - b] * rows_near[0] + taps[5 - b] * rows_near[1] + taps[2 - b] * rows_near[2]
                    for b in range(3)
                ]
                value = column_sums(sums[0], sums[1], sums[2], column, cols - 1)
                value = value * slope_one[row, :, chunk_lanes(index, lane, LANES)].astype(F32)
                expanded[row * cols : (row + 1) * cols, lanes] = value.astype(BF16)
        total[...] += nt_dot(expanded[...], expand[:, chunk_lanes(index)])
        return carry

    lax.fori_loop(0, chunks, step, 0)
    inputs[4].wait()
    for row in range(own):
        at = slice(row * cols, (row + 1) * cols)
        values = slab[row].astype(F32)
        rms = rms_scale(values)
        normed = values * rms
        grad = total[at]
        inner = jnp.mean(grad * normed, -1, keepdims=True)
        out_ref[row] = (grad_first[at] + rms * (grad - normed * inner)).astype(BF16)


def backward(bands, cotangent, other, rim, slab, first, edges, grad_slab, grad, pair_row, next_row, slope_one,
             slope_two, w_expand, kernel, w_project):
    own, cols, width = slab.shape
    hidden_width = w_expand.shape[1]
    chunks = hidden_width // CHUNK
    return pl.pallas_call(
        backward_body,
        in_specs=[in_scalars()] + [in_hbm()] * 8 + [in_vmem()] * 2 + [in_hbm()] * 3 + [in_vmem(), in_hbm()],
        out_specs=in_vmem(),
        out_shape=jax.ShapeDtypeStruct((own, cols, width), BF16),
        scratch_shapes=[
            pltpu.VMEM((2, cols, width), BF16),
            pltpu.VMEM((own, cols, width), BF16),
            pltpu.VMEM((own * cols, width), F32),
            pltpu.VMEM((2 * cols, width), F32),
            pltpu.VMEM((own, cols, width), BF16),
            pltpu.VMEM((own, cols, width), BF16),
            pltpu.VMEM((own, cols, hidden_width), BF16),
            pltpu.VMEM((own + 2, cols, hidden_width), BF16),
            pltpu.VMEM((width, hidden_width), BF16),
            pltpu.VMEM((hidden_width, width), BF16),
            pltpu.VMEM((own * cols, width), F32),
            pltpu.VMEM(((own + 2) * cols, width), BF16),
            pltpu.VMEM((own + 2, cols, CHUNK), F32),
            pltpu.VMEM((own * cols, CHUNK), BF16),
            pltpu.VMEM((own * cols, width), F32),
            pltpu.SemaphoreType.DMA((2,)),
            pltpu.SemaphoreType.DMA((5,)),
            pltpu.SemaphoreType.DMA((4, chunks)),
        ],
        compiler_params=params(26),
        cost_estimate=pl.CostEstimate(
            flops=16 * 10**9,
            bytes_accessed=48 * MIB,
            transcendentals=0,
        ),
        name="bottleneck_backward",
    )(bands, held(cotangent), held(other), held(rim), held(slab), held(first), held(edges), held(grad_slab), held(grad),
      near(pair_row), near(next_row), held(slope_one), held(slope_two), held(w_expand), near(kernel),
      held(w_project))


def window_groups(size):
    stride = size // 8
    return [[first + stride * k for k in range(8)] for first in range(stride)]


def exchange_windows(rows):
    groups = window_groups(lax.axis_size("row"))
    return lax.all_to_all(
        rows, "row", split_axis=0, concat_axis=0, tiled=True, axis_index_groups=groups
    )


def swap_pair(rows):
    size = lax.axis_size("row")
    return lax.ppermute(rows, "row", [(i, i ^ 1) for i in range(size)])


def swap_next(rows):
    size = lax.axis_size("row")
    pairs = [(i, i + 1) for i in range(1, size - 1, 2)]
    return lax.ppermute(rows, "row", pairs + [(j, i) for i, j in pairs])


def place_rows(even, other, leads, leader_share):
    size = GRID_ROWS
    first, second = even[:BAND], even[BAND:]
    share = jnp.where(leads, leader_share, 2 * size - leader_share)
    zeros = jnp.zeros_like(first)
    low = jnp.where(leads | (share == size), first, jnp.where(share < size, second, other))
    mid = jnp.where(share < size, zeros, jnp.where(leads | (share == size), second, first))
    high = jnp.where(share > size, jnp.where(leads, other, second), zeros)
    return jnp.concatenate([low, mid, high], 0)


def on_device(features, row_bands, w_expand, kernel, w_project, w_qkv, w_out, cotangent):
    capacity, cols, width = features.shape
    device = lax.axis_index("row")
    parity = device % 2
    leads = parity == 0

    rim = swap_next(rim_rows(row_bands, features, cotangent))
    other_cotangent = swap_pair(cotangent)
    other_features = swap_pair(features)
    grad_slab = even_rows(row_bands, cotangent, other_cotangent)

    grad_windows = exchange_windows(grad_slab)
    edges, first, normed, slab, expanded, mixed = forward(
        row_bands, features, other_features, rim, w_expand, kernel, w_project
    )
    normed, grad_windows = lax.optimization_barrier((normed, grad_windows))
    normed_windows = exchange_windows(normed)
    shape = (8, GRID_ROWS // 8, cols, width)
    slope_one, slope_two = slopes(expanded, mixed)
    grad_attended = attended_gradient(grad_windows.reshape(shape), w_out)
    normed_windows, slope_one, slope_two, grad_attended = lax.optimization_barrier(
        (normed_windows, slope_one, slope_two, grad_attended)
    )
    grad_normed, weights, values = attention(normed_windows.reshape(shape), grad_attended, w_qkv)
    grad_rows = exchange_windows(grad_normed.reshape(GRID_ROWS, cols, width))
    added = attend(weights, values, w_out, shape)
    leader_share = BAND * row_bands[device - parity]
    grad_rows, added, leader_share = lax.optimization_barrier((grad_rows, added, leader_share))
    top, bottom = grad_rows[:1], grad_rows[GRID_ROWS - 1 :]
    sent_next, sent_pair = jnp.where(leads, top, bottom), jnp.where(leads, bottom, top)
    added, sent_next, sent_pair = lax.optimization_barrier((added, sent_next, sent_pair))
    next_row, pair_row = swap_next(sent_next), swap_pair(sent_pair)
    added_rows = exchange_windows(added.reshape(GRID_ROWS, cols, width))
    grad_input = backward(
        row_bands, cotangent, other_cotangent, rim, slab, first, edges, grad_slab, grad_rows, pair_row, next_row,
        slope_one, slope_two, w_expand, kernel, w_project,
    )
    def sent(rows):
        return jnp.where(leads, rows[BAND:], rows[:BAND])

    other_grad = swap_pair(sent(grad_input))
    grad_input, added_rows = lax.optimization_barrier((grad_input, added_rows))
    final = (first.reshape(GRID_ROWS, cols, width) + added_rows.astype(F32)).astype(BF16)
    other_final = swap_pair(sent(final))
    return (
        place_rows(final, other_final, leads, leader_share),
        place_rows(grad_input, other_grad, leads, leader_share),
    )


def solution(mesh):
    return jax.shard_map(
        on_device,
        mesh=mesh,
        in_specs=(
            P(("parts", "row"), None, None),
            P("parts"),
            P(),
            P(),
            P(),
            P(),
            P(),
            P(("parts", "row"), None, None),
        ),
        out_specs=(P(("parts", "row"), None, None), P(("parts", "row"), None, None)),
        check_vma=False,
    )
```

```python
import math

import jax
import jax.numpy as jnp
from jax import lax
from jax.experimental import pallas as pl
from jax.experimental.pallas import tpu as pltpu
from jax.sharding import PartitionSpec as P

HEADS = 16
GRID_ROWS = 16
BAND = 8
RIM = 2
EPSILON = 1e-06
CHUNK = 512
WIDE = 256
GROUP_BACKWARD = 9
LANES = 128
ROOT = math.sqrt(2.0 / math.pi)
CUBIC = 0.044715
F32 = jnp.float32
BF16 = jnp.bfloat16
MIB = 1024 * 1024


def nt_dot(left, right):
    return lax.dot_general(left, right, (((1,), (1,)), ((), ())), preferred_element_type=F32)


def tn_dot(left, right):
    return lax.dot_general(left, right, (((0,), (0,)), ((), ())), preferred_element_type=F32)


def nn_dot(left, right):
    return jnp.dot(left, right, preferred_element_type=F32)


def rms_scale(values):
    return lax.rsqrt(jnp.mean(values * values, -1, keepdims=True) + EPSILON)


def gelu_parts(v):
    square = v * v
    cdf = 0.5 + 0.5 * jnp.tanh(v * (ROOT + (ROOT * CUBIC) * square))
    return square, cdf, v * cdf


def gelu(v):
    return gelu_parts(v)[2]


def gelu_slope(v):
    square, cdf, value = gelu_parts(v)
    return cdf + (value - value * cdf) * (2.0 * ROOT + (6.0 * ROOT * CUBIC) * square)


def whole(shape, space=None):
    zeros = (0,) * len(shape)
    return pl.BlockSpec(shape, lambda *_: zeros)


def params(mebibytes=56):
    return pltpu.CompilerParams(vmem_limit_bytes=mebibytes * MIB)


def in_vmem():
    return pl.BlockSpec(memory_space=pltpu.VMEM)


def in_hbm():
    return pl.BlockSpec(memory_space=pltpu.HBM)


def held(array):
    return pltpu.with_memory_space_constraint(array, pltpu.HBM)


def near(array):
    return pltpu.with_memory_space_constraint(array, pltpu.VMEM)


def in_scalars():
    return pl.BlockSpec(memory_space=pltpu.SMEM)


def shares(bands_ref):
    device = lax.axis_index("row")
    parity = lax.rem(device, 2)
    return parity, BAND * bands_ref[device - parity], BAND * bands_ref[device]


def place(bands_ref, first):
    parity, leader_share, _ = shares(bands_ref)
    row = first + GRID_ROWS * parity
    beyond = (row < 0) | (row >= 2 * GRID_ROWS)
    in_leader = row < leader_share
    in_own = in_leader == (parity == 0)
    source = jnp.where(beyond, 2, jnp.where(in_own, 0, 1))
    return source, jnp.where(beyond, 0, jnp.where(in_leader, row, row - leader_share))


def start_pull(bands_ref, first, sources, rows, target, sem, rim_row=0):
    where, row = place(bands_ref, first)
    row = jnp.where(where == 2, rim_row, row)
    for number, source in enumerate(sources):

        @pl.when(where == number)
        def _():
            pltpu.make_async_copy(source.at[pl.ds(row, rows)], target, sem).start()


def wait_pull(sources, rows, target, sem):
    pltpu.make_async_copy(sources[0].at[pl.ds(0, rows)], target, sem).wait()


def even_body(bands_ref, own_ref, other_ref, out_ref):
    for half in range(2):
        where, row = place(bands_ref, BAND * half)
        for number, source in enumerate((own_ref, other_ref)):

            @pl.when(where == number)
            def _():
                out_ref[BAND * half : BAND * half + BAND] = source[pl.ds(row, BAND)]


def even_rows(bands, own, other):
    shape = (GRID_ROWS,) + own.shape[1:]
    return pl.pallas_call(
        even_body,
        in_specs=[in_scalars(), in_vmem(), in_vmem()],
        out_specs=in_vmem(),
        out_shape=jax.ShapeDtypeStruct(shape, own.dtype),
        compiler_params=params(8),
        name="even_rows",
    )(bands, near(own), near(other))


def rim_body(bands_ref, features_ref, cotangent_ref, out_ref, bands, choices, sems):
    fetch_bands = pltpu.make_async_copy(bands_ref, bands, sems.at[0])
    fetch_bands.start()
    copies = []
    for choice in range(4):
        first = max(0, BAND * choice - RIM)
        second = max(0, BAND * choice - 1)
        copies.append(
            pltpu.make_async_copy(
                features_ref.at[pl.ds(first, RIM)], choices.at[choice, pl.ds(0, RIM)], sems.at[1 + choice]
            )
        )
        copies.append(
            pltpu.make_async_copy(
                cotangent_ref.at[pl.ds(second, 1)], choices.at[choice, pl.ds(RIM, 1)], sems.at[5 + choice]
            )
        )
    for copy in copies:
        copy.start()
    fetch_bands.wait()
    device = lax.axis_index("row")
    choice = jnp.where(lax.rem(device, 2) == 0, 0, bands[device])
    for copy in copies:
        copy.wait()
    out_ref[...] = choices[choice]


def rim_rows(bands, features, cotangent):
    shape = (RIM + 1,) + features.shape[1:]
    return pl.pallas_call(
        rim_body,
        in_specs=[in_hbm(), in_hbm(), in_hbm()],
        out_specs=in_vmem(),
        out_shape=jax.ShapeDtypeStruct(shape, features.dtype),
        scratch_shapes=[
            pltpu.SMEM(bands.shape, bands.dtype),
            pltpu.VMEM((4,) + shape, features.dtype),
            pltpu.SemaphoreType.DMA((9,)),
        ],
        compiler_params=params(8),
        name="rim_rows",
    )(held(bands), held(features), held(cotangent))


def column_sums(left, mid, right, column, last):
    from_left = jnp.where(column == 0, 0.0, pltpu.roll(left, 1, 0))
    from_right = jnp.where(column == last, 0.0, pltpu.roll(right, last, 0))
    return mid + from_left + from_right


def spread_taps(taps_ref, lanes, cols):
    taps = taps_ref[:, lanes].astype(F32)
    return [jnp.broadcast_to(taps[i : i + 1], (cols, LANES)) for i in range(9)]


def chunk_lanes(index, lane=0, count=CHUNK):
    return pl.ds(pl.multiple_of(index * CHUNK + lane, LANES), count)


def forward_body(bands_ref, features_ref, other_ref, rim_ref, expand_ref, taps_ref, project_ref, first_ref,
                 own_first_ref, normed_ref, slab_ref, expanded_ref, mixed_ref, slab, normed_one, expand, project,
                 expanded, hidden_a, hidden_b, mixed, two_a, two_b, total, normed, row_sems,
                 weight_sems, chunk_sems, out_sems):
    rows, cols, width = slab.shape
    own = rows - 2 * RIM
    chunks = expand_ref.shape[1] // CHUNK

    sources = (features_ref, other_ref, rim_ref)
    pieces = [(0, RIM), (RIM, BAND), (RIM + BAND, BAND), (RIM + 2 * BAND, RIM)]
    for index, (first, count) in enumerate(pieces):
        start_pull(bands_ref, first - RIM, sources, count, slab.at[pl.ds(first, count)], row_sems.at[index])

    def fetch_expand(index):
        lanes = chunk_lanes(index)
        return pltpu.make_async_copy(expand_ref.at[:, lanes], expand.at[:, lanes], weight_sems.at[0, index])

    def fetch_project(index):
        lanes = chunk_lanes(index)
        return pltpu.make_async_copy(project_ref.at[lanes], project.at[lanes], weight_sems.at[1, index])

    def store_expanded(index):
        lanes = chunk_lanes(index)
        return pltpu.make_async_copy(
            expanded.at[:, :, lanes], expanded_ref.at[:, :, lanes], chunk_sems.at[0, index]
        )

    def store_mixed(index):
        lanes = chunk_lanes(index)
        return pltpu.make_async_copy(mixed.at[:, :, lanes], mixed_ref.at[:, :, lanes], chunk_sems.at[1, index])

    fetch_expand(0).start()
    fetch_expand(1).start()
    fetch_project(0).start()
    for index, (first, count) in enumerate(pieces):
        wait_pull(sources, count, slab.at[pl.ds(first, count)], row_sems.at[index])
    store_slab = pltpu.make_async_copy(slab.at[pl.ds(RIM, own)], slab_ref, out_sems.at[0])
    store_slab.start()
    for row in range(0, rows, 2):
        at = slice(row * cols, (row + 2) * cols)
        values = slab[row : row + 2].astype(F32).reshape(2 * cols, width)
        normed_one[at] = (values * rms_scale(values)).astype(BF16)
    total[...] = slab[1 : rows - 1].astype(F32).reshape((rows - 2) * cols, width)
    column = lax.broadcasted_iota(jnp.int32, (cols, LANES), 0)

    def expand_piece(chunk, hidden, row, lane):
        weights = expand[:, chunk_lanes(jnp.minimum(chunk, chunks - 1), lane, WIDE)]
        product = nn_dot(normed_one[row * cols : (row + 4) * cols, :], weights)
        for inner in range(4):
            for at in range(0, WIDE, LANES):
                values = product[inner * cols : (inner + 1) * cols, at : at + LANES]
                lanes = slice(lane + at, lane + at + LANES)
                hidden[row + inner, :, lanes] = gelu(values).astype(BF16).astype(F32)
                if RIM <= row + inner < RIM + own:
                    expanded[row + inner - RIM, :, chunk_lanes(chunk, lane + at, LANES)] = values.astype(BF16)

    def project_piece(chunk, hidden_two, row, lane):
        at = slice(row * cols, (row + 6) * cols)
        weights = project[pl.ds(pl.multiple_of(chunk * CHUNK, CHUNK), CHUNK), lane : lane + WIDE]
        total[at, lane : lane + WIDE] += nn_dot(hidden_two[at, :], weights)

    def mix_piece(chunk, hidden, hidden_two, taps, row, lane):
        lanes = slice(lane, lane + LANES)
        rows_near = [hidden[row + a, :, lanes] for a in range(3)]
        sums = [
            taps[b] * rows_near[0] + taps[3 + b] * rows_near[1] + taps[6 + b] * rows_near[2] for b in range(3)
        ]
        values = column_sums(sums[0], sums[1], sums[2], column, cols - 1)
        hidden_two[row * cols : (row + 1) * cols, lanes] = gelu(values).astype(BF16)
        mixed[row, :, chunk_lanes(chunk, lane, LANES)] = values.astype(BF16)

    expand_places = [(row, lane) for lane in range(0, CHUNK, WIDE) for row in range(0, rows, 4)]
    project_places = [(row, lane) for lane in range(0, width, WIDE) for row in range(0, rows - 2, 6)]

    def stage(chunk, hidden, hidden_two, next_hidden, last_two):
        products = [lambda at=at: expand_piece(chunk + 1, next_hidden, *at) for at in expand_places]
        for number, at in enumerate(project_places):
            piece = lambda at=at: project_piece(jnp.maximum(chunk - 1, 0), last_two, *at)
            products.insert(min(3 * number, len(products)), piece)
        pieces = [(row, lane) for lane in range(0, CHUNK, LANES) for row in range(rows - 2)]
        done = 0
        for number, (row, lane) in enumerate(pieces):
            if number % (rows - 2) == 0:
                taps = spread_taps(taps_ref, chunk_lanes(chunk, lane, LANES), cols)
            while done * len(pieces) <= number * len(products) and done < len(products):
                products[done]()
                done += 1
            mix_piece(chunk, hidden, hidden_two, taps, row, lane)
        for piece in products[done:]:
            piece()

    def store_chunk(chunk):
        store_expanded(chunk).start()
        store_mixed(chunk).start()

    def step(index, carry):
        even = 2 * index

        @pl.when(index > 0)
        def _():
            fetch_project(even - 1).wait()

        fetch_expand(even + 1).wait()

        @pl.when(index + 1 < chunks // 2)
        def _():
            fetch_expand(even + 2).start()

        fetch_project(even + 1).start()
        stage(even, hidden_a, two_a, hidden_b, two_b)
        store_chunk(even)
        fetch_project(even).wait()

        @pl.when(index + 1 < chunks // 2)
        def _():
            fetch_expand(even + 2).wait()
            fetch_expand(even + 3).start()
            fetch_project(even + 2).start()

        stage(even + 1, hidden_b, two_b, hidden_a, two_a)
        store_chunk(even + 1)
        return carry

    two_b[...] = jnp.zeros_like(two_b)
    fetch_expand(0).wait()
    for row, lane in expand_places:
        expand_piece(0, hidden_a, row, lane)
    lax.fori_loop(0, chunks // 2, step, 0)
    fetch_project(chunks - 1).wait()
    total[...] += nn_dot(two_b[...], project[pl.ds((chunks - 1) * CHUNK, CHUNK), :])
    for row in range(1, own + 1):
        first = total[row * cols : (row + 1) * cols]
        normed[row - 1] = (first * rms_scale(first)).astype(BF16)
    store_normed = pltpu.make_async_copy(normed, normed_ref, out_sems.at[1])
    store_above = pltpu.make_async_copy(total.at[pl.ds(0, cols)], first_ref.at[pl.ds(0, cols)], out_sems.at[2])
    store_below = pltpu.make_async_copy(
        total.at[pl.ds((own + 1) * cols, cols)], first_ref.at[pl.ds(cols, cols)], out_sems.at[3]
    )
    store_own = pltpu.make_async_copy(total.at[pl.ds(cols, own * cols)], own_first_ref, out_sems.at[4])
    store_normed.start()
    store_above.start()
    store_below.start()
    store_own.start()
    for index in range(chunks):
        store_expanded(index).wait()
        store_mixed(index).wait()
    store_slab.wait()
    store_normed.wait()
    store_above.wait()
    store_below.wait()
    store_own.wait()


def forward(bands, features, other, rim, w_expand, kernel, w_project):
    capacity, cols, width = features.shape
    own, rows = GRID_ROWS, GRID_ROWS + 2 * RIM
    hidden_width = w_expand.shape[1]
    chunks = hidden_width // CHUNK
    return pl.pallas_call(
        forward_body,
        in_specs=[in_scalars(), in_hbm(), in_vmem(), in_vmem(), in_hbm(), in_vmem(), in_hbm()],
        out_specs=[in_hbm()] * 6,
        out_shape=[
            pltpu.HBM((2 * cols, width), F32),
            pltpu.HBM((own * cols, width), F32),
            pltpu.HBM((own, cols, width), BF16),
            pltpu.HBM((own, cols, width), BF16),
            pltpu.HBM((own, cols, hidden_width), BF16),
            pltpu.HBM((rows - 2, cols, hidden_width), BF16),
        ],
        scratch_shapes=[
            pltpu.VMEM((rows, cols, width), BF16),
            pltpu.VMEM((rows * cols, width), BF16),
            pltpu.VMEM((width, hidden_width), BF16),
            pltpu.VMEM((hidden_width, width), BF16),
            pltpu.VMEM((own, cols, hidden_width + CHUNK), BF16),
            pltpu.VMEM((rows, cols, CHUNK), F32),
            pltpu.VMEM((rows, cols, CHUNK), F32),
            pltpu.VMEM((rows - 2, cols, hidden_width), BF16),
            pltpu.VMEM(((rows - 2) * cols, CHUNK), BF16),
            pltpu.VMEM(((rows - 2) * cols, CHUNK), BF16),
            pltpu.VMEM(((rows - 2) * cols, width), F32),
            pltpu.VMEM((own, cols, width), BF16),
            pltpu.SemaphoreType.DMA((4,)),
            pltpu.SemaphoreType.DMA((2, chunks)),
            pltpu.SemaphoreType.DMA((2, chunks)),
            pltpu.SemaphoreType.DMA((5,)),
        ],
        compiler_params=params(28),
        cost_estimate=pl.CostEstimate(
            flops=16 * 10**9,
            bytes_accessed=48 * MIB,
            transcendentals=2 * rows * cols * hidden_width,
        ),
        name="bottleneck_forward",
    )(bands, held(features), near(other), near(rim), held(w_expand), near(kernel), held(w_project))


def slopes_body(expanded_ref, mixed_ref, slope_one_ref, slope_two_ref):
    for source, target in ((expanded_ref, slope_one_ref), (mixed_ref, slope_two_ref)):
        rows, _, chunk = source.shape
        for row in range(rows):
            for lane in range(0, chunk, LANES):
                lanes = slice(lane, lane + LANES)
                target[row, :, lanes] = gelu_slope(source[row, :, lanes].astype(F32)).astype(BF16)


def slopes(expanded, mixed):
    hidden_width = expanded.shape[2]
    blocks = [
        pl.BlockSpec(values.shape[:2] + (CHUNK,), lambda j: (0, 0, j)) for values in (expanded, mixed)
    ]
    return pl.pallas_call(
        slopes_body,
        grid=(hidden_width // CHUNK,),
        in_specs=blocks,
        out_specs=blocks,
        out_shape=[jax.ShapeDtypeStruct(values.shape, BF16) for values in (expanded, mixed)],
        compiler_params=params(),
        cost_estimate=pl.CostEstimate(
            flops=15 * (expanded.size + mixed.size),
            bytes_accessed=6 * (expanded.size + mixed.size),
            transcendentals=expanded.size + mixed.size,
        ),
        name="gelu_slopes",
    )(expanded, mixed)


def lane_tiles(width):
    return [slice(at, at + LANES) for at in range(0, width, LANES)]


def window_places(own, cols):
    return [(r, q) for r in range(own) for q in range(cols // 8)]


def to_windows(source_ref, rows_wide, target):
    groups, own, cols, width = source_ref.shape
    span = groups * 8
    for tile, lanes in enumerate(lane_tiles(width)):
        for group in range(groups):
            rows_wide[tile, group] = source_ref[group, :, :, lanes].astype(F32)
        for index, (r, q) in enumerate(window_places(own, cols)):
            pieces = [
                rows_wide[tile, group, r, pl.ds(q, 8, stride=cols // 8), :] for group in range(groups)
            ]
            rows = slice(index * span, (index + 1) * span)
            target[rows, lanes] = jnp.concatenate(pieces, axis=0).astype(BF16)


def to_rows(values, rows_wide, target_ref):
    groups, own, cols, width = target_ref.shape
    span = groups * 8
    for tile, lanes in enumerate(lane_tiles(width)):
        for index, (r, q) in enumerate(window_places(own, cols)):
            for group in range(groups):
                first = index * span + group * 8
                rows_wide[tile, group, r, pl.ds(q, 8, stride=cols // 8), :] = values[first : first + 8, lanes]
        for group in range(groups):
            target_ref[group, :, :, lanes] = rows_wide[tile, group].astype(BF16)


def wide_scratch(shape):
    groups, own, cols, width = shape
    return pltpu.VMEM((width // LANES, groups, own, cols, LANES), F32)


def grad_attended_body(cotangent_ref, out_ref, grad_ref, rows_wide, in_windows):
    to_windows(cotangent_ref, rows_wide, in_windows)
    grad_ref[...] = nt_dot(in_windows[...], out_ref[...]).astype(BF16)


def attended_gradient(cotangent, w_out):
    groups, own, cols, width = cotangent.shape
    shape = (groups * own * cols, width)
    return pl.pallas_call(
        grad_attended_body,
        grid=(1,),
        in_specs=[whole(cotangent.shape), whole(w_out.shape)],
        out_specs=whole(shape),
        out_shape=jax.ShapeDtypeStruct(shape, BF16),
        scratch_shapes=[wide_scratch(cotangent.shape), pltpu.VMEM(shape, BF16)],
        compiler_params=params(),
        cost_estimate=pl.CostEstimate(
            flops=2 * shape[0] * width * width, bytes_accessed=2 * 1024 * 1024, transcendentals=0
        ),
        name="attended_gradient",
    )(cotangent, w_out)


def per_query(values, weights, span, head_dim, scale=1.0):
    wide = nn_dot(values.T, weights)
    half = LANES // 2
    own = jnp.concatenate([wide[:half, :LANES], wide[half:, LANES:]], axis=0) * scale
    own = own.astype(BF16).T
    lane_head = lax.broadcasted_iota(jnp.int32, (span, LANES), 1) // head_dim
    return jnp.where(lane_head % 2 == 0, own[:span].astype(F32), own[span:].astype(F32)).astype(BF16)


def attention_body(normed_ref, grad_attended_ref, qkv_ref, grad_ref, weights_ref, values_ref, rows_wide,
                   in_windows, projected, grad_projected, grad_attended, qkv, grad, weights, in_sems, out_sems):
    groups, own, cols, width = normed_ref.shape
    span = groups * 8
    windows = own * cols // 8
    head_dim = width // HEADS
    heads = LANES // head_dim
    scale = 1.0 / math.sqrt(head_dim)
    steepness = scale * math.log2(math.e)

    fetch_qkv = pltpu.make_async_copy(qkv_ref, qkv, in_sems.at[0])
    fetch_grad = pltpu.make_async_copy(grad_attended_ref, grad_attended, in_sems.at[1])
    fetch_qkv.start()
    fetch_grad.start()
    to_windows(normed_ref, rows_wide, in_windows)
    fetch_qkv.wait()
    projected[...] = nn_dot(in_windows[...], qkv[...]).astype(BF16)
    store_values = pltpu.make_async_copy(projected.at[:, pl.ds(2 * width, width)], values_ref, out_sems.at[0])
    store_values.start()
    fetch_grad.wait()

    row_head = lax.broadcasted_iota(jnp.int32, (heads * span, LANES), 0) // span
    lane_head = lax.broadcasted_iota(jnp.int32, (heads * span, LANES), 1) // head_dim
    mask = (row_head == lane_head).astype(F32).astype(BF16)

    def spread(values):
        return jnp.concatenate([values] * heads, axis=0) * mask

    def window(index, carry):
        rows = pl.ds(pl.multiple_of(index * span, span), span)
        for part in range(width // LANES):
            q_at, k_at, v_at = (
                slice(t * width + part * LANES, t * width + (part + 1) * LANES) for t in range(3)
            )
            q, k, v = projected[rows, q_at], projected[rows, k_at], projected[rows, v_at]
            q_wide = spread(q)
            g_wide = spread(grad_attended[rows, q_at])
            scores = nt_dot(k, q_wide)
            powers = jnp.exp2((scores - jnp.max(scores, axis=0, keepdims=True)) * steepness)
            shares = powers * (1.0 / jnp.sum(powers, axis=0, keepdims=True))
            half = shares.astype(BF16)
            weights[index, :, part * heads * span : (part + 1) * heads * span] = half
            grad_weights = nt_dot(v, g_wide)
            row_dot = jnp.sum(shares * grad_weights, axis=0, keepdims=True)
            grad_scores = (shares * (grad_weights - row_dot)).astype(BF16)
            grad_projected[rows, q_at] = per_query(k, grad_scores, span, head_dim, scale)
            grad_projected[rows, k_at] = (nn_dot(grad_scores, q_wide) * scale).astype(BF16)
            grad_projected[rows, v_at] = nn_dot(half, g_wide).astype(BF16)
        return carry

    lax.fori_loop(0, windows, window, 0, unroll=4)
    store_weights = pltpu.make_async_copy(weights, weights_ref, out_sems.at[1])
    store_weights.start()
    to_rows(nt_dot(grad_projected[...], qkv[...]), rows_wide, grad)
    store_grad = pltpu.make_async_copy(grad, grad_ref, out_sems.at[2])
    store_grad.start()
    store_values.wait()
    store_weights.wait()
    store_grad.wait()


def attention(normed, grad_attended, w_qkv):
    groups, own, cols, width = normed.shape
    span = groups * 8
    tokens = groups * own * cols
    out_shapes = [normed.shape, (tokens // span, span, HEADS * span), (tokens, width)]
    return pl.pallas_call(
        attention_body,
        in_specs=[in_vmem(), in_hbm(), in_hbm()],
        out_specs=[in_hbm()] * 3,
        out_shape=[pltpu.HBM(shape, BF16) for shape in out_shapes],
        scratch_shapes=[
            wide_scratch(normed.shape),
            pltpu.VMEM((tokens, width), BF16),
            pltpu.VMEM((tokens, 3 * width), BF16),
            pltpu.VMEM((tokens, 3 * width), BF16),
            pltpu.VMEM((tokens, width), BF16),
            pltpu.VMEM(w_qkv.shape, BF16),
            pltpu.VMEM(normed.shape, BF16),
            pltpu.VMEM(out_shapes[1], BF16),
            pltpu.SemaphoreType.DMA((2,)),
            pltpu.SemaphoreType.DMA((3,)),
        ],
        compiler_params=params(18),
        cost_estimate=pl.CostEstimate(
            flops=16 * tokens * width * width,
            bytes_accessed=4 * 1024 * 1024,
            transcendentals=tokens * span * HEADS,
        ),
        name="window_attention",
    )(near(normed), held(grad_attended), held(w_qkv))


def attended_body(weights_ref, values_ref, out_ref, added_ref, rows_wide, attended):
    windows, span, wide = weights_ref.shape
    width = values_ref.shape[1]
    heads = LANES * HEADS // width
    for index in range(windows):
        rows = slice(index * span, (index + 1) * span)
        for part, lanes in enumerate(lane_tiles(width)):
            weights = weights_ref[index, :, part * heads * span : (part + 1) * heads * span]
            attended[rows, lanes] = per_query(values_ref[rows, lanes], weights, span, width // HEADS)
    to_rows(nn_dot(attended[...], out_ref[...]), rows_wide, added_ref)


def attend(weights, values, w_out, shape):
    return pl.pallas_call(
        attended_body,
        grid=(1,),
        in_specs=[whole(weights.shape), whole(values.shape), whole(w_out.shape)],
        out_specs=whole(shape),
        out_shape=jax.ShapeDtypeStruct(shape, BF16),
        scratch_shapes=[wide_scratch(shape), pltpu.VMEM(values.shape, BF16)],
        compiler_params=params(),
        cost_estimate=pl.CostEstimate(
            flops=4 * values.size * values.shape[1], bytes_accessed=3 * 1024 * 1024, transcendentals=0
        ),
        name="attended_output",
    )(weights, values, w_out)


def backward_body(bands_ref, cotangent_ref, other_ref, rim_ref, slab_ref, first_ref, edges_ref, grad_slab_ref,
                  grad_ref, pair_ref, next_ref, slope_one_ref, slope_two_ref, expand_ref, taps_ref, project_ref,
                  out_ref, rims, slab, first, edges, grad_slab, grad_in, slope_one, slope_two, expand, project,
                  grad_first, grad_rows, mixed, expanded, total, row_sems,
                  in_sems, chunk_sems):
    own, cols, width = slab.shape
    chunks = expand_ref.shape[1] // CHUNK

    sources = (cotangent_ref, other_ref, rim_ref)
    sides = list(enumerate((-1, own)))
    for side, place_first in sides:
        start_pull(bands_ref, place_first, sources, 1, rims.at[pl.ds(side, 1)], row_sems.at[side], RIM)
    inputs = [
        pltpu.make_async_copy(source, target, in_sems.at[index])
        for index, (source, target) in enumerate(
            ((first_ref, first), (grad_ref, grad_in), (grad_slab_ref, grad_slab), (edges_ref, edges), (slab_ref, slab))
        )
    ]
    for copy in inputs:
        copy.start()

    def fetches(index):
        lanes = chunk_lanes(index)
        pairs = (
            (project_ref.at[lanes], project.at[lanes]),
            (slope_two_ref.at[:, :, lanes], slope_two.at[:, :, lanes]),
            (slope_one_ref.at[:, :, lanes], slope_one.at[:, :, lanes]),
            (expand_ref.at[:, lanes], expand.at[:, lanes]),
        )
        return [
            pltpu.make_async_copy(source, target, chunk_sems.at[number, index])
            for number, (source, target) in enumerate(pairs)
        ]

    for copy in fetches(0):
        copy.start()

    def through_norm(cotangent, grad, first):
        rms = rms_scale(first)
        normed = first * rms
        grad = grad.astype(F32)
        inner = jnp.mean(grad * normed, -1, keepdims=True)
        return cotangent.astype(F32) + rms * (grad - normed * inner)

    for copy in inputs[:4]:
        copy.wait()
    for row in range(own):
        at = slice(row * cols, (row + 1) * cols)
        result = through_norm(grad_slab[row], grad_in[row], first[at])
        grad_first[at] = result
        grad_rows[(row + 1) * cols : (row + 2) * cols] = result.astype(BF16)
    for side, place_first in sides:
        wait_pull(sources, 1, rims.at[pl.ds(side, 1)], row_sems.at[side])
    leads = lax.rem(lax.axis_index("row"), 2) == 0
    above = jnp.where(leads, next_ref[0].astype(F32), pair_ref[0].astype(F32))
    below = jnp.where(leads, pair_ref[0].astype(F32), next_ref[0].astype(F32))
    last = (own + 1) * cols
    grad_rows[0:cols] = through_norm(rims[0], above, edges[:cols]).astype(BF16)
    grad_rows[last:] = through_norm(rims[1], below, edges[cols:]).astype(BF16)
    column = lax.broadcasted_iota(jnp.int32, (cols, LANES), 0)

    total[...] = jnp.zeros_like(total)

    def step(index, carry):
        @pl.when(index + 1 < chunks)
        def _():
            for copy in fetches(index + 1):
                copy.start()

        for copy in fetches(index):
            copy.wait()
        weights = project[chunk_lanes(index), :]
        for row in range(0, own + 2, GROUP_BACKWARD):
            product = nt_dot(grad_rows[row * cols : (row + GROUP_BACKWARD) * cols, :], weights)
            for inner in range(GROUP_BACKWARD):
                for lane in range(0, CHUNK, LANES):
                    lanes = slice(lane, lane + LANES)
                    slope = slope_two[row + inner, :, chunk_lanes(index, lane, LANES)].astype(F32)
                    value = product[inner * cols : (inner + 1) * cols, lanes] * slope
                    mixed[row + inner, :, lanes] = value.astype(BF16).astype(F32)

        for lane in range(0, CHUNK, LANES):
            lanes = slice(lane, lane + LANES)
            taps = spread_taps(taps_ref, chunk_lanes(index, lane, LANES), cols)
            for row in range(own):
                rows_near = [mixed[row + a, :, lanes] for a in range(3)]
                sums = [
                    taps[8 - b] * rows_near[0] + taps[5 - b] * rows_near[1] + taps[2 - b] * rows_near[2]
                    for b in range(3)
                ]
                value = column_sums(sums[0], sums[1], sums[2], column, cols - 1)
                value = value * slope_one[row, :, chunk_lanes(index, lane, LANES)].astype(F32)
                expanded[row * cols : (row + 1) * cols, lanes] = value.astype(BF16)
        total[...] += nt_dot(expanded[...], expand[:, chunk_lanes(index)])
        return carry

    lax.fori_loop(0, chunks, step, 0)
    inputs[4].wait()
    for row in range(own):
        at = slice(row * cols, (row + 1) * cols)
        values = slab[row].astype(F32)
        rms = rms_scale(values)
        normed = values * rms
        grad = total[at]
        inner = jnp.mean(grad * normed, -1, keepdims=True)
        out_ref[row] = (grad_first[at] + rms * (grad - normed * inner)).astype(BF16)


def backward(bands, cotangent, other, rim, slab, first, edges, grad_slab, grad, pair_row, next_row, slope_one,
             slope_two, w_expand, kernel, w_project):
    own, cols, width = slab.shape
    hidden_width = w_expand.shape[1]
    chunks = hidden_width // CHUNK
    return pl.pallas_call(
        backward_body,
        in_specs=[in_scalars()] + [in_hbm()] * 8 + [in_vmem()] * 2 + [in_hbm()] * 3 + [in_vmem(), in_hbm()],
        out_specs=in_vmem(),
        out_shape=jax.ShapeDtypeStruct((own, cols, width), BF16),
        scratch_shapes=[
            pltpu.VMEM((2, cols, width), BF16),
            pltpu.VMEM((own, cols, width), BF16),
            pltpu.VMEM((own * cols, width), F32),
            pltpu.VMEM((2 * cols, width), F32),
            pltpu.VMEM((own, cols, width), BF16),
            pltpu.VMEM((own, cols, width), BF16),
            pltpu.VMEM((own, cols, hidden_width), BF16),
            pltpu.VMEM((own + 2, cols, hidden_width), BF16),
            pltpu.VMEM((width, hidden_width), BF16),
            pltpu.VMEM((hidden_width, width), BF16),
            pltpu.VMEM((own * cols, width), F32),
            pltpu.VMEM(((own + 2) * cols, width), BF16),
            pltpu.VMEM((own + 2, cols, CHUNK), F32),
            pltpu.VMEM((own * cols, CHUNK), BF16),
            pltpu.VMEM((own * cols, width), F32),
            pltpu.SemaphoreType.DMA((2,)),
            pltpu.SemaphoreType.DMA((5,)),
            pltpu.SemaphoreType.DMA((4, chunks)),
        ],
        compiler_params=params(26),
        cost_estimate=pl.CostEstimate(
            flops=16 * 10**9,
            bytes_accessed=48 * MIB,
            transcendentals=0,
        ),
        name="bottleneck_backward",
    )(bands, held(cotangent), held(other), held(rim), held(slab), held(first), held(edges), held(grad_slab), held(grad),
      near(pair_row), near(next_row), held(slope_one), held(slope_two), held(w_expand), near(kernel),
      held(w_project))


def window_groups(size):
    stride = size // 8
    return [[first + stride * k for k in range(8)] for first in range(stride)]


def exchange_windows(rows):
    groups = window_groups(lax.axis_size("row"))
    return lax.all_to_all(
        rows, "row", split_axis=0, concat_axis=0, tiled=True, axis_index_groups=groups
    )


def swap_pair(rows):
    size = lax.axis_size("row")
    return lax.ppermute(rows, "row", [(i, i ^ 1) for i in range(size)])


def swap_next(rows):
    size = lax.axis_size("row")
    pairs = [(i, i + 1) for i in range(1, size - 1, 2)]
    return lax.ppermute(rows, "row", pairs + [(j, i) for i, j in pairs])


def place_rows(even, other, leads, leader_share):
    size = GRID_ROWS
    first, second = even[:BAND], even[BAND:]
    share = jnp.where(leads, leader_share, 2 * size - leader_share)
    zeros = jnp.zeros_like(first)
    low = jnp.where(leads | (share == size), first, jnp.where(share < size, second, other))
    mid = jnp.where(share < size, zeros, jnp.where(leads | (share == size), second, first))
    high = jnp.where(share > size, jnp.where(leads, other, second), zeros)
    return jnp.concatenate([low, mid, high], 0)


def on_device(features, row_bands, w_expand, kernel, w_project, w_qkv, w_out, cotangent):
    capacity, cols, width = features.shape
    device = lax.axis_index("row")
    parity = device % 2
    leads = parity == 0

    rim = swap_next(rim_rows(row_bands, features, cotangent))
    other_cotangent = swap_pair(cotangent)
    other_features = swap_pair(features)
    grad_slab = even_rows(row_bands, cotangent, other_cotangent)

    grad_windows = exchange_windows(grad_slab)
    edges, first, normed, slab, expanded, mixed = forward(
        row_bands, features, other_features, rim, w_expand, kernel, w_project
    )
    normed, grad_windows = lax.optimization_barrier((normed, grad_windows))
    normed_windows = exchange_windows(normed)
    shape = (8, GRID_ROWS // 8, cols, width)
    slope_one, slope_two = slopes(expanded, mixed)
    grad_attended = attended_gradient(grad_windows.reshape(shape), w_out)
    normed_windows, slope_one, slope_two, grad_attended = lax.optimization_barrier(
        (normed_windows, slope_one, slope_two, grad_attended)
    )
    grad_normed, weights, values = attention(normed_windows.reshape(shape), grad_attended, w_qkv)
    grad_rows = exchange_windows(grad_normed.reshape(GRID_ROWS, cols, width))
    added = attend(weights, values, w_out, shape)
    leader_share = BAND * row_bands[device - parity]
    grad_rows, added, leader_share = lax.optimization_barrier((grad_rows, added, leader_share))
    top, bottom = grad_rows[:1], grad_rows[GRID_ROWS - 1 :]
    sent_next, sent_pair = jnp.where(leads, top, bottom), jnp.where(leads, bottom, top)
    added, sent_next, sent_pair = lax.optimization_barrier((added, sent_next, sent_pair))
    next_row, pair_row = swap_next(sent_next), swap_pair(sent_pair)
    added_rows = exchange_windows(added.reshape(GRID_ROWS, cols, width))
    grad_input = backward(
        row_bands, cotangent, other_cotangent, rim, slab, first, edges, grad_slab, grad_rows, pair_row, next_row,
        slope_one, slope_two, w_expand, kernel, w_project,
    )
    def sent(rows):
        return jnp.where(leads, rows[BAND:], rows[:BAND])

    other_grad = swap_pair(sent(grad_input))
    grad_input, added_rows = lax.optimization_barrier((grad_input, added_rows))
    final = (first.reshape(GRID_ROWS, cols, width) + added_rows.astype(F32)).astype(BF16)
    other_final = swap_pair(sent(final))
    return (
        place_rows(final, other_final, leads, leader_share),
        place_rows(grad_input, other_grad, leads, leader_share),
    )


def solution(mesh):
    return jax.shard_map(
        on_device,
        mesh=mesh,
        in_specs=(
            P(("parts", "row"), None, None),
            P("parts"),
            P(),
            P(),
            P(),
            P(),
            P(),
            P(("parts", "row"), None, None),
        ),
        out_specs=(P(("parts", "row"), None, None), P(("parts", "row"), None, None)),
        check_vma=False,
    )
```

```python
import math

import jax
import jax.numpy as jnp
from jax import lax
from jax.experimental import pallas as pl
from jax.experimental.pallas import tpu as pltpu
from jax.sharding import PartitionSpec as P

HEADS = 16
GRID_ROWS = 16
BAND = 8
RIM = 2
EPSILON = 1e-06
CHUNK = 512
HALF = 256
GROUP_FORWARD = 10
GROUP_BACKWARD = 9
LANES = 128
ROOT = math.sqrt(2.0 / math.pi)
CUBIC = 0.044715
F32 = jnp.float32
BF16 = jnp.bfloat16
MIB = 1024 * 1024


def nt_dot(left, right):
    return lax.dot_general(left, right, (((1,), (1,)), ((), ())), preferred_element_type=F32)


def tn_dot(left, right):
    return lax.dot_general(left, right, (((0,), (0,)), ((), ())), preferred_element_type=F32)


def nn_dot(left, right):
    return jnp.dot(left, right, preferred_element_type=F32)


def rms_scale(values):
    return lax.rsqrt(jnp.mean(values * values, -1, keepdims=True) + EPSILON)


def gelu_parts(v):
    square = v * v
    cdf = 0.5 + 0.5 * jnp.tanh(v * (ROOT + (ROOT * CUBIC) * square))
    return square, cdf, v * cdf


def gelu(v):
    return gelu_parts(v)[2]


def gelu_slope(v):
    square, cdf, value = gelu_parts(v)
    return cdf + (value - value * cdf) * (2.0 * ROOT + (6.0 * ROOT * CUBIC) * square)


def whole(shape, space=None):
    zeros = (0,) * len(shape)
    return pl.BlockSpec(shape, lambda *_: zeros)


def params(mebibytes=56):
    return pltpu.CompilerParams(vmem_limit_bytes=mebibytes * MIB)


def in_vmem():
    return pl.BlockSpec(memory_space=pltpu.VMEM)


def in_hbm():
    return pl.BlockSpec(memory_space=pltpu.HBM)


def held(array):
    return pltpu.with_memory_space_constraint(array, pltpu.HBM)


def near(array):
    return pltpu.with_memory_space_constraint(array, pltpu.VMEM)


def in_scalars():
    return pl.BlockSpec(memory_space=pltpu.SMEM)


def shares(bands_ref):
    device = lax.axis_index("row")
    parity = lax.rem(device, 2)
    return parity, BAND * bands_ref[device - parity], BAND * bands_ref[device]


def place(bands_ref, first):
    parity, leader_share, _ = shares(bands_ref)
    row = first + GRID_ROWS * parity
    beyond = (row < 0) | (row >= 2 * GRID_ROWS)
    in_leader = row < leader_share
    in_own = in_leader == (parity == 0)
    source = jnp.where(beyond, 2, jnp.where(in_own, 0, 1))
    return source, jnp.where(beyond, 0, jnp.where(in_leader, row, row - leader_share))


def start_pull(bands_ref, first, sources, rows, target, sem, rim_row=0):
    where, row = place(bands_ref, first)
    row = jnp.where(where == 2, rim_row, row)
    for number, source in enumerate(sources):

        @pl.when(where == number)
        def _():
            pltpu.make_async_copy(source.at[pl.ds(row, rows)], target, sem).start()


def wait_pull(sources, rows, target, sem):
    pltpu.make_async_copy(sources[0].at[pl.ds(0, rows)], target, sem).wait()


def even_body(bands_ref, own_ref, other_ref, out_ref):
    for half in range(2):
        where, row = place(bands_ref, BAND * half)
        for number, source in enumerate((own_ref, other_ref)):

            @pl.when(where == number)
            def _():
                out_ref[BAND * half : BAND * half + BAND] = source[pl.ds(row, BAND)]


def even_rows(bands, own, other):
    shape = (GRID_ROWS,) + own.shape[1:]
    return pl.pallas_call(
        even_body,
        in_specs=[in_scalars(), in_vmem(), in_vmem()],
        out_specs=in_vmem(),
        out_shape=jax.ShapeDtypeStruct(shape, own.dtype),
        compiler_params=params(8),
        name="even_rows",
    )(bands, near(own), near(other))


def rim_body(bands_ref, features_ref, cotangent_ref, out_ref, sems):
    parity, _, share = shares(bands_ref)
    leads = parity == 0
    copies = [
        pltpu.make_async_copy(
            features_ref.at[pl.ds(jnp.where(leads, 0, share - RIM), RIM)], out_ref.at[pl.ds(0, RIM)], sems.at[0]
        ),
        pltpu.make_async_copy(
            cotangent_ref.at[pl.ds(jnp.where(leads, 0, share - 1), 1)], out_ref.at[pl.ds(RIM, 1)], sems.at[1]
        ),
    ]
    for copy in copies:
        copy.start()
    for copy in copies:
        copy.wait()


def rim_rows(bands, features, cotangent):
    shape = (RIM + 1,) + features.shape[1:]
    return pl.pallas_call(
        rim_body,
        in_specs=[in_scalars(), in_hbm(), in_hbm()],
        out_specs=in_vmem(),
        out_shape=jax.ShapeDtypeStruct(shape, features.dtype),
        scratch_shapes=[pltpu.SemaphoreType.DMA((2,))],
        compiler_params=params(8),
        name="rim_rows",
    )(bands, held(features), held(cotangent))


def column_sums(left, mid, right, column, last):
    from_left = jnp.where(column == 0, 0.0, pltpu.roll(left, 1, 0))
    from_right = jnp.where(column == last, 0.0, pltpu.roll(right, last, 0))
    return mid + from_left + from_right


def spread_taps(taps_ref, lanes, cols):
    taps = taps_ref[:, lanes].astype(F32)
    return [jnp.broadcast_to(taps[i : i + 1], (cols, LANES)) for i in range(9)]


def chunk_lanes(index, lane=0, count=CHUNK):
    return pl.ds(pl.multiple_of(index * CHUNK + lane, LANES), count)


def forward_body(bands_ref, features_ref, other_ref, rim_ref, expand_ref, taps_ref, project_ref, first_ref,
                 own_first_ref, normed_ref, slab_ref, expanded_ref, mixed_ref, slab, normed_one, expand, project,
                 expanded, hidden, mixed, hidden_two, total, normed, row_sems,
                 weight_sems, chunk_sems, out_sems):
    rows, cols, width = slab.shape
    own = rows - 2 * RIM
    chunks = expand_ref.shape[1] // CHUNK

    sources = (features_ref, other_ref, rim_ref)
    pieces = [(0, RIM), (RIM, BAND), (RIM + BAND, BAND), (RIM + 2 * BAND, RIM)]
    for index, (first, count) in enumerate(pieces):
        start_pull(bands_ref, first - RIM, sources, count, slab.at[pl.ds(first, count)], row_sems.at[index])

    def fetch_expand(index):
        lanes = chunk_lanes(index)
        return pltpu.make_async_copy(expand_ref.at[:, lanes], expand.at[:, lanes], weight_sems.at[0, index])

    def fetch_project(index):
        lanes = chunk_lanes(index)
        return pltpu.make_async_copy(project_ref.at[lanes], project.at[lanes], weight_sems.at[1, index])

    def store_expanded(index):
        lanes = chunk_lanes(index)
        return pltpu.make_async_copy(
            expanded.at[:, :, lanes], expanded_ref.at[:, :, lanes], chunk_sems.at[0, index]
        )

    def store_mixed(index):
        lanes = chunk_lanes(index)
        return pltpu.make_async_copy(mixed.at[:, :, lanes], mixed_ref.at[:, :, lanes], chunk_sems.at[1, index])

    fetch_expand(0).start()
    fetch_project(0).start()
    for index, (first, count) in enumerate(pieces):
        wait_pull(sources, count, slab.at[pl.ds(first, count)], row_sems.at[index])
    store_slab = pltpu.make_async_copy(slab.at[pl.ds(RIM, own)], slab_ref, out_sems.at[0])
    store_slab.start()
    for row in range(0, rows, 2):
        at = slice(row * cols, (row + 2) * cols)
        values = slab[row : row + 2].astype(F32).reshape(2 * cols, width)
        normed_one[at] = (values * rms_scale(values)).astype(BF16)
    total[...] = slab[1 : rows - 1].astype(F32).reshape((rows - 2) * cols, width)
    column = lax.broadcasted_iota(jnp.int32, (cols, LANES), 0)

    def step(index, carry):
        @pl.when(index + 1 < chunks)
        def _():
            fetch_expand(index + 1).start()
            fetch_project(index + 1).start()

        fetch_expand(index).wait()
        for start in range(0, CHUNK, HALF):
            weights = expand[:, chunk_lanes(index, start, HALF)]
            for row in range(0, rows, GROUP_FORWARD):
                product = nn_dot(normed_one[row * cols : (row + GROUP_FORWARD) * cols, :], weights)
                for inner in range(GROUP_FORWARD):
                    for lane in range(0, HALF, LANES):
                        values = product[inner * cols : (inner + 1) * cols, lane : lane + LANES]
                        at = slice(start + lane, start + lane + LANES)
                        hidden[row + inner, :, at] = gelu(values).astype(BF16).astype(F32)
                        if RIM <= row + inner < RIM + own:
                            expanded[row + inner - RIM, :, chunk_lanes(index, start + lane, LANES)] = values.astype(BF16)
        store_expanded(index).start()

        for lane in range(0, CHUNK, LANES):
            lanes = slice(lane, lane + LANES)
            taps = spread_taps(taps_ref, chunk_lanes(index, lane, LANES), cols)
            for row in range(rows - 2):
                rows_near = [hidden[row + a, :, lanes] for a in range(3)]
                sums = [
                    taps[b] * rows_near[0] + taps[3 + b] * rows_near[1] + taps[6 + b] * rows_near[2] for b in range(3)
                ]
                values = column_sums(sums[0], sums[1], sums[2], column, cols - 1)
                hidden_two[row * cols : (row + 1) * cols, lanes] = gelu(values).astype(BF16)
                mixed[row, :, chunk_lanes(index, lane, LANES)] = values.astype(BF16)
        store_mixed(index).start()
        fetch_project(index).wait()
        total[...] += nn_dot(hidden_two[...], project[chunk_lanes(index), :])
        return carry

    lax.fori_loop(0, chunks, step, 0)
    for row in range(1, own + 1):
        first = total[row * cols : (row + 1) * cols]
        normed[row - 1] = (first * rms_scale(first)).astype(BF16)
    store_normed = pltpu.make_async_copy(normed, normed_ref, out_sems.at[1])
    store_above = pltpu.make_async_copy(total.at[pl.ds(0, cols)], first_ref.at[pl.ds(0, cols)], out_sems.at[2])
    store_below = pltpu.make_async_copy(
        total.at[pl.ds((own + 1) * cols, cols)], first_ref.at[pl.ds(cols, cols)], out_sems.at[3]
    )
    store_own = pltpu.make_async_copy(total.at[pl.ds(cols, own * cols)], own_first_ref, out_sems.at[4])
    store_normed.start()
    store_above.start()
    store_below.start()
    store_own.start()
    for index in range(chunks):
        store_expanded(index).wait()
        store_mixed(index).wait()
    store_slab.wait()
    store_normed.wait()
    store_above.wait()
    store_below.wait()
    store_own.wait()


def forward(bands, features, other, rim, w_expand, kernel, w_project):
    capacity, cols, width = features.shape
    own, rows = GRID_ROWS, GRID_ROWS + 2 * RIM
    hidden_width = w_expand.shape[1]
    chunks = hidden_width // CHUNK
    return pl.pallas_call(
        forward_body,
        in_specs=[in_scalars(), in_hbm(), in_vmem(), in_vmem(), in_hbm(), in_vmem(), in_hbm()],
        out_specs=[in_hbm()] * 6,
        out_shape=[
            pltpu.HBM((2 * cols, width), F32),
            pltpu.HBM((own * cols, width), F32),
            pltpu.HBM((own, cols, width), BF16),
            pltpu.HBM((own, cols, width), BF16),
            pltpu.HBM((own, cols, hidden_width), BF16),
            pltpu.HBM((rows - 2, cols, hidden_width), BF16),
        ],
        scratch_shapes=[
            pltpu.VMEM((rows, cols, width), BF16),
            pltpu.VMEM((rows * cols, width), BF16),
            pltpu.VMEM((width, hidden_width), BF16),
            pltpu.VMEM((hidden_width, width), BF16),
            pltpu.VMEM((own, cols, hidden_width), BF16),
            pltpu.VMEM((rows, cols, CHUNK), F32),
            pltpu.VMEM((rows - 2, cols, hidden_width), BF16),
            pltpu.VMEM(((rows - 2) * cols, CHUNK), BF16),
            pltpu.VMEM(((rows - 2) * cols, width), F32),
            pltpu.VMEM((own, cols, width), BF16),
            pltpu.SemaphoreType.DMA((4,)),
            pltpu.SemaphoreType.DMA((2, chunks)),
            pltpu.SemaphoreType.DMA((2, chunks)),
            pltpu.SemaphoreType.DMA((5,)),
        ],
        compiler_params=params(24),
        cost_estimate=pl.CostEstimate(
            flops=16 * 10**9,
            bytes_accessed=48 * MIB,
            transcendentals=2 * rows * cols * hidden_width,
        ),
        name="bottleneck_forward",
    )(bands, held(features), near(other), near(rim), held(w_expand), near(kernel), held(w_project))


def slopes_body(expanded_ref, mixed_ref, slope_one_ref, slope_two_ref):
    for source, target in ((expanded_ref, slope_one_ref), (mixed_ref, slope_two_ref)):
        rows, _, chunk = source.shape
        for row in range(rows):
            for lane in range(0, chunk, LANES):
                lanes = slice(lane, lane + LANES)
                target[row, :, lanes] = gelu_slope(source[row, :, lanes].astype(F32)).astype(BF16)


def slopes(expanded, mixed):
    hidden_width = expanded.shape[2]
    blocks = [
        pl.BlockSpec(values.shape[:2] + (CHUNK,), lambda j: (0, 0, j)) for values in (expanded, mixed)
    ]
    return pl.pallas_call(
        slopes_body,
        grid=(hidden_width // CHUNK,),
        in_specs=blocks,
        out_specs=blocks,
        out_shape=[jax.ShapeDtypeStruct(values.shape, BF16) for values in (expanded, mixed)],
        compiler_params=params(),
        cost_estimate=pl.CostEstimate(
            flops=15 * (expanded.size + mixed.size),
            bytes_accessed=6 * (expanded.size + mixed.size),
            transcendentals=expanded.size + mixed.size,
        ),
        name="gelu_slopes",
    )(expanded, mixed)


def lane_tiles(width):
    return [slice(at, at + LANES) for at in range(0, width, LANES)]


def window_places(own, cols):
    return [(r, q) for r in range(own) for q in range(cols // 8)]


def to_windows(source_ref, rows_wide, target):
    groups, own, cols, width = source_ref.shape
    span = groups * 8
    for tile, lanes in enumerate(lane_tiles(width)):
        for group in range(groups):
            rows_wide[tile, group] = source_ref[group, :, :, lanes].astype(F32)
        for index, (r, q) in enumerate(window_places(own, cols)):
            pieces = [
                rows_wide[tile, group, r, pl.ds(q, 8, stride=cols // 8), :] for group in range(groups)
            ]
            rows = slice(index * span, (index + 1) * span)
            target[rows, lanes] = jnp.concatenate(pieces, axis=0).astype(BF16)


def to_rows(values, rows_wide, target_ref):
    groups, own, cols, width = target_ref.shape
    span = groups * 8
    for tile, lanes in enumerate(lane_tiles(width)):
        for index, (r, q) in enumerate(window_places(own, cols)):
            for group in range(groups):
                first = index * span + group * 8
                rows_wide[tile, group, r, pl.ds(q, 8, stride=cols // 8), :] = values[first : first + 8, lanes]
        for group in range(groups):
            target_ref[group, :, :, lanes] = rows_wide[tile, group].astype(BF16)


def wide_scratch(shape):
    groups, own, cols, width = shape
    return pltpu.VMEM((width // LANES, groups, own, cols, LANES), F32)


def grad_attended_body(cotangent_ref, out_ref, grad_ref, rows_wide, in_windows):
    to_windows(cotangent_ref, rows_wide, in_windows)
    grad_ref[...] = nt_dot(in_windows[...], out_ref[...]).astype(BF16)


def attended_gradient(cotangent, w_out):
    groups, own, cols, width = cotangent.shape
    shape = (groups * own * cols, width)
    return pl.pallas_call(
        grad_attended_body,
        grid=(1,),
        in_specs=[whole(cotangent.shape), whole(w_out.shape)],
        out_specs=whole(shape),
        out_shape=jax.ShapeDtypeStruct(shape, BF16),
        scratch_shapes=[wide_scratch(cotangent.shape), pltpu.VMEM(shape, BF16)],
        compiler_params=params(),
        cost_estimate=pl.CostEstimate(
            flops=2 * shape[0] * width * width, bytes_accessed=2 * 1024 * 1024, transcendentals=0
        ),
        name="attended_gradient",
    )(cotangent, w_out)


def per_query(values, weights, span, head_dim, scale=1.0):
    wide = nn_dot(values.T, weights)
    half = LANES // 2
    own = jnp.concatenate([wide[:half, :LANES], wide[half:, LANES:]], axis=0) * scale
    own = own.astype(BF16).T
    lane_head = lax.broadcasted_iota(jnp.int32, (span, LANES), 1) // head_dim
    return jnp.where(lane_head % 2 == 0, own[:span].astype(F32), own[span:].astype(F32)).astype(BF16)


def attention_body(normed_ref, grad_attended_ref, qkv_ref, grad_ref, weights_ref, values_ref, rows_wide,
                   in_windows, projected, grad_projected, grad_attended, qkv, grad, weights, in_sems, out_sems):
    groups, own, cols, width = normed_ref.shape
    span = groups * 8
    windows = own * cols // 8
    head_dim = width // HEADS
    heads = LANES // head_dim
    scale = 1.0 / math.sqrt(head_dim)
    steepness = scale * math.log2(math.e)

    fetch_qkv = pltpu.make_async_copy(qkv_ref, qkv, in_sems.at[0])
    fetch_grad = pltpu.make_async_copy(grad_attended_ref, grad_attended, in_sems.at[1])
    fetch_qkv.start()
    fetch_grad.start()
    to_windows(normed_ref, rows_wide, in_windows)
    fetch_qkv.wait()
    projected[...] = nn_dot(in_windows[...], qkv[...]).astype(BF16)
    store_values = pltpu.make_async_copy(projected.at[:, pl.ds(2 * width, width)], values_ref, out_sems.at[0])
    store_values.start()
    fetch_grad.wait()

    row_head = lax.broadcasted_iota(jnp.int32, (heads * span, LANES), 0) // span
    lane_head = lax.broadcasted_iota(jnp.int32, (heads * span, LANES), 1) // head_dim
    mask = (row_head == lane_head).astype(F32).astype(BF16)

    def spread(values):
        return jnp.concatenate([values] * heads, axis=0) * mask

    def window(index, carry):
        rows = pl.ds(pl.multiple_of(index * span, span), span)
        parts = range(width // LANES)
        places = [
            [slice(t * width + part * LANES, t * width + (part + 1) * LANES) for t in range(3)] for part in parts
        ]
        keys = [projected[rows, k_at] for _, k_at, _ in places]
        q_wide = [spread(projected[rows, q_at]) for q_at, _, _ in places]
        scores = [nt_dot(keys[part], q_wide[part]) for part in parts]
        g_wide = [spread(grad_attended[rows, q_at]) for q_at, _, _ in places]
        grad_weights = [nt_dot(projected[rows, places[part][2]], g_wide[part]) for part in parts]
        powers = [
            jnp.exp2((score - jnp.max(score, axis=0, keepdims=True)) * steepness) for score in scores
        ]
        shares = [power * (1.0 / jnp.sum(power, axis=0, keepdims=True)) for power in powers]
        halves = [share.astype(BF16) for share in shares]
        row_dots = [jnp.sum(shares[part] * grad_weights[part], axis=0, keepdims=True) for part in parts]
        grad_scores = [(shares[part] * (grad_weights[part] - row_dots[part])).astype(BF16) for part in parts]
        for part in parts:
            weights[index, :, part * heads * span : (part + 1) * heads * span] = halves[part]
        grad_values = [nn_dot(halves[part], g_wide[part]) for part in parts]
        grad_keys = [nn_dot(grad_scores[part], q_wide[part]) for part in parts]
        grad_queries = [per_query(keys[part], grad_scores[part], span, head_dim, scale) for part in parts]
        for part, (q_at, k_at, v_at) in enumerate(places):
            grad_projected[rows, v_at] = grad_values[part].astype(BF16)
            grad_projected[rows, k_at] = (grad_keys[part] * scale).astype(BF16)
            grad_projected[rows, q_at] = grad_queries[part]
        return carry

    lax.fori_loop(0, windows, window, 0, unroll=4)
    store_weights = pltpu.make_async_copy(weights, weights_ref, out_sems.at[1])
    store_weights.start()
    to_rows(nt_dot(grad_projected[...], qkv[...]), rows_wide, grad)
    store_grad = pltpu.make_async_copy(grad, grad_ref, out_sems.at[2])
    store_grad.start()
    store_values.wait()
    store_weights.wait()
    store_grad.wait()


def attention(normed, grad_attended, w_qkv):
    groups, own, cols, width = normed.shape
    span = groups * 8
    tokens = groups * own * cols
    out_shapes = [normed.shape, (tokens // span, span, HEADS * span), (tokens, width)]
    return pl.pallas_call(
        attention_body,
        in_specs=[in_vmem(), in_hbm(), in_hbm()],
        out_specs=[in_hbm()] * 3,
        out_shape=[pltpu.HBM(shape, BF16) for shape in out_shapes],
        scratch_shapes=[
            wide_scratch(normed.shape),
            pltpu.VMEM((tokens, width), BF16),
            pltpu.VMEM((tokens, 3 * width), BF16),
            pltpu.VMEM((tokens, 3 * width), BF16),
            pltpu.VMEM((tokens, width), BF16),
            pltpu.VMEM(w_qkv.shape, BF16),
            pltpu.VMEM(normed.shape, BF16),
            pltpu.VMEM(out_shapes[1], BF16),
            pltpu.SemaphoreType.DMA((2,)),
            pltpu.SemaphoreType.DMA((3,)),
        ],
        compiler_params=params(18),
        cost_estimate=pl.CostEstimate(
            flops=16 * tokens * width * width,
            bytes_accessed=4 * 1024 * 1024,
            transcendentals=tokens * span * HEADS,
        ),
        name="window_attention",
    )(near(normed), held(grad_attended), held(w_qkv))


def attended_body(weights_ref, values_ref, out_ref, added_ref, rows_wide, attended):
    windows, span, wide = weights_ref.shape
    width = values_ref.shape[1]
    heads = LANES * HEADS // width
    for index in range(windows):
        rows = slice(index * span, (index + 1) * span)
        for part, lanes in enumerate(lane_tiles(width)):
            weights = weights_ref[index, :, part * heads * span : (part + 1) * heads * span]
            attended[rows, lanes] = per_query(values_ref[rows, lanes], weights, span, width // HEADS)
    to_rows(nn_dot(attended[...], out_ref[...]), rows_wide, added_ref)


def attend(weights, values, w_out, shape):
    return pl.pallas_call(
        attended_body,
        grid=(1,),
        in_specs=[whole(weights.shape), whole(values.shape), whole(w_out.shape)],
        out_specs=whole(shape),
        out_shape=jax.ShapeDtypeStruct(shape, BF16),
        scratch_shapes=[wide_scratch(shape), pltpu.VMEM(values.shape, BF16)],
        compiler_params=params(),
        cost_estimate=pl.CostEstimate(
            flops=4 * values.size * values.shape[1], bytes_accessed=3 * 1024 * 1024, transcendentals=0
        ),
        name="attended_output",
    )(weights, values, w_out)


def backward_body(bands_ref, cotangent_ref, other_ref, rim_ref, slab_ref, first_ref, edges_ref, grad_slab_ref,
                  grad_ref, pair_ref, next_ref, slope_one_ref, slope_two_ref, expand_ref, taps_ref, project_ref,
                  out_ref, rims, slab, first, edges, grad_slab, grad_in, slope_one, slope_two, expand, project,
                  grad_first, grad_rows, mixed, expanded, total, row_sems,
                  in_sems, chunk_sems):
    own, cols, width = slab.shape
    chunks = expand_ref.shape[1] // CHUNK

    sources = (cotangent_ref, other_ref, rim_ref)
    sides = list(enumerate((-1, own)))
    for side, place_first in sides:
        start_pull(bands_ref, place_first, sources, 1, rims.at[pl.ds(side, 1)], row_sems.at[side], RIM)
    inputs = [
        pltpu.make_async_copy(source, target, in_sems.at[index])
        for index, (source, target) in enumerate(
            ((first_ref, first), (grad_ref, grad_in), (grad_slab_ref, grad_slab), (edges_ref, edges), (slab_ref, slab))
        )
    ]
    for copy in inputs:
        copy.start()

    def fetches(index):
        lanes = chunk_lanes(index)
        pairs = (
            (project_ref.at[lanes], project.at[lanes]),
            (slope_two_ref.at[:, :, lanes], slope_two.at[:, :, lanes]),
            (slope_one_ref.at[:, :, lanes], slope_one.at[:, :, lanes]),
            (expand_ref.at[:, lanes], expand.at[:, lanes]),
        )
        return [
            pltpu.make_async_copy(source, target, chunk_sems.at[number, index])
            for number, (source, target) in enumerate(pairs)
        ]

    for copy in fetches(0):
        copy.start()

    def through_norm(cotangent, grad, first):
        rms = rms_scale(first)
        normed = first * rms
        grad = grad.astype(F32)
        inner = jnp.mean(grad * normed, -1, keepdims=True)
        return cotangent.astype(F32) + rms * (grad - normed * inner)

    for copy in inputs[:4]:
        copy.wait()
    for row in range(own):
        at = slice(row * cols, (row + 1) * cols)
        result = through_norm(grad_slab[row], grad_in[row], first[at])
        grad_first[at] = result
        grad_rows[(row + 1) * cols : (row + 2) * cols] = result.astype(BF16)
    for side, place_first in sides:
        wait_pull(sources, 1, rims.at[pl.ds(side, 1)], row_sems.at[side])
    leads = lax.rem(lax.axis_index("row"), 2) == 0
    above = jnp.where(leads, next_ref[0].astype(F32), pair_ref[0].astype(F32))
    below = jnp.where(leads, pair_ref[0].astype(F32), next_ref[0].astype(F32))
    last = (own + 1) * cols
    grad_rows[0:cols] = through_norm(rims[0], above, edges[:cols]).astype(BF16)
    grad_rows[last:] = through_norm(rims[1], below, edges[cols:]).astype(BF16)
    column = lax.broadcasted_iota(jnp.int32, (cols, LANES), 0)

    total[...] = jnp.zeros_like(total)

    def step(index, carry):
        @pl.when(index + 1 < chunks)
        def _():
            for copy in fetches(index + 1):
                copy.start()

        for copy in fetches(index):
            copy.wait()
        for start in range(0, CHUNK, HALF):
            weights = project[chunk_lanes(index, start, HALF), :]
            for row in range(0, own + 2, GROUP_BACKWARD):
                product = nt_dot(grad_rows[row * cols : (row + GROUP_BACKWARD) * cols, :], weights)
                for inner in range(GROUP_BACKWARD):
                    for lane in range(0, HALF, LANES):
                        slope = slope_two[row + inner, :, chunk_lanes(index, start + lane, LANES)].astype(F32)
                        value = product[inner * cols : (inner + 1) * cols, lane : lane + LANES] * slope
                        at = slice(start + lane, start + lane + LANES)
                        mixed[row + inner, :, at] = value.astype(BF16).astype(F32)

        for lane in range(0, CHUNK, LANES):
            lanes = slice(lane, lane + LANES)
            taps = spread_taps(taps_ref, chunk_lanes(index, lane, LANES), cols)
            for row in range(own):
                rows_near = [mixed[row + a, :, lanes] for a in range(3)]
                sums = [
                    taps[8 - b] * rows_near[0] + taps[5 - b] * rows_near[1] + taps[2 - b] * rows_near[2]
                    for b in range(3)
                ]
                value = column_sums(sums[0], sums[1], sums[2], column, cols - 1)
                value = value * slope_one[row, :, chunk_lanes(index, lane, LANES)].astype(F32)
                expanded[row * cols : (row + 1) * cols, lanes] = value.astype(BF16)
        total[...] += nt_dot(expanded[...], expand[:, chunk_lanes(index)])
        return carry

    lax.fori_loop(0, chunks, step, 0)
    inputs[4].wait()
    for row in range(own):
        at = slice(row * cols, (row + 1) * cols)
        values = slab[row].astype(F32)
        rms = rms_scale(values)
        normed = values * rms
        grad = total[at]
        inner = jnp.mean(grad * normed, -1, keepdims=True)
        out_ref[row] = (grad_first[at] + rms * (grad - normed * inner)).astype(BF16)


def backward(bands, cotangent, other, rim, slab, first, edges, grad_slab, grad, pair_row, next_row, slope_one,
             slope_two, w_expand, kernel, w_project):
    own, cols, width = slab.shape
    hidden_width = w_expand.shape[1]
    chunks = hidden_width // CHUNK
    return pl.pallas_call(
        backward_body,
        in_specs=[in_scalars()] + [in_hbm()] * 8 + [in_vmem()] * 2 + [in_hbm()] * 3 + [in_vmem(), in_hbm()],
        out_specs=in_vmem(),
        out_shape=jax.ShapeDtypeStruct((own, cols, width), BF16),
        scratch_shapes=[
            pltpu.VMEM((2, cols, width), BF16),
            pltpu.VMEM((own, cols, width), BF16),
            pltpu.VMEM((own * cols, width), F32),
            pltpu.VMEM((2 * cols, width), F32),
            pltpu.VMEM((own, cols, width), BF16),
            pltpu.VMEM((own, cols, width), BF16),
            pltpu.VMEM((own, cols, hidden_width), BF16),
            pltpu.VMEM((own + 2, cols, hidden_width), BF16),
            pltpu.VMEM((width, hidden_width), BF16),
            pltpu.VMEM((hidden_width, width), BF16),
            pltpu.VMEM((own * cols, width), F32),
            pltpu.VMEM(((own + 2) * cols, width), BF16),
            pltpu.VMEM((own + 2, cols, CHUNK), F32),
            pltpu.VMEM((own * cols, CHUNK), BF16),
            pltpu.VMEM((own * cols, width), F32),
            pltpu.SemaphoreType.DMA((2,)),
            pltpu.SemaphoreType.DMA((5,)),
            pltpu.SemaphoreType.DMA((4, chunks)),
        ],
        compiler_params=params(26),
        cost_estimate=pl.CostEstimate(
            flops=16 * 10**9,
            bytes_accessed=48 * MIB,
            transcendentals=0,
        ),
        name="bottleneck_backward",
    )(bands, held(cotangent), held(other), held(rim), held(slab), held(first), held(edges), held(grad_slab), held(grad),
      near(pair_row), near(next_row), held(slope_one), held(slope_two), held(w_expand), near(kernel),
      held(w_project))


def window_groups(size):
    stride = size // 8
    return [[first + stride * k for k in range(8)] for first in range(stride)]


def exchange_windows(rows):
    groups = window_groups(lax.axis_size("row"))
    return lax.all_to_all(
        rows, "row", split_axis=0, concat_axis=0, tiled=True, axis_index_groups=groups
    )


def swap_pair(rows):
    size = lax.axis_size("row")
    return lax.ppermute(rows, "row", [(i, i ^ 1) for i in range(size)])


def swap_next(rows):
    size = lax.axis_size("row")
    pairs = [(i, i + 1) for i in range(1, size - 1, 2)]
    return lax.ppermute(rows, "row", pairs + [(j, i) for i, j in pairs])


def place_rows(even, other, leads, leader_share):
    size = GRID_ROWS
    first, second = even[:BAND], even[BAND:]
    share = jnp.where(leads, leader_share, 2 * size - leader_share)
    zeros = jnp.zeros_like(first)
    low = jnp.where(leads | (share == size), first, jnp.where(share < size, second, other))
    mid = jnp.where(share < size, zeros, jnp.where(leads | (share == size), second, first))
    high = jnp.where(share > size, jnp.where(leads, other, second), zeros)
    return jnp.concatenate([low, mid, high], 0)


def on_device(features, row_bands, w_expand, kernel, w_project, w_qkv, w_out, cotangent):
    capacity, cols, width = features.shape
    device = lax.axis_index("row")
    parity = device % 2
    leads = parity == 0

    rim = swap_next(rim_rows(row_bands, features, cotangent))
    other_cotangent = swap_pair(cotangent)
    other_features = swap_pair(features)
    grad_slab = even_rows(row_bands, cotangent, other_cotangent)

    grad_windows = exchange_windows(grad_slab)
    edges, first, normed, slab, expanded, mixed = forward(
        row_bands, features, other_features, rim, w_expand, kernel, w_project
    )
    normed, grad_windows = lax.optimization_barrier((normed, grad_windows))
    normed_windows = exchange_windows(normed)
    shape = (8, GRID_ROWS // 8, cols, width)
    slope_one, slope_two = slopes(expanded, mixed)
    grad_attended = attended_gradient(grad_windows.reshape(shape), w_out)
    normed_windows, slope_one, slope_two, grad_attended = lax.optimization_barrier(
        (normed_windows, slope_one, slope_two, grad_attended)
    )
    grad_normed, weights, values = attention(normed_windows.reshape(shape), grad_attended, w_qkv)
    grad_rows = exchange_windows(grad_normed.reshape(GRID_ROWS, cols, width))
    added = attend(weights, values, w_out, shape)
    leader_share = BAND * row_bands[device - parity]
    grad_rows, added, leader_share = lax.optimization_barrier((grad_rows, added, leader_share))
    top, bottom = grad_rows[:1], grad_rows[GRID_ROWS - 1 :]
    sent_next, sent_pair = jnp.where(leads, top, bottom), jnp.where(leads, bottom, top)
    added, sent_next, sent_pair = lax.optimization_barrier((added, sent_next, sent_pair))
    next_row, pair_row = swap_next(sent_next), swap_pair(sent_pair)
    added_rows = exchange_windows(added.reshape(GRID_ROWS, cols, width))
    grad_input = backward(
        row_bands, cotangent, other_cotangent, rim, slab, first, edges, grad_slab, grad_rows, pair_row, next_row,
        slope_one, slope_two, w_expand, kernel, w_project,
    )
    def sent(rows):
        return jnp.where(leads, rows[BAND:], rows[:BAND])

    other_grad = swap_pair(sent(grad_input))
    grad_input, added_rows = lax.optimization_barrier((grad_input, added_rows))
    final = (first.reshape(GRID_ROWS, cols, width) + added_rows.astype(F32)).astype(BF16)
    other_final = swap_pair(sent(final))
    return (
        place_rows(final, other_final, leads, leader_share),
        place_rows(grad_input, other_grad, leads, leader_share),
    )


def solution(mesh):
    return jax.shard_map(
        on_device,
        mesh=mesh,
        in_specs=(
            P(("parts", "row"), None, None),
            P("parts"),
            P(),
            P(),
            P(),
            P(),
            P(),
            P(("parts", "row"), None, None),
        ),
        out_specs=(P(("parts", "row"), None, None), P(("parts", "row"), None, None)),
        check_vma=False,
    )
```

```python
import math

import jax
import jax.numpy as jnp
from jax import lax
from jax.experimental import pallas as pl
from jax.experimental.pallas import tpu as pltpu
from jax.sharding import PartitionSpec as P

HEADS = 16
GRID_ROWS = 16
BAND = 8
RIM = 2
EPSILON = 1e-06
CHUNK = 512
HALF = 256
GROUP_FORWARD = 10
GROUP_BACKWARD = 9
LANES = 128
ROOT = math.sqrt(2.0 / math.pi)
CUBIC = 0.044715
F32 = jnp.float32
BF16 = jnp.bfloat16
MIB = 1024 * 1024


def nt_dot(left, right):
    return lax.dot_general(left, right, (((1,), (1,)), ((), ())), preferred_element_type=F32)


def tn_dot(left, right):
    return lax.dot_general(left, right, (((0,), (0,)), ((), ())), preferred_element_type=F32)


def nn_dot(left, right):
    return jnp.dot(left, right, preferred_element_type=F32)


def rms_scale(values):
    return lax.rsqrt(jnp.mean(values * values, -1, keepdims=True) + EPSILON)


def gelu_parts(v):
    square = v * v
    cdf = 0.5 + 0.5 * jnp.tanh(v * (ROOT + (ROOT * CUBIC) * square))
    return square, cdf, v * cdf


def gelu(v):
    return gelu_parts(v)[2]


def gelu_slope(v):
    square, cdf, value = gelu_parts(v)
    return cdf + (value - value * cdf) * (2.0 * ROOT + (6.0 * ROOT * CUBIC) * square)


def whole(shape, space=None):
    zeros = (0,) * len(shape)
    return pl.BlockSpec(shape, lambda *_: zeros)


def params(mebibytes=56):
    return pltpu.CompilerParams(vmem_limit_bytes=mebibytes * MIB)


def in_vmem():
    return pl.BlockSpec(memory_space=pltpu.VMEM)


def in_hbm():
    return pl.BlockSpec(memory_space=pltpu.HBM)


def held(array):
    return pltpu.with_memory_space_constraint(array, pltpu.HBM)


def near(array):
    return pltpu.with_memory_space_constraint(array, pltpu.VMEM)


def in_scalars():
    return pl.BlockSpec(memory_space=pltpu.SMEM)


def shares(bands_ref):
    device = lax.axis_index("row")
    parity = lax.rem(device, 2)
    return parity, BAND * bands_ref[device - parity], BAND * bands_ref[device]


def place(bands_ref, first):
    parity, leader_share, _ = shares(bands_ref)
    row = first + GRID_ROWS * parity
    beyond = (row < 0) | (row >= 2 * GRID_ROWS)
    in_leader = row < leader_share
    in_own = in_leader == (parity == 0)
    source = jnp.where(beyond, 2, jnp.where(in_own, 0, 1))
    return source, jnp.where(beyond, 0, jnp.where(in_leader, row, row - leader_share))


def start_pull(bands_ref, first, sources, rows, target, sem, rim_row=0):
    where, row = place(bands_ref, first)
    row = jnp.where(where == 2, rim_row, row)
    for number, source in enumerate(sources):

        @pl.when(where == number)
        def _():
            pltpu.make_async_copy(source.at[pl.ds(row, rows)], target, sem).start()


def wait_pull(sources, rows, target, sem):
    pltpu.make_async_copy(sources[0].at[pl.ds(0, rows)], target, sem).wait()


def even_body(bands_ref, own_ref, other_ref, out_ref, sems):
    targets = [out_ref.at[pl.ds(BAND * half, BAND)] for half in range(2)]
    for half in range(2):
        start_pull(bands_ref, BAND * half, (own_ref, other_ref), BAND, targets[half], sems.at[half])
    for half in range(2):
        wait_pull((own_ref,), BAND, targets[half], sems.at[half])


def even_rows(bands, own, other):
    return pl.pallas_call(
        even_body,
        in_specs=[in_scalars(), in_vmem(), in_vmem()],
        out_specs=in_hbm(),
        out_shape=pltpu.HBM((GRID_ROWS,) + own.shape[1:], own.dtype),
        scratch_shapes=[pltpu.SemaphoreType.DMA((2,))],
        compiler_params=params(8),
        name="even_rows",
    )(bands, near(own), near(other))


def rim_body(bands_ref, features_ref, cotangent_ref, out_ref, sems):
    parity, _, share = shares(bands_ref)
    leads = parity == 0
    copies = [
        pltpu.make_async_copy(
            features_ref.at[pl.ds(jnp.where(leads, 0, share - RIM), RIM)], out_ref.at[pl.ds(0, RIM)], sems.at[0]
        ),
        pltpu.make_async_copy(
            cotangent_ref.at[pl.ds(jnp.where(leads, 0, share - 1), 1)], out_ref.at[pl.ds(RIM, 1)], sems.at[1]
        ),
    ]
    for copy in copies:
        copy.start()
    for copy in copies:
        copy.wait()


def rim_rows(bands, features, cotangent):
    shape = (RIM + 1,) + features.shape[1:]
    return pl.pallas_call(
        rim_body,
        in_specs=[in_scalars(), in_hbm(), in_hbm()],
        out_specs=in_vmem(),
        out_shape=jax.ShapeDtypeStruct(shape, features.dtype),
        scratch_shapes=[pltpu.SemaphoreType.DMA((2,))],
        compiler_params=params(8),
        name="rim_rows",
    )(bands, held(features), held(cotangent))


def column_sums(left, mid, right, column, last):
    from_left = jnp.where(column == 0, 0.0, pltpu.roll(left, 1, 0))
    from_right = jnp.where(column == last, 0.0, pltpu.roll(right, last, 0))
    return mid + from_left + from_right


def spread_taps(taps_ref, lanes, cols):
    taps = taps_ref[:, lanes].astype(F32)
    return [jnp.broadcast_to(taps[i : i + 1], (cols, LANES)) for i in range(9)]


def chunk_lanes(index, lane=0, count=CHUNK):
    return pl.ds(pl.multiple_of(index * CHUNK + lane, LANES), count)


def forward_body(bands_ref, features_ref, other_ref, rim_ref, expand_ref, taps_ref, project_ref, first_ref,
                 own_first_ref, normed_ref, slab_ref, expanded_ref, mixed_ref, slab, normed_one, expand, project,
                 expanded, hidden, mixed, hidden_two, total, normed, row_sems,
                 weight_sems, chunk_sems, out_sems):
    rows, cols, width = slab.shape
    own = rows - 2 * RIM
    chunks = expand_ref.shape[1] // CHUNK

    sources = (features_ref, other_ref, rim_ref)
    pieces = [(0, RIM), (RIM, BAND), (RIM + BAND, BAND), (RIM + 2 * BAND, RIM)]
    for index, (first, count) in enumerate(pieces):
        start_pull(bands_ref, first - RIM, sources, count, slab.at[pl.ds(first, count)], row_sems.at[index])

    def fetch_expand(index):
        lanes = chunk_lanes(index)
        return pltpu.make_async_copy(expand_ref.at[:, lanes], expand.at[:, lanes], weight_sems.at[0, index])

    def fetch_project(index):
        lanes = chunk_lanes(index)
        return pltpu.make_async_copy(project_ref.at[lanes], project.at[lanes], weight_sems.at[1, index])

    def store_expanded(index):
        lanes = chunk_lanes(index)
        return pltpu.make_async_copy(
            expanded.at[:, :, lanes], expanded_ref.at[:, :, lanes], chunk_sems.at[0, index]
        )

    def store_mixed(index):
        lanes = chunk_lanes(index)
        return pltpu.make_async_copy(mixed.at[:, :, lanes], mixed_ref.at[:, :, lanes], chunk_sems.at[1, index])

    fetch_expand(0).start()
    fetch_project(0).start()
    for index, (first, count) in enumerate(pieces):
        wait_pull(sources, count, slab.at[pl.ds(first, count)], row_sems.at[index])
    store_slab = pltpu.make_async_copy(slab.at[pl.ds(RIM, own)], slab_ref, out_sems.at[0])
    store_slab.start()
    for row in range(0, rows, 2):
        at = slice(row * cols, (row + 2) * cols)
        values = slab[row : row + 2].astype(F32).reshape(2 * cols, width)
        normed_one[at] = (values * rms_scale(values)).astype(BF16)
    total[...] = slab[1 : rows - 1].astype(F32).reshape((rows - 2) * cols, width)
    column = lax.broadcasted_iota(jnp.int32, (cols, LANES), 0)

    def step(index, carry):
        @pl.when(index + 1 < chunks)
        def _():
            fetch_expand(index + 1).start()
            fetch_project(index + 1).start()

        fetch_expand(index).wait()
        for start in range(0, CHUNK, HALF):
            weights = expand[:, chunk_lanes(index, start, HALF)]
            for row in range(0, rows, GROUP_FORWARD):
                product = nn_dot(normed_one[row * cols : (row + GROUP_FORWARD) * cols, :], weights)
                for inner in range(GROUP_FORWARD):
                    for lane in range(0, HALF, LANES):
                        values = product[inner * cols : (inner + 1) * cols, lane : lane + LANES]
                        at = slice(start + lane, start + lane + LANES)
                        hidden[row + inner, :, at] = gelu(values).astype(BF16).astype(F32)
                        if RIM <= row + inner < RIM + own:
                            expanded[row + inner - RIM, :, chunk_lanes(index, start + lane, LANES)] = values.astype(BF16)
        store_expanded(index).start()

        for lane in range(0, CHUNK, LANES):
            lanes = slice(lane, lane + LANES)
            taps = spread_taps(taps_ref, chunk_lanes(index, lane, LANES), cols)
            for row in range(rows - 2):
                rows_near = [hidden[row + a, :, lanes] for a in range(3)]
                sums = [
                    taps[b] * rows_near[0] + taps[3 + b] * rows_near[1] + taps[6 + b] * rows_near[2] for b in range(3)
                ]
                values = column_sums(sums[0], sums[1], sums[2], column, cols - 1)
                hidden_two[row * cols : (row + 1) * cols, lanes] = gelu(values).astype(BF16)
                mixed[row, :, chunk_lanes(index, lane, LANES)] = values.astype(BF16)
        store_mixed(index).start()
        fetch_project(index).wait()
        total[...] += nn_dot(hidden_two[...], project[chunk_lanes(index), :])
        return carry

    lax.fori_loop(0, chunks, step, 0)
    for row in range(1, own + 1):
        first = total[row * cols : (row + 1) * cols]
        normed[row - 1] = (first * rms_scale(first)).astype(BF16)
    store_normed = pltpu.make_async_copy(normed, normed_ref, out_sems.at[1])
    store_above = pltpu.make_async_copy(total.at[pl.ds(0, cols)], first_ref.at[pl.ds(0, cols)], out_sems.at[2])
    store_below = pltpu.make_async_copy(
        total.at[pl.ds((own + 1) * cols, cols)], first_ref.at[pl.ds(cols, cols)], out_sems.at[3]
    )
    store_own = pltpu.make_async_copy(total.at[pl.ds(cols, own * cols)], own_first_ref, out_sems.at[4])
    store_normed.start()
    store_above.start()
    store_below.start()
    store_own.start()
    for index in range(chunks):
        store_expanded(index).wait()
        store_mixed(index).wait()
    store_slab.wait()
    store_normed.wait()
    store_above.wait()
    store_below.wait()
    store_own.wait()


def forward(bands, features, other, rim, w_expand, kernel, w_project):
    capacity, cols, width = features.shape
    own, rows = GRID_ROWS, GRID_ROWS + 2 * RIM
    hidden_width = w_expand.shape[1]
    chunks = hidden_width // CHUNK
    return pl.pallas_call(
        forward_body,
        in_specs=[in_scalars(), in_hbm(), in_vmem(), in_vmem(), in_hbm(), in_vmem(), in_hbm()],
        out_specs=[in_hbm()] * 6,
        out_shape=[
            pltpu.HBM((2 * cols, width), F32),
            pltpu.HBM((own * cols, width), F32),
            pltpu.HBM((own, cols, width), BF16),
            pltpu.HBM((own, cols, width), BF16),
            pltpu.HBM((own, cols, hidden_width), BF16),
            pltpu.HBM((rows - 2, cols, hidden_width), BF16),
        ],
        scratch_shapes=[
            pltpu.VMEM((rows, cols, width), BF16),
            pltpu.VMEM((rows * cols, width), BF16),
            pltpu.VMEM((width, hidden_width), BF16),
            pltpu.VMEM((hidden_width, width), BF16),
            pltpu.VMEM((own, cols, hidden_width), BF16),
            pltpu.VMEM((rows, cols, CHUNK), F32),
            pltpu.VMEM((rows - 2, cols, hidden_width), BF16),
            pltpu.VMEM(((rows - 2) * cols, CHUNK), BF16),
            pltpu.VMEM(((rows - 2) * cols, width), F32),
            pltpu.VMEM((own, cols, width), BF16),
            pltpu.SemaphoreType.DMA((4,)),
            pltpu.SemaphoreType.DMA((2, chunks)),
            pltpu.SemaphoreType.DMA((2, chunks)),
            pltpu.SemaphoreType.DMA((5,)),
        ],
        compiler_params=params(24),
        cost_estimate=pl.CostEstimate(
            flops=16 * 10**9,
            bytes_accessed=48 * MIB,
            transcendentals=2 * rows * cols * hidden_width,
        ),
        name="bottleneck_forward",
    )(bands, held(features), near(other), near(rim), held(w_expand), near(kernel), held(w_project))


def slopes_body(expanded_ref, mixed_ref, slope_one_ref, slope_two_ref):
    for source, target in ((expanded_ref, slope_one_ref), (mixed_ref, slope_two_ref)):
        rows, _, chunk = source.shape
        for row in range(rows):
            for lane in range(0, chunk, LANES):
                lanes = slice(lane, lane + LANES)
                target[row, :, lanes] = gelu_slope(source[row, :, lanes].astype(F32)).astype(BF16)


def slopes(expanded, mixed):
    hidden_width = expanded.shape[2]
    blocks = [
        pl.BlockSpec(values.shape[:2] + (CHUNK,), lambda j: (0, 0, j)) for values in (expanded, mixed)
    ]
    return pl.pallas_call(
        slopes_body,
        grid=(hidden_width // CHUNK,),
        in_specs=blocks,
        out_specs=blocks,
        out_shape=[jax.ShapeDtypeStruct(values.shape, BF16) for values in (expanded, mixed)],
        compiler_params=params(),
        cost_estimate=pl.CostEstimate(
            flops=15 * (expanded.size + mixed.size),
            bytes_accessed=6 * (expanded.size + mixed.size),
            transcendentals=expanded.size + mixed.size,
        ),
        name="gelu_slopes",
    )(expanded, mixed)


def lane_tiles(width):
    return [slice(at, at + LANES) for at in range(0, width, LANES)]


def window_places(own, cols):
    return [(r, q) for r in range(own) for q in range(cols // 8)]


def to_windows(source_ref, rows_wide, target):
    groups, own, cols, width = source_ref.shape
    span = groups * 8
    for tile, lanes in enumerate(lane_tiles(width)):
        for group in range(groups):
            rows_wide[tile, group] = source_ref[group, :, :, lanes].astype(F32)
        for index, (r, q) in enumerate(window_places(own, cols)):
            pieces = [
                rows_wide[tile, group, r, pl.ds(q, 8, stride=cols // 8), :] for group in range(groups)
            ]
            rows = slice(index * span, (index + 1) * span)
            target[rows, lanes] = jnp.concatenate(pieces, axis=0).astype(BF16)


def to_rows(values, rows_wide, target_ref):
    groups, own, cols, width = target_ref.shape
    span = groups * 8
    for tile, lanes in enumerate(lane_tiles(width)):
        for index, (r, q) in enumerate(window_places(own, cols)):
            for group in range(groups):
                first = index * span + group * 8
                rows_wide[tile, group, r, pl.ds(q, 8, stride=cols // 8), :] = values[first : first + 8, lanes]
        for group in range(groups):
            target_ref[group, :, :, lanes] = rows_wide[tile, group].astype(BF16)


def wide_scratch(shape):
    groups, own, cols, width = shape
    return pltpu.VMEM((width // LANES, groups, own, cols, LANES), F32)


def grad_attended_body(cotangent_ref, out_ref, grad_ref, rows_wide, in_windows):
    to_windows(cotangent_ref, rows_wide, in_windows)
    grad_ref[...] = nt_dot(in_windows[...], out_ref[...]).astype(BF16)


def attended_gradient(cotangent, w_out):
    groups, own, cols, width = cotangent.shape
    shape = (groups * own * cols, width)
    return pl.pallas_call(
        grad_attended_body,
        grid=(1,),
        in_specs=[whole(cotangent.shape), whole(w_out.shape)],
        out_specs=whole(shape),
        out_shape=jax.ShapeDtypeStruct(shape, BF16),
        scratch_shapes=[wide_scratch(cotangent.shape), pltpu.VMEM(shape, BF16)],
        compiler_params=params(),
        cost_estimate=pl.CostEstimate(
            flops=2 * shape[0] * width * width, bytes_accessed=2 * 1024 * 1024, transcendentals=0
        ),
        name="attended_gradient",
    )(cotangent, w_out)


def per_query(values, weights, span, head_dim, scale=1.0):
    wide = nn_dot(values.T, weights)
    half = LANES // 2
    own = jnp.concatenate([wide[:half, :LANES], wide[half:, LANES:]], axis=0) * scale
    own = own.astype(BF16).T
    lane_head = lax.broadcasted_iota(jnp.int32, (span, LANES), 1) // head_dim
    return jnp.where(lane_head % 2 == 0, own[:span].astype(F32), own[span:].astype(F32)).astype(BF16)


def attention_body(normed_ref, grad_attended_ref, qkv_ref, grad_ref, weights_ref, values_ref, rows_wide,
                   in_windows, projected, grad_projected, grad_attended, qkv, grad, weights, in_sems, out_sems):
    groups, own, cols, width = normed_ref.shape
    span = groups * 8
    windows = own * cols // 8
    head_dim = width // HEADS
    heads = LANES // head_dim
    scale = 1.0 / math.sqrt(head_dim)
    steepness = scale * math.log2(math.e)

    fetch_qkv = pltpu.make_async_copy(qkv_ref, qkv, in_sems.at[0])
    fetch_grad = pltpu.make_async_copy(grad_attended_ref, grad_attended, in_sems.at[1])
    fetch_qkv.start()
    fetch_grad.start()
    to_windows(normed_ref, rows_wide, in_windows)
    fetch_qkv.wait()
    projected[...] = nn_dot(in_windows[...], qkv[...]).astype(BF16)
    store_values = pltpu.make_async_copy(projected.at[:, pl.ds(2 * width, width)], values_ref, out_sems.at[0])
    store_values.start()
    fetch_grad.wait()

    row_head = lax.broadcasted_iota(jnp.int32, (heads * span, LANES), 0) // span
    lane_head = lax.broadcasted_iota(jnp.int32, (heads * span, LANES), 1) // head_dim
    mask = (row_head == lane_head).astype(F32).astype(BF16)

    def spread(values):
        return jnp.concatenate([values] * heads, axis=0) * mask

    parts = range(width // LANES)
    lane_places = [
        [slice(t * width + part * LANES, t * width + (part + 1) * LANES) for t in range(3)] for part in parts
    ]

    def two_windows(index, carry):
        places = []
        for number in (2 * index, 2 * index + 1):
            rows = pl.ds(pl.multiple_of(number * span, span), span)
            places += [(number, part, rows) + tuple(lane_places[part]) for part in parts]
        keys = [projected[rows, k_at] for _, _, rows, _, k_at, _ in places]
        q_wide = [spread(projected[rows, q_at]) for _, _, rows, q_at, _, _ in places]
        scores = [nt_dot(k, q) for k, q in zip(keys, q_wide)]
        g_wide = [spread(grad_attended[rows, q_at]) for _, _, rows, q_at, _, _ in places]
        grad_weights = [nt_dot(projected[place[2], place[5]], g) for place, g in zip(places, g_wide)]
        powers = [
            jnp.exp2((score - jnp.max(score, axis=0, keepdims=True)) * steepness) for score in scores
        ]
        shares = [power * (1.0 / jnp.sum(power, axis=0, keepdims=True)) for power in powers]
        halves = [share.astype(BF16) for share in shares]
        row_dots = [jnp.sum(s * g, axis=0, keepdims=True) for s, g in zip(shares, grad_weights)]
        grad_scores = [(s * (g - d)).astype(BF16) for s, g, d in zip(shares, grad_weights, row_dots)]
        for (number, part, *_), half in zip(places, halves):
            weights[number, :, part * heads * span : (part + 1) * heads * span] = half
        grad_values = [nn_dot(half, g) for half, g in zip(halves, g_wide)]
        grad_keys = [nn_dot(scored, q) for scored, q in zip(grad_scores, q_wide)]
        grad_queries = [per_query(k, scored, span, head_dim, scale) for k, scored in zip(keys, grad_scores)]
        for number, (_, _, rows, q_at, k_at, v_at) in enumerate(places):
            grad_projected[rows, v_at] = grad_values[number].astype(BF16)
            grad_projected[rows, k_at] = (grad_keys[number] * scale).astype(BF16)
            grad_projected[rows, q_at] = grad_queries[number]
        return carry

    lax.fori_loop(0, windows // 2, two_windows, 0, unroll=2)
    store_weights = pltpu.make_async_copy(weights, weights_ref, out_sems.at[1])
    store_weights.start()
    to_rows(nt_dot(grad_projected[...], qkv[...]), rows_wide, grad)
    store_grad = pltpu.make_async_copy(grad, grad_ref, out_sems.at[2])
    store_grad.start()
    store_values.wait()
    store_weights.wait()
    store_grad.wait()


def attention(normed, grad_attended, w_qkv):
    groups, own, cols, width = normed.shape
    span = groups * 8
    tokens = groups * own * cols
    out_shapes = [normed.shape, (tokens // span, span, HEADS * span), (tokens, width)]
    return pl.pallas_call(
        attention_body,
        in_specs=[in_vmem(), in_hbm(), in_hbm()],
        out_specs=[in_hbm()] * 3,
        out_shape=[pltpu.HBM(shape, BF16) for shape in out_shapes],
        scratch_shapes=[
            wide_scratch(normed.shape),
            pltpu.VMEM((tokens, width), BF16),
            pltpu.VMEM((tokens, 3 * width), BF16),
            pltpu.VMEM((tokens, 3 * width), BF16),
            pltpu.VMEM((tokens, width), BF16),
            pltpu.VMEM(w_qkv.shape, BF16),
            pltpu.VMEM(normed.shape, BF16),
            pltpu.VMEM(out_shapes[1], BF16),
            pltpu.SemaphoreType.DMA((2,)),
            pltpu.SemaphoreType.DMA((3,)),
        ],
        compiler_params=params(18),
        cost_estimate=pl.CostEstimate(
            flops=16 * tokens * width * width,
            bytes_accessed=4 * 1024 * 1024,
            transcendentals=tokens * span * HEADS,
        ),
        name="window_attention",
    )(near(normed), held(grad_attended), held(w_qkv))


def attended_body(weights_ref, values_ref, out_ref, added_ref, rows_wide, attended):
    windows, span, wide = weights_ref.shape
    width = values_ref.shape[1]
    heads = LANES * HEADS // width
    for index in range(windows):
        rows = slice(index * span, (index + 1) * span)
        for part, lanes in enumerate(lane_tiles(width)):
            weights = weights_ref[index, :, part * heads * span : (part + 1) * heads * span]
            attended[rows, lanes] = per_query(values_ref[rows, lanes], weights, span, width // HEADS)
    to_rows(nn_dot(attended[...], out_ref[...]), rows_wide, added_ref)


def attend(weights, values, w_out, shape):
    return pl.pallas_call(
        attended_body,
        grid=(1,),
        in_specs=[whole(weights.shape), whole(values.shape), whole(w_out.shape)],
        out_specs=whole(shape),
        out_shape=jax.ShapeDtypeStruct(shape, BF16),
        scratch_shapes=[wide_scratch(shape), pltpu.VMEM(values.shape, BF16)],
        compiler_params=params(),
        cost_estimate=pl.CostEstimate(
            flops=4 * values.size * values.shape[1], bytes_accessed=3 * 1024 * 1024, transcendentals=0
        ),
        name="attended_output",
    )(weights, values, w_out)


def backward_body(bands_ref, cotangent_ref, other_ref, rim_ref, slab_ref, first_ref, edges_ref, grad_slab_ref,
                  grad_ref, pair_ref, next_ref, slope_one_ref, slope_two_ref, expand_ref, taps_ref, project_ref,
                  out_ref, rims, slab, first, edges, grad_slab, grad_in, slope_one, slope_two, expand, project,
                  grad_first, grad_rows, mixed, expanded, total, row_sems,
                  in_sems, chunk_sems):
    own, cols, width = slab.shape
    chunks = expand_ref.shape[1] // CHUNK

    sources = (cotangent_ref, other_ref, rim_ref)
    sides = list(enumerate((-1, own)))
    for side, place_first in sides:
        start_pull(bands_ref, place_first, sources, 1, rims.at[pl.ds(side, 1)], row_sems.at[side], RIM)
    inputs = [
        pltpu.make_async_copy(source, target, in_sems.at[index])
        for index, (source, target) in enumerate(
            ((first_ref, first), (grad_ref, grad_in), (grad_slab_ref, grad_slab), (edges_ref, edges), (slab_ref, slab))
        )
    ]
    for copy in inputs:
        copy.start()

    def fetches(index):
        lanes = chunk_lanes(index)
        pairs = (
            (project_ref.at[lanes], project.at[lanes]),
            (slope_two_ref.at[:, :, lanes], slope_two.at[:, :, lanes]),
            (slope_one_ref.at[:, :, lanes], slope_one.at[:, :, lanes]),
            (expand_ref.at[:, lanes], expand.at[:, lanes]),
        )
        return [
            pltpu.make_async_copy(source, target, chunk_sems.at[number, index])
            for number, (source, target) in enumerate(pairs)
        ]

    for copy in fetches(0):
        copy.start()

    def through_norm(cotangent, grad, first):
        rms = rms_scale(first)
        normed = first * rms
        grad = grad.astype(F32)
        inner = jnp.mean(grad * normed, -1, keepdims=True)
        return cotangent.astype(F32) + rms * (grad - normed * inner)

    for copy in inputs[:4]:
        copy.wait()
    for row in range(own):
        at = slice(row * cols, (row + 1) * cols)
        result = through_norm(grad_slab[row], grad_in[row], first[at])
        grad_first[at] = result
        grad_rows[(row + 1) * cols : (row + 2) * cols] = result.astype(BF16)
    for side, place_first in sides:
        wait_pull(sources, 1, rims.at[pl.ds(side, 1)], row_sems.at[side])
    leads = lax.rem(lax.axis_index("row"), 2) == 0
    above = jnp.where(leads, next_ref[0].astype(F32), pair_ref[0].astype(F32))
    below = jnp.where(leads, pair_ref[0].astype(F32), next_ref[0].astype(F32))
    last = (own + 1) * cols
    grad_rows[0:cols] = through_norm(rims[0], above, edges[:cols]).astype(BF16)
    grad_rows[last:] = through_norm(rims[1], below, edges[cols:]).astype(BF16)
    column = lax.broadcasted_iota(jnp.int32, (cols, LANES), 0)

    total[...] = jnp.zeros_like(total)

    def step(index, carry):
        @pl.when(index + 1 < chunks)
        def _():
            for copy in fetches(index + 1):
                copy.start()

        for copy in fetches(index):
            copy.wait()
        for start in range(0, CHUNK, HALF):
            weights = project[chunk_lanes(index, start, HALF), :]
            for row in range(0, own + 2, GROUP_BACKWARD):
                product = nt_dot(grad_rows[row * cols : (row + GROUP_BACKWARD) * cols, :], weights)
                for inner in range(GROUP_BACKWARD):
                    for lane in range(0, HALF, LANES):
                        slope = slope_two[row + inner, :, chunk_lanes(index, start + lane, LANES)].astype(F32)
                        value = product[inner * cols : (inner + 1) * cols, lane : lane + LANES] * slope
                        at = slice(start + lane, start + lane + LANES)
                        mixed[row + inner, :, at] = value.astype(BF16).astype(F32)

        for lane in range(0, CHUNK, LANES):
            lanes = slice(lane, lane + LANES)
            taps = spread_taps(taps_ref, chunk_lanes(index, lane, LANES), cols)
            for row in range(own):
                rows_near = [mixed[row + a, :, lanes] for a in range(3)]
                sums = [
                    taps[8 - b] * rows_near[0] + taps[5 - b] * rows_near[1] + taps[2 - b] * rows_near[2]
                    for b in range(3)
                ]
                value = column_sums(sums[0], sums[1], sums[2], column, cols - 1)
                value = value * slope_one[row, :, chunk_lanes(index, lane, LANES)].astype(F32)
                expanded[row * cols : (row + 1) * cols, lanes] = value.astype(BF16)
        total[...] += nt_dot(expanded[...], expand[:, chunk_lanes(index)])
        return carry

    lax.fori_loop(0, chunks, step, 0)
    inputs[4].wait()
    for row in range(own):
        at = slice(row * cols, (row + 1) * cols)
        values = slab[row].astype(F32)
        rms = rms_scale(values)
        normed = values * rms
        grad = total[at]
        inner = jnp.mean(grad * normed, -1, keepdims=True)
        out_ref[row] = (grad_first[at] + rms * (grad - normed * inner)).astype(BF16)


def backward(bands, cotangent, other, rim, slab, first, edges, grad_slab, grad, pair_row, next_row, slope_one,
             slope_two, w_expand, kernel, w_project):
    own, cols, width = slab.shape
    hidden_width = w_expand.shape[1]
    chunks = hidden_width // CHUNK
    return pl.pallas_call(
        backward_body,
        in_specs=[in_scalars()] + [in_hbm()] * 8 + [in_vmem()] * 2 + [in_hbm()] * 3 + [in_vmem(), in_hbm()],
        out_specs=in_vmem(),
        out_shape=jax.ShapeDtypeStruct((own, cols, width), BF16),
        scratch_shapes=[
            pltpu.VMEM((2, cols, width), BF16),
            pltpu.VMEM((own, cols, width), BF16),
            pltpu.VMEM((own * cols, width), F32),
            pltpu.VMEM((2 * cols, width), F32),
            pltpu.VMEM((own, cols, width), BF16),
            pltpu.VMEM((own, cols, width), BF16),
            pltpu.VMEM((own, cols, hidden_width), BF16),
            pltpu.VMEM((own + 2, cols, hidden_width), BF16),
            pltpu.VMEM((width, hidden_width), BF16),
            pltpu.VMEM((hidden_width, width), BF16),
            pltpu.VMEM((own * cols, width), F32),
            pltpu.VMEM(((own + 2) * cols, width), BF16),
            pltpu.VMEM((own + 2, cols, CHUNK), F32),
            pltpu.VMEM((own * cols, CHUNK), BF16),
            pltpu.VMEM((own * cols, width), F32),
            pltpu.SemaphoreType.DMA((2,)),
            pltpu.SemaphoreType.DMA((5,)),
            pltpu.SemaphoreType.DMA((4, chunks)),
        ],
        compiler_params=params(26),
        cost_estimate=pl.CostEstimate(
            flops=16 * 10**9,
            bytes_accessed=48 * MIB,
            transcendentals=0,
        ),
        name="bottleneck_backward",
    )(bands, held(cotangent), held(other), held(rim), held(slab), held(first), held(edges), held(grad_slab), held(grad),
      near(pair_row), near(next_row), held(slope_one), held(slope_two), held(w_expand), near(kernel),
      held(w_project))


def window_groups(size):
    stride = size // 8
    return [[first + stride * k for k in range(8)] for first in range(stride)]


def exchange_windows(rows):
    groups = window_groups(lax.axis_size("row"))
    return lax.all_to_all(
        rows, "row", split_axis=0, concat_axis=0, tiled=True, axis_index_groups=groups
    )


def swap_pair(rows):
    size = lax.axis_size("row")
    return lax.ppermute(rows, "row", [(i, i ^ 1) for i in range(size)])


def swap_next(rows):
    size = lax.axis_size("row")
    pairs = [(i, i + 1) for i in range(1, size - 1, 2)]
    return lax.ppermute(rows, "row", pairs + [(j, i) for i, j in pairs])


def place_rows(even, other, leads, leader_share):
    size = GRID_ROWS
    first, second = even[:BAND], even[BAND:]
    share = jnp.where(leads, leader_share, 2 * size - leader_share)
    zeros = jnp.zeros_like(first)
    low = jnp.where(leads | (share == size), first, jnp.where(share < size, second, other))
    mid = jnp.where(share < size, zeros, jnp.where(leads | (share == size), second, first))
    high = jnp.where(share > size, jnp.where(leads, other, second), zeros)
    return jnp.concatenate([low, mid, high], 0)


def on_device(features, row_bands, w_expand, kernel, w_project, w_qkv, w_out, cotangent):
    capacity, cols, width = features.shape
    device = lax.axis_index("row")
    parity = device % 2
    leads = parity == 0

    rim = swap_next(rim_rows(row_bands, features, cotangent))
    other_cotangent = swap_pair(cotangent)
    other_features = swap_pair(features)
    grad_slab = even_rows(row_bands, cotangent, other_cotangent)

    grad_windows = exchange_windows(grad_slab)
    edges, first, normed, slab, expanded, mixed = forward(
        row_bands, features, other_features, rim, w_expand, kernel, w_project
    )
    normed, grad_windows = lax.optimization_barrier((normed, grad_windows))
    normed_windows = exchange_windows(normed)
    shape = (8, GRID_ROWS // 8, cols, width)
    slope_one, slope_two = slopes(expanded, mixed)
    grad_attended = attended_gradient(grad_windows.reshape(shape), w_out)
    normed_windows, slope_one, slope_two, grad_attended = lax.optimization_barrier(
        (normed_windows, slope_one, slope_two, grad_attended)
    )
    grad_normed, weights, values = attention(normed_windows.reshape(shape), grad_attended, w_qkv)
    grad_rows = exchange_windows(grad_normed.reshape(GRID_ROWS, cols, width))
    added = attend(weights, values, w_out, shape)
    leader_share = BAND * row_bands[device - parity]
    grad_rows, added, leader_share = lax.optimization_barrier((grad_rows, added, leader_share))
    top, bottom = grad_rows[:1], grad_rows[GRID_ROWS - 1 :]
    sent_next, sent_pair = jnp.where(leads, top, bottom), jnp.where(leads, bottom, top)
    added, sent_next, sent_pair = lax.optimization_barrier((added, sent_next, sent_pair))
    next_row, pair_row = swap_next(sent_next), swap_pair(sent_pair)
    added_rows = exchange_windows(added.reshape(GRID_ROWS, cols, width))
    grad_input = backward(
        row_bands, cotangent, other_cotangent, rim, slab, first, edges, grad_slab, grad_rows, pair_row, next_row,
        slope_one, slope_two, w_expand, kernel, w_project,
    )
    def sent(rows):
        return jnp.where(leads, rows[BAND:], rows[:BAND])

    other_grad = swap_pair(sent(grad_input))
    grad_input, added_rows = lax.optimization_barrier((grad_input, added_rows))
    final = (first.reshape(GRID_ROWS, cols, width) + added_rows.astype(F32)).astype(BF16)
    other_final = swap_pair(sent(final))
    return (
        place_rows(final, other_final, leads, leader_share),
        place_rows(grad_input, other_grad, leads, leader_share),
    )


def solution(mesh):
    return jax.shard_map(
        on_device,
        mesh=mesh,
        in_specs=(
            P(("parts", "row"), None, None),
            P("parts"),
            P(),
            P(),
            P(),
            P(),
            P(),
            P(("parts", "row"), None, None),
        ),
        out_specs=(P(("parts", "row"), None, None), P(("parts", "row"), None, None)),
        check_vma=False,
    )
```

```python
import math

import jax
import jax.numpy as jnp
from jax import lax
from jax.experimental import pallas as pl
from jax.experimental.pallas import tpu as pltpu
from jax.sharding import PartitionSpec as P

HEADS = 16
GRID_ROWS = 16
BAND = 8
RIM = 2
EPSILON = 1e-06
CHUNK = 512
HALF = 256
GROUP_FORWARD = 10
GROUP_BACKWARD = 9
LANES = 128
ROOT = math.sqrt(2.0 / math.pi)
CUBIC = 0.044715
F32 = jnp.float32
BF16 = jnp.bfloat16
MIB = 1024 * 1024


def nt_dot(left, right):
    return lax.dot_general(left, right, (((1,), (1,)), ((), ())), preferred_element_type=F32)


def tn_dot(left, right):
    return lax.dot_general(left, right, (((0,), (0,)), ((), ())), preferred_element_type=F32)


def nn_dot(left, right):
    return jnp.dot(left, right, preferred_element_type=F32)


def rms_scale(values):
    return lax.rsqrt(jnp.mean(values * values, -1, keepdims=True) + EPSILON)


def gelu_parts(v):
    square = v * v
    cdf = 0.5 + 0.5 * jnp.tanh(v * (ROOT + (ROOT * CUBIC) * square))
    return square, cdf, v * cdf


def gelu(v):
    return gelu_parts(v)[2]


def gelu_slope(v):
    square, cdf, value = gelu_parts(v)
    return cdf + (value - value * cdf) * (2.0 * ROOT + (6.0 * ROOT * CUBIC) * square)


def whole(shape, space=None):
    zeros = (0,) * len(shape)
    return pl.BlockSpec(shape, lambda *_: zeros)


def params(mebibytes=56):
    return pltpu.CompilerParams(vmem_limit_bytes=mebibytes * MIB)


def in_vmem():
    return pl.BlockSpec(memory_space=pltpu.VMEM)


def in_hbm():
    return pl.BlockSpec(memory_space=pltpu.HBM)


def held(array):
    return pltpu.with_memory_space_constraint(array, pltpu.HBM)


def near(array):
    return pltpu.with_memory_space_constraint(array, pltpu.VMEM)


def in_scalars():
    return pl.BlockSpec(memory_space=pltpu.SMEM)


def shares(bands_ref):
    device = lax.axis_index("row")
    parity = lax.rem(device, 2)
    return parity, BAND * bands_ref[device - parity], BAND * bands_ref[device]


def place(bands_ref, first):
    parity, leader_share, _ = shares(bands_ref)
    row = first + GRID_ROWS * parity
    beyond = (row < 0) | (row >= 2 * GRID_ROWS)
    in_leader = row < leader_share
    in_own = in_leader == (parity == 0)
    source = jnp.where(beyond, 2, jnp.where(in_own, 0, 1))
    return source, jnp.where(beyond, 0, jnp.where(in_leader, row, row - leader_share))


def start_pull(bands_ref, first, sources, rows, target, sem, rim_row=0):
    where, row = place(bands_ref, first)
    row = jnp.where(where == 2, rim_row, row)
    for number, source in enumerate(sources):

        @pl.when(where == number)
        def _():
            pltpu.make_async_copy(source.at[pl.ds(row, rows)], target, sem).start()


def wait_pull(sources, rows, target, sem):
    pltpu.make_async_copy(sources[0].at[pl.ds(0, rows)], target, sem).wait()


def even_body(bands_ref, own_ref, other_ref, out_ref, sems):
    targets = [out_ref.at[pl.ds(BAND * half, BAND)] for half in range(2)]
    for half in range(2):
        start_pull(bands_ref, BAND * half, (own_ref, other_ref), BAND, targets[half], sems.at[half])
    for half in range(2):
        wait_pull((own_ref,), BAND, targets[half], sems.at[half])


def even_rows(bands, own, other):
    return pl.pallas_call(
        even_body,
        in_specs=[in_scalars(), in_vmem(), in_vmem()],
        out_specs=in_hbm(),
        out_shape=pltpu.HBM((GRID_ROWS,) + own.shape[1:], own.dtype),
        scratch_shapes=[pltpu.SemaphoreType.DMA((2,))],
        compiler_params=params(8),
        name="even_rows",
    )(bands, near(own), near(other))


def rim_body(bands_ref, features_ref, cotangent_ref, out_ref, sems):
    parity, _, share = shares(bands_ref)
    leads = parity == 0
    copies = [
        pltpu.make_async_copy(
            features_ref.at[pl.ds(jnp.where(leads, 0, share - RIM), RIM)], out_ref.at[pl.ds(0, RIM)], sems.at[0]
        ),
        pltpu.make_async_copy(
            cotangent_ref.at[pl.ds(jnp.where(leads, 0, share - 1), 1)], out_ref.at[pl.ds(RIM, 1)], sems.at[1]
        ),
    ]
    for copy in copies:
        copy.start()
    for copy in copies:
        copy.wait()


def rim_rows(bands, features, cotangent):
    shape = (RIM + 1,) + features.shape[1:]
    return pl.pallas_call(
        rim_body,
        in_specs=[in_scalars(), in_hbm(), in_hbm()],
        out_specs=in_vmem(),
        out_shape=jax.ShapeDtypeStruct(shape, features.dtype),
        scratch_shapes=[pltpu.SemaphoreType.DMA((2,))],
        compiler_params=params(8),
        name="rim_rows",
    )(bands, held(features), held(cotangent))


def column_sums(left, mid, right, column, last):
    from_left = jnp.where(column == 0, 0.0, pltpu.roll(left, 1, 0))
    from_right = jnp.where(column == last, 0.0, pltpu.roll(right, last, 0))
    return mid + from_left + from_right


def spread_taps(taps_ref, lanes, cols):
    taps = taps_ref[:, lanes].astype(F32)
    return [jnp.broadcast_to(taps[i : i + 1], (cols, LANES)) for i in range(9)]


def chunk_lanes(index, lane=0, count=CHUNK):
    return pl.ds(pl.multiple_of(index * CHUNK + lane, LANES), count)


def forward_body(bands_ref, features_ref, other_ref, rim_ref, expand_ref, taps_ref, project_ref, first_ref,
                 own_first_ref, normed_ref, slab_ref, expanded_ref, mixed_ref, slab, normed_one, expand, project,
                 expanded, hidden, mixed, hidden_two, total, normed, row_sems,
                 weight_sems, chunk_sems, out_sems):
    rows, cols, width = slab.shape
    own = rows - 2 * RIM
    chunks = expand_ref.shape[1] // CHUNK

    sources = (features_ref, other_ref, rim_ref)
    pieces = [(0, RIM), (RIM, BAND), (RIM + BAND, BAND), (RIM + 2 * BAND, RIM)]
    for index, (first, count) in enumerate(pieces):
        start_pull(bands_ref, first - RIM, sources, count, slab.at[pl.ds(first, count)], row_sems.at[index])

    def fetch_expand(index):
        lanes = chunk_lanes(index)
        return pltpu.make_async_copy(expand_ref.at[:, lanes], expand.at[:, lanes], weight_sems.at[0, index])

    def fetch_project(index):
        lanes = chunk_lanes(index)
        return pltpu.make_async_copy(project_ref.at[lanes], project.at[lanes], weight_sems.at[1, index])

    def store_expanded(index):
        lanes = chunk_lanes(index)
        return pltpu.make_async_copy(
            expanded.at[:, :, lanes], expanded_ref.at[:, :, lanes], chunk_sems.at[0, index]
        )

    def store_mixed(index):
        lanes = chunk_lanes(index)
        return pltpu.make_async_copy(mixed.at[:, :, lanes], mixed_ref.at[:, :, lanes], chunk_sems.at[1, index])

    fetch_expand(0).start()
    fetch_project(0).start()
    for index, (first, count) in enumerate(pieces):
        wait_pull(sources, count, slab.at[pl.ds(first, count)], row_sems.at[index])
    store_slab = pltpu.make_async_copy(slab.at[pl.ds(RIM, own)], slab_ref, out_sems.at[0])
    store_slab.start()
    for row in range(0, rows, 2):
        at = slice(row * cols, (row + 2) * cols)
        values = slab[row : row + 2].astype(F32).reshape(2 * cols, width)
        normed_one[at] = (values * rms_scale(values)).astype(BF16)
    total[...] = slab[1 : rows - 1].astype(F32).reshape((rows - 2) * cols, width)
    column = lax.broadcasted_iota(jnp.int32, (cols, LANES), 0)

    def step(index, carry):
        @pl.when(index + 1 < chunks)
        def _():
            fetch_expand(index + 1).start()
            fetch_project(index + 1).start()

        fetch_expand(index).wait()
        for start in range(0, CHUNK, HALF):
            weights = expand[:, chunk_lanes(index, start, HALF)]
            for row in range(0, rows, GROUP_FORWARD):
                product = nn_dot(normed_one[row * cols : (row + GROUP_FORWARD) * cols, :], weights)
                for inner in range(GROUP_FORWARD):
                    for lane in range(0, HALF, LANES):
                        values = product[inner * cols : (inner + 1) * cols, lane : lane + LANES]
                        at = slice(start + lane, start + lane + LANES)
                        hidden[row + inner, :, at] = gelu(values).astype(BF16).astype(F32)
                        if RIM <= row + inner < RIM + own:
                            expanded[row + inner - RIM, :, chunk_lanes(index, start + lane, LANES)] = values.astype(BF16)
        store_expanded(index).start()

        for lane in range(0, CHUNK, LANES):
            lanes = slice(lane, lane + LANES)
            taps = spread_taps(taps_ref, chunk_lanes(index, lane, LANES), cols)
            for row in range(rows - 2):
                rows_near = [hidden[row + a, :, lanes] for a in range(3)]
                sums = [
                    taps[b] * rows_near[0] + taps[3 + b] * rows_near[1] + taps[6 + b] * rows_near[2] for b in range(3)
                ]
                values = column_sums(sums[0], sums[1], sums[2], column, cols - 1)
                hidden_two[row * cols : (row + 1) * cols, lanes] = gelu(values).astype(BF16)
                mixed[row, :, chunk_lanes(index, lane, LANES)] = values.astype(BF16)
        store_mixed(index).start()
        fetch_project(index).wait()
        total[...] += nn_dot(hidden_two[...], project[chunk_lanes(index), :])
        return carry

    lax.fori_loop(0, chunks, step, 0)
    for row in range(1, own + 1):
        first = total[row * cols : (row + 1) * cols]
        normed[row - 1] = (first * rms_scale(first)).astype(BF16)
    store_normed = pltpu.make_async_copy(normed, normed_ref, out_sems.at[1])
    store_above = pltpu.make_async_copy(total.at[pl.ds(0, cols)], first_ref.at[pl.ds(0, cols)], out_sems.at[2])
    store_below = pltpu.make_async_copy(
        total.at[pl.ds((own + 1) * cols, cols)], first_ref.at[pl.ds(cols, cols)], out_sems.at[3]
    )
    store_own = pltpu.make_async_copy(total.at[pl.ds(cols, own * cols)], own_first_ref, out_sems.at[4])
    store_normed.start()
    store_above.start()
    store_below.start()
    store_own.start()
    for index in range(chunks):
        store_expanded(index).wait()
        store_mixed(index).wait()
    store_slab.wait()
    store_normed.wait()
    store_above.wait()
    store_below.wait()
    store_own.wait()


def forward(bands, features, other, rim, w_expand, kernel, w_project):
    capacity, cols, width = features.shape
    own, rows = GRID_ROWS, GRID_ROWS + 2 * RIM
    hidden_width = w_expand.shape[1]
    chunks = hidden_width // CHUNK
    return pl.pallas_call(
        forward_body,
        in_specs=[in_scalars(), in_hbm(), in_vmem(), in_vmem(), in_hbm(), in_vmem(), in_hbm()],
        out_specs=[in_hbm()] * 6,
        out_shape=[
            pltpu.HBM((2 * cols, width), F32),
            pltpu.HBM((own * cols, width), F32),
            pltpu.HBM((own, cols, width), BF16),
            pltpu.HBM((own, cols, width), BF16),
            pltpu.HBM((own, cols, hidden_width), BF16),
            pltpu.HBM((rows - 2, cols, hidden_width), BF16),
        ],
        scratch_shapes=[
            pltpu.VMEM((rows, cols, width), BF16),
            pltpu.VMEM((rows * cols, width), BF16),
            pltpu.VMEM((width, hidden_width), BF16),
            pltpu.VMEM((hidden_width, width), BF16),
            pltpu.VMEM((own, cols, hidden_width), BF16),
            pltpu.VMEM((rows, cols, CHUNK), F32),
            pltpu.VMEM((rows - 2, cols, hidden_width), BF16),
            pltpu.VMEM(((rows - 2) * cols, CHUNK), BF16),
            pltpu.VMEM(((rows - 2) * cols, width), F32),
            pltpu.VMEM((own, cols, width), BF16),
            pltpu.SemaphoreType.DMA((4,)),
            pltpu.SemaphoreType.DMA((2, chunks)),
            pltpu.SemaphoreType.DMA((2, chunks)),
            pltpu.SemaphoreType.DMA((5,)),
        ],
        compiler_params=params(24),
        cost_estimate=pl.CostEstimate(
            flops=16 * 10**9,
            bytes_accessed=48 * MIB,
            transcendentals=2 * rows * cols * hidden_width,
        ),
        name="bottleneck_forward",
    )(bands, held(features), near(other), near(rim), held(w_expand), near(kernel), held(w_project))


def slopes_body(expanded_ref, mixed_ref, slope_one_ref, slope_two_ref):
    for source, target in ((expanded_ref, slope_one_ref), (mixed_ref, slope_two_ref)):
        rows, _, chunk = source.shape
        for row in range(rows):
            for lane in range(0, chunk, LANES):
                lanes = slice(lane, lane + LANES)
                target[row, :, lanes] = gelu_slope(source[row, :, lanes].astype(F32)).astype(BF16)


def slopes(expanded, mixed):
    hidden_width = expanded.shape[2]
    blocks = [
        pl.BlockSpec(values.shape[:2] + (CHUNK,), lambda j: (0, 0, j)) for values in (expanded, mixed)
    ]
    return pl.pallas_call(
        slopes_body,
        grid=(hidden_width // CHUNK,),
        in_specs=blocks,
        out_specs=blocks,
        out_shape=[jax.ShapeDtypeStruct(values.shape, BF16) for values in (expanded, mixed)],
        compiler_params=params(),
        cost_estimate=pl.CostEstimate(
            flops=15 * (expanded.size + mixed.size),
            bytes_accessed=6 * (expanded.size + mixed.size),
            transcendentals=expanded.size + mixed.size,
        ),
        name="gelu_slopes",
    )(expanded, mixed)


def lane_tiles(width):
    return [slice(at, at + LANES) for at in range(0, width, LANES)]


def window_places(own, cols):
    return [(r, q) for r in range(own) for q in range(cols // 8)]


def to_windows(source_ref, rows_wide, target):
    groups, own, cols, width = source_ref.shape
    span = groups * 8
    for tile, lanes in enumerate(lane_tiles(width)):
        for group in range(groups):
            rows_wide[tile, group] = source_ref[group, :, :, lanes].astype(F32)
        for index, (r, q) in enumerate(window_places(own, cols)):
            pieces = [
                rows_wide[tile, group, r, pl.ds(q, 8, stride=cols // 8), :] for group in range(groups)
            ]
            rows = slice(index * span, (index + 1) * span)
            target[rows, lanes] = jnp.concatenate(pieces, axis=0).astype(BF16)


def to_rows(values, rows_wide, target_ref, start=0):
    groups, own, cols, width = target_ref.shape
    span = groups * 8
    for tile, lanes in enumerate(lane_tiles(values.shape[1])):
        for index, (r, q) in enumerate(window_places(own, cols)):
            for group in range(groups):
                first = index * span + group * 8
                rows_wide[tile, group, r, pl.ds(q, 8, stride=cols // 8), :] = values[first : first + 8, lanes]
        for group in range(groups):
            at = slice(start + lanes.start, start + lanes.stop)
            target_ref[group, :, :, at] = rows_wide[tile, group].astype(BF16)


def wide_scratch(shape):
    groups, own, cols, width = shape
    return pltpu.VMEM((width // LANES, groups, own, cols, LANES), F32)


def grad_attended_body(cotangent_ref, out_ref, grad_ref, rows_wide, in_windows):
    to_windows(cotangent_ref, rows_wide, in_windows)
    grad_ref[...] = nt_dot(in_windows[...], out_ref[...]).astype(BF16)


def attended_gradient(cotangent, w_out):
    groups, own, cols, width = cotangent.shape
    shape = (groups * own * cols, width)
    return pl.pallas_call(
        grad_attended_body,
        grid=(1,),
        in_specs=[whole(cotangent.shape), whole(w_out.shape)],
        out_specs=whole(shape),
        out_shape=jax.ShapeDtypeStruct(shape, BF16),
        scratch_shapes=[wide_scratch(cotangent.shape), pltpu.VMEM(shape, BF16)],
        compiler_params=params(),
        cost_estimate=pl.CostEstimate(
            flops=2 * shape[0] * width * width, bytes_accessed=2 * 1024 * 1024, transcendentals=0
        ),
        name="attended_gradient",
    )(cotangent, w_out)


def per_query(values, weights, span, head_dim, scale=1.0):
    wide = nn_dot(values.T, weights)
    half = LANES // 2
    own = jnp.concatenate([wide[:half, :LANES], wide[half:, LANES:]], axis=0) * scale
    own = own.astype(BF16).T
    lane_head = lax.broadcasted_iota(jnp.int32, (span, LANES), 1) // head_dim
    return jnp.where(lane_head % 2 == 0, own[:span].astype(F32), own[span:].astype(F32)).astype(BF16)


def attention_body(normed_ref, grad_attended_ref, qkv_ref, grad_ref, weights_ref, values_ref, rows_wide,
                   in_windows, projected, grad_projected, grad_attended, qkv, grad, weights, in_sems, out_sems):
    groups, own, cols, width = normed_ref.shape
    span = groups * 8
    windows = own * cols // 8
    head_dim = width // HEADS
    heads = LANES // head_dim
    scale = 1.0 / math.sqrt(head_dim)
    steepness = scale * math.log2(math.e)

    fetch_qkv = pltpu.make_async_copy(qkv_ref, qkv, in_sems.at[0])
    fetch_grad = pltpu.make_async_copy(grad_attended_ref, grad_attended, in_sems.at[1])
    fetch_qkv.start()
    fetch_grad.start()
    to_windows(normed_ref, rows_wide, in_windows)
    fetch_qkv.wait()
    projected[...] = nn_dot(in_windows[...], qkv[...]).astype(BF16)
    store_values = pltpu.make_async_copy(projected.at[:, pl.ds(2 * width, width)], values_ref, out_sems.at[0])
    store_values.start()
    fetch_grad.wait()

    row_head = lax.broadcasted_iota(jnp.int32, (heads * span, LANES), 0) // span
    lane_head = lax.broadcasted_iota(jnp.int32, (heads * span, LANES), 1) // head_dim
    mask = (row_head == lane_head).astype(F32).astype(BF16)

    def spread(values):
        return jnp.concatenate([values] * heads, axis=0) * mask

    parts = range(width // LANES)
    lane_places = [
        [slice(t * width + part * LANES, t * width + (part + 1) * LANES) for t in range(3)] for part in parts
    ]

    def two_windows(index, carry):
        places = []
        for number in (2 * index, 2 * index + 1):
            rows = pl.ds(pl.multiple_of(number * span, span), span)
            places += [(number, part, rows) + tuple(lane_places[part]) for part in parts]
        keys = [projected[rows, k_at] for _, _, rows, _, k_at, _ in places]
        q_wide = [spread(projected[rows, q_at]) for _, _, rows, q_at, _, _ in places]
        scores = [nt_dot(k, q) for k, q in zip(keys, q_wide)]
        g_wide = [spread(grad_attended[rows, q_at]) for _, _, rows, q_at, _, _ in places]
        grad_weights = [nt_dot(projected[place[2], place[5]], g) for place, g in zip(places, g_wide)]
        powers = [
            jnp.exp2((score - jnp.max(score, axis=0, keepdims=True)) * steepness) for score in scores
        ]
        shares = [power * (1.0 / jnp.sum(power, axis=0, keepdims=True)) for power in powers]
        halves = [share.astype(BF16) for share in shares]
        row_dots = [jnp.sum(s * g, axis=0, keepdims=True) for s, g in zip(shares, grad_weights)]
        grad_scores = [(s * (g - d)).astype(BF16) for s, g, d in zip(shares, grad_weights, row_dots)]
        for (number, part, *_), half in zip(places, halves):
            weights[number, :, part * heads * span : (part + 1) * heads * span] = half
        grad_values = [nn_dot(half, g) for half, g in zip(halves, g_wide)]
        grad_keys = [nn_dot(scored, q) for scored, q in zip(grad_scores, q_wide)]
        grad_queries = [per_query(k, scored, span, head_dim, scale) for k, scored in zip(keys, grad_scores)]
        for number, (_, _, rows, q_at, k_at, v_at) in enumerate(places):
            grad_projected[rows, v_at] = grad_values[number].astype(BF16)
            grad_projected[rows, k_at] = (grad_keys[number] * scale).astype(BF16)
            grad_projected[rows, q_at] = grad_queries[number]
        return carry

    lax.fori_loop(0, windows // 2, two_windows, 0, unroll=2)
    store_weights = pltpu.make_async_copy(weights, weights_ref, out_sems.at[1])
    store_weights.start()
    stores = []
    half = width // 2
    for number in range(2):
        start = number * half
        to_rows(nt_dot(grad_projected[...], qkv[start : start + half, :]), rows_wide, grad, start)
        lanes = pl.ds(start, half)
        stores.append(
            pltpu.make_async_copy(grad.at[:, :, :, lanes], grad_ref.at[:, :, :, lanes], out_sems.at[2 + number])
        )
        stores[-1].start()
    store_values.wait()
    store_weights.wait()
    for store in stores:
        store.wait()


def attention(normed, grad_attended, w_qkv):
    groups, own, cols, width = normed.shape
    span = groups * 8
    tokens = groups * own * cols
    out_shapes = [normed.shape, (tokens // span, span, HEADS * span), (tokens, width)]
    return pl.pallas_call(
        attention_body,
        in_specs=[in_vmem(), in_hbm(), in_hbm()],
        out_specs=[in_hbm()] * 3,
        out_shape=[pltpu.HBM(shape, BF16) for shape in out_shapes],
        scratch_shapes=[
            wide_scratch(normed.shape),
            pltpu.VMEM((tokens, width), BF16),
            pltpu.VMEM((tokens, 3 * width), BF16),
            pltpu.VMEM((tokens, 3 * width), BF16),
            pltpu.VMEM((tokens, width), BF16),
            pltpu.VMEM(w_qkv.shape, BF16),
            pltpu.VMEM(normed.shape, BF16),
            pltpu.VMEM(out_shapes[1], BF16),
            pltpu.SemaphoreType.DMA((2,)),
            pltpu.SemaphoreType.DMA((4,)),
        ],
        compiler_params=params(18),
        cost_estimate=pl.CostEstimate(
            flops=16 * tokens * width * width,
            bytes_accessed=4 * 1024 * 1024,
            transcendentals=tokens * span * HEADS,
        ),
        name="window_attention",
    )(near(normed), held(grad_attended), held(w_qkv))


def attended_body(weights_ref, values_ref, out_ref, added_ref, rows_wide, attended):
    windows, span, wide = weights_ref.shape
    width = values_ref.shape[1]
    heads = LANES * HEADS // width
    for index in range(windows):
        rows = slice(index * span, (index + 1) * span)
        for part, lanes in enumerate(lane_tiles(width)):
            weights = weights_ref[index, :, part * heads * span : (part + 1) * heads * span]
            attended[rows, lanes] = per_query(values_ref[rows, lanes], weights, span, width // HEADS)
    to_rows(nn_dot(attended[...], out_ref[...]), rows_wide, added_ref)


def attend(weights, values, w_out, shape):
    return pl.pallas_call(
        attended_body,
        grid=(1,),
        in_specs=[whole(weights.shape), whole(values.shape), whole(w_out.shape)],
        out_specs=whole(shape),
        out_shape=jax.ShapeDtypeStruct(shape, BF16),
        scratch_shapes=[wide_scratch(shape), pltpu.VMEM(values.shape, BF16)],
        compiler_params=params(),
        cost_estimate=pl.CostEstimate(
            flops=4 * values.size * values.shape[1], bytes_accessed=3 * 1024 * 1024, transcendentals=0
        ),
        name="attended_output",
    )(weights, values, w_out)


def backward_body(bands_ref, cotangent_ref, other_ref, rim_ref, slab_ref, first_ref, edges_ref, grad_slab_ref,
                  grad_ref, pair_ref, next_ref, slope_one_ref, slope_two_ref, expand_ref, taps_ref, project_ref,
                  out_ref, rims, slab, first, edges, grad_slab, grad_in, slope_one, slope_two, expand, project,
                  grad_first, grad_rows, mixed, expanded, total, row_sems,
                  in_sems, chunk_sems):
    own, cols, width = slab.shape
    chunks = expand_ref.shape[1] // CHUNK

    sources = (cotangent_ref, other_ref, rim_ref)
    sides = list(enumerate((-1, own)))
    for side, place_first in sides:
        start_pull(bands_ref, place_first, sources, 1, rims.at[pl.ds(side, 1)], row_sems.at[side], RIM)
    inputs = [
        pltpu.make_async_copy(source, target, in_sems.at[index])
        for index, (source, target) in enumerate(
            ((first_ref, first), (grad_ref, grad_in), (grad_slab_ref, grad_slab), (edges_ref, edges), (slab_ref, slab))
        )
    ]
    for copy in inputs:
        copy.start()

    def fetches(index):
        lanes = chunk_lanes(index)
        pairs = (
            (project_ref.at[lanes], project.at[lanes]),
            (slope_two_ref.at[:, :, lanes], slope_two.at[:, :, lanes]),
            (slope_one_ref.at[:, :, lanes], slope_one.at[:, :, lanes]),
            (expand_ref.at[:, lanes], expand.at[:, lanes]),
        )
        return [
            pltpu.make_async_copy(source, target, chunk_sems.at[number, index])
            for number, (source, target) in enumerate(pairs)
        ]

    for copy in fetches(0):
        copy.start()

    def through_norm(cotangent, grad, first):
        rms = rms_scale(first)
        normed = first * rms
        grad = grad.astype(F32)
        inner = jnp.mean(grad * normed, -1, keepdims=True)
        return cotangent.astype(F32) + rms * (grad - normed * inner)

    for copy in inputs[:4]:
        copy.wait()
    for row in range(own):
        at = slice(row * cols, (row + 1) * cols)
        result = through_norm(grad_slab[row], grad_in[row], first[at])
        grad_first[at] = result
        grad_rows[(row + 1) * cols : (row + 2) * cols] = result.astype(BF16)
    for side, place_first in sides:
        wait_pull(sources, 1, rims.at[pl.ds(side, 1)], row_sems.at[side])
    leads = lax.rem(lax.axis_index("row"), 2) == 0
    above = jnp.where(leads, next_ref[0].astype(F32), pair_ref[0].astype(F32))
    below = jnp.where(leads, pair_ref[0].astype(F32), next_ref[0].astype(F32))
    last = (own + 1) * cols
    grad_rows[0:cols] = through_norm(rims[0], above, edges[:cols]).astype(BF16)
    grad_rows[last:] = through_norm(rims[1], below, edges[cols:]).astype(BF16)
    column = lax.broadcasted_iota(jnp.int32, (cols, LANES), 0)

    total[...] = jnp.zeros_like(total)

    def step(index, carry):
        @pl.when(index + 1 < chunks)
        def _():
            for copy in fetches(index + 1):
                copy.start()

        for copy in fetches(index):
            copy.wait()
        for start in range(0, CHUNK, HALF):
            weights = project[chunk_lanes(index, start, HALF), :]
            for row in range(0, own + 2, GROUP_BACKWARD):
                product = nt_dot(grad_rows[row * cols : (row + GROUP_BACKWARD) * cols, :], weights)
                for inner in range(GROUP_BACKWARD):
                    for lane in range(0, HALF, LANES):
                        slope = slope_two[row + inner, :, chunk_lanes(index, start + lane, LANES)].astype(F32)
                        value = product[inner * cols : (inner + 1) * cols, lane : lane + LANES] * slope
                        at = slice(start + lane, start + lane + LANES)
                        mixed[row + inner, :, at] = value.astype(BF16).astype(F32)

        for lane in range(0, CHUNK, LANES):
            lanes = slice(lane, lane + LANES)
            taps = spread_taps(taps_ref, chunk_lanes(index, lane, LANES), cols)
            for row in range(own):
                rows_near = [mixed[row + a, :, lanes] for a in range(3)]
                sums = [
                    taps[8 - b] * rows_near[0] + taps[5 - b] * rows_near[1] + taps[2 - b] * rows_near[2]
                    for b in range(3)
                ]
                value = column_sums(sums[0], sums[1], sums[2], column, cols - 1)
                value = value * slope_one[row, :, chunk_lanes(index, lane, LANES)].astype(F32)
                expanded[row * cols : (row + 1) * cols, lanes] = value.astype(BF16)
        total[...] += nt_dot(expanded[...], expand[:, chunk_lanes(index)])
        return carry

    lax.fori_loop(0, chunks, step, 0)
    inputs[4].wait()
    for row in range(own):
        at = slice(row * cols, (row + 1) * cols)
        values = slab[row].astype(F32)
        rms = rms_scale(values)
        normed = values * rms
        grad = total[at]
        inner = jnp.mean(grad * normed, -1, keepdims=True)
        out_ref[row] = (grad_first[at] + rms * (grad - normed * inner)).astype(BF16)


def backward(bands, cotangent, other, rim, slab, first, edges, grad_slab, grad, pair_row, next_row, slope_one,
             slope_two, w_expand, kernel, w_project):
    own, cols, width = slab.shape
    hidden_width = w_expand.shape[1]
    chunks = hidden_width // CHUNK
    return pl.pallas_call(
        backward_body,
        in_specs=[in_scalars()] + [in_hbm()] * 8 + [in_vmem()] * 2 + [in_hbm()] * 3 + [in_vmem(), in_hbm()],
        out_specs=in_vmem(),
        out_shape=jax.ShapeDtypeStruct((own, cols, width), BF16),
        scratch_shapes=[
            pltpu.VMEM((2, cols, width), BF16),
            pltpu.VMEM((own, cols, width), BF16),
            pltpu.VMEM((own * cols, width), F32),
            pltpu.VMEM((2 * cols, width), F32),
            pltpu.VMEM((own, cols, width), BF16),
            pltpu.VMEM((own, cols, width), BF16),
            pltpu.VMEM((own, cols, hidden_width), BF16),
            pltpu.VMEM((own + 2, cols, hidden_width), BF16),
            pltpu.VMEM((width, hidden_width), BF16),
            pltpu.VMEM((hidden_width, width), BF16),
            pltpu.VMEM((own * cols, width), F32),
            pltpu.VMEM(((own + 2) * cols, width), BF16),
            pltpu.VMEM((own + 2, cols, CHUNK), F32),
            pltpu.VMEM((own * cols, CHUNK), BF16),
            pltpu.VMEM((own * cols, width), F32),
            pltpu.SemaphoreType.DMA((2,)),
            pltpu.SemaphoreType.DMA((5,)),
            pltpu.SemaphoreType.DMA((4, chunks)),
        ],
        compiler_params=params(26),
        cost_estimate=pl.CostEstimate(
            flops=16 * 10**9,
            bytes_accessed=48 * MIB,
            transcendentals=0,
        ),
        name="bottleneck_backward",
    )(bands, held(cotangent), held(other), held(rim), held(slab), held(first), held(edges), held(grad_slab), held(grad),
      near(pair_row), near(next_row), held(slope_one), held(slope_two), held(w_expand), near(kernel),
      held(w_project))


def window_groups(size):
    stride = size // 8
    return [[first + stride * k for k in range(8)] for first in range(stride)]


def exchange_windows(rows):
    groups = window_groups(lax.axis_size("row"))
    return lax.all_to_all(
        rows, "row", split_axis=0, concat_axis=0, tiled=True, axis_index_groups=groups
    )


def swap_pair(rows):
    size = lax.axis_size("row")
    return lax.ppermute(rows, "row", [(i, i ^ 1) for i in range(size)])


def swap_next(rows):
    size = lax.axis_size("row")
    pairs = [(i, i + 1) for i in range(1, size - 1, 2)]
    return lax.ppermute(rows, "row", pairs + [(j, i) for i, j in pairs])


def place_rows(even, other, leads, leader_share):
    size = GRID_ROWS
    first, second = even[:BAND], even[BAND:]
    share = jnp.where(leads, leader_share, 2 * size - leader_share)
    zeros = jnp.zeros_like(first)
    low = jnp.where(leads | (share == size), first, jnp.where(share < size, second, other))
    mid = jnp.where(share < size, zeros, jnp.where(leads | (share == size), second, first))
    high = jnp.where(share > size, jnp.where(leads, other, second), zeros)
    return jnp.concatenate([low, mid, high], 0)


def on_device(features, row_bands, w_expand, kernel, w_project, w_qkv, w_out, cotangent):
    capacity, cols, width = features.shape
    device = lax.axis_index("row")
    parity = device % 2
    leads = parity == 0

    rim = swap_next(rim_rows(row_bands, features, cotangent))
    other_cotangent = swap_pair(cotangent)
    other_features = swap_pair(features)
    grad_slab = even_rows(row_bands, cotangent, other_cotangent)

    grad_windows = exchange_windows(grad_slab)
    edges, first, normed, slab, expanded, mixed = forward(
        row_bands, features, other_features, rim, w_expand, kernel, w_project
    )
    normed, grad_windows = lax.optimization_barrier((normed, grad_windows))
    normed_windows = exchange_windows(normed)
    shape = (8, GRID_ROWS // 8, cols, width)
    slope_one, slope_two = slopes(expanded, mixed)
    grad_attended = attended_gradient(grad_windows.reshape(shape), w_out)
    normed_windows, slope_one, slope_two, grad_attended = lax.optimization_barrier(
        (normed_windows, slope_one, slope_two, grad_attended)
    )
    grad_normed, weights, values = attention(normed_windows.reshape(shape), grad_attended, w_qkv)
    grad_rows = exchange_windows(grad_normed.reshape(GRID_ROWS, cols, width))
    added = attend(weights, values, w_out, shape)
    leader_share = BAND * row_bands[device - parity]
    grad_rows, added, leader_share = lax.optimization_barrier((grad_rows, added, leader_share))
    top, bottom = grad_rows[:1], grad_rows[GRID_ROWS - 1 :]
    sent_next, sent_pair = jnp.where(leads, top, bottom), jnp.where(leads, bottom, top)
    added, sent_next, sent_pair = lax.optimization_barrier((added, sent_next, sent_pair))
    next_row, pair_row = swap_next(sent_next), swap_pair(sent_pair)
    added_rows = exchange_windows(added.reshape(GRID_ROWS, cols, width))
    grad_input = backward(
        row_bands, cotangent, other_cotangent, rim, slab, first, edges, grad_slab, grad_rows, pair_row, next_row,
        slope_one, slope_two, w_expand, kernel, w_project,
    )
    def sent(rows):
        return jnp.where(leads, rows[BAND:], rows[:BAND])

    other_grad = swap_pair(sent(grad_input))
    grad_input, added_rows = lax.optimization_barrier((grad_input, added_rows))
    final = (first.reshape(GRID_ROWS, cols, width) + added_rows.astype(F32)).astype(BF16)
    other_final = swap_pair(sent(final))
    return (
        place_rows(final, other_final, leads, leader_share),
        place_rows(grad_input, other_grad, leads, leader_share),
    )


def solution(mesh):
    return jax.shard_map(
        on_device,
        mesh=mesh,
        in_specs=(
            P(("parts", "row"), None, None),
            P("parts"),
            P(),
            P(),
            P(),
            P(),
            P(),
            P(("parts", "row"), None, None),
        ),
        out_specs=(P(("parts", "row"), None, None), P(("parts", "row"), None, None)),
        check_vma=False,
    )
```
